32 devices in a mesh: pipe: 4 (over y, x), dp: 8 (over z, core).
Axes of the slice: x: 2, y: 2, z: 4, core: 2. Of those that a mesh axis runs over, the one named last changes fastest.
Arguments:
- inputs: bfloat16 [4, 16, 784, 384], P(None, 'dp'), may hold values from -6 to 6
- cotangent: bfloat16 [4, 16, 784, 384], P(None, 'dp'), may hold values from -6 to 6
- pad_mask: int32 [4, 16, 784], P(None, 'dp'), may hold values from 0 to 1, as said below
- region_ids: int32 [4, 16, 784], P(None, 'dp'), may hold values from 0 to 35, as said below
- norm1_gain: float32 [2, 384], P(None, 'dp'), may hold values from 0.5 to 1.5
- norm1_bias: float32 [2, 384], P(None, 'dp'), may hold values from -1.5 to 1.5
- qkv_weight: float32 [2, 384, 1152], P(None, 'dp'), may hold values from -0.3125 to 0.3125
- qv_bias: float32 [2, 768], P(None, 'dp'), may hold values from -3 to 3
- rel_table: float32 [2, 169, 12], replicated, may hold values from -4 to 4
- proj_weight: float32 [2, 384, 384], P(None, 'dp'), may hold values from -0.875 to 0.875
- proj_bias: float32 [2, 384], P(None, 'dp'), may hold values from -1.5 to 1.5
- norm2_gain: float32 [2, 384], P(None, 'dp'), may hold values from 0.5 to 1.5
- norm2_bias: float32 [2, 384], P(None, 'dp'), may hold values from -1.5 to 1.5
- fc1_weight: float32 [2, 384, 1536], P(None, 'dp'), may hold values from -0.3125 to 0.3125
- fc1_bias: float32 [2, 1536], P(None, 'dp'), may hold values from -3 to 3
- fc2_weight: float32 [2, 1536, 384], P(None, 'dp'), may hold values from -0.21875 to 0.21875
- fc2_bias: float32 [2, 384], P(None, 'dp'), may hold values from -1.5 to 1.5
Outputs:
- activations: bfloat16 [4, 4, 16, 784, 384], P('pipe', None, 'dp')
- input_grads: bfloat16 [4, 4, 16, 784, 384], P('pipe', None, 'dp')
- grad_norm1_gain: float32 [2, 384], P(None, 'dp')
- grad_norm1_bias: float32 [2, 384], P(None, 'dp')
- grad_qkv_weight: float32 [2, 384, 1152], P(None, 'dp')
- grad_qv_bias: float32 [2, 768], P(None, 'dp')
- grad_rel_table: float32 [2, 169, 12], replicated
- grad_proj_weight: float32 [2, 384, 384], P(None, 'dp')
- grad_proj_bias: float32 [2, 384], P(None, 'dp')
- grad_norm2_gain: float32 [2, 384], P(None, 'dp')
- grad_norm2_bias: float32 [2, 384], P(None, 'dp')
- grad_fc1_weight: float32 [2, 384, 1536], P(None, 'dp')
- grad_fc1_bias: float32 [2, 1536], P(None, 'dp')
- grad_fc2_weight: float32 [2, 1536, 384], P(None, 'dp')
- grad_fc2_bias: float32 [2, 384], P(None, 'dp')
The draws below stay inside these ranges and needn't reach their ends.
Inputs may be any that keep to these rules, and one draw needn't show every extreme that they name: `pad_mask`: 1 marks a cell of an image. A canvas holds either four equal square images, one in each quarter of the canvas, all real, or one image of 24 x 24 cells in its upper left corner with the rest padding. `region_ids`: cells of different images have different ids; within an image, cells share an id exactly when they lie in the same one of three bands of rows and of columns (the first 3, then up to 4 before the image's padded end, then the rest).
All inputs are finite; a program needn't handle non-finite values.
Results may differ from the reference program's by a relative error of at most 0.018.
Values may be sent and summed in bfloat16 or wider, within the bound.
A program may use at most 192 MiB of HBM per device.

```python
import jax
import jax.numpy as jnp
from jax import lax

D = 384
HEADS = 12
FF = 1536
WIN = 7
SHIFT = 3
GRID = 28
IMAGE = 24
BLOCKS = 2
MICRO = 4
HEAD = 32
CELLS = 784
TABLE = 169
CANVASES = 16
N_PIPE = 4


def band_class(position, extent):
    return jnp.where(position < SHIFT, 0, jnp.where(position < extent - (WIN - SHIFT), 1, 2))


def canvas_layout(key):
    canvas_kind = jax.random.randint(jax.random.fold_in(key, 71), (MICRO, CANVASES), 0, 2)
    canvas_kind = canvas_kind.at[0, 0].set(0).at[0, 1].set(1)
    labels = jax.random.permutation(jax.random.fold_in(key, 72), 36).astype(jnp.int32)
    cell_ids = jnp.arange(CELLS)
    row_pos = cell_ids // GRID
    col_pos = cell_ids % GRID
    half_side = GRID // 2
    four_image = row_pos // half_side * 2 + col_pos // half_side
    four_class = band_class(row_pos % half_side, half_side) * 3 + band_class(col_pos % half_side, half_side)
    one_class = band_class(row_pos, GRID) * 3 + band_class(col_pos, GRID)
    four_label = labels[four_image * 9 + four_class]
    one_label = labels[one_class]
    real_one = ((row_pos < IMAGE) & (col_pos < IMAGE)).astype(jnp.int32)
    is_single = canvas_kind[:, :, None] == 1
    pad_cells = jnp.where(is_single, real_one[None, None, :], 1)
    region_cells = jnp.where(is_single, one_label[None, None, :], four_label[None, None, :])
    return (pad_cells.astype(jnp.int32), region_cells.astype(jnp.int32))


def draw_pad_mask(key, part):
    shared = canvas_layout(key)
    return shared[0]


def draw_region_ids(key, part):
    shared = canvas_layout(key)
    return shared[1]


def level_of(rng, shape, cuts, low, top_value):
    level = 1.0
    for axis_at, parts in cuts:
        draws = jax.random.uniform(jax.random.fold_in(jax.random.fold_in(rng, 6), axis_at), (parts,), jnp.float32, low / len(cuts), top_value / len(cuts))
        level = level * jnp.repeat(jnp.exp(draws), shape[axis_at] // parts).reshape((-1,) + (1,) * (len(shape) - 1 - axis_at))
    return level


def gaussian(own_key, dims, width, reach, cuts=(), dtype=jnp.bfloat16):
    level = level_of(own_key, dims, cuts, -0.22, 0.18) if cuts else 1.0
    array = jax.random.normal(own_key, dims, jnp.float32) * width * level
    return jnp.minimum(jnp.maximum(array, -reach), reach).astype(dtype)


def setup_inputs(seed: int = 0) -> dict:
    streams_of = jax.random.split(jax.random.key(seed), 18)
    return {
        "inputs": gaussian(streams_of[0], (MICRO, CANVASES, CELLS, D), 1.0, 6.0, ((1, 8),)),
        "cotangent": gaussian(streams_of[1], (MICRO, CANVASES, CELLS, D), 1.0, 6.0, ((1, 8),)),
        "pad_mask": draw_pad_mask(jax.random.fold_in(streams_of[17], 71), 0),
        "region_ids": draw_region_ids(jax.random.fold_in(streams_of[17], 71), 0),
        "norm1_gain": jnp.clip(1.0 + 0.1 * jax.random.normal(streams_of[4], (BLOCKS, D), jnp.float32), 0.5, 1.5),
        "norm1_bias": gaussian(streams_of[5], (BLOCKS, D), 0.3, 1.5, ((1, 8),), jnp.float32),
        "qkv_weight": gaussian(streams_of[6], (BLOCKS, D, 3 * D), D ** -0.5, 0.3125, ((1, 8),), jnp.float32),
        "qv_bias": gaussian(streams_of[7], (BLOCKS, 2 * D), 0.5, 3.0, ((1, 8),), jnp.float32),
        "rel_table": gaussian(streams_of[8], (BLOCKS, TABLE, HEADS), 1.0, 4.0, (), jnp.float32),
        "proj_weight": gaussian(streams_of[9], (BLOCKS, D, D), (D // 8) ** -0.5, 0.875, ((1, 8),), jnp.float32),
        "proj_bias": gaussian(streams_of[10], (BLOCKS, D), 0.3, 1.5, ((1, 8),), jnp.float32),
        "norm2_gain": jnp.clip(1.0 + 0.1 * jax.random.normal(streams_of[11], (BLOCKS, D), jnp.float32), 0.5, 1.5),
        "norm2_bias": gaussian(streams_of[12], (BLOCKS, D), 0.3, 1.5, ((1, 8),), jnp.float32),
        "fc1_weight": gaussian(streams_of[13], (BLOCKS, D, FF), D ** -0.5, 0.3125, ((1, 8),), jnp.float32),
        "fc1_bias": gaussian(streams_of[14], (BLOCKS, FF), 0.5, 3.0, ((1, 8),), jnp.float32),
        "fc2_weight": gaussian(streams_of[15], (BLOCKS, FF, D), (FF // 2) ** -0.5, 0.21875, ((1, 8),), jnp.float32),
        "fc2_bias": gaussian(streams_of[16], (BLOCKS, D), 0.3, 1.5, ((1, 8),), jnp.float32),
    }


@jax.custom_vjp
def low(v):
    return lax.optimization_barrier(v.astype(jnp.bfloat16)).astype(jnp.float32)

@jax.custom_vjp
def low_back(v):
    return v

def low_keep(v):
    return (low(v), None)

def low_pass(kept, grad):
    return (grad,)

def back_keep(v):
    return (v, None)

def back_low(kept, grad):
    return (low(grad),)
low.defvjp(low_keep, low_pass)
low_back.defvjp(back_keep, back_low)
norm_eps = 1e-05
masked_score = -1e+30
group_size = 4
highest = lax.Precision.HIGHEST

def layer_norm(values, gain, bias):
    mean_val = lax.optimization_barrier(jnp.mean(values, axis=-1, keepdims=True))
    centered = values - mean_val
    spread = lax.optimization_barrier(jnp.mean(centered * centered, axis=-1, keepdims=True))
    return centered * lax.rsqrt(spread + norm_eps) * gain + bias

def window_view(values, shift_cells):
    canvases = values.shape[0]
    channels = values.shape[-1]
    side_count = GRID // WIN
    mapped = values.reshape(canvases, GRID, GRID, channels)
    mapped = jnp.roll(mapped, (-shift_cells, -shift_cells), axis=(1, 2))
    mapped = mapped.reshape(canvases, side_count, WIN, side_count, WIN, channels).transpose(0, 1, 3, 2, 4, 5)
    return mapped.reshape(canvases * side_count * side_count, WIN * WIN, channels)

def canvas_view(values, shift_cells, canvases):
    channels = values.shape[-1]
    side_count = GRID // WIN
    mapped = values.reshape(canvases, side_count, side_count, WIN, WIN, channels).transpose(0, 1, 3, 2, 4, 5)
    mapped = mapped.reshape(canvases, GRID, GRID, channels)
    mapped = jnp.roll(mapped, (shift_cells, shift_cells), axis=(1, 2))
    return mapped.reshape(canvases, CELLS, channels)

def position_onehot():
    cell_ids = jnp.arange(WIN * WIN)
    row_pos = cell_ids // WIN
    col_pos = cell_ids % WIN
    index_map = (row_pos[:, None] - row_pos[None, :] + WIN - 1) * (2 * WIN - 1) + col_pos[:, None] - col_pos[None, :] + WIN - 1
    return (index_map[:, :, None] == jnp.arange(TABLE)[None, None, :]).astype(jnp.float32)

def attention_section(incoming, params, table, pad_rows, region_rows, shift_cells):
    gain, bias, qkv_w, qv_b, proj_w, proj_b = params
    canvases = incoming.shape[0]
    normed = low(layer_norm(incoming, gain, bias))
    q_bias, v_bias = jnp.split(qv_b, 2)
    bias_full = jnp.concatenate([q_bias, jnp.zeros_like(q_bias), v_bias])
    qkv = low(low_back(jnp.einsum('ncd,de->nce', normed, qkv_w, precision=highest) + bias_full))
    windows = window_view(qkv, shift_cells)
    window_count = windows.shape[0]
    queries = windows[:, :, :D].reshape(window_count, WIN * WIN, HEADS, HEAD)
    key_heads = windows[:, :, D:2 * D].reshape(window_count, WIN * WIN, HEADS, HEAD)
    value_heads = windows[:, :, 2 * D:].reshape(window_count, WIN * WIN, HEADS, HEAD)
    rel_bias = jnp.einsum('ijt,th->hij', position_onehot(), table, precision=highest)
    scores = jnp.einsum('wihd,wjhd->whij', queries, key_heads, precision=highest) * HEAD ** (-0.5) + rel_bias[None]
    pad_win = window_view(pad_rows[:, :, None], shift_cells)[:, :, 0]
    region_win = window_view(region_rows[:, :, None], shift_cells)[:, :, 0]
    same_region = region_win[:, :, None] == region_win[:, None, :]
    open_key = (pad_win[:, None, :] == 1) | (pad_win[:, :, None] == 0)
    allowed = (same_region & open_key)[:, None]
    scores = low_back(jnp.where(allowed, scores, masked_score))
    row_top = lax.optimization_barrier(jnp.max(scores, axis=-1, keepdims=True))
    exponent = jnp.exp(scores - row_top)
    softmaxed = exponent / lax.optimization_barrier(jnp.sum(exponent, axis=-1, keepdims=True))
    attended = jnp.einsum('whij,wjhd->wihd', low(softmaxed), value_heads, precision=highest)
    attended = low(low_back(attended.reshape(window_count, WIN * WIN, D)))
    merged = canvas_view(attended, shift_cells, canvases)
    return incoming + (jnp.einsum('ncd,de->nce', merged, proj_w, precision=highest) + proj_b)

def mlp_section(incoming, params):
    gain, bias, fc1_w, fc1_b, fc2_w, fc2_b = params
    normed = low(layer_norm(incoming, gain, bias))
    pre_act = low_back(jnp.einsum('ncd,df->ncf', normed, fc1_w, precision=highest) + fc1_b)
    hidden = low(jax.nn.gelu(pre_act, approximate=False))
    return incoming + (jnp.einsum('ncf,fd->ncd', hidden, fc2_w, precision=highest) + fc2_b)

def forward(masters, tap_values, inputs_one, pad_one, region_one):
    lowered = [low(master) for master in masters]
    flowing = inputs_one
    outputs = []
    for section_id in range(N_PIPE):
        block_id = section_id // 2
        incoming = low_back(flowing + tap_values[section_id])
        own = [master[block_id] for master in lowered]
        if section_id % 2 == 0:
            summed = attention_section(incoming, (own[0], own[1], own[2], own[3], own[5], own[6]), own[4], pad_one, region_one * block_id, SHIFT * block_id)
        else:
            summed = mlp_section(incoming, (own[7], own[8], own[9], own[10], own[11], own[12]))
        flowing = low(summed)
        outputs.append(flowing)
    return (flowing, jnp.stack(outputs))

def reference(inputs, cotangent, pad_mask, region_ids, norm1_gain, norm1_bias, qkv_weight, qv_bias, rel_table, proj_weight, proj_bias, norm2_gain, norm2_bias, fc1_weight, fc1_bias, fc2_weight, fc2_bias):
    masters = (norm1_gain, norm1_bias, qkv_weight, qv_bias, rel_table, proj_weight, proj_bias, norm2_gain, norm2_bias, fc1_weight, fc1_bias, fc2_weight, fc2_bias)
    groups = MICRO * CANVASES // group_size
    inputs_g = inputs.astype(jnp.float32).reshape(groups, group_size, CELLS, D)
    cot_g = cotangent.astype(jnp.float32).reshape(groups, group_size, CELLS, D)
    pad_g = pad_mask.reshape(groups, group_size, CELLS)
    region_g = region_ids.reshape(groups, group_size, CELLS)

    def group_step(totals, group_item):
        inputs_one, cot_one, pad_one, region_one = group_item
        tap_zeros = jnp.zeros((N_PIPE, group_size, CELLS, D), jnp.float32)

        def wrapped(masters_in, taps_in):
            return forward(masters_in, taps_in, inputs_one, pad_one, region_one)
        final_out, pullback, section_outs = jax.vjp(wrapped, masters, tap_zeros, has_aux=True)
        grad_masters, grad_taps = pullback(cot_one)
        totals = jax.tree.map(jnp.add, totals, grad_masters)
        return (totals, (section_outs.astype(jnp.bfloat16), grad_taps.astype(jnp.bfloat16)))
    zero_totals = jax.tree.map(jnp.zeros_like, masters)
    totals, (section_outs, tap_grads) = lax.scan(group_step, zero_totals, (inputs_g, cot_g, pad_g, region_g))
    activations = section_outs.transpose(1, 0, 2, 3, 4).reshape(N_PIPE, MICRO, CANVASES, CELLS, D)
    input_grads = tap_grads.transpose(1, 0, 2, 3, 4).reshape(N_PIPE, MICRO, CANVASES, CELLS, D)
    return (activations, input_grads, totals[0], totals[1], totals[2], totals[3], totals[4], totals[5], totals[6], totals[7], totals[8], totals[9], totals[10], totals[11], totals[12])
```

```python
import functools

import jax
import jax.numpy as jnp
import numpy as np
from jax import lax
from jax.experimental import pallas as pl
from jax.experimental.pallas import tpu as pltpu
from jax.sharding import PartitionSpec as P

HEADS = 12
WIN = 7
SHIFT = 3
GRID = 28
CELLS = 784
D = 384
FF = 1536
HEAD = 32
SIDE = 4
WINDOWS = 16
PLACES = 64
WROWS = WINDOWS * PLACES
GROUPS = 3
TILE = 112
SCALE = HEAD**-0.5
NORM_EPS = 1e-05
MASKED = -1e30
BF = jnp.bfloat16
F32 = jnp.float32

ERF_P = 0.3275911 / np.sqrt(2.0)
ERF_A = [0.5 * a for a in (0.254829592, -0.284496736, 1.421413741, -1.453152027, 1.061405429)]
PHI_0 = 1.0 / np.sqrt(2.0 * np.pi)


def nn(a, b):
    return lax.dot_general(a, b, (((1,), (0,)), ((), ())), preferred_element_type=F32)


def nt(a, b):
    return lax.dot_general(a, b, (((1,), (1,)), ((), ())), preferred_element_type=F32)


def tn(a, b):
    return lax.dot_general(a, b, (((0,), (0,)), ((), ())), preferred_element_type=F32)


def segments(shift):
    runs = []
    for wr in range(SIDE):
        for r in range(WIN):
            row = (wr * WIN + r + shift) % GRID
            for wc in range(SIDE):
                col = (wc * WIN + shift) % GRID
                place = (wr * SIDE + wc) * PLACES + r * 8
                first = min(WIN, GRID - col)
                runs.append((row * GRID + col, place, first))
                if first < WIN:
                    runs.append((row * GRID, place + first, WIN - first))
    return runs


def to_windows(src, dst, shift):
    for cell, place, count in segments(shift):
        dst[pl.ds(place, count), :] = src[pl.ds(cell, count), :]


def to_canvas(src, dst, shift):
    for cell, place, count in segments(shift):
        dst[pl.ds(cell, count), :] = src[pl.ds(place, count), :]


def row_block(t, size):
    return pl.ds(pl.multiple_of(t * size, 16), size)


def standardized(v):
    centered = v - jnp.mean(v, axis=-1, keepdims=True)
    spread = jnp.mean(centered * centered, axis=-1, keepdims=True)
    rs = lax.rsqrt(spread + NORM_EPS)
    return centered * rs, rs


def by_eights(v):
    return jnp.sum(v.reshape(v.shape[0] // 8, 8, v.shape[1]), axis=0)


def gelu_parts(x):
    den = 1.0 + ERF_P * jnp.abs(x)
    t = pl.reciprocal(den, approx=True)
    t = t * (2.0 - den * t)
    e = jnp.exp(-0.5 * x * x)
    poly = ERF_A[4]
    for a in ERF_A[3::-1]:
        poly = poly * t + a
    tail = poly * t * e
    cdf = jnp.where(x >= 0.0, 1.0 - tail, tail)
    return x * cdf, cdf + x * (e * PHI_0)


def head_of_lane():
    return lax.broadcasted_iota(jnp.int32, (PLACES, 128), 1) >> 5


def by_head(x, lanes):
    zero = jnp.zeros_like(x)
    return jnp.concatenate([jnp.where(lanes == h, x, zero) for h in range(4)], axis=0)


def own_head(wide, lanes):
    out = wide[3 * PLACES :]
    for h in (2, 1, 0):
        out = jnp.where(lanes == h, wide[h * PLACES : (h + 1) * PLACES], out)
    return out


def kernel(
    canvases,
    x_hbm,
    cot_hbm,
    code_hbm,
    wqkv,
    wproj,
    fc1,
    fc2,
    vec,
    bias,
    act_hbm,
    igrad_hbm,
    g_qkv,
    g_proj,
    g_fc1,
    g_fc2t,
    g_vec,
    g_tab,
    xin,
    cot,
    code,
    codew,
    act,
    igrad,
    hqw,
    qkv,
    probs,
    att,
    hq2,
    hid,
    dgelu,
    canvf,
    winf,
    winz,
    gzw,
    go,
    gqkv,
    wide_t,
    in_sem,
    out_sem,
):
    for ref in (g_qkv, g_proj, g_fc1, g_fc2t):
        for b in range(2):

            @pl.loop(0, D // 16)
            def _(i):
                ref[b, row_block(i, 16), :] = jnp.zeros((16, ref.shape[2]), F32)

    g_vec[...] = jnp.zeros_like(g_vec)
    g_tab[...] = jnp.zeros_like(g_tab)
    winf[...] = jnp.zeros_like(winf)
    codew[...] = jnp.zeros_like(codew)

    def vector(b, kind, width=D):
        return vec[b, kind : kind + 1, :width]

    def add_vec(b, kind, part, start=0):
        g_vec[b, kind, :, start : start + part.shape[1]] += part

    def attention_forward(b, x, out):
        lanes = head_of_lane()

        @pl.loop(0, CELLS // TILE)
        def _(t):
            rows = row_block(t, TILE)
            xhat, _ = standardized(x[rows, :].astype(F32))
            canvf[rows, :] = xhat * vector(b, 0) + vector(b, 1)

        to_windows(canvf, winf, SHIFT * b)
        to_windows(code, codew, SHIFT * b)

        @pl.loop(0, 4)
        def _(t):
            rows = row_block(t, 256)
            hq = winf[rows, :].astype(BF)
            hqw[b, rows, :] = hq
            for part in range(3):
                cols = slice(part * D, (part + 1) * D)
                acc = nn(hq, wqkv[b, :, cols]) + vec[b, 6:7, cols]
                if part == 0:
                    acc = acc * SCALE
                qkv[b, rows, cols] = acc.astype(BF)

        @pl.loop(0, WINDOWS)
        def _(w):
            rows = row_block(w, PLACES)
            cells = codew[rows, :]
            region = (cells >> 1) * b
            pad = (cells & 1).astype(F32)
            lane = lax.broadcasted_iota(jnp.int32, (PLACES, 128), 1)
            same = jnp.where(lane == region, 1.0, 0.0)
            left = jnp.where(lane == 127, 1.0 - pad, same).astype(BF)
            right = jnp.where(lane == 127, -pad, same).astype(BF)
            agree = nt(left, jnp.concatenate([right, right], axis=0))
            mask = jnp.where(agree > 0.5, 0.0, MASKED)
            mask = jnp.concatenate([mask, mask], axis=1)
            for g in range(GROUPS):
                q = qkv[b, rows, g * 128 : (g + 1) * 128]
                k = qkv[b, rows, D + g * 128 : D + (g + 1) * 128]
                v = qkv[b, rows, 2 * D + g * 128 : 2 * D + (g + 1) * 128]
                s = nt(k, by_head(q, lanes)) + bias[b, g] + mask
                e = jnp.exp(s - jnp.max(s, axis=0, keepdims=True))
                p = (e * (1.0 / jnp.sum(e, axis=0, keepdims=True))).astype(BF)
                probs[b, w * GROUPS + g] = p
                att[b, rows, g * 128 : (g + 1) * 128] = own_head(tn(p, v), lanes).astype(BF)

        @pl.loop(0, 4)
        def _(t):
            rows = row_block(t, 256)
            winz[rows, :] = nn(att[b, rows, :], wproj[b])

        to_canvas(winz, canvf, SHIFT * b)

        @pl.loop(0, CELLS // TILE)
        def _(t):
            rows = row_block(t, TILE)
            out[rows, :] = (x[rows, :].astype(F32) + (canvf[rows, :] + vector(b, 2))).astype(BF)

    def mlp_forward(b, x, out):
        @pl.loop(0, CELLS // TILE)
        def _(t):
            rows = row_block(t, TILE)
            xhat, _ = standardized(x[rows, :].astype(F32))
            hq2[b, rows, :] = (xhat * vector(b, 3) + vector(b, 4)).astype(BF)

        @pl.loop(0, FF // 256)
        def _(c):
            cols = pl.ds(pl.multiple_of(c * 256, 256), 256)
            pre = nn(hq2[b], fc1[b, :, cols]) + vec[b, 7:8, cols]
            for r in range(0, CELLS, 16):
                h, dg = gelu_parts(pre[r : r + 16])
                hid[b, r : r + 16, cols] = h.astype(BF)
                dgelu[b, r : r + 16, cols] = dg.astype(BF)

        z = nn(hid[b], fc2[b])
        for r in range(0, CELLS, TILE):
            rows = slice(r, r + TILE)
            out[rows, :] = (x[rows, :].astype(F32) + (z[rows] + vector(b, 5))).astype(BF)

    def norm_backward(b, kind, x, gz, out):
        @pl.loop(0, CELLS // TILE)
        def _(t):
            rows = row_block(t, TILE)
            xhat, rs = standardized(x[rows, :].astype(F32))
            gn = canvf[rows, :]
            gzf = gz[rows, :].astype(F32)
            add_vec(b, kind, by_eights(gn * xhat))
            add_vec(b, kind + 1, by_eights(gn))
            add_vec(b, kind + 2, by_eights(gzf))
            g = gn * vector(b, kind)
            mg = jnp.mean(g, axis=-1, keepdims=True)
            mgx = jnp.mean(g * xhat, axis=-1, keepdims=True)
            out[rows, :] = (gzf + rs * (g - mg - xhat * mgx)).astype(BF)

    def mlp_backward(b, x, gz, out):
        wide_t[0, :, :CELLS] = hq2[b].T
        wide_t[1, :, :CELLS] = gz[...].T

        @pl.loop(0, FF // 256)
        def _(c):
            cols = pl.ds(pl.multiple_of(c * 256, 256), 256)
            gh = nt(gz[...], fc2[b, cols, :])
            sums = jnp.zeros((8, 256), F32)
            for r in range(0, CELLS, 16):
                gp = (gh[r : r + 16] * dgelu[b, r : r + 16, cols].astype(F32)).astype(BF)
                dgelu[b, r : r + 16, cols] = gp
                sums = sums + by_eights(gp.astype(F32))
            g_vec[b, 7, :, cols] += sums
            g_fc1[b, :, cols] += nn(wide_t[0, :, :CELLS], dgelu[b, :, cols])
            g_fc2t[b, :, cols] += nn(wide_t[1, :, :CELLS], hid[b, :, cols])

        canvf[...] = nt(dgelu[b], fc1[b])
        norm_backward(b, 3, x, gz, out)

    def attention_backward(b, x, gz, out):
        lanes = head_of_lane()

        @pl.loop(0, CELLS // TILE)
        def _(t):
            rows = row_block(t, TILE)
            canvf[rows, :] = gz[rows, :].astype(F32)

        to_windows(canvf, winf, SHIFT * b)

        @pl.loop(0, 4)
        def _(t):
            rows = row_block(t, 256)
            gw = winf[rows, :].astype(BF)
            gzw[rows, :] = gw
            go[rows, :] = nt(gw, wproj[b]).astype(BF)

        g_proj[b] += tn(att[b], gzw[...])

        @pl.loop(0, WINDOWS)
        def _(w):
            rows = row_block(w, PLACES)
            for g in range(GROUPS):
                at = [slice(part * D + g * 128, part * D + (g + 1) * 128) for part in range(3)]
                q, k, v = (qkv[b, rows, cols] for cols in at)
                go_wide = by_head(go[rows, at[0]], lanes)
                p_low = probs[b, w * GROUPS + g]
                p = p_low.astype(F32)
                pd = p * nt(v, go_wide)
                ds = (pd - p * jnp.sum(pd, axis=0, keepdims=True)).astype(BF)
                g_tab[b, g] += ds.astype(F32)
                gqkv[rows, at[0]] = (own_head(tn(ds, k), lanes) * SCALE).astype(BF)
                gqkv[rows, at[1]] = nn(ds, by_head(q, lanes)).astype(BF)
                gqkv[rows, at[2]] = nn(p_low, go_wide).astype(BF)

        wide_t[0] = hqw[b].T
        for part in range(3):
            cols = slice(part * D, (part + 1) * D)
            g_qkv[b, :, cols] += nn(wide_t[0], gqkv[:, cols])

        @pl.loop(0, 4)
        def _(t):
            rows = row_block(t, 256)
            gq = gqkv[rows, :]
            add_vec(b, 6, by_eights(gq.astype(F32)))
            winz[rows, :] = nt(gq, wqkv[b])

        to_canvas(winz, canvf, SHIFT * b)
        norm_backward(b, 0, x, gz, out)

    @pl.loop(0, canvases)
    def _(n):
        loads = [
            pltpu.make_async_copy(x_hbm.at[n], xin, in_sem.at[0]),
            pltpu.make_async_copy(cot_hbm.at[n], cot, in_sem.at[1]),
            pltpu.make_async_copy(code_hbm.at[n], code, in_sem.at[2]),
        ]
        for load in loads:
            load.start()
        for load in loads:
            load.wait()
        stores = []

        def store(src, dst):
            stores.append(pltpu.make_async_copy(src, dst, out_sem.at[len(stores)]))
            stores[-1].start()

        x = xin
        for s in range(4):
            (mlp_forward if s % 2 else attention_forward)(s // 2, x, act.at[s])
            x = act.at[s]
            store(x, act_hbm.at[s, n])
        gz = cot
        for s in (3, 2, 1, 0):
            x = act.at[s - 1] if s else xin
            (mlp_backward if s % 2 else attention_backward)(s // 2, x, gz, igrad.at[s])
            gz = igrad.at[s]
            store(gz, igrad_hbm.at[s, n])
        for copy in stores:
            copy.wait()


def compute(x, cot, code, wqkv, wproj, fc1, fc2, vec, bias):
    canvases = x.shape[0]
    shape = jax.ShapeDtypeStruct
    hbm = pl.BlockSpec(memory_space=pl.ANY)
    vmem = pl.BlockSpec(memory_space=pltpu.VMEM)
    return pl.pallas_call(
        functools.partial(kernel, canvases),
        out_shape=(
            shape((4, canvases, CELLS, D), BF),
            shape((4, canvases, CELLS, D), BF),
            shape((2, D, 3 * D), F32),
            shape((2, D, D), F32),
            shape((2, D, FF), F32),
            shape((2, D, FF), F32),
            shape((2, 8, 8, FF), F32),
            shape((2, GROUPS, PLACES, 256), F32),
        ),
        in_specs=[hbm] * 3 + [vmem] * 6,
        out_specs=(hbm,) * 2 + (vmem,) * 6,
        scratch_shapes=[
            pltpu.VMEM((CELLS, D), BF),
            pltpu.VMEM((CELLS, D), BF),
            pltpu.VMEM((CELLS, 128), jnp.int32),
            pltpu.VMEM((WROWS, 128), jnp.int32),
            pltpu.VMEM((4, CELLS, D), BF),
            pltpu.VMEM((4, CELLS, D), BF),
            pltpu.VMEM((2, WROWS, D), BF),
            pltpu.VMEM((2, WROWS, 3 * D), BF),
            pltpu.VMEM((2, WINDOWS * GROUPS, PLACES, 256), BF),
            pltpu.VMEM((2, WROWS, D), BF),
            pltpu.VMEM((2, CELLS, D), BF),
            pltpu.VMEM((2, CELLS, FF), BF),
            pltpu.VMEM((2, CELLS, FF), BF),
            pltpu.VMEM((CELLS, D), F32),
            pltpu.VMEM((WROWS, D), F32),
            pltpu.VMEM((WROWS, D), F32),
            pltpu.VMEM((WROWS, D), BF),
            pltpu.VMEM((WROWS, D), BF),
            pltpu.VMEM((WROWS, 3 * D), BF),
            pltpu.VMEM((2, D, WROWS), BF),
            pltpu.SemaphoreType.DMA((3,)),
            pltpu.SemaphoreType.DMA((8,)),
        ],
        compiler_params=pltpu.CompilerParams(vmem_limit_bytes=64 * 1024 * 1024 - 65536),
    )(x, cot, code, wqkv, wproj, fc1, fc2, vec, bias)


def place_pairs():
    place = np.arange(PLACES)
    r, c = place // 8, place % 8
    index = (r[None, :] - r[:, None] + WIN - 1) * (2 * WIN - 1) + c[None, :] - c[:, None] + WIN - 1
    real = (r < WIN) & (c < WIN)
    return index, real[:, None] & real[None, :], real


def pair_onehot():
    index, both, _ = place_pairs()
    table = (2 * WIN - 1) ** 2
    hot = (np.where(both, index, -1).reshape(-1)[None, :] == np.arange(table)[:, None])
    return hot.astype(np.float32)


def body(
    inputs,
    cotangent,
    pad_mask,
    region_ids,
    norm1_gain,
    norm1_bias,
    qkv_weight,
    qv_bias,
    rel_table,
    proj_weight,
    proj_bias,
    norm2_gain,
    norm2_bias,
    fc1_weight,
    fc1_bias,
    fc2_weight,
    fc2_bias,
):
    mine = lax.axis_index("pipe")

    def own(a):
        return lax.dynamic_index_in_dim(a, mine, 0, keepdims=False)

    x, cot = own(inputs), own(cotangent)
    code = own(region_ids) * 2 + own(pad_mask)
    code = jnp.broadcast_to(code[:, :, None], code.shape + (128,))

    def gathered(a):
        return lax.all_gather(a.astype(BF), "dp", axis=1, tiled=True)

    vectors = (norm1_gain, norm1_bias, proj_bias, norm2_gain, norm2_bias, fc2_bias, qv_bias, fc1_bias)
    sizes = [v.shape[1] for v in vectors]
    ends = np.cumsum([0] + sizes)
    packed = lax.all_gather(jnp.concatenate(vectors, axis=1).astype(BF), "dp", axis=1)
    parts = [packed[:, :, a:b].reshape(2, -1).astype(F32) for a, b in zip(ends[:-1], ends[1:])]
    qv = parts[6]
    parts[6] = jnp.concatenate([qv[:, :D], jnp.zeros_like(qv[:, :D]), qv[:, D:]], axis=1)
    vec = jnp.stack([jnp.pad(p, ((0, 0), (0, FF - p.shape[1]))) for p in parts], axis=1)

    hot = pair_onehot()
    _, _, real = place_pairs()
    rel = lax.dot_general(
        rel_table.astype(BF), jnp.asarray(hot, BF), (((1,), (0,)), ((), ())), preferred_element_type=F32
    )
    rel = rel.reshape(2, GROUPS, 4, PLACES, PLACES).transpose(0, 1, 3, 2, 4)
    rel = jnp.where(jnp.asarray(real)[None, None, :, None, None], rel, MASKED)
    rel = rel.reshape(2, GROUPS, PLACES, 256)

    act, igrad, g_qkv, g_proj, g_fc1, g_fc2t, g_vec, g_tab = compute(
        x,
        cot,
        code,
        gathered(qkv_weight),
        gathered(proj_weight),
        gathered(fc1_weight),
        gathered(fc2_weight),
        vec,
        rel,
    )

    def to_sections(a):
        return lax.all_to_all(a, "pipe", split_axis=0, concat_axis=0)[None]

    def to_owners(g):
        shared = lax.psum_scatter(g, "dp", scatter_dimension=1, tiled=True)
        return lax.psum(shared, "pipe")

    g_vec = jnp.sum(g_vec, axis=2)
    kinds = [g_vec[:, i] for i in range(8)]
    qv_sum = jnp.concatenate([kinds[6][:, :D], kinds[6][:, 2 * D : 3 * D]], axis=1)
    rows = [kinds[0], kinds[1], kinds[2], kinds[3], kinds[4], kinds[5], qv_sum, kinds[7]]
    rows = [
        r[:, : n * lax.axis_size("dp")].reshape(2, -1, n) for r, n in zip(rows, sizes)
    ]
    g_small = to_owners(jnp.concatenate(rows, axis=2))[:, 0]
    small = [g_small[:, a:b] for a, b in zip(ends[:-1], ends[1:])]

    pairs = g_tab.reshape(2, GROUPS, PLACES, 4, PLACES).transpose(0, 1, 3, 2, 4)
    pairs = pairs.reshape(2, HEADS, PLACES * PLACES)
    g_table = lax.dot_general(
        jnp.broadcast_to(jnp.asarray(hot), (2,) + hot.shape),
        pairs,
        (((2,), (2,)), ((0,), (0,))),
        precision=lax.Precision.HIGHEST,
        preferred_element_type=F32,
    )
    g_table = lax.psum(g_table, ("pipe", "dp"))

    return (
        to_sections(act),
        to_sections(igrad),
        small[0],
        small[1],
        to_owners(g_qkv),
        small[6],
        g_table,
        to_owners(g_proj),
        small[2],
        small[3],
        small[4],
        to_owners(g_fc1),
        small[7],
        to_owners(g_fc2t.transpose(0, 2, 1)),
        small[5],
    )


def solution(mesh):
    cols = P(None, "dp")
    rows = P(None, "dp", None)
    return jax.shard_map(
        body,
        mesh=mesh,
        in_specs=(
            P(None, "dp", None, None),
            P(None, "dp", None, None),
            rows,
            rows,
            cols,
            cols,
            rows,
            cols,
            P(),
            rows,
            cols,
            cols,
            cols,
            rows,
            cols,
            rows,
            cols,
        ),
        out_specs=(
            P("pipe", None, "dp", None, None),
            P("pipe", None, "dp", None, None),
            cols,
            cols,
            rows,
            cols,
            P(),
            rows,
            cols,
            cols,
            cols,
            rows,
            cols,
            rows,
            cols,
        ),
        check_vma=False,
    )
```

```python
import functools

import jax
import jax.numpy as jnp
import numpy as np
from jax import lax
from jax.experimental import pallas as pl
from jax.experimental.pallas import tpu as pltpu
from jax.sharding import PartitionSpec as P

HEADS = 12
WIN = 7
SHIFT = 3
GRID = 28
CELLS = 784
D = 384
FF = 1536
HEAD = 32
SIDE = 4
WINDOWS = 16
PLACES = 64
WROWS = WINDOWS * PLACES
GROUPS = 3
TILE = 112
SCALE = HEAD**-0.5
NORM_EPS = 1e-05
MASKED = -1e30
BF = jnp.bfloat16
F32 = jnp.float32

ERF_P = 0.3275911 / np.sqrt(2.0)
ERF_A = [0.5 * a for a in (0.254829592, -0.284496736, 1.421413741, -1.453152027, 1.061405429)]
PHI_0 = 1.0 / np.sqrt(2.0 * np.pi)


def nn(a, b):
    return lax.dot_general(a, b, (((1,), (0,)), ((), ())), preferred_element_type=F32)


def nt(a, b):
    return lax.dot_general(a, b, (((1,), (1,)), ((), ())), preferred_element_type=F32)


def tn(a, b):
    return lax.dot_general(a, b, (((0,), (0,)), ((), ())), preferred_element_type=F32)


def segments(shift):
    runs = []
    for wr in range(SIDE):
        for r in range(WIN):
            row = (wr * WIN + r + shift) % GRID
            for wc in range(SIDE):
                col = (wc * WIN + shift) % GRID
                place = (wr * SIDE + wc) * PLACES + r * 8
                first = min(WIN, GRID - col)
                runs.append((row * GRID + col, place, first))
                if first < WIN:
                    runs.append((row * GRID, place + first, WIN - first))
    return runs


def to_windows(src, dst, shift):
    for cell, place, count in segments(shift):
        dst[pl.ds(place, count), :] = src[pl.ds(cell, count), :]


def to_canvas(src, dst, shift):
    for cell, place, count in segments(shift):
        dst[pl.ds(cell, count), :] = src[pl.ds(place, count), :]


def row_block(t, size):
    return pl.ds(pl.multiple_of(t * size, 16), size)


def standardized(v):
    centered = v - jnp.mean(v, axis=-1, keepdims=True)
    spread = jnp.mean(centered * centered, axis=-1, keepdims=True)
    rs = lax.rsqrt(spread + NORM_EPS)
    return centered * rs, rs


def by_eights(v):
    return jnp.sum(v.reshape(v.shape[0] // 8, 8, v.shape[1]), axis=0)


def gelu_parts(x):
    den = 1.0 + ERF_P * jnp.abs(x)
    t = pl.reciprocal(den, approx=True)
    t = t * (2.0 - den * t)
    e = jnp.exp(-0.5 * x * x)
    poly = ERF_A[4]
    for a in ERF_A[3::-1]:
        poly = poly * t + a
    tail = poly * t * e
    cdf = jnp.where(x >= 0.0, 1.0 - tail, tail)
    return x * cdf, cdf + x * (e * PHI_0)


def head_of_lane():
    return lax.broadcasted_iota(jnp.int32, (PLACES, 128), 1) >> 5


def by_head(x, lanes):
    zero = jnp.zeros_like(x)
    return jnp.concatenate([jnp.where(lanes == h, x, zero) for h in range(4)], axis=0)


def own_head(wide, lanes):
    out = wide[3 * PLACES :]
    for h in (2, 1, 0):
        out = jnp.where(lanes == h, wide[h * PLACES : (h + 1) * PLACES], out)
    return out


def kernel(
    canvases,
    x_hbm,
    cot_hbm,
    code_hbm,
    wqkv,
    wproj,
    fc1,
    fc2,
    vec,
    bias,
    act_hbm,
    igrad_hbm,
    g_qkv,
    g_proj,
    g_fc1,
    g_fc2t,
    g_vec,
    g_tab,
    xin,
    cot,
    code,
    codew,
    act,
    igrad,
    hqw,
    qkv,
    probs,
    att,
    hq2,
    hid,
    dgelu,
    canvf,
    winf,
    winz,
    gzw,
    go,
    gqkv,
    wide_t,
    in_sem,
    local_sem,
    send_sem,
    recv_sem,
):
    me = lax.axis_index("pipe")
    barrier = pltpu.get_barrier_semaphore()
    for k in range(1, 4):
        pl.semaphore_signal(
            barrier, inc=1, device_id={"pipe": lax.rem(me + k, 4)}, device_id_type=pl.DeviceIdType.MESH
        )
    pl.semaphore_wait(barrier, 3)

    for ref in (g_qkv, g_proj, g_fc1, g_fc2t):
        for b in range(2):

            @pl.loop(0, D // 16)
            def _(i):
                ref[b, row_block(i, 16), :] = jnp.zeros((16, ref.shape[2]), F32)

    g_vec[...] = jnp.zeros_like(g_vec)
    g_tab[...] = jnp.zeros_like(g_tab)
    winf[...] = jnp.zeros_like(winf)
    codew[...] = jnp.zeros_like(codew)

    def vector(b, kind, width=D):
        return vec[b, kind : kind + 1, :width]

    def add_vec(b, kind, part, start=0):
        g_vec[b, kind, :, start : start + part.shape[1]] += part

    def attention_forward(b, x, out):
        lanes = head_of_lane()

        @pl.loop(0, CELLS // TILE)
        def _(t):
            rows = row_block(t, TILE)
            xhat, _ = standardized(x[rows, :].astype(F32))
            canvf[rows, :] = xhat * vector(b, 0) + vector(b, 1)

        to_windows(canvf, winf, SHIFT * b)
        to_windows(code, codew, SHIFT * b)

        @pl.loop(0, 4)
        def _(t):
            rows = row_block(t, 256)
            hq = winf[rows, :].astype(BF)
            hqw[b, rows, :] = hq
            for part in range(3):
                cols = slice(part * D, (part + 1) * D)
                acc = nn(hq, wqkv[b, :, cols]) + vec[b, 6:7, cols]
                if part == 0:
                    acc = acc * SCALE
                qkv[b, rows, cols] = acc.astype(BF)

        @pl.loop(0, WINDOWS)
        def _(w):
            rows = row_block(w, PLACES)
            cells = codew[rows, :]
            region = (cells >> 1) * b
            pad = (cells & 1).astype(F32)
            lane = lax.broadcasted_iota(jnp.int32, (PLACES, 128), 1)
            same = jnp.where(lane == region, 1.0, 0.0)
            left = jnp.where(lane == 127, 1.0 - pad, same).astype(BF)
            right = jnp.where(lane == 127, -pad, same).astype(BF)
            agree = nt(left, jnp.concatenate([right, right], axis=0))
            mask = jnp.where(agree > 0.5, 0.0, MASKED)
            mask = jnp.concatenate([mask, mask], axis=1)
            for g in range(GROUPS):
                q = qkv[b, rows, g * 128 : (g + 1) * 128]
                k = qkv[b, rows, D + g * 128 : D + (g + 1) * 128]
                v = qkv[b, rows, 2 * D + g * 128 : 2 * D + (g + 1) * 128]
                s = nt(k, by_head(q, lanes)) + bias[b, g] + mask
                e = jnp.exp(s - jnp.max(s, axis=0, keepdims=True))
                p = (e * (1.0 / jnp.sum(e, axis=0, keepdims=True))).astype(BF)
                probs[b, w * GROUPS + g] = p
                att[b, rows, g * 128 : (g + 1) * 128] = own_head(tn(p, v), lanes).astype(BF)

        @pl.loop(0, 4)
        def _(t):
            rows = row_block(t, 256)
            winz[rows, :] = nn(att[b, rows, :], wproj[b])

        to_canvas(winz, canvf, SHIFT * b)

        @pl.loop(0, CELLS // TILE)
        def _(t):
            rows = row_block(t, TILE)
            out[rows, :] = (x[rows, :].astype(F32) + (canvf[rows, :] + vector(b, 2))).astype(BF)

    def mlp_forward(b, x, out):
        @pl.loop(0, CELLS // TILE)
        def _(t):
            rows = row_block(t, TILE)
            xhat, _ = standardized(x[rows, :].astype(F32))
            hq2[b, rows, :] = (xhat * vector(b, 3) + vector(b, 4)).astype(BF)

        @pl.loop(0, FF // 256)
        def _(c):
            cols = pl.ds(pl.multiple_of(c * 256, 256), 256)
            pre = nn(hq2[b], fc1[b, :, cols]) + vec[b, 7:8, cols]
            for r in range(0, CELLS, 16):
                h, dg = gelu_parts(pre[r : r + 16])
                hid[b, r : r + 16, cols] = h.astype(BF)
                dgelu[b, r : r + 16, cols] = dg.astype(BF)

        z = nn(hid[b], fc2[b])
        for r in range(0, CELLS, TILE):
            rows = slice(r, r + TILE)
            out[rows, :] = (x[rows, :].astype(F32) + (z[rows] + vector(b, 5))).astype(BF)

    def norm_backward(b, kind, x, gz, out):
        @pl.loop(0, CELLS // TILE)
        def _(t):
            rows = row_block(t, TILE)
            xhat, rs = standardized(x[rows, :].astype(F32))
            gn = canvf[rows, :]
            gzf = gz[rows, :].astype(F32)
            add_vec(b, kind, by_eights(gn * xhat))
            add_vec(b, kind + 1, by_eights(gn))
            add_vec(b, kind + 2, by_eights(gzf))
            g = gn * vector(b, kind)
            mg = jnp.mean(g, axis=-1, keepdims=True)
            mgx = jnp.mean(g * xhat, axis=-1, keepdims=True)
            out[rows, :] = (gzf + rs * (g - mg - xhat * mgx)).astype(BF)

    def mlp_backward(b, x, gz, out):
        wide_t[0, :, :CELLS] = hq2[b].T
        wide_t[1, :, :CELLS] = gz[...].T

        @pl.loop(0, FF // 256)
        def _(c):
            cols = pl.ds(pl.multiple_of(c * 256, 256), 256)
            gh = nt(gz[...], fc2[b, cols, :])
            sums = jnp.zeros((8, 256), F32)
            for r in range(0, CELLS, 16):
                gp = (gh[r : r + 16] * dgelu[b, r : r + 16, cols].astype(F32)).astype(BF)
                dgelu[b, r : r + 16, cols] = gp
                sums = sums + by_eights(gp.astype(F32))
            g_vec[b, 7, :, cols] += sums
            g_fc1[b, :, cols] += nn(wide_t[0, :, :CELLS], dgelu[b, :, cols])
            g_fc2t[b, :, cols] += nn(wide_t[1, :, :CELLS], hid[b, :, cols])

        canvf[...] = nt(dgelu[b], fc1[b])
        norm_backward(b, 3, x, gz, out)

    def attention_backward(b, x, gz, out):
        lanes = head_of_lane()

        @pl.loop(0, CELLS // TILE)
        def _(t):
            rows = row_block(t, TILE)
            canvf[rows, :] = gz[rows, :].astype(F32)

        to_windows(canvf, winf, SHIFT * b)

        @pl.loop(0, 4)
        def _(t):
            rows = row_block(t, 256)
            gw = winf[rows, :].astype(BF)
            gzw[rows, :] = gw
            go[rows, :] = nt(gw, wproj[b]).astype(BF)

        g_proj[b] += tn(att[b], gzw[...])

        @pl.loop(0, WINDOWS)
        def _(w):
            rows = row_block(w, PLACES)
            for g in range(GROUPS):
                at = [slice(part * D + g * 128, part * D + (g + 1) * 128) for part in range(3)]
                q, k, v = (qkv[b, rows, cols] for cols in at)
                go_wide = by_head(go[rows, at[0]], lanes)
                p_low = probs[b, w * GROUPS + g]
                p = p_low.astype(F32)
                pd = p * nt(v, go_wide)
                ds = (pd - p * jnp.sum(pd, axis=0, keepdims=True)).astype(BF)
                g_tab[b, g] += ds.astype(F32)
                gqkv[rows, at[0]] = (own_head(tn(ds, k), lanes) * SCALE).astype(BF)
                gqkv[rows, at[1]] = nn(ds, by_head(q, lanes)).astype(BF)
                gqkv[rows, at[2]] = nn(p_low, go_wide).astype(BF)

        wide_t[0] = hqw[b].T
        for part in range(3):
            cols = slice(part * D, (part + 1) * D)
            g_qkv[b, :, cols] += nn(wide_t[0], gqkv[:, cols])

        @pl.loop(0, 4)
        def _(t):
            rows = row_block(t, 256)
            gq = gqkv[rows, :]
            add_vec(b, 6, by_eights(gq.astype(F32)))
            winz[rows, :] = nt(gq, wqkv[b])

        to_canvas(winz, canvf, SHIFT * b)
        norm_backward(b, 0, x, gz, out)

    def push(kind, s, n, start):
        src = (act, igrad)[kind].at[s]
        dst = (act_hbm, igrad_hbm)[kind].at[me, n]
        local = pltpu.make_async_copy(src, dst, local_sem.at[kind, n])
        remote = pltpu.make_async_remote_copy(
            src_ref=src,
            dst_ref=dst,
            send_sem=send_sem.at[kind, s, n],
            recv_sem=recv_sem.at[kind, me, n],
            device_id={"pipe": s},
            device_id_type=pl.DeviceIdType.MESH,
        )

        @pl.when(me == s)
        def _():
            local.start() if start else local.wait()

        @pl.when(me != s)
        def _():
            remote.start() if start else remote.wait_send()

    def arrived(kind, k, n):
        sender = lax.rem(me + k, 4)
        pltpu.make_async_remote_copy(
            src_ref=(act, igrad)[kind].at[0],
            dst_ref=(act_hbm, igrad_hbm)[kind].at[sender, n],
            send_sem=send_sem.at[kind, 0, n],
            recv_sem=recv_sem.at[kind, sender, n],
            device_id={"pipe": sender},
            device_id_type=pl.DeviceIdType.MESH,
        ).wait_recv()

    def freed(kind, s, n):
        @pl.when(n > 0)
        def _():
            push(kind, s, n - 1, False)

    @pl.loop(0, canvases)
    def _(n):
        loads = [
            pltpu.make_async_copy(x_hbm.at[n], xin, in_sem.at[0]),
            pltpu.make_async_copy(cot_hbm.at[n], cot, in_sem.at[1]),
            pltpu.make_async_copy(code_hbm.at[n], code, in_sem.at[2]),
        ]
        for load in loads:
            load.start()
        for load in loads:
            load.wait()

        x = xin
        for s in range(4):
            freed(0, s, n)
            (mlp_forward if s % 2 else attention_forward)(s // 2, x, act.at[s])
            x = act.at[s]
            push(0, s, n, True)
        gz = cot
        for s in (3, 2, 1, 0):
            freed(1, s, n)
            x = act.at[s - 1] if s else xin
            (mlp_backward if s % 2 else attention_backward)(s // 2, x, gz, igrad.at[s])
            gz = igrad.at[s]
            push(1, s, n, True)

    for kind in range(2):
        for s in range(4):
            push(kind, s, canvases - 1, False)
        for k in range(1, 4):
            for n in range(canvases):
                arrived(kind, k, n)


def compute(x, cot, code, wqkv, wproj, fc1, fc2, vec, bias):
    canvases = x.shape[0]
    shape = jax.ShapeDtypeStruct
    hbm = pl.BlockSpec(memory_space=pl.ANY)
    vmem = pl.BlockSpec(memory_space=pltpu.VMEM)
    return pl.pallas_call(
        functools.partial(kernel, canvases),
        out_shape=(
            shape((4, canvases, CELLS, D), BF),
            shape((4, canvases, CELLS, D), BF),
            shape((2, D, 3 * D), F32),
            shape((2, D, D), F32),
            shape((2, D, FF), F32),
            shape((2, D, FF), F32),
            shape((2, 8, 8, FF), F32),
            shape((2, GROUPS, PLACES, 256), F32),
        ),
        in_specs=[hbm] * 3 + [vmem] * 6,
        out_specs=(hbm,) * 2 + (vmem,) * 6,
        scratch_shapes=[
            pltpu.VMEM((CELLS, D), BF),
            pltpu.VMEM((CELLS, D), BF),
            pltpu.VMEM((CELLS, 128), jnp.int32),
            pltpu.VMEM((WROWS, 128), jnp.int32),
            pltpu.VMEM((4, CELLS, D), BF),
            pltpu.VMEM((4, CELLS, D), BF),
            pltpu.VMEM((2, WROWS, D), BF),
            pltpu.VMEM((2, WROWS, 3 * D), BF),
            pltpu.VMEM((2, WINDOWS * GROUPS, PLACES, 256), BF),
            pltpu.VMEM((2, WROWS, D), BF),
            pltpu.VMEM((2, CELLS, D), BF),
            pltpu.VMEM((2, CELLS, FF), BF),
            pltpu.VMEM((2, CELLS, FF), BF),
            pltpu.VMEM((CELLS, D), F32),
            pltpu.VMEM((WROWS, D), F32),
            pltpu.VMEM((WROWS, D), F32),
            pltpu.VMEM((WROWS, D), BF),
            pltpu.VMEM((WROWS, D), BF),
            pltpu.VMEM((WROWS, 3 * D), BF),
            pltpu.VMEM((2, D, WROWS), BF),
            pltpu.SemaphoreType.DMA((3,)),
            pltpu.SemaphoreType.DMA((2, canvases)),
            pltpu.SemaphoreType.DMA((2, 4, canvases)),
            pltpu.SemaphoreType.DMA((2, 4, canvases)),
        ],
        compiler_params=pltpu.CompilerParams(
            vmem_limit_bytes=64 * 1024 * 1024 - 65536, collective_id=0, has_side_effects=True
        ),
    )(x, cot, code, wqkv, wproj, fc1, fc2, vec, bias)


def place_pairs():
    place = np.arange(PLACES)
    r, c = place // 8, place % 8
    index = (r[None, :] - r[:, None] + WIN - 1) * (2 * WIN - 1) + c[None, :] - c[:, None] + WIN - 1
    real = (r < WIN) & (c < WIN)
    return index, real[:, None] & real[None, :], real


def pair_onehot():
    index, both, _ = place_pairs()
    table = (2 * WIN - 1) ** 2
    hot = (np.where(both, index, -1).reshape(-1)[None, :] == np.arange(table)[:, None])
    return hot.astype(np.float32)


def body(
    inputs,
    cotangent,
    pad_mask,
    region_ids,
    norm1_gain,
    norm1_bias,
    qkv_weight,
    qv_bias,
    rel_table,
    proj_weight,
    proj_bias,
    norm2_gain,
    norm2_bias,
    fc1_weight,
    fc1_bias,
    fc2_weight,
    fc2_bias,
):
    mine = lax.axis_index("pipe")

    def own(a):
        return lax.dynamic_index_in_dim(a, mine, 0, keepdims=False)

    x, cot = own(inputs), own(cotangent)
    code = own(region_ids) * 2 + own(pad_mask)
    code = jnp.broadcast_to(code[:, :, None], code.shape + (128,))

    def gathered(a):
        return lax.all_gather(a.astype(BF), "dp", axis=1, tiled=True)

    vectors = (norm1_gain, norm1_bias, proj_bias, norm2_gain, norm2_bias, fc2_bias, qv_bias, fc1_bias)
    sizes = [v.shape[1] for v in vectors]
    ends = np.cumsum([0] + sizes)
    packed = lax.all_gather(jnp.concatenate(vectors, axis=1).astype(BF), "dp", axis=1)
    parts = [packed[:, :, a:b].reshape(2, -1).astype(F32) for a, b in zip(ends[:-1], ends[1:])]
    qv = parts[6]
    parts[6] = jnp.concatenate([qv[:, :D], jnp.zeros_like(qv[:, :D]), qv[:, D:]], axis=1)
    vec = jnp.stack([jnp.pad(p, ((0, 0), (0, FF - p.shape[1]))) for p in parts], axis=1)

    hot = pair_onehot()
    _, _, real = place_pairs()
    rel = lax.dot_general(
        rel_table.astype(BF), jnp.asarray(hot, BF), (((1,), (0,)), ((), ())), preferred_element_type=F32
    )
    rel = rel.reshape(2, GROUPS, 4, PLACES, PLACES).transpose(0, 1, 3, 2, 4)
    rel = jnp.where(jnp.asarray(real)[None, None, :, None, None], rel, MASKED)
    rel = rel.reshape(2, GROUPS, PLACES, 256)

    act, igrad, g_qkv, g_proj, g_fc1, g_fc2t, g_vec, g_tab = compute(
        x,
        cot,
        code,
        gathered(qkv_weight),
        gathered(proj_weight),
        gathered(fc1_weight),
        gathered(fc2_weight),
        vec,
        rel,
    )

    def to_owners(g):
        shared = lax.psum_scatter(g, "dp", scatter_dimension=1, tiled=True)
        return lax.psum(shared, "pipe")

    g_vec = jnp.sum(g_vec, axis=2)
    kinds = [g_vec[:, i] for i in range(8)]
    qv_sum = jnp.concatenate([kinds[6][:, :D], kinds[6][:, 2 * D : 3 * D]], axis=1)
    rows = [kinds[0], kinds[1], kinds[2], kinds[3], kinds[4], kinds[5], qv_sum, kinds[7]]
    rows = [
        r[:, : n * lax.axis_size("dp")].reshape(2, -1, n) for r, n in zip(rows, sizes)
    ]
    g_small = to_owners(jnp.concatenate(rows, axis=2))[:, 0]
    small = [g_small[:, a:b] for a, b in zip(ends[:-1], ends[1:])]

    pairs = g_tab.reshape(2, GROUPS, PLACES, 4, PLACES).transpose(0, 1, 3, 2, 4)
    pairs = pairs.reshape(2, HEADS, PLACES * PLACES)
    g_table = lax.dot_general(
        jnp.broadcast_to(jnp.asarray(hot), (2,) + hot.shape),
        pairs,
        (((2,), (2,)), ((0,), (0,))),
        precision=lax.Precision.HIGHEST,
        preferred_element_type=F32,
    )
    g_table = lax.psum(g_table, ("pipe", "dp"))

    return (
        act[None],
        igrad[None],
        small[0],
        small[1],
        to_owners(g_qkv),
        small[6],
        g_table,
        to_owners(g_proj),
        small[2],
        small[3],
        small[4],
        to_owners(g_fc1),
        small[7],
        to_owners(g_fc2t.transpose(0, 2, 1)),
        small[5],
    )


def solution(mesh):
    cols = P(None, "dp")
    rows = P(None, "dp", None)
    return jax.shard_map(
        body,
        mesh=mesh,
        in_specs=(
            P(None, "dp", None, None),
            P(None, "dp", None, None),
            rows,
            rows,
            cols,
            cols,
            rows,
            cols,
            P(),
            rows,
            cols,
            cols,
            cols,
            rows,
            cols,
            rows,
            cols,
        ),
        out_specs=(
            P("pipe", None, "dp", None, None),
            P("pipe", None, "dp", None, None),
            cols,
            cols,
            rows,
            cols,
            P(),
            rows,
            cols,
            cols,
            cols,
            rows,
            cols,
            rows,
            cols,
        ),
        check_vma=False,
    )
```

```python
import functools
import types

import jax
import jax.numpy as jnp
import numpy as np
from jax import lax
from jax.experimental import pallas as pl
from jax.experimental.pallas import tpu as pltpu
from jax.sharding import PartitionSpec as P

HEADS = 12
WIN = 7
SHIFT = 3
GRID = 28
CELLS = 784
D = 384
FF = 1536
HEAD = 32
SIDE = 4
WINDOWS = 16
PLACES = 64
WROWS = WINDOWS * PLACES
GROUPS = 3
TILE = 112
SCALE = HEAD**-0.5
NORM_EPS = 1e-05
MASKED = -1e30
BF = jnp.bfloat16
F32 = jnp.float32

ERF_P = 0.3275911 / np.sqrt(2.0)
ERF_A = [0.5 * a for a in (0.254829592, -0.284496736, 1.421413741, -1.453152027, 1.061405429)]
PHI_0 = 1.0 / np.sqrt(2.0 * np.pi)


def nn(a, b):
    return lax.dot_general(a, b, (((1,), (0,)), ((), ())), preferred_element_type=F32)


def nt(a, b):
    return lax.dot_general(a, b, (((1,), (1,)), ((), ())), preferred_element_type=F32)


def tn(a, b):
    return lax.dot_general(a, b, (((0,), (0,)), ((), ())), preferred_element_type=F32)


def segments(shift):
    runs = []
    for wr in range(SIDE):
        for r in range(WIN):
            row = (wr * WIN + r + shift) % GRID
            for wc in range(SIDE):
                col = (wc * WIN + shift) % GRID
                place = (wr * SIDE + wc) * PLACES + r * 8
                first = min(WIN, GRID - col)
                runs.append((row * GRID + col, place, first))
                if first < WIN:
                    runs.append((row * GRID, place + first, WIN - first))
    return runs


def to_windows(src, dst, shift):
    for cell, place, count in segments(shift):
        dst[pl.ds(place, count), :] = src[pl.ds(cell, count), :]


def to_canvas(src, dst, shift):
    for cell, place, count in segments(shift):
        dst[pl.ds(cell, count), :] = src[pl.ds(place, count), :]


def row_block(t, size):
    return pl.ds(pl.multiple_of(t * size, 16), size)


def standardized(v):
    centered = v - jnp.mean(v, axis=-1, keepdims=True)
    spread = jnp.mean(centered * centered, axis=-1, keepdims=True)
    rs = lax.rsqrt(spread + NORM_EPS)
    return centered * rs, rs


def by_eights(v):
    return jnp.sum(v.reshape(v.shape[0] // 8, 8, v.shape[1]), axis=0)


def gelu_parts(x):
    den = 1.0 + ERF_P * jnp.abs(x)
    t = pl.reciprocal(den, approx=True)
    t = t * (2.0 - den * t)
    e = jnp.exp(-0.5 * x * x)
    poly = ERF_A[4]
    for a in ERF_A[3::-1]:
        poly = poly * t + a
    tail = poly * t * e
    cdf = jnp.where(x >= 0.0, 1.0 - tail, tail)
    return x * cdf, cdf + x * (e * PHI_0)


def real_places(rows):
    place = lax.broadcasted_iota(jnp.int32, (rows, 1), 0)
    return ((place & 7) < WIN) & (((place >> 3) & 7) < WIN)


def head_of_lane():
    return lax.broadcasted_iota(jnp.int32, (PLACES, 128), 1) >> 5


def by_head(x, lanes):
    zero = jnp.zeros_like(x)
    return jnp.concatenate([jnp.where(lanes == h, x, zero) for h in range(4)], axis=0)


def own_head(wide, lanes):
    out = wide[3 * PLACES :]
    for h in (2, 1, 0):
        out = jnp.where(lanes == h, wide[h * PLACES : (h + 1) * PLACES], out)
    return out


MESH = pl.DeviceIdType.MESH
ATT_ROWS = 256
MLP_ROWS = 384
SMALL = 192


def kernel(names, linked, canvases, *refs):
    r = types.SimpleNamespace(**dict(zip(names, refs)))
    me = lax.axis_index("pipe")
    xin, cot, code, codew, buf = r.xin, r.cot, r.code, r.codew, r.buf
    hqw, qkv, probs, att = r.hqw, r.qkv, r.probs, r.att
    hq2, hid, dgelu = r.hq2, r.hid, r.dgelu
    canvf, winf, gzw, wide_t = r.canvf, r.winf, r.gzw, r.wide_t
    g_qkv, g_proj, g_fc1, g_fc2, g_vec, g_tab = r.g_qkv, r.g_proj, r.g_fc1, r.g_fc2, r.g_vec, r.g_tab
    wqkv, wproj, fc1, fc2, vec, bias = r.wqkv, r.wproj, r.fc1, r.fc2, r.vec, r.bias
    if linked:
        d = lax.axis_index("dp")
        z, c = d // 2, d % 2
        sibling = {"dp": 2 * z + 1 - c}

    def z_peer(k):
        return {"dp": 2 * lax.rem(z + k, 4) + c}

    def pipe_peer(k):
        return {"pipe": lax.rem(me + k, 4)}

    def dp_peer(k):
        return {"dp": lax.rem(d + k, 8)}

    def remote(src, dst, send, recv, device):
        return pltpu.make_async_remote_copy(
            src_ref=src, dst_ref=dst, send_sem=send, recv_sem=recv, device_id=device, device_id_type=MESH
        )

    barrier = pltpu.get_barrier_semaphore()
    partners = [pipe_peer(k) for k in range(1, 4)]
    if linked:
        partners += [dp_peer(k) for k in range(1, 8)]
    for partner in partners:
        pl.semaphore_signal(barrier, inc=1, device_id=partner, device_id_type=MESH)

    full = ((wqkv, wproj), (fc1, fc2), (wqkv, wproj), (fc1, fc2))
    heights = ((48, 48), (48, 192), (48, 48), (48, 192))

    def shard(sec, a, owner):
        h = heights[sec][a]
        return full[sec][a].at[sec // 2, pl.ds(pl.multiple_of(owner * h, 16), h), :]

    def to_z(sec, a, k):
        own = shard(sec, a, d)
        return remote(own, own, r.wz_send.at[sec, a, k - 1], r.wz_recv.at[sec, a, k - 1], z_peer(k))

    def from_z(sec, a, k):
        block = shard(sec, a, 2 * lax.rem(z + 4 - k, 4) + c)
        return remote(block, block, r.wz_send.at[sec, a, k - 1], r.wz_recv.at[sec, a, k - 1], z_peer(k))

    def to_sibling(sec, a, k):
        block = shard(sec, a, 2 * lax.rem(z + 4 - k, 4) + c)
        return remote(block, block, r.ws_send.at[sec, a, k], r.ws_recv.at[sec, a, k], sibling)

    def from_sibling(sec, a, k):
        block = shard(sec, a, 2 * lax.rem(z + 4 - k, 4) + 1 - c)
        return remote(block, block, r.ws_send.at[sec, a, k], r.ws_recv.at[sec, a, k], sibling)

    def send_weights(sec):
        for a in range(2):
            for k in range(1, 4):
                to_z(sec, a, k).start()
            to_sibling(sec, a, 0).start()

    def take_weights(sec):
        for k in range(1, 4):
            for a in range(2):
                from_z(sec, a, k).wait_recv()
                to_sibling(sec, a, k).start()
        for k in range(4):
            for a in range(2):
                from_sibling(sec, a, k).wait_recv()

    def weights_sent():
        for sec in range(4):
            for a in range(2):
                for k in range(1, 4):
                    to_z(sec, a, k).wait_send()
                for k in range(4):
                    to_sibling(sec, a, k).wait_send()

    def pack_copy(k):
        return remote(
            r.packs.at[d], r.packs.at[d], r.pk_send.at[k - 1], r.pk_recv.at[k - 1], dp_peer(k)
        )

    def pack_arrival(k):
        slot = r.packs.at[lax.rem(d + 8 - k, 8)]
        return remote(slot, slot, r.pk_send.at[k - 1], r.pk_recv.at[k - 1], dp_peer(k))

    def place_vectors():
        row = lax.broadcasted_iota(jnp.int32, (16, 1), 0) & 7
        lane = lax.broadcasted_iota(jnp.int32, (256, 256), 0)
        goal = lax.broadcasted_iota(jnp.int32, (256, 256), 1)
        vec[...] = jnp.zeros_like(vec)
        for width, kinds in ((48, row < 6), (96, row == 6), (192, row == 7)):
            for owner in range(8):
                at = owner * width
                if width == 96 and owner >= 4:
                    at += D
                start = at // 128 * 128
                hot = jnp.where((lane < width) & (goal == lane + (at - start)), 1.0, 0.0).astype(BF)
                part = jnp.where(kinds, nn(r.packs[owner], hot), 0.0)
                vec[:, start : start + 256] += part

    def pieces(sec, owner):
        b = sec // 2
        out = []

        def matrix(ref, h):
            for t in range(h // 48):
                rows = pl.ds(pl.multiple_of(owner * h + t * 48, 16), 48)
                for j in range(ref.shape[2] // D):
                    load = functools.partial(lambda ref, rows, j: ref[b, rows, j * D : (j + 1) * D], ref, rows, j)
                    out.append((len(out) * 48, 48, load))

        def small():
            rows = pl.ds(pl.multiple_of(owner * 8, 8), 8)
            parts = [g_tab[b, rows, j * D : (j + 1) * D] for j in range(2)]
            parts += [g_vec[b, owner, :, j * D : (j + 1) * D] for j in range(4)]
            return jnp.concatenate(parts + [jnp.zeros((16, D), F32)], axis=0)

        if sec % 2:
            matrix(g_fc1, 48)
            matrix(g_fc2, 192)
        else:
            matrix(g_qkv, 48)
            matrix(g_proj, 48)
            out.append((SMALL, 64, small))
        return out

    def reduce_refs(sec):
        kind = "m" if sec % 2 else "a"
        return types.SimpleNamespace(
            **{n: getattr(r, kind + "_" + n) for n in ("st_a", "rc_a", "st_b", "rc_b", "st_c", "rc_c", "fin")}
        )

    def step_1(sec):
        q = reduce_refs(sec)
        if sec < 2:
            copy_a(sec + 2).wait_send()
        for i in range(4):
            for row, rows, load in pieces(sec, 2 * i + 1 - c):
                q.st_a[i, row : row + rows, :] = load().astype(BF)
        copy_a(sec).start()

    def copy_a(sec):
        q = reduce_refs(sec)
        return remote(q.st_a, q.rc_a, r.ra_send.at[sec], r.ra_recv.at[sec], sibling)

    def copy_b(sec, k):
        q = reduce_refs(sec)
        return remote(
            q.st_b.at[k - 1], q.rc_b.at[k - 1], r.rb_send.at[sec, k - 1], r.rb_recv.at[sec, k - 1], z_peer(k)
        )

    def step_2(sec):
        q = reduce_refs(sec)
        copy_a(sec).wait_recv()
        for k in range(1, 4):
            if sec < 2:
                copy_b(sec + 2, k).wait_send()
            i = lax.rem(z + k, 4)
            for row, rows, load in pieces(sec, 2 * i + c):
                at = slice(row, row + rows)
                q.st_b[k - 1, at, :] = (load() + q.rc_a[i, at, :].astype(F32)).astype(BF)
            copy_b(sec, k).start()

    def quarter(sec, ref, who):
        rows = (MLP_ROWS if sec % 2 else ATT_ROWS) // 4
        return ref.at[pl.ds(pl.multiple_of(who * rows, 16), rows), :]

    def copy_c(sec, k):
        q = reduce_refs(sec)
        return remote(
            quarter(sec, q.st_c, lax.rem(me + k, 4)),
            q.rc_c.at[k - 1],
            r.rc_send.at[sec, k - 1],
            r.rc_recv.at[sec, k - 1],
            pipe_peer(k),
        )

    def step_3(sec):
        q = reduce_refs(sec)
        for k in range(1, 4):
            copy_b(sec, k).wait_recv()
            if sec < 2:
                copy_c(sec + 2, k).wait_send()
        for row, rows, load in pieces(sec, d):
            at = slice(row, row + rows)
            total = load() + q.rc_a[z, at, :].astype(F32)
            for k in range(3):
                total = total + q.rc_b[k, at, :].astype(F32)
            q.st_c[at, :] = total.astype(BF)
        for k in range(1, 4):
            copy_c(sec, k).start()

    def copy_f(sec, k):
        q = reduce_refs(sec)
        own = quarter(sec, q.fin, me)
        return remote(own, own, r.rf_send.at[sec, k - 1], r.rf_recv.at[sec, k - 1], pipe_peer(k))

    def step_4(sec):
        q = reduce_refs(sec)
        for k in range(1, 4):
            copy_c(sec, k).wait_recv()
            if sec < 2:
                copy_f(sec + 2, k).wait_send()
        total = quarter(sec, q.st_c, me)[...].astype(F32)
        for k in range(3):
            total = total + q.rc_c[k].astype(F32)
        quarter(sec, q.fin, me)[...] = total.astype(BF)
        for k in range(1, 4):
            copy_f(sec, k).start()

    def copy_s(b, k):
        rows = pl.ds(SMALL, 64)
        return remote(
            r.a_fin.at[rows, :], r.o_small.at[b, d], r.rs_send.at[b, k - 1], r.rs_recv.at[b, k - 1], dp_peer(k)
        )

    def own_small(b):
        return pltpu.make_async_copy(r.a_fin.at[pl.ds(SMALL, 64), :], r.o_small.at[b, d], r.os_sem.at[b])

    def outputs(sec):
        pairs = ((g_fc1, r.o_fc1, 48), (g_fc2, r.o_fc2, 192)) if sec % 2 else (
            (g_qkv, r.o_qkv, 48), (g_proj, r.o_proj, 48))
        b = sec // 2
        return [
            pltpu.make_async_copy(ref.at[b, pl.ds(0, h), :], out.at[b], r.go_sem.at[sec, i])
            for i, (ref, out, h) in enumerate(pairs)
        ]

    def step_5(sec):
        q = reduce_refs(sec)
        b = sec // 2
        for k in range(1, 4):
            got = quarter(sec, q.fin, lax.rem(me + 4 - k, 4))
            remote(got, got, r.rf_send.at[sec, k - 1], r.rf_recv.at[sec, k - 1], pipe_peer(k)).wait_recv()
        if sec % 2 == 0:
            for k in range(1, 8):
                copy_s(b, k).start()
            own_small(b).start()
        row = 0
        for ref, h in ((g_fc1, 48), (g_fc2, 192)) if sec % 2 else ((g_qkv, 48), (g_proj, 48)):
            for t in range(h // 48):
                for j in range(ref.shape[2] // D):
                    ref[b, t * 48 : (t + 1) * 48, j * D : (j + 1) * D] = q.fin[row : row + 48, :].astype(F32)
                    row += 48
        for out in outputs(sec):
            out.start()

    def smalls_sent(b):
        for k in range(1, 8):
            copy_s(b, k).wait_send()
        own_small(b).wait()

    def reductions_done():
        for sec in (1, 0):
            copy_a(sec).wait_send()
            for k in range(1, 4):
                copy_b(sec, k).wait_send()
                copy_c(sec, k).wait_send()
                copy_f(sec, k).wait_send()
        for sec in range(4):
            for out in outputs(sec):
                out.wait()
        smalls_sent(0)
        for b in range(2):
            for k in range(1, 8):
                rows = pl.ds(SMALL, 64)
                remote(
                    r.a_fin.at[rows, :],
                    r.o_small.at[b, lax.rem(d + 8 - k, 8)],
                    r.rs_send.at[b, k - 1],
                    r.rs_recv.at[b, k - 1],
                    dp_peer(k),
                ).wait_recv()

    if linked:
        loads = [
            pltpu.make_async_copy(src, dst.at[:, pl.ds(0, h), :], r.sh_sem.at[i])
            for i, (src, dst, h) in enumerate(
                ((r.s_qkv, g_qkv, 48), (r.s_proj, g_proj, 48), (r.s_fc1, g_fc1, 48), (r.s_fc2, g_fc2, 192))
            )
        ]
        for load in loads:
            load.start()
        r.packs[d] = r.pack[...]
        for load in loads:
            load.wait()
        for ref, wide, h in ((wqkv, g_qkv, 48), (wproj, g_proj, 48), (fc1, g_fc1, 48), (fc2, g_fc2, 192)):
            for b in range(2):
                for t in range(h // 48):
                    rows = pl.ds(pl.multiple_of(d * h + t * 48, 16), 48)
                    ref[b, rows, :] = wide[b, t * 48 : (t + 1) * 48, :].astype(BF)
    pl.semaphore_wait(barrier, len(partners))
    if linked:
        for k in range(1, 8):
            pack_copy(k).start()
        send_weights(0)

    for ref in (g_qkv, g_proj, g_fc1, g_fc2):
        for b in range(2):

            @pl.loop(0, ref.shape[1] // 16)
            def _(i):
                ref[b, row_block(i, 16), :] = jnp.zeros((16, ref.shape[2]), F32)

    g_vec[...] = jnp.zeros_like(g_vec)
    g_tab[...] = jnp.zeros_like(g_tab)
    codew[...] = jnp.zeros_like(codew)

    if linked:
        for k in range(1, 8):
            pack_arrival(k).wait_recv()
        place_vectors()
        take_weights(0)

    def vector(b, kind, width=D):
        return vec[b * 8 + kind : b * 8 + kind + 1, :width]

    def add_vec(b, kind, part):
        g_vec[b, kind, :, : part.shape[1]] += part

    def windowed(rows, count):
        return jnp.where(real_places(count), winf[rows, :], 0.0).astype(BF)

    def attention_forward(b, x, out):
        lanes = head_of_lane()

        @pl.loop(0, CELLS // TILE)
        def _(t):
            rows = row_block(t, TILE)
            xhat, _ = standardized(x[rows, :].astype(F32))
            canvf[rows, :] = xhat * vector(b, 0) + vector(b, 1)

        to_windows(canvf, winf, SHIFT * b)
        to_windows(code, codew, SHIFT * b)

        @pl.loop(0, 4)
        def _(t):
            rows = row_block(t, 256)
            hq = windowed(rows, 256)
            hqw[b, rows, :] = hq
            for part in range(3):
                cols = slice(part * D, (part + 1) * D)
                acc = nn(hq, wqkv[b, :, cols]) + vec[b * 8 + 6 : b * 8 + 7, cols]
                if part == 0:
                    acc = acc * SCALE
                qkv[b, rows, cols] = acc.astype(BF)

        @pl.loop(0, WINDOWS)
        def _(w):
            rows = row_block(w, PLACES)
            cells = codew[rows, :]
            region = (cells >> 1) * b
            pad = (cells & 1).astype(F32)
            lane = lax.broadcasted_iota(jnp.int32, (PLACES, 128), 1)
            same = jnp.where(lane == region, 1.0, 0.0)
            left = jnp.where(lane == 127, 1.0 - pad, same).astype(BF)
            right = jnp.where(lane == 127, -pad, same).astype(BF)
            agree = nt(left, jnp.concatenate([right, right], axis=0))
            mask = jnp.where(agree > 0.5, 0.0, MASKED)
            mask = jnp.concatenate([mask, mask], axis=1)
            for g in range(GROUPS):
                q = qkv[b, rows, g * 128 : (g + 1) * 128]
                k = qkv[b, rows, D + g * 128 : D + (g + 1) * 128]
                v = qkv[b, rows, 2 * D + g * 128 : 2 * D + (g + 1) * 128]
                s = nt(k, by_head(q, lanes)) + bias[b, g] + mask
                e = jnp.exp(s - jnp.max(s, axis=0, keepdims=True))
                p = (e * (1.0 / jnp.sum(e, axis=0, keepdims=True))).astype(BF)
                probs[b, w * GROUPS + g] = p
                att[b, rows, g * 128 : (g + 1) * 128] = own_head(tn(p, v), lanes).astype(BF)

        @pl.loop(0, 4)
        def _(t):
            rows = row_block(t, 256)
            winf[rows, :] = nn(att[b, rows, :], wproj[b])

        to_canvas(winf, canvf, SHIFT * b)

        @pl.loop(0, CELLS // TILE)
        def _(t):
            rows = row_block(t, TILE)
            out[rows, :] = (x[rows, :].astype(F32) + (canvf[rows, :] + vector(b, 2))).astype(BF)

    def mlp_forward(b, x, out):
        @pl.loop(0, CELLS // TILE)
        def _(t):
            rows = row_block(t, TILE)
            xhat, _ = standardized(x[rows, :].astype(F32))
            hq2[b, rows, :] = (xhat * vector(b, 3) + vector(b, 4)).astype(BF)

        @pl.loop(0, FF // 256)
        def _(i):
            cols = pl.ds(pl.multiple_of(i * 256, 256), 256)
            pre = nn(hq2[b], fc1[b, :, cols]) + vec[b * 8 + 7 : b * 8 + 8, cols]
            for at in range(0, CELLS, 16):
                h, dg = gelu_parts(pre[at : at + 16])
                hid[b, at : at + 16, cols] = h.astype(BF)
                dgelu[b, at : at + 16, cols] = dg.astype(BF)

        total = nn(hid[b], fc2[b])
        for at in range(0, CELLS, TILE):
            rows = slice(at, at + TILE)
            out[rows, :] = (x[rows, :].astype(F32) + (total[rows] + vector(b, 5))).astype(BF)

    def norm_backward(b, kind, x, gz, out):
        @pl.loop(0, CELLS // TILE)
        def _(t):
            rows = row_block(t, TILE)
            xhat, rs = standardized(x[rows, :].astype(F32))
            gn = canvf[rows, :]
            gzf = gz[rows, :].astype(F32)
            add_vec(b, kind, by_eights(gn * xhat))
            add_vec(b, kind + 1, by_eights(gn))
            add_vec(b, 5 if kind else 2, by_eights(gzf))
            g = gn * vector(b, kind)
            mg = jnp.mean(g, axis=-1, keepdims=True)
            mgx = jnp.mean(g * xhat, axis=-1, keepdims=True)
            out[rows, :] = (gzf + rs * (g - mg - xhat * mgx)).astype(BF)

    def mlp_backward(b, x, gz, out, free_out, hook):
        hook(0)
        wide_t[:, :CELLS] = hq2[b].T

        def chunk(i):
            cols = pl.ds(pl.multiple_of(i * 256, 256), 256)
            gh = nt(gz[...], fc2[b, cols, :])
            sums = jnp.zeros((8, 256), F32)
            for at in range(0, CELLS, 16):
                gp = (gh[at : at + 16] * dgelu[b, at : at + 16, cols].astype(F32)).astype(BF)
                dgelu[b, at : at + 16, cols] = gp
                sums = sums + by_eights(gp.astype(F32))
            g_vec[b, 7, :, cols] += sums
            g_fc1[b, :, cols] += nn(wide_t[:, :CELLS], dgelu[b, :, cols])
            g_fc2[b, cols, :] += tn(hid[b, :, cols], gz[...])

        pl.loop(0, FF // 512)(chunk)
        hook(1)
        pl.loop(FF // 512, FF // 256)(chunk)
        hook(2)
        canvf[...] = nt(dgelu[b], fc1[b])
        hook(3)
        free_out()
        norm_backward(b, 3, x, gz, out)
        hook(4)

    def attention_backward(b, x, gz, out, free_out, hook):
        lanes = head_of_lane()
        hook(0)

        @pl.loop(0, CELLS // TILE)
        def _(t):
            rows = row_block(t, TILE)
            canvf[rows, :] = gz[rows, :].astype(F32)

        to_windows(canvf, winf, SHIFT * b)

        @pl.loop(0, 4)
        def _(t):
            rows = row_block(t, 256)
            gzw[rows, :] = windowed(rows, 256)

        g_proj[b] += tn(att[b], gzw[...])

        @pl.loop(0, 4)
        def _(t):
            rows = row_block(t, 256)
            att[b, rows, :] = nt(gzw[rows, :], wproj[b]).astype(BF)

        hook(1)

        def window(w):
            rows = row_block(w, PLACES)
            for g in range(GROUPS):
                at = [slice(part * D + g * 128, part * D + (g + 1) * 128) for part in range(3)]
                q, k, v = (qkv[b, rows, cols] for cols in at)
                go_wide = by_head(att[b, rows, at[0]], lanes)
                p_low = probs[b, w * GROUPS + g]
                p = p_low.astype(F32)
                pd = p * nt(v, go_wide)
                ds = (pd - p * jnp.sum(pd, axis=0, keepdims=True)).astype(BF)
                g_tab[b, :, g * 256 : (g + 1) * 256] += ds.astype(F32)
                qkv[b, rows, at[0]] = (own_head(tn(ds, k), lanes) * SCALE).astype(BF)
                qkv[b, rows, at[1]] = nn(ds, by_head(q, lanes)).astype(BF)
                qkv[b, rows, at[2]] = nn(p_low, go_wide).astype(BF)

        pl.loop(0, WINDOWS // 2)(window)
        hook(2)
        pl.loop(WINDOWS // 2, WINDOWS)(window)
        hook(3)

        @pl.loop(0, 4)
        def _(t):
            rows = row_block(t, 256)
            gq = qkv[b, rows, :]
            add_vec(b, 6, by_eights(gq.astype(F32)))
            winf[rows, :] = nt(gq, wqkv[b])

        to_canvas(winf, canvf, SHIFT * b)
        free_out()
        norm_backward(b, 0, x, gz, out)

    def attention_weights(b):
        wide_t[...] = hqw[b].T
        for part in range(3):
            cols = slice(part * D, (part + 1) * D)
            g_qkv[b, :, cols] += nn(wide_t[...], qkv[b, :, cols])

    def push(kind, s, n, start):
        src = buf.at[s]
        dst = (r.act_hbm, r.igrad_hbm)[kind].at[me, n]
        local = pltpu.make_async_copy(src, dst, r.local_sem.at[kind, n])
        away = remote(src, dst, r.send_sem.at[kind, s, n], r.recv_sem.at[kind, me, n], {"pipe": s})

        @pl.when(me == s)
        def _():
            local.start() if start else local.wait()

        @pl.when(me != s)
        def _():
            away.start() if start else away.wait_send()

    def arrived(kind, k, n):
        sender = lax.rem(me + k, 4)
        dst = (r.act_hbm, r.igrad_hbm)[kind].at[sender, n]
        remote(
            buf.at[0], dst, r.send_sem.at[kind, 0, n], r.recv_sem.at[kind, sender, n], {"pipe": sender}
        ).wait_recv()

    steps = (step_1, step_2, step_3, step_4, step_5)
    schedule = {
        (2, 0): ((1, 3),),
        (2, 1): ((2, 3),),
        (2, 4): ((3, 3),),
        (2, 5): ((4, 3),),
        (1, 0): ((1, 2), (5, 3)),
        (1, 1): ((2, 2),),
        (1, 4): ((3, 2),),
        (0, 0): ((1, 1),),
        (0, 1): ((2, 1), (4, 2)),
        (0, 2): ((5, 2),),
        (0, 4): ((3, 1),),
        (0, 5): ((4, 1),),
    }

    @pl.loop(0, canvases)
    def _(n):
        def hook(sec, i):
            todo = schedule.get((sec, i), ())
            if linked and todo:

                @pl.when(n == canvases - 1)
                def _():
                    for step, of in todo:
                        steps[step - 1](of)

        def weights_for(sec):
            if linked:

                @pl.when(n == 0)
                def _():
                    take_weights(sec)

        def weights_from(sec):
            if linked:

                @pl.when(n == 0)
                def _():
                    send_weights(sec)

        loads = [
            pltpu.make_async_copy(r.x_hbm.at[me, n], xin, r.in_sem.at[0]),
            pltpu.make_async_copy(r.cot_hbm.at[me, n], cot, r.in_sem.at[1]),
            pltpu.make_async_copy(r.code_hbm.at[n], code, r.in_sem.at[2]),
        ]
        for load in loads:
            load.start()
        for load in loads:
            load.wait()

        x = xin
        for s in range(4):
            if s < 3:
                weights_from(s + 1)

            @pl.when(n > 0)
            def _():
                push(1, s, n - 1, False)

            (mlp_forward if s % 2 else attention_forward)(s // 2, x, buf.at[s])
            x = buf.at[s]
            push(0, s, n, True)
            if s < 3:
                weights_for(s + 1)
        gz = cot
        for s in (3, 2, 1, 0):
            x = buf.at[s - 1] if s else xin
            backward = mlp_backward if s % 2 else attention_backward
            backward(
                s // 2, x, gz, buf.at[s], functools.partial(push, 0, s, n, False), functools.partial(hook, s)
            )
            gz = buf.at[s]
            push(1, s, n, True)
            if s % 2 == 0:
                hook(s, 4)
                attention_weights(s // 2)
                hook(s, 5)

    if linked:
        step_5(1)
        step_1(0)
        step_2(0)
        smalls_sent(1)
        step_3(0)
        step_4(0)
        step_5(0)
        reductions_done()
        weights_sent()
        for k in range(1, 8):
            pack_copy(k).wait_send()
    for kind in range(2):
        for k in range(1, 4):
            for n in range(canvases):
                arrived(kind, k, n)
    for s in range(4):
        push(1, s, canvases - 1, False)


def compute(linked, operands):
    canvases = operands["x_hbm"].shape[1]
    shape = jax.ShapeDtypeStruct
    hbm = pl.BlockSpec(memory_space=pl.ANY)
    vmem = pl.BlockSpec(memory_space=pltpu.VMEM)
    dma = pltpu.SemaphoreType.DMA
    full = {
        "wqkv": ((2, D, 3 * D), BF),
        "wproj": ((2, D, D), BF),
        "fc1": ((2, D, FF), BF),
        "fc2": ((2, FF, D), BF),
        "vec": ((16, FF), F32),
    }
    grads = {
        "g_qkv": ((2, D, 3 * D), F32),
        "g_proj": ((2, D, D), F32),
        "g_fc1": ((2, D, FF), F32),
        "g_fc2": ((2, FF, D), F32),
        "g_vec": ((2, 8, 8, FF), F32),
        "g_tab": ((2, PLACES, GROUPS * 256), F32),
    }
    outs = {"act_hbm": ((4, canvases, CELLS, D), BF), "igrad_hbm": ((4, canvases, CELLS, D), BF)}
    scratch = {
        "xin": ((CELLS, D), BF),
        "cot": ((CELLS, D), BF),
        "code": ((CELLS, 128), jnp.int32),
        "codew": ((WROWS, 128), jnp.int32),
        "buf": ((4, CELLS, D), BF),
        "hqw": ((2, WROWS, D), BF),
        "qkv": ((2, WROWS, 3 * D), BF),
        "probs": ((2, WINDOWS * GROUPS, PLACES, 256), BF),
        "att": ((2, WROWS, D), BF),
        "hq2": ((2, CELLS, D), BF),
        "hid": ((2, CELLS, FF), BF),
        "dgelu": ((2, CELLS, FF), BF),
        "canvf": ((CELLS, D), F32),
        "winf": ((WROWS, D), F32),
        "gzw": ((WROWS, D), BF),
        "wide_t": ((D, WROWS), BF),
    }
    sems = {
        "in_sem": (3,),
        "local_sem": (2, canvases),
        "send_sem": (2, 4, canvases),
        "recv_sem": (2, 4, canvases),
    }
    if linked:
        outs |= {
            "o_qkv": ((2, 48, 3 * D), F32),
            "o_proj": ((2, 48, D), F32),
            "o_fc1": ((2, 48, FF), F32),
            "o_fc2": ((2, 192, D), F32),
            "o_small": ((2, 8, 64, D), BF),
        }
        scratch |= full | grads
        scratch["packs"] = ((8, 16, 256), BF)
        for kind, rows in (("m_", MLP_ROWS), ("a_", ATT_ROWS)):
            scratch |= {
                kind + "st_a": ((4, rows, D), BF),
                kind + "rc_a": ((4, rows, D), BF),
                kind + "st_b": ((3, rows, D), BF),
                kind + "rc_b": ((3, rows, D), BF),
                kind + "st_c": ((rows, D), BF),
                kind + "rc_c": ((3, rows // 4, D), BF),
                kind + "fin": ((rows, D), BF),
            }
        sems |= {
            "sh_sem": (4,),
            "os_sem": (2,),
            "go_sem": (4, 2),
            "wz_send": (4, 2, 3),
            "wz_recv": (4, 2, 3),
            "ws_send": (4, 2, 4),
            "ws_recv": (4, 2, 4),
            "pk_send": (7,),
            "pk_recv": (7,),
            "ra_send": (4,),
            "ra_recv": (4,),
            "rb_send": (4, 3),
            "rb_recv": (4, 3),
            "rc_send": (4, 3),
            "rc_recv": (4, 3),
            "rf_send": (4, 3),
            "rf_recv": (4, 3),
            "rs_send": (2, 7),
            "rs_recv": (2, 7),
        }
    else:
        outs |= grads
    in_vmem = set(grads) | set(full) | {"bias", "pack"}
    names = tuple(operands) + tuple(outs) + tuple(scratch) + tuple(sems)
    results = pl.pallas_call(
        functools.partial(kernel, names, linked, canvases),
        out_shape=tuple(shape(*o) for o in outs.values()),
        in_specs=[vmem if name in in_vmem else hbm for name in operands],
        out_specs=tuple(vmem if name in in_vmem else hbm for name in outs),
        scratch_shapes=[pltpu.VMEM(*v) for v in scratch.values()] + [dma(v) for v in sems.values()],
        compiler_params=pltpu.CompilerParams(
            vmem_limit_bytes=64 * 1024 * 1024 - 65536, collective_id=0, has_side_effects=True
        ),
    )(*operands.values())
    return dict(zip(outs, results))


def place_pairs():
    place = np.arange(PLACES)
    r, c = place // 8, place % 8
    index = (r[None, :] - r[:, None] + WIN - 1) * (2 * WIN - 1) + c[None, :] - c[:, None] + WIN - 1
    real = (r < WIN) & (c < WIN)
    return index, real[:, None] & real[None, :], real


def pair_onehot():
    index, both, _ = place_pairs()
    table = (2 * WIN - 1) ** 2
    hot = (np.where(both, index, -1).reshape(-1)[None, :] == np.arange(table)[:, None])
    return hot.astype(np.float32)


def body(
    inputs,
    cotangent,
    pad_mask,
    region_ids,
    norm1_gain,
    norm1_bias,
    qkv_weight,
    qv_bias,
    rel_table,
    proj_weight,
    proj_bias,
    norm2_gain,
    norm2_bias,
    fc1_weight,
    fc1_bias,
    fc2_weight,
    fc2_bias,
):
    owners = lax.axis_size("dp")
    linked = owners == 8
    mine = lax.axis_index("pipe")

    def own(a):
        return lax.dynamic_index_in_dim(a, mine, 0, keepdims=False)

    code = own(region_ids) * 2 + own(pad_mask)
    code = jnp.broadcast_to(code[:, :, None], code.shape + (128,))

    hot = pair_onehot()
    _, _, real = place_pairs()
    rel = lax.dot_general(
        rel_table.astype(BF), jnp.asarray(hot, BF), (((1,), (0,)), ((), ())), preferred_element_type=F32
    )
    rel = rel.reshape(2, GROUPS, 4, PLACES, PLACES).transpose(0, 1, 3, 2, 4)
    rel = jnp.where(jnp.asarray(real)[None, None, :, None, None], rel, MASKED)
    rel = rel.reshape(2, GROUPS, PLACES, 256)

    operands = {"x_hbm": inputs, "cot_hbm": cotangent, "code_hbm": code, "bias": rel}
    vectors = (norm1_gain, norm1_bias, proj_bias, norm2_gain, norm2_bias, fc2_bias, qv_bias, fc1_bias)
    sizes = [v.shape[1] for v in vectors]
    ends = np.cumsum([0] + sizes)
    if linked:
        pack = jnp.stack([jnp.pad(v, ((0, 0), (0, 256 - v.shape[1]))) for v in vectors], axis=1)
        operands |= {
            "pack": pack.reshape(16, 256).astype(BF),
            "s_qkv": qkv_weight,
            "s_proj": proj_weight,
            "s_fc1": fc1_weight,
            "s_fc2": fc2_weight,
        }
    else:

        def gathered(a):
            return lax.all_gather(a.astype(BF), "dp", axis=1, tiled=True)

        packed = lax.all_gather(jnp.concatenate(vectors, axis=1).astype(BF), "dp", axis=1)
        parts = [packed[:, :, a:b].reshape(2, -1).astype(F32) for a, b in zip(ends[:-1], ends[1:])]
        qv = parts[6]
        parts[6] = jnp.concatenate([qv[:, :D], jnp.zeros_like(qv[:, :D]), qv[:, D:]], axis=1)
        vec = jnp.stack([jnp.pad(p, ((0, 0), (0, FF - p.shape[1]))) for p in parts], axis=1)
        operands |= {
            "wqkv": gathered(qkv_weight),
            "wproj": gathered(proj_weight),
            "fc1": gathered(fc1_weight),
            "fc2": gathered(fc2_weight),
            "vec": vec.reshape(16, FF),
        }

    out = compute(linked, operands)

    def to_owners(g):
        shared = lax.psum_scatter(g, "dp", scatter_dimension=1, tiled=True)
        return lax.psum(shared, "pipe")

    if linked:
        small = out["o_small"].astype(F32)
        g_tab = jnp.concatenate([small[:, :, :8], small[:, :, 8:16]], axis=3).reshape(2, PLACES, GROUPS * 256)
        g_vec = jnp.concatenate([small[:, :, 16 + 8 * j : 24 + 8 * j] for j in range(4)], axis=3)
    else:
        g_tab, g_vec = out["g_tab"], out["g_vec"]

    g_vec = jnp.sum(g_vec, axis=2)
    kinds = [g_vec[:, i] for i in range(8)]
    qv_sum = jnp.concatenate([kinds[6][:, :D], kinds[6][:, 2 * D : 3 * D]], axis=1)
    rows = [kinds[0], kinds[1], kinds[2], kinds[3], kinds[4], kinds[5], qv_sum, kinds[7]]
    if linked:
        at = lax.axis_index("dp")
        small = [lax.dynamic_slice_in_dim(v, at * n, n, 1) for v, n in zip(rows, sizes)]
    else:
        rows = [v[:, : n * owners].reshape(2, -1, n) for v, n in zip(rows, sizes)]
        g_small = to_owners(jnp.concatenate(rows, axis=2))[:, 0]
        small = [g_small[:, a:b] for a, b in zip(ends[:-1], ends[1:])]

    pairs = g_tab.reshape(2, PLACES, HEADS, PLACES).transpose(0, 2, 1, 3)
    pairs = pairs.reshape(2, HEADS, PLACES * PLACES)
    g_table = lax.dot_general(
        jnp.broadcast_to(jnp.asarray(hot), (2,) + hot.shape),
        pairs,
        (((2,), (2,)), ((0,), (0,))),
        precision=lax.Precision.HIGHEST,
        preferred_element_type=F32,
    )
    if linked:
        big = [out[name] for name in ("o_qkv", "o_proj", "o_fc1", "o_fc2")]
    else:
        g_table = lax.psum(g_table, ("pipe", "dp"))
        big = [to_owners(out[name]) for name in ("g_qkv", "g_proj", "g_fc1", "g_fc2")]

    return (
        out["act_hbm"][None],
        out["igrad_hbm"][None],
        small[0],
        small[1],
        big[0],
        small[6],
        g_table,
        big[1],
        small[2],
        small[3],
        small[4],
        big[2],
        small[7],
        big[3],
        small[5],
    )


def solution(mesh):
    cols = P(None, "dp")
    rows = P(None, "dp", None)
    return jax.shard_map(
        body,
        mesh=mesh,
        in_specs=(
            P(None, "dp", None, None),
            P(None, "dp", None, None),
            rows,
            rows,
            cols,
            cols,
            rows,
            cols,
            P(),
            rows,
            cols,
            cols,
            cols,
            rows,
            cols,
            rows,
            cols,
        ),
        out_specs=(
            P("pipe", None, "dp", None, None),
            P("pipe", None, "dp", None, None),
            cols,
            cols,
            rows,
            cols,
            P(),
            rows,
            cols,
            cols,
            cols,
            rows,
            cols,
            rows,
            cols,
        ),
        check_vma=False,
    )
```

```python
import functools
import types

import jax
import jax.numpy as jnp
import numpy as np
from jax import lax
from jax.experimental import pallas as pl
from jax.experimental.pallas import tpu as pltpu
from jax.sharding import PartitionSpec as P

HEADS = 12
WIN = 7
SHIFT = 3
GRID = 28
CELLS = 784
D = 384
FF = 1536
HEAD = 32
SIDE = 4
WINDOWS = 16
PLACES = 64
WROWS = WINDOWS * PLACES
GROUPS = 3
TILE = 112
SCALE = HEAD**-0.5
NORM_EPS = 1e-05
MASKED = -1e30
BF = jnp.bfloat16
F32 = jnp.float32

ERF_P = 0.3275911 / np.sqrt(2.0)
ERF_A = [0.5 * a for a in (0.254829592, -0.284496736, 1.421413741, -1.453152027, 1.061405429)]
PHI_0 = 1.0 / np.sqrt(2.0 * np.pi)


def nn(a, b):
    return lax.dot_general(a, b, (((1,), (0,)), ((), ())), preferred_element_type=F32)


def nt(a, b):
    return lax.dot_general(a, b, (((1,), (1,)), ((), ())), preferred_element_type=F32)


def tn(a, b):
    return lax.dot_general(a, b, (((0,), (0,)), ((), ())), preferred_element_type=F32)


def segments(shift):
    runs = []
    for wr in range(SIDE):
        for r in range(WIN):
            row = (wr * WIN + r + shift) % GRID
            for wc in range(SIDE):
                col = (wc * WIN + shift) % GRID
                place = (wr * SIDE + wc) * PLACES + r * 8
                first = min(WIN, GRID - col)
                runs.append((row * GRID + col, place, first))
                if first < WIN:
                    runs.append((row * GRID, place + first, WIN - first))
    return runs


def to_windows(src, dst, shift):
    for cell, place, count in segments(shift):
        dst[pl.ds(place, count), :] = src[pl.ds(cell, count), :]


def to_canvas(src, dst, shift):
    for cell, place, count in segments(shift):
        dst[pl.ds(cell, count), :] = src[pl.ds(place, count), :]


def row_block(t, size):
    return pl.ds(pl.multiple_of(t * size, 16), size)


def standardized(v):
    centered = v - jnp.mean(v, axis=-1, keepdims=True)
    spread = jnp.mean(centered * centered, axis=-1, keepdims=True)
    rs = lax.rsqrt(spread + NORM_EPS)
    return centered * rs, rs


def by_eights(v):
    return jnp.sum(v.reshape(v.shape[0] // 8, 8, v.shape[1]), axis=0)


def gelu_parts(x):
    den = 1.0 + ERF_P * jnp.abs(x)
    t = pl.reciprocal(den, approx=True)
    t = t * (2.0 - den * t)
    e = jnp.exp(-0.5 * x * x)
    poly = ERF_A[4]
    for a in ERF_A[3::-1]:
        poly = poly * t + a
    tail = poly * t * e
    cdf = jnp.where(x >= 0.0, 1.0 - tail, tail)
    return x * cdf, cdf + x * (e * PHI_0)


def real_places(rows):
    place = lax.broadcasted_iota(jnp.int32, (rows, 1), 0)
    return ((place & 7) < WIN) & (((place >> 3) & 7) < WIN)


def head_of_lane():
    return lax.broadcasted_iota(jnp.int32, (PLACES, 128), 1) >> 5


def by_head(x, lanes):
    zero = jnp.zeros_like(x)
    return jnp.concatenate([jnp.where(lanes == h, x, zero) for h in range(4)], axis=0)


def own_head(wide, lanes):
    out = wide[3 * PLACES :]
    for h in (2, 1, 0):
        out = jnp.where(lanes == h, wide[h * PLACES : (h + 1) * PLACES], out)
    return out


MESH = pl.DeviceIdType.MESH
ATT_ROWS = 256
MLP_ROWS = 384
SMALL = 192


def kernel(names, linked, canvases, *refs):
    r = types.SimpleNamespace(**dict(zip(names, refs)))
    me = lax.axis_index("pipe")
    xin, cot, code, codew, buf = r.xin, r.cot, r.code, r.codew, r.buf
    hqw, qkv, probs, att = r.hqw, r.qkv, r.probs, r.att
    hq2, hid, dgelu = r.hq2, r.hid, r.dgelu
    canvf, winf, gzw, wide_t = r.canvf, r.winf, r.gzw, r.wide_t
    g_qkv, g_proj, g_fc1, g_fc2, g_vec, g_tab = r.g_qkv, r.g_proj, r.g_fc1, r.g_fc2, r.g_vec, r.g_tab
    wqkv, wproj, fc1, fc2, vec, bias = r.wqkv, r.wproj, r.fc1, r.fc2, r.vec, r.bias
    if linked:
        d = lax.axis_index("dp")
        z, c = d // 2, d % 2
        sibling = {"dp": 2 * z + 1 - c}

    def z_peer(k):
        return {"dp": 2 * lax.rem(z + k, 4) + c}

    def pipe_peer(k):
        return {"pipe": lax.rem(me + k, 4)}

    def dp_peer(k):
        return {"dp": lax.rem(d + k, 8)}

    def remote(src, dst, send, recv, device):
        return pltpu.make_async_remote_copy(
            src_ref=src, dst_ref=dst, send_sem=send, recv_sem=recv, device_id=device, device_id_type=MESH
        )

    barrier = pltpu.get_barrier_semaphore()
    partners = [pipe_peer(k) for k in range(1, 4)]
    if linked:
        partners += [dp_peer(k) for k in range(1, 8)]
    for partner in partners:
        pl.semaphore_signal(barrier, inc=1, device_id=partner, device_id_type=MESH)

    full = ((wqkv, wproj), (fc1, fc2), (wqkv, wproj), (fc1, fc2))
    heights = ((48, 48), (48, 192), (48, 48), (48, 192))

    def shard(sec, a, owner):
        h = heights[sec][a]
        return full[sec][a].at[sec // 2, pl.ds(pl.multiple_of(owner * h, 16), h), :]

    def to_z(sec, a, k):
        own = shard(sec, a, d)
        return remote(own, own, r.wz_send.at[sec, a, k - 1], r.wz_recv.at[sec, a, k - 1], z_peer(k))

    def from_z(sec, a, k):
        block = shard(sec, a, 2 * lax.rem(z + 4 - k, 4) + c)
        return remote(block, block, r.wz_send.at[sec, a, k - 1], r.wz_recv.at[sec, a, k - 1], z_peer(k))

    def to_sibling(sec, a, k):
        block = shard(sec, a, 2 * lax.rem(z + 4 - k, 4) + c)
        return remote(block, block, r.ws_send.at[sec, a, k], r.ws_recv.at[sec, a, k], sibling)

    def from_sibling(sec, a, k):
        block = shard(sec, a, 2 * lax.rem(z + 4 - k, 4) + 1 - c)
        return remote(block, block, r.ws_send.at[sec, a, k], r.ws_recv.at[sec, a, k], sibling)

    def send_weights(sec):
        for a in range(2):
            for k in range(1, 4):
                to_z(sec, a, k).start()
            to_sibling(sec, a, 0).start()

    def take_weights(sec):
        for k in range(1, 4):
            for a in range(2):
                from_z(sec, a, k).wait_recv()
                to_sibling(sec, a, k).start()
        for k in range(4):
            for a in range(2):
                from_sibling(sec, a, k).wait_recv()

    def weights_sent():
        for sec in range(4):
            for a in range(2):
                for k in range(1, 4):
                    to_z(sec, a, k).wait_send()
                for k in range(4):
                    to_sibling(sec, a, k).wait_send()

    def pack_copy(k):
        return remote(
            r.packs.at[d], r.packs.at[d], r.pk_send.at[k - 1], r.pk_recv.at[k - 1], dp_peer(k)
        )

    def pack_arrival(k):
        slot = r.packs.at[lax.rem(d + 8 - k, 8)]
        return remote(slot, slot, r.pk_send.at[k - 1], r.pk_recv.at[k - 1], dp_peer(k))

    def place_vectors():
        row = lax.broadcasted_iota(jnp.int32, (16, 1), 0) & 7
        lane = lax.broadcasted_iota(jnp.int32, (256, 256), 0)
        goal = lax.broadcasted_iota(jnp.int32, (256, 256), 1)
        vec[...] = jnp.zeros_like(vec)
        for width, kinds in ((48, row < 6), (96, row == 6), (192, row == 7)):
            for owner in range(8):
                at = owner * width
                if width == 96 and owner >= 4:
                    at += D
                start = at // 128 * 128
                hot = jnp.where((lane < width) & (goal == lane + (at - start)), 1.0, 0.0).astype(BF)
                part = jnp.where(kinds, nn(r.packs[owner], hot), 0.0)
                vec[:, start : start + 256] += part

    def pieces(sec, owner):
        b = sec // 2
        out = []

        def matrix(ref, h):
            for t in range(h // 48):
                rows = pl.ds(pl.multiple_of(owner * h + t * 48, 16), 48)
                for j in range(ref.shape[2] // D):
                    load = functools.partial(lambda ref, rows, j: ref[b, rows, j * D : (j + 1) * D], ref, rows, j)
                    out.append((len(out) * 48, 48, load))

        def small():
            rows = pl.ds(pl.multiple_of(owner * 8, 8), 8)
            parts = [g_tab[b, rows, j * D : (j + 1) * D] for j in range(2)]
            parts += [g_vec[b, owner, :, j * D : (j + 1) * D] for j in range(4)]
            return jnp.concatenate(parts + [jnp.zeros((16, D), F32)], axis=0)

        if sec % 2:
            matrix(g_fc1, 48)
            matrix(g_fc2, 192)
        else:
            matrix(g_qkv, 48)
            matrix(g_proj, 48)
            out.append((SMALL, 64, small))
        return out

    def reduce_refs(sec):
        kind = "m" if sec % 2 else "a"
        return types.SimpleNamespace(
            **{n: getattr(r, kind + "_" + n) for n in ("st_a", "rc_a", "st_b", "rc_b", "st_c", "rc_c", "fin")}
        )

    def step_1(sec):
        q = reduce_refs(sec)
        if sec < 2:
            copy_a(sec + 2).wait_send()
        for i in range(4):
            for row, rows, load in pieces(sec, 2 * i + 1 - c):
                q.st_a[i, row : row + rows, :] = load().astype(BF)
        copy_a(sec).start()

    def copy_a(sec):
        q = reduce_refs(sec)
        return remote(q.st_a, q.rc_a, r.ra_send.at[sec], r.ra_recv.at[sec], sibling)

    def copy_b(sec, k):
        q = reduce_refs(sec)
        return remote(
            q.st_b.at[k - 1], q.rc_b.at[k - 1], r.rb_send.at[sec, k - 1], r.rb_recv.at[sec, k - 1], z_peer(k)
        )

    def step_2(sec):
        q = reduce_refs(sec)
        copy_a(sec).wait_recv()
        for k in range(1, 4):
            if sec < 2:
                copy_b(sec + 2, k).wait_send()
            i = lax.rem(z + k, 4)
            for row, rows, load in pieces(sec, 2 * i + c):
                at = slice(row, row + rows)
                q.st_b[k - 1, at, :] = (load() + q.rc_a[i, at, :].astype(F32)).astype(BF)
            copy_b(sec, k).start()
        if sec < 2:
            for k in range(1, 4):
                copy_c(sec + 2, k).wait_send()
        for row, rows, load in pieces(sec, d):
            at = slice(row, row + rows)
            q.st_c[at, :] = (load() + q.rc_a[z, at, :].astype(F32)).astype(BF)

    def quarter(sec, ref, who):
        rows = (MLP_ROWS if sec % 2 else ATT_ROWS) // 4
        return ref.at[pl.ds(pl.multiple_of(who * rows, 16), rows), :]

    def copy_c(sec, k):
        q = reduce_refs(sec)
        return remote(
            quarter(sec, q.st_c, lax.rem(me + k, 4)),
            q.rc_c.at[k - 1],
            r.rc_send.at[sec, k - 1],
            r.rc_recv.at[sec, k - 1],
            pipe_peer(k),
        )

    def step_3(sec):
        q = reduce_refs(sec)
        for k in range(1, 4):
            copy_b(sec, k).wait_recv()
        for row in range(0, q.st_c.shape[0], 64):
            at = slice(row, row + 64)
            total = q.st_c[at, :].astype(F32)
            for k in range(3):
                total = total + q.rc_b[k, at, :].astype(F32)
            q.st_c[at, :] = total.astype(BF)
        for k in range(1, 4):
            copy_c(sec, k).start()

    def copy_f(sec, k):
        q = reduce_refs(sec)
        own = quarter(sec, q.fin, me)
        return remote(own, own, r.rf_send.at[sec, k - 1], r.rf_recv.at[sec, k - 1], pipe_peer(k))

    def step_4(sec):
        q = reduce_refs(sec)
        for k in range(1, 4):
            copy_c(sec, k).wait_recv()
            if sec < 2:
                copy_f(sec + 2, k).wait_send()
        total = quarter(sec, q.st_c, me)[...].astype(F32)
        for k in range(3):
            total = total + q.rc_c[k].astype(F32)
        quarter(sec, q.fin, me)[...] = total.astype(BF)
        for k in range(1, 4):
            copy_f(sec, k).start()

    def copy_s(b, k):
        rows = pl.ds(SMALL, 64)
        return remote(
            r.a_fin.at[rows, :], r.o_small.at[b, d], r.rs_send.at[b, k - 1], r.rs_recv.at[b, k - 1], dp_peer(k)
        )

    def own_small(b):
        return pltpu.make_async_copy(r.a_fin.at[pl.ds(SMALL, 64), :], r.o_small.at[b, d], r.os_sem.at[b])

    def outputs(sec):
        pairs = ((g_fc1, r.o_fc1, 48), (g_fc2, r.o_fc2, 192)) if sec % 2 else (
            (g_qkv, r.o_qkv, 48), (g_proj, r.o_proj, 48))
        b = sec // 2
        return [
            pltpu.make_async_copy(ref.at[b, pl.ds(0, h), :], out.at[b], r.go_sem.at[sec, i])
            for i, (ref, out, h) in enumerate(pairs)
        ]

    def step_5(sec):
        q = reduce_refs(sec)
        b = sec // 2
        for k in range(1, 4):
            got = quarter(sec, q.fin, lax.rem(me + 4 - k, 4))
            remote(got, got, r.rf_send.at[sec, k - 1], r.rf_recv.at[sec, k - 1], pipe_peer(k)).wait_recv()
        if sec % 2 == 0:
            for k in range(1, 8):
                copy_s(b, k).start()
            own_small(b).start()
        row = 0
        for ref, h in ((g_fc1, 48), (g_fc2, 192)) if sec % 2 else ((g_qkv, 48), (g_proj, 48)):
            for t in range(h // 48):
                for j in range(ref.shape[2] // D):
                    ref[b, t * 48 : (t + 1) * 48, j * D : (j + 1) * D] = q.fin[row : row + 48, :].astype(F32)
                    row += 48
        for out in outputs(sec):
            out.start()

    def smalls_sent(b):
        for k in range(1, 8):
            copy_s(b, k).wait_send()
        own_small(b).wait()

    def reductions_done():
        for sec in (1, 0):
            copy_a(sec).wait_send()
            for k in range(1, 4):
                copy_b(sec, k).wait_send()
                copy_c(sec, k).wait_send()
                copy_f(sec, k).wait_send()
        for sec in range(4):
            for out in outputs(sec):
                out.wait()
        smalls_sent(0)
        for b in range(2):
            for k in range(1, 8):
                rows = pl.ds(SMALL, 64)
                remote(
                    r.a_fin.at[rows, :],
                    r.o_small.at[b, lax.rem(d + 8 - k, 8)],
                    r.rs_send.at[b, k - 1],
                    r.rs_recv.at[b, k - 1],
                    dp_peer(k),
                ).wait_recv()

    if linked:
        loads = [
            pltpu.make_async_copy(src, dst.at[:, pl.ds(0, h), :], r.sh_sem.at[i])
            for i, (src, dst, h) in enumerate(
                ((r.s_qkv, g_qkv, 48), (r.s_proj, g_proj, 48), (r.s_fc1, g_fc1, 48), (r.s_fc2, g_fc2, 192))
            )
        ]
        for load in loads:
            load.start()
        r.packs[d] = r.pack[...]
        for load in loads:
            load.wait()
        for ref, wide, h in ((wqkv, g_qkv, 48), (wproj, g_proj, 48), (fc1, g_fc1, 48), (fc2, g_fc2, 192)):
            for b in range(2):
                for t in range(h // 48):
                    rows = pl.ds(pl.multiple_of(d * h + t * 48, 16), 48)
                    ref[b, rows, :] = wide[b, t * 48 : (t + 1) * 48, :].astype(BF)
    pl.semaphore_wait(barrier, len(partners))
    if linked:
        for k in range(1, 8):
            pack_copy(k).start()
        send_weights(0)

    for ref in (g_qkv, g_proj, g_fc1, g_fc2):
        for b in range(2):

            @pl.loop(0, ref.shape[1] // 16)
            def _(i):
                ref[b, row_block(i, 16), :] = jnp.zeros((16, ref.shape[2]), F32)

    g_vec[...] = jnp.zeros_like(g_vec)
    g_tab[...] = jnp.zeros_like(g_tab)
    codew[...] = jnp.zeros_like(codew)

    if linked:
        for k in range(1, 8):
            pack_arrival(k).wait_recv()
        place_vectors()
        take_weights(0)
        for sec in range(1, 4):
            send_weights(sec)

    def vector(b, kind, width=D):
        return vec[b * 8 + kind : b * 8 + kind + 1, :width]

    def add_vec(b, kind, part):
        g_vec[b, kind, :, : part.shape[1]] += part

    def windowed(rows, count):
        return jnp.where(real_places(count), winf[rows, :], 0.0).astype(BF)

    def attention_forward(b, x, out):
        lanes = head_of_lane()

        @pl.loop(0, CELLS // TILE)
        def _(t):
            rows = row_block(t, TILE)
            xhat, _ = standardized(x[rows, :].astype(F32))
            canvf[rows, :] = xhat * vector(b, 0) + vector(b, 1)

        to_windows(canvf, winf, SHIFT * b)
        to_windows(code, codew, SHIFT * b)

        @pl.loop(0, 4)
        def _(t):
            rows = row_block(t, 256)
            hq = windowed(rows, 256)
            hqw[b, rows, :] = hq
            for part in range(3):
                cols = slice(part * D, (part + 1) * D)
                acc = nn(hq, wqkv[b, :, cols]) + vec[b * 8 + 6 : b * 8 + 7, cols]
                if part == 0:
                    acc = acc * SCALE
                qkv[b, rows, cols] = acc.astype(BF)

        @pl.loop(0, WINDOWS)
        def _(w):
            rows = row_block(w, PLACES)
            cells = codew[rows, :]
            region = (cells >> 1) * b
            pad = (cells & 1).astype(F32)
            lane = lax.broadcasted_iota(jnp.int32, (PLACES, 128), 1)
            same = jnp.where(lane == region, 1.0, 0.0)
            left = jnp.where(lane == 127, 1.0 - pad, same).astype(BF)
            right = jnp.where(lane == 127, -pad, same).astype(BF)
            agree = nt(left, jnp.concatenate([right, right], axis=0))
            mask = jnp.where(agree > 0.5, 0.0, MASKED)
            mask = jnp.concatenate([mask, mask], axis=1)
            for g in range(GROUPS):
                q = qkv[b, rows, g * 128 : (g + 1) * 128]
                k = qkv[b, rows, D + g * 128 : D + (g + 1) * 128]
                v = qkv[b, rows, 2 * D + g * 128 : 2 * D + (g + 1) * 128]
                s = nt(k, by_head(q, lanes)) + bias[b, g] + mask
                e = jnp.exp(s - jnp.max(s, axis=0, keepdims=True))
                p = (e * (1.0 / jnp.sum(e, axis=0, keepdims=True))).astype(BF)
                probs[b, w * GROUPS + g] = p
                att[b, rows, g * 128 : (g + 1) * 128] = own_head(tn(p, v), lanes).astype(BF)

        @pl.loop(0, 4)
        def _(t):
            rows = row_block(t, 256)
            winf[rows, :] = nn(att[b, rows, :], wproj[b])

        to_canvas(winf, canvf, SHIFT * b)

        @pl.loop(0, CELLS // TILE)
        def _(t):
            rows = row_block(t, TILE)
            out[rows, :] = (x[rows, :].astype(F32) + (canvf[rows, :] + vector(b, 2))).astype(BF)

    def mlp_forward(b, x, out):
        @pl.loop(0, CELLS // TILE)
        def _(t):
            rows = row_block(t, TILE)
            xhat, _ = standardized(x[rows, :].astype(F32))
            hq2[b, rows, :] = (xhat * vector(b, 3) + vector(b, 4)).astype(BF)

        @pl.loop(0, FF // 256)
        def _(i):
            cols = pl.ds(pl.multiple_of(i * 256, 256), 256)
            pre = nn(hq2[b], fc1[b, :, cols]) + vec[b * 8 + 7 : b * 8 + 8, cols]
            for at in range(0, CELLS, 16):
                h, dg = gelu_parts(pre[at : at + 16])
                hid[b, at : at + 16, cols] = h.astype(BF)
                dgelu[b, at : at + 16, cols] = dg.astype(BF)

        total = nn(hid[b], fc2[b])
        for at in range(0, CELLS, TILE):
            rows = slice(at, at + TILE)
            out[rows, :] = (x[rows, :].astype(F32) + (total[rows] + vector(b, 5))).astype(BF)

    def norm_backward(b, kind, x, gz, out):
        @pl.loop(0, CELLS // TILE)
        def _(t):
            rows = row_block(t, TILE)
            xhat, rs = standardized(x[rows, :].astype(F32))
            gn = canvf[rows, :]
            gzf = gz[rows, :].astype(F32)
            add_vec(b, kind, by_eights(gn * xhat))
            add_vec(b, kind + 1, by_eights(gn))
            add_vec(b, 5 if kind else 2, by_eights(gzf))
            g = gn * vector(b, kind)
            mg = jnp.mean(g, axis=-1, keepdims=True)
            mgx = jnp.mean(g * xhat, axis=-1, keepdims=True)
            out[rows, :] = (gzf + rs * (g - mg - xhat * mgx)).astype(BF)

    def mlp_backward(b, x, gz, out, free_out, hook):
        hook(0)
        wide_t[:, :CELLS] = hq2[b].T

        def chunk(i):
            cols = pl.ds(pl.multiple_of(i * 256, 256), 256)
            gh = nt(gz[...], fc2[b, cols, :])
            sums = jnp.zeros((8, 256), F32)
            for at in range(0, CELLS, 16):
                gp = (gh[at : at + 16] * dgelu[b, at : at + 16, cols].astype(F32)).astype(BF)
                dgelu[b, at : at + 16, cols] = gp
                sums = sums + by_eights(gp.astype(F32))
            g_vec[b, 7, :, cols] += sums
            g_fc1[b, :, cols] += nn(wide_t[:, :CELLS], dgelu[b, :, cols])
            g_fc2[b, cols, :] += tn(hid[b, :, cols], gz[...])

        pl.loop(0, FF // 512)(chunk)
        hook(1)
        pl.loop(FF // 512, FF // 256)(chunk)
        hook(2)
        canvf[...] = nt(dgelu[b], fc1[b])
        hook(3)
        free_out()
        norm_backward(b, 3, x, gz, out)
        hook(4)

    def attention_backward(b, x, gz, out, free_out, hook):
        lanes = head_of_lane()
        hook(0)

        @pl.loop(0, CELLS // TILE)
        def _(t):
            rows = row_block(t, TILE)
            canvf[rows, :] = gz[rows, :].astype(F32)

        to_windows(canvf, winf, SHIFT * b)

        @pl.loop(0, 4)
        def _(t):
            rows = row_block(t, 256)
            gzw[rows, :] = windowed(rows, 256)

        g_proj[b] += tn(att[b], gzw[...])

        @pl.loop(0, 4)
        def _(t):
            rows = row_block(t, 256)
            att[b, rows, :] = nt(gzw[rows, :], wproj[b]).astype(BF)

        hook(1)

        def window(w):
            rows = row_block(w, PLACES)
            for g in range(GROUPS):
                at = [slice(part * D + g * 128, part * D + (g + 1) * 128) for part in range(3)]
                q, k, v = (qkv[b, rows, cols] for cols in at)
                go_wide = by_head(att[b, rows, at[0]], lanes)
                p_low = probs[b, w * GROUPS + g]
                p = p_low.astype(F32)
                pd = p * nt(v, go_wide)
                ds = (pd - p * jnp.sum(pd, axis=0, keepdims=True)).astype(BF)
                g_tab[b, :, g * 256 : (g + 1) * 256] += ds.astype(F32)
                qkv[b, rows, at[0]] = (own_head(tn(ds, k), lanes) * SCALE).astype(BF)
                qkv[b, rows, at[1]] = nn(ds, by_head(q, lanes)).astype(BF)
                qkv[b, rows, at[2]] = nn(p_low, go_wide).astype(BF)

        pl.loop(0, WINDOWS // 2)(window)
        hook(2)
        pl.loop(WINDOWS // 2, WINDOWS)(window)
        hook(3)

        @pl.loop(0, 4)
        def _(t):
            rows = row_block(t, 256)
            gq = qkv[b, rows, :]
            add_vec(b, 6, by_eights(gq.astype(F32)))
            winf[rows, :] = nt(gq, wqkv[b])

        to_canvas(winf, canvf, SHIFT * b)
        free_out()
        norm_backward(b, 0, x, gz, out)

    def attention_weights(b):
        wide_t[...] = hqw[b].T
        for part in range(3):
            cols = slice(part * D, (part + 1) * D)
            g_qkv[b, :, cols] += nn(wide_t[...], qkv[b, :, cols])

    def push(kind, s, n, start):
        src = buf.at[s]
        dst = (r.act_hbm, r.igrad_hbm)[kind].at[me, n]
        local = pltpu.make_async_copy(src, dst, r.local_sem.at[kind, n])
        away = remote(src, dst, r.send_sem.at[kind, s, n], r.recv_sem.at[kind, me, n], {"pipe": s})

        @pl.when(me == s)
        def _():
            local.start() if start else local.wait()

        @pl.when(me != s)
        def _():
            away.start() if start else away.wait_send()

    def arrived(kind, k, n):
        sender = lax.rem(me + k, 4)
        dst = (r.act_hbm, r.igrad_hbm)[kind].at[sender, n]
        remote(
            buf.at[0], dst, r.send_sem.at[kind, 0, n], r.recv_sem.at[kind, sender, n], {"pipe": sender}
        ).wait_recv()

    steps = (step_1, step_2, step_3, step_4, step_5)
    schedule = {
        (3, 2): ((1, 3),),
        (2, 0): ((2, 3),),
        (2, 4): ((3, 3), (1, 2)),
        (1, 0): ((2, 2),),
        (1, 1): ((4, 3),),
        (1, 2): ((1, 1),),
        (0, 0): ((3, 2), (2, 1)),
        (0, 1): ((5, 3),),
        (0, 2): ((4, 2),),
        (0, 3): ((5, 2), (3, 1)),
        (0, 4): ((4, 1),),
    }

    @pl.loop(0, canvases)
    def _(n):
        def hook(sec, i):
            todo = schedule.get((sec, i), ())
            if linked and todo:

                @pl.when(n == canvases - 1)
                def _():
                    for step, of in todo:
                        steps[step - 1](of)

        def weights_for(sec):
            if linked:

                @pl.when(n == 0)
                def _():
                    take_weights(sec)

        loads = [
            pltpu.make_async_copy(r.x_hbm.at[me, n], xin, r.in_sem.at[0]),
            pltpu.make_async_copy(r.cot_hbm.at[me, n], cot, r.in_sem.at[1]),
            pltpu.make_async_copy(r.code_hbm.at[n], code, r.in_sem.at[2]),
        ]
        for load in loads:
            load.start()
        for load in loads:
            load.wait()

        x = xin
        for s in range(4):
            @pl.when(n > 0)
            def _():
                push(1, s, n - 1, False)

            (mlp_forward if s % 2 else attention_forward)(s // 2, x, buf.at[s])
            x = buf.at[s]
            push(0, s, n, True)
            if s < 3:
                weights_for(s + 1)
        gz = cot
        for s in (3, 2, 1, 0):
            x = buf.at[s - 1] if s else xin
            backward = mlp_backward if s % 2 else attention_backward
            backward(
                s // 2, x, gz, buf.at[s], functools.partial(push, 0, s, n, False), functools.partial(hook, s)
            )
            gz = buf.at[s]
            push(1, s, n, True)
            if s % 2 == 0:
                attention_weights(s // 2)
                hook(s, 4)

    if linked:
        step_5(1)
        step_1(0)
        step_2(0)
        smalls_sent(1)
        step_3(0)
        step_4(0)
        step_5(0)
        reductions_done()
        weights_sent()
        for k in range(1, 8):
            pack_copy(k).wait_send()
    for kind in range(2):
        for k in range(1, 4):
            for n in range(canvases):
                arrived(kind, k, n)
    for s in range(4):
        push(1, s, canvases - 1, False)


def compute(linked, operands):
    canvases = operands["x_hbm"].shape[1]
    shape = jax.ShapeDtypeStruct
    hbm = pl.BlockSpec(memory_space=pl.ANY)
    vmem = pl.BlockSpec(memory_space=pltpu.VMEM)
    dma = pltpu.SemaphoreType.DMA
    full = {
        "wqkv": ((2, D, 3 * D), BF),
        "wproj": ((2, D, D), BF),
        "fc1": ((2, D, FF), BF),
        "fc2": ((2, FF, D), BF),
        "vec": ((16, FF), F32),
    }
    grads = {
        "g_qkv": ((2, D, 3 * D), F32),
        "g_proj": ((2, D, D), F32),
        "g_fc1": ((2, D, FF), F32),
        "g_fc2": ((2, FF, D), F32),
        "g_vec": ((2, 8, 8, FF), F32),
        "g_tab": ((2, PLACES, GROUPS * 256), F32),
    }
    outs = {"act_hbm": ((4, canvases, CELLS, D), BF), "igrad_hbm": ((4, canvases, CELLS, D), BF)}
    scratch = {
        "xin": ((CELLS, D), BF),
        "cot": ((CELLS, D), BF),
        "code": ((CELLS, 128), jnp.int32),
        "codew": ((WROWS, 128), jnp.int32),
        "buf": ((4, CELLS, D), BF),
        "hqw": ((2, WROWS, D), BF),
        "qkv": ((2, WROWS, 3 * D), BF),
        "probs": ((2, WINDOWS * GROUPS, PLACES, 256), BF),
        "att": ((2, WROWS, D), BF),
        "hq2": ((2, CELLS, D), BF),
        "hid": ((2, CELLS, FF), BF),
        "dgelu": ((2, CELLS, FF), BF),
        "canvf": ((CELLS, D), F32),
        "winf": ((WROWS, D), F32),
        "gzw": ((WROWS, D), BF),
        "wide_t": ((D, WROWS), BF),
    }
    sems = {
        "in_sem": (3,),
        "local_sem": (2, canvases),
        "send_sem": (2, 4, canvases),
        "recv_sem": (2, 4, canvases),
    }
    if linked:
        outs |= {
            "o_qkv": ((2, 48, 3 * D), F32),
            "o_proj": ((2, 48, D), F32),
            "o_fc1": ((2, 48, FF), F32),
            "o_fc2": ((2, 192, D), F32),
            "o_small": ((2, 8, 64, D), BF),
        }
        scratch |= full | grads
        scratch["packs"] = ((8, 16, 256), BF)
        for kind, rows in (("m_", MLP_ROWS), ("a_", ATT_ROWS)):
            scratch |= {
                kind + "st_a": ((4, rows, D), BF),
                kind + "rc_a": ((4, rows, D), BF),
                kind + "st_b": ((3, rows, D), BF),
                kind + "rc_b": ((3, rows, D), BF),
                kind + "st_c": ((rows, D), BF),
                kind + "rc_c": ((3, rows // 4, D), BF),
                kind + "fin": ((rows, D), BF),
            }
        sems |= {
            "sh_sem": (4,),
            "os_sem": (2,),
            "go_sem": (4, 2),
            "wz_send": (4, 2, 3),
            "wz_recv": (4, 2, 3),
            "ws_send": (4, 2, 4),
            "ws_recv": (4, 2, 4),
            "pk_send": (7,),
            "pk_recv": (7,),
            "ra_send": (4,),
            "ra_recv": (4,),
            "rb_send": (4, 3),
            "rb_recv": (4, 3),
            "rc_send": (4, 3),
            "rc_recv": (4, 3),
            "rf_send": (4, 3),
            "rf_recv": (4, 3),
            "rs_send": (2, 7),
            "rs_recv": (2, 7),
        }
    else:
        outs |= grads
    in_vmem = set(grads) | set(full) | {"bias", "pack"}
    names = tuple(operands) + tuple(outs) + tuple(scratch) + tuple(sems)
    results = pl.pallas_call(
        functools.partial(kernel, names, linked, canvases),
        out_shape=tuple(shape(*o) for o in outs.values()),
        in_specs=[vmem if name in in_vmem else hbm for name in operands],
        out_specs=tuple(vmem if name in in_vmem else hbm for name in outs),
        scratch_shapes=[pltpu.VMEM(*v) for v in scratch.values()] + [dma(v) for v in sems.values()],
        compiler_params=pltpu.CompilerParams(
            vmem_limit_bytes=64 * 1024 * 1024 - 65536, collective_id=0, has_side_effects=True
        ),
    )(*operands.values())
    return dict(zip(outs, results))


def place_pairs():
    place = np.arange(PLACES)
    r, c = place // 8, place % 8
    index = (r[None, :] - r[:, None] + WIN - 1) * (2 * WIN - 1) + c[None, :] - c[:, None] + WIN - 1
    real = (r < WIN) & (c < WIN)
    return index, real[:, None] & real[None, :], real


def pair_onehot():
    index, both, _ = place_pairs()
    table = (2 * WIN - 1) ** 2
    hot = (np.where(both, index, -1).reshape(-1)[None, :] == np.arange(table)[:, None])
    return hot.astype(np.float32)


def body(
    inputs,
    cotangent,
    pad_mask,
    region_ids,
    norm1_gain,
    norm1_bias,
    qkv_weight,
    qv_bias,
    rel_table,
    proj_weight,
    proj_bias,
    norm2_gain,
    norm2_bias,
    fc1_weight,
    fc1_bias,
    fc2_weight,
    fc2_bias,
):
    owners = lax.axis_size("dp")
    linked = owners == 8
    mine = lax.axis_index("pipe")

    def own(a):
        return lax.dynamic_index_in_dim(a, mine, 0, keepdims=False)

    code = own(region_ids) * 2 + own(pad_mask)
    code = jnp.broadcast_to(code[:, :, None], code.shape + (128,))

    hot = pair_onehot()
    _, _, real = place_pairs()
    rel = lax.dot_general(
        rel_table.astype(BF), jnp.asarray(hot, BF), (((1,), (0,)), ((), ())), preferred_element_type=F32
    )
    rel = rel.reshape(2, GROUPS, 4, PLACES, PLACES).transpose(0, 1, 3, 2, 4)
    rel = jnp.where(jnp.asarray(real)[None, None, :, None, None], rel, MASKED)
    rel = rel.reshape(2, GROUPS, PLACES, 256)

    operands = {"x_hbm": inputs, "cot_hbm": cotangent, "code_hbm": code, "bias": rel}
    vectors = (norm1_gain, norm1_bias, proj_bias, norm2_gain, norm2_bias, fc2_bias, qv_bias, fc1_bias)
    sizes = [v.shape[1] for v in vectors]
    ends = np.cumsum([0] + sizes)
    if linked:
        pack = jnp.stack([jnp.pad(v, ((0, 0), (0, 256 - v.shape[1]))) for v in vectors], axis=1)
        operands |= {
            "pack": pack.reshape(16, 256).astype(BF),
            "s_qkv": qkv_weight,
            "s_proj": proj_weight,
            "s_fc1": fc1_weight,
            "s_fc2": fc2_weight,
        }
    else:

        def gathered(a):
            return lax.all_gather(a.astype(BF), "dp", axis=1, tiled=True)

        packed = lax.all_gather(jnp.concatenate(vectors, axis=1).astype(BF), "dp", axis=1)
        parts = [packed[:, :, a:b].reshape(2, -1).astype(F32) for a, b in zip(ends[:-1], ends[1:])]
        qv = parts[6]
        parts[6] = jnp.concatenate([qv[:, :D], jnp.zeros_like(qv[:, :D]), qv[:, D:]], axis=1)
        vec = jnp.stack([jnp.pad(p, ((0, 0), (0, FF - p.shape[1]))) for p in parts], axis=1)
        operands |= {
            "wqkv": gathered(qkv_weight),
            "wproj": gathered(proj_weight),
            "fc1": gathered(fc1_weight),
            "fc2": gathered(fc2_weight),
            "vec": vec.reshape(16, FF),
        }

    out = compute(linked, operands)

    def to_owners(g):
        shared = lax.psum_scatter(g, "dp", scatter_dimension=1, tiled=True)
        return lax.psum(shared, "pipe")

    if linked:
        small = out["o_small"].astype(F32)
        g_tab = jnp.concatenate([small[:, :, :8], small[:, :, 8:16]], axis=3).reshape(2, PLACES, GROUPS * 256)
        g_vec = jnp.concatenate([small[:, :, 16 + 8 * j : 24 + 8 * j] for j in range(4)], axis=3)
    else:
        g_tab, g_vec = out["g_tab"], out["g_vec"]

    g_vec = jnp.sum(g_vec, axis=2)
    kinds = [g_vec[:, i] for i in range(8)]
    qv_sum = jnp.concatenate([kinds[6][:, :D], kinds[6][:, 2 * D : 3 * D]], axis=1)
    rows = [kinds[0], kinds[1], kinds[2], kinds[3], kinds[4], kinds[5], qv_sum, kinds[7]]
    if linked:
        at = lax.axis_index("dp")
        small = [lax.dynamic_slice_in_dim(v, at * n, n, 1) for v, n in zip(rows, sizes)]
    else:
        rows = [v[:, : n * owners].reshape(2, -1, n) for v, n in zip(rows, sizes)]
        g_small = to_owners(jnp.concatenate(rows, axis=2))[:, 0]
        small = [g_small[:, a:b] for a, b in zip(ends[:-1], ends[1:])]

    pairs = g_tab.reshape(2, PLACES, HEADS, PLACES).transpose(0, 2, 1, 3)
    pairs = pairs.reshape(2, HEADS, PLACES * PLACES)
    g_table = lax.dot_general(
        jnp.broadcast_to(jnp.asarray(hot), (2,) + hot.shape),
        pairs,
        (((2,), (2,)), ((0,), (0,))),
        precision=lax.Precision.HIGHEST,
        preferred_element_type=F32,
    )
    if linked:
        big = [out[name] for name in ("o_qkv", "o_proj", "o_fc1", "o_fc2")]
    else:
        g_table = lax.psum(g_table, ("pipe", "dp"))
        big = [to_owners(out[name]) for name in ("g_qkv", "g_proj", "g_fc1", "g_fc2")]

    return (
        out["act_hbm"][None],
        out["igrad_hbm"][None],
        small[0],
        small[1],
        big[0],
        small[6],
        g_table,
        big[1],
        small[2],
        small[3],
        small[4],
        big[2],
        small[7],
        big[3],
        small[5],
    )


def solution(mesh):
    cols = P(None, "dp")
    rows = P(None, "dp", None)
    return jax.shard_map(
        body,
        mesh=mesh,
        in_specs=(
            P(None, "dp", None, None),
            P(None, "dp", None, None),
            rows,
            rows,
            cols,
            cols,
            rows,
            cols,
            P(),
            rows,
            cols,
            cols,
            cols,
            rows,
            cols,
            rows,
            cols,
        ),
        out_specs=(
            P("pipe", None, "dp", None, None),
            P("pipe", None, "dp", None, None),
            cols,
            cols,
            rows,
            cols,
            P(),
            rows,
            cols,
            cols,
            cols,
            rows,
            cols,
            rows,
            cols,
        ),
        check_vma=False,
    )
```

```python
import functools
import types

import jax
import jax.numpy as jnp
import numpy as np
from jax import lax
from jax.experimental import pallas as pl
from jax.experimental.pallas import tpu as pltpu
from jax.sharding import PartitionSpec as P

HEADS = 12
WIN = 7
SHIFT = 3
GRID = 28
CELLS = 784
D = 384
FF = 1536
HEAD = 32
SIDE = 4
WINDOWS = 16
PLACES = 64
WROWS = WINDOWS * PLACES
GROUPS = 3
TILE = 112
SCALE = HEAD**-0.5
NORM_EPS = 1e-05
MASKED = -1e30
BF = jnp.bfloat16
F32 = jnp.float32

ERF_P = 0.3275911 / np.sqrt(2.0)
ERF_A = [0.5 * a for a in (0.254829592, -0.284496736, 1.421413741, -1.453152027, 1.061405429)]
PHI_0 = 1.0 / np.sqrt(2.0 * np.pi)


def nn(a, b):
    return lax.dot_general(a, b, (((1,), (0,)), ((), ())), preferred_element_type=F32)


def nt(a, b):
    return lax.dot_general(a, b, (((1,), (1,)), ((), ())), preferred_element_type=F32)


def tn(a, b):
    return lax.dot_general(a, b, (((0,), (0,)), ((), ())), preferred_element_type=F32)


def segments(shift):
    runs = []
    for wr in range(SIDE):
        for r in range(WIN):
            row = (wr * WIN + r + shift) % GRID
            for wc in range(SIDE):
                col = (wc * WIN + shift) % GRID
                place = (wr * SIDE + wc) * PLACES + r * 8
                first = min(WIN, GRID - col)
                runs.append((row * GRID + col, place, first))
                if first < WIN:
                    runs.append((row * GRID, place + first, WIN - first))
    return runs


def to_windows(src, dst, shift):
    for cell, place, count in segments(shift):
        dst[pl.ds(place, count), :] = src[pl.ds(cell, count), :]


def to_canvas(src, dst, shift):
    for cell, place, count in segments(shift):
        dst[pl.ds(cell, count), :] = src[pl.ds(place, count), :]


def row_block(t, size):
    return pl.ds(pl.multiple_of(t * size, 16), size)


def standardized(v):
    centered = v - jnp.mean(v, axis=-1, keepdims=True)
    spread = jnp.mean(centered * centered, axis=-1, keepdims=True)
    rs = lax.rsqrt(spread + NORM_EPS)
    return centered * rs, rs


def by_eights(v):
    return jnp.sum(v.reshape(v.shape[0] // 8, 8, v.shape[1]), axis=0)


def gelu_parts(x):
    den = 1.0 + ERF_P * jnp.abs(x)
    t = pl.reciprocal(den, approx=True)
    t = t * (2.0 - den * t)
    e = jnp.exp(-0.5 * x * x)
    poly = ERF_A[4]
    for a in ERF_A[3::-1]:
        poly = poly * t + a
    tail = poly * t * e
    cdf = jnp.where(x >= 0.0, 1.0 - tail, tail)
    return x * cdf, cdf + x * (e * PHI_0)


def real_places(rows):
    place = lax.broadcasted_iota(jnp.int32, (rows, 1), 0)
    return ((place & 7) < WIN) & (((place >> 3) & 7) < WIN)


def head_of_lane():
    return lax.broadcasted_iota(jnp.int32, (PLACES, 128), 1) >> 5


def by_head(x, lanes):
    zero = jnp.zeros_like(x)
    return jnp.concatenate([jnp.where(lanes == h, x, zero) for h in range(4)], axis=0)


def own_head(wide, lanes):
    out = wide[3 * PLACES :]
    for h in (2, 1, 0):
        out = jnp.where(lanes == h, wide[h * PLACES : (h + 1) * PLACES], out)
    return out


MESH = pl.DeviceIdType.MESH
ATT_ROWS = 256
MLP_ROWS = 384
SMALL = 192


def kernel(names, linked, canvases, *refs):
    r = types.SimpleNamespace(**dict(zip(names, refs)))
    me = lax.axis_index("pipe")
    xin, cot, code, codew, buf = r.xin, r.cot, r.code, r.codew, r.buf
    hqw, qkv, probs, att = r.hqw, r.qkv, r.probs, r.att
    hq2, hid, dgelu = r.hq2, r.hid, r.dgelu
    canvf, winf, gzw, wide_t = r.canvf, r.winf, r.gzw, r.wide_t
    g_qkv, g_proj, g_fc1, g_fc2t, g_vec, g_tab = r.g_qkv, r.g_proj, r.g_fc1, r.g_fc2t, r.g_vec, r.g_tab
    wat, fc1, fc2, vec, bias = r.wat, r.fc1, r.fc2, r.vec, r.bias
    if linked:
        d = lax.axis_index("dp")
        z, c = d // 2, d % 2
        sibling = {"dp": 2 * z + 1 - c}

    def z_peer(k):
        return {"dp": 2 * lax.rem(z + k, 4) + c}

    def pipe_peer(k):
        return {"pipe": lax.rem(me + k, 4)}

    def dp_peer(k):
        return {"dp": lax.rem(d + k, 8)}

    def remote(src, dst, send, recv, device):
        return pltpu.make_async_remote_copy(
            src_ref=src, dst_ref=dst, send_sem=send, recv_sem=recv, device_id=device, device_id_type=MESH
        )

    barrier = pltpu.get_barrier_semaphore()
    partners = [pipe_peer(k) for k in range(1, 4)]
    if linked:
        partners += [dp_peer(k) for k in range(1, 8)]
    for partner in partners:
        pl.semaphore_signal(barrier, inc=1, device_id=partner, device_id_type=MESH)

    full = ((wat,), (fc1, fc2), (wat,), (fc1, fc2))

    def owner_back(k):
        return 2 * lax.rem(z + 4 - k, 4) + c

    def shard(sec, a, owner):
        h = 192 if a else 48
        return full[sec][a].at[sec // 2, pl.ds(pl.multiple_of(owner * h, 16), h), :]

    def part(sec, a, owner, place):
        if a:
            return fc2.at[sec // 2, pl.ds(pl.multiple_of(owner * 192 + place * 48, 16), 48), :]
        rows = pl.ds(pl.multiple_of(owner * 48, 16), 48)
        return full[sec][0].at[sec // 2, rows, pl.ds(pl.multiple_of(place * D, 128), D)]

    def to_z(sec, a, k):
        own = part(sec, a, d, me)
        return remote(own, own, r.wz_send.at[sec, a, k - 1], r.wz_recv.at[sec, a, k - 1], z_peer(k))

    def to_places(sec, a, k, j):
        got = part(sec, a, owner_back(k), me)
        return remote(
            got, got, r.wx_send.at[sec, a, k - 1, j - 1], r.wx_recv.at[sec, a, k - 1, j - 1], pipe_peer(j)
        )

    def to_sibling(sec, a, k):
        block = shard(sec, a, owner_back(k))
        return remote(block, block, r.ws_send.at[sec, a, k], r.ws_recv.at[sec, a, k], sibling)

    def weights_1(sec):
        for a in range(len(full[sec])):
            for k in range(1, 4):
                to_z(sec, a, k).start()
            to_sibling(sec, a, 0).start()

    def weights_2(sec):
        for k in range(1, 4):
            for a in range(len(full[sec])):
                got = part(sec, a, owner_back(k), me)
                remote(got, got, r.wz_send.at[sec, a, k - 1], r.wz_recv.at[sec, a, k - 1], z_peer(k)).wait_recv()
                for j in range(1, 4):
                    to_places(sec, a, k, j).start()

    def weights_3(sec):
        for k in range(1, 4):
            for a in range(len(full[sec])):
                for j in range(1, 4):
                    got = part(sec, a, owner_back(k), lax.rem(me + 4 - j, 4))
                    remote(
                        got, got, r.wx_send.at[sec, a, k - 1, j - 1], r.wx_recv.at[sec, a, k - 1, j - 1], pipe_peer(j)
                    ).wait_recv()
                to_sibling(sec, a, k).start()

    def weights_4(sec):
        for k in range(4):
            for a in range(len(full[sec])):
                block = shard(sec, a, 2 * lax.rem(z + 4 - k, 4) + 1 - c)
                remote(block, block, r.ws_send.at[sec, a, k], r.ws_recv.at[sec, a, k], sibling).wait_recv()

    def weights_sent():
        for sec in range(4):
            for a in range(len(full[sec])):
                for k in range(4):
                    to_sibling(sec, a, k).wait_send()
                    if k:
                        to_z(sec, a, k).wait_send()
                        for j in range(1, 4):
                            to_places(sec, a, k, j).wait_send()

    def pack_copy(k):
        return remote(
            r.packs.at[d], r.packs.at[d], r.pk_send.at[k - 1], r.pk_recv.at[k - 1], dp_peer(k)
        )

    def pack_arrival(k):
        slot = r.packs.at[lax.rem(d + 8 - k, 8)]
        return remote(slot, slot, r.pk_send.at[k - 1], r.pk_recv.at[k - 1], dp_peer(k))

    def place_vectors():
        row = lax.broadcasted_iota(jnp.int32, (16, 1), 0) & 7
        lane = lax.broadcasted_iota(jnp.int32, (256, 256), 0)
        goal = lax.broadcasted_iota(jnp.int32, (256, 256), 1)
        vec[...] = jnp.zeros_like(vec)
        for width, kinds in ((48, row < 6), (96, row == 6), (192, row == 7)):
            for owner in range(8):
                at = owner * width
                if width == 96 and owner >= 4:
                    at += D
                start = at // 128 * 128
                hot = jnp.where((lane < width) & (goal == lane + (at - start)), 1.0, 0.0).astype(BF)
                part = jnp.where(kinds, nn(r.packs[owner], hot), 0.0)
                vec[:, start : start + 256] += part

    def pieces(sec, owner):
        b = sec // 2
        out = []

        def matrix(ref, h):
            for t in range(h // 48):
                rows = pl.ds(pl.multiple_of(owner * h + t * 48, 16), 48)
                for j in range(ref.shape[2] // D):
                    load = functools.partial(lambda ref, rows, j: ref[b, rows, j * D : (j + 1) * D], ref, rows, j)
                    out.append((len(out) * 48, 48, load))

        def small():
            rows = pl.ds(pl.multiple_of(owner * 8, 8), 8)
            parts = [g_tab[b, rows, j * D : (j + 1) * D] for j in range(2)]
            parts += [g_vec[b, owner, :, j * D : (j + 1) * D] for j in range(4)]
            return jnp.concatenate(parts + [jnp.zeros((16, D), F32)], axis=0)

        if sec % 2:
            matrix(g_fc1, 48)
        else:
            matrix(g_qkv, 48)
            matrix(g_proj, 48)
            out.append((SMALL, 64, small))
        return out

    def reduce_refs(sec):
        kind = "m" if sec % 2 else "a"
        return types.SimpleNamespace(
            **{n: getattr(r, kind + "_" + n) for n in ("st_a", "rc_a", "st_b", "rc_b", "st_c", "rc_c", "fin")}
        )

    def step_1(sec):
        q = reduce_refs(sec)
        if sec < 2:
            copy_a(sec + 2).wait_send()
            for k in range(1, 4):
                copy_b(sec + 2, k).wait_send()
                copy_c(sec + 2, k).wait_send()
        for k in range(4):
            i = lax.rem(z + k, 4)
            kept = q.st_b.at[k - 1] if k else q.st_c
            for row, rows, load in pieces(sec, 2 * i + 1 - c):
                q.st_a[i, row : row + rows, :] = load().astype(BF)
            for row, rows, load in pieces(sec, 2 * i + c):
                kept[row : row + rows, :] = load().astype(BF)
            if sec % 2:
                winf[:D, :] = g_fc2t[sec // 2, :, pl.ds(pl.multiple_of(i * D, 128), D)].T
                for t in range(0, 192, 48):
                    at = slice(192 + t, 240 + t)
                    q.st_a[i, at, :] = winf[pl.ds(pl.multiple_of((1 - c) * 192 + t, 16), 48), :].astype(BF)
                    kept[at, :] = winf[pl.ds(pl.multiple_of(c * 192 + t, 16), 48), :].astype(BF)
        copy_a(sec).start()

    def copy_a(sec):
        q = reduce_refs(sec)
        return remote(q.st_a, q.rc_a, r.ra_send.at[sec], r.ra_recv.at[sec], sibling)

    def copy_b(sec, k):
        q = reduce_refs(sec)
        return remote(
            q.st_b.at[k - 1], q.rc_b.at[k - 1], r.rb_send.at[sec, k - 1], r.rb_recv.at[sec, k - 1], z_peer(k)
        )

    def step_2(sec):
        q = reduce_refs(sec)
        copy_a(sec).wait_recv()
        for k in (1, 2, 3, 0):
            i = lax.rem(z + k, 4)
            kept = q.st_b.at[k - 1] if k else q.st_c
            for row in range(0, kept.shape[0], 64):
                at = slice(row, row + 64)
                kept[at, :] = (kept[at, :].astype(F32) + q.rc_a[i, at, :].astype(F32)).astype(BF)
            if k:
                copy_b(sec, k).start()

    def quarter(sec, ref, who):
        rows = (MLP_ROWS if sec % 2 else ATT_ROWS) // 4
        return ref.at[pl.ds(pl.multiple_of(who * rows, 16), rows), :]

    def copy_c(sec, k):
        q = reduce_refs(sec)
        return remote(
            quarter(sec, q.st_c, lax.rem(me + k, 4)),
            q.rc_c.at[k - 1],
            r.rc_send.at[sec, k - 1],
            r.rc_recv.at[sec, k - 1],
            pipe_peer(k),
        )

    def step_3(sec):
        q = reduce_refs(sec)
        for k in range(1, 4):
            copy_b(sec, k).wait_recv()
        for row in range(0, q.st_c.shape[0], 64):
            at = slice(row, row + 64)
            total = q.st_c[at, :].astype(F32)
            for k in range(3):
                total = total + q.rc_b[k, at, :].astype(F32)
            q.st_c[at, :] = total.astype(BF)
        for k in range(1, 4):
            copy_c(sec, k).start()

    def copy_f(sec, k):
        q = reduce_refs(sec)
        own = quarter(sec, q.fin, me)
        return remote(own, own, r.rf_send.at[sec, k - 1], r.rf_recv.at[sec, k - 1], pipe_peer(k))

    def step_4(sec):
        q = reduce_refs(sec)
        for k in range(1, 4):
            copy_c(sec, k).wait_recv()
            if sec < 2:
                copy_f(sec + 2, k).wait_send()
        total = quarter(sec, q.st_c, me)[...].astype(F32)
        for k in range(3):
            total = total + q.rc_c[k].astype(F32)
        quarter(sec, q.fin, me)[...] = total.astype(BF)
        for k in range(1, 4):
            copy_f(sec, k).start()

    def copy_s(b, k):
        rows = pl.ds(SMALL, 64)
        return remote(
            r.a_fin.at[rows, :], r.o_small.at[b, d], r.rs_send.at[b, k - 1], r.rs_recv.at[b, k - 1], dp_peer(k)
        )

    def own_small(b):
        return pltpu.make_async_copy(r.a_fin.at[pl.ds(SMALL, 64), :], r.o_small.at[b, d], r.os_sem.at[b])

    def outputs(sec):
        pairs = ((g_fc1, r.o_fc1, 48), (g_fc2t, r.o_fc2, 192)) if sec % 2 else (
            (g_qkv, r.o_qkv, 48), (g_proj, r.o_proj, 48))
        b = sec // 2
        return [
            pltpu.make_async_copy(ref.at[b, pl.ds(0, h), pl.ds(0, out.shape[2])], out.at[b], r.go_sem.at[sec, i])
            for i, (ref, out, h) in enumerate(pairs)
        ]

    def step_5(sec):
        q = reduce_refs(sec)
        b = sec // 2
        for k in range(1, 4):
            got = quarter(sec, q.fin, lax.rem(me + 4 - k, 4))
            remote(got, got, r.rf_send.at[sec, k - 1], r.rf_recv.at[sec, k - 1], pipe_peer(k)).wait_recv()
        if sec % 2 == 0:
            for k in range(1, 8):
                copy_s(b, k).start()
            own_small(b).start()
        row = 0
        for ref, h, n in ((g_fc1, 48, 4), (g_fc2t, 192, 1)) if sec % 2 else ((g_qkv, 48, 3), (g_proj, 48, 1)):
            for t in range(h // 48):
                for j in range(n):
                    ref[b, t * 48 : (t + 1) * 48, j * D : (j + 1) * D] = q.fin[row : row + 48, :].astype(F32)
                    row += 48
        for out in outputs(sec):
            out.start()

    def smalls_sent(b):
        for k in range(1, 8):
            copy_s(b, k).wait_send()
        own_small(b).wait()

    def reductions_done():
        for sec in (1, 0):
            copy_a(sec).wait_send()
            for k in range(1, 4):
                copy_b(sec, k).wait_send()
                copy_c(sec, k).wait_send()
                copy_f(sec, k).wait_send()
        for sec in range(4):
            for out in outputs(sec):
                out.wait()
        smalls_sent(0)
        for b in range(2):
            for k in range(1, 8):
                rows = pl.ds(SMALL, 64)
                remote(
                    r.a_fin.at[rows, :],
                    r.o_small.at[b, lax.rem(d + 8 - k, 8)],
                    r.rs_send.at[b, k - 1],
                    r.rs_recv.at[b, k - 1],
                    dp_peer(k),
                ).wait_recv()

    if linked:
        lands = ((r.s_qkv, g_qkv, 48, wat, 0), (r.s_proj, g_proj, 48, wat, 3 * D), (r.s_fc1, g_fc1, 48, fc1, 0), (r.s_fc2, g_fc2t, 192, fc2, 0))
        loads = [
            pltpu.make_async_copy(src, dst.at[:, pl.ds(0, h), pl.ds(0, src.shape[2])], r.sh_sem.at[i])
            for i, (src, dst, h, _, _) in enumerate(lands)
        ]
        for load in loads:
            load.start()
        r.packs[d] = r.pack[...]
        for load in loads:
            load.wait()
        for src, wide, h, ref, col in lands:
            n = src.shape[2]
            for b in range(2):
                for t in range(h // 48):
                    rows = pl.ds(pl.multiple_of(d * h + t * 48, 16), 48)
                    ref[b, rows, col : col + n] = wide[b, t * 48 : (t + 1) * 48, :n].astype(BF)
    pl.semaphore_wait(barrier, len(partners))
    if linked:
        for k in range(1, 8):
            pack_copy(k).start()
        weights_1(0)

    for ref in (g_qkv, g_proj, g_fc1, g_fc2t):
        for b in range(2):

            @pl.loop(0, ref.shape[1] // 16)
            def _(i):
                ref[b, row_block(i, 16), :] = jnp.zeros((16, ref.shape[2]), F32)

    g_vec[...] = jnp.zeros_like(g_vec)
    g_tab[...] = jnp.zeros_like(g_tab)
    codew[...] = jnp.zeros_like(codew)

    if linked:
        weights_2(0)
        for sec in range(1, 4):
            weights_1(sec)
        for k in range(1, 8):
            pack_arrival(k).wait_recv()
        place_vectors()
        weights_3(0)
        weights_4(0)

    def vector(b, kind, width=D):
        return vec[b * 8 + kind : b * 8 + kind + 1, :width]

    def add_vec(b, kind, part):
        g_vec[b, kind, :, : part.shape[1]] += part

    def windowed(rows, count):
        return jnp.where(real_places(count), winf[rows, :], 0.0).astype(BF)

    def by_two(start, stop, step):
        @pl.loop(start // 2, stop // 2)
        def _(i):
            step(2 * i)
            step(2 * i + 1)

    def attention_forward(b, x, out, hook):
        lanes = head_of_lane()

        @pl.loop(0, CELLS // TILE)
        def _(t):
            rows = row_block(t, TILE)
            xhat, _ = standardized(x[rows, :].astype(F32))
            canvf[rows, :] = xhat * vector(b, 0) + vector(b, 1)

        to_windows(canvf, winf, SHIFT * b)
        to_windows(code, codew, SHIFT * b)

        @pl.loop(0, 4)
        def _(t):
            rows = row_block(t, 256)
            hq = windowed(rows, 256)
            hqw[b, rows, :] = hq
            for part in range(3):
                cols = slice(part * D, (part + 1) * D)
                acc = nn(hq, wat[b, :, cols]) + vec[b * 8 + 6 : b * 8 + 7, cols]
                if part == 0:
                    acc = acc * SCALE
                qkv[b, rows, cols] = acc.astype(BF)

        hook(0)

        def window(w):
            rows = row_block(w, PLACES)
            cells = codew[rows, :]
            region = (cells >> 1) * b
            pad = (cells & 1).astype(F32)
            lane = lax.broadcasted_iota(jnp.int32, (PLACES, 128), 1)
            same = jnp.where(lane == region, 1.0, 0.0)
            left = jnp.where(lane == 127, 1.0 - pad, same).astype(BF)
            right = jnp.where(lane == 127, -pad, same).astype(BF)
            agree = nt(left, jnp.concatenate([right, right], axis=0))
            mask = jnp.where(agree > 0.5, 0.0, MASKED)
            mask = jnp.concatenate([mask, mask], axis=1)
            for g in range(GROUPS):
                q = qkv[b, rows, g * 128 : (g + 1) * 128]
                k = qkv[b, rows, D + g * 128 : D + (g + 1) * 128]
                v = qkv[b, rows, 2 * D + g * 128 : 2 * D + (g + 1) * 128]
                s = nt(k, by_head(q, lanes)) + bias[b, g] + mask
                e = jnp.exp(s - jnp.max(s, axis=0, keepdims=True))
                p = (e * (1.0 / jnp.sum(e, axis=0, keepdims=True))).astype(BF)
                probs[b, w * GROUPS + g] = p
                att[b, rows, g * 128 : (g + 1) * 128] = own_head(tn(p, v), lanes).astype(BF)

        by_two(0, WINDOWS // 2, window)
        hook(1)
        by_two(WINDOWS // 2, WINDOWS, window)
        hook(2)

        @pl.loop(0, 4)
        def _(t):
            rows = row_block(t, 256)
            winf[rows, :] = nn(att[b, rows, :], wat[b, :, 3 * D :])

        to_canvas(winf, canvf, SHIFT * b)

        @pl.loop(0, CELLS // TILE)
        def _(t):
            rows = row_block(t, TILE)
            out[rows, :] = (x[rows, :].astype(F32) + (canvf[rows, :] + vector(b, 2))).astype(BF)

    def mlp_forward(b, x, out, hook):
        @pl.loop(0, CELLS // TILE)
        def _(t):
            rows = row_block(t, TILE)
            xhat, _ = standardized(x[rows, :].astype(F32))
            hq2[b, rows, :] = (xhat * vector(b, 3) + vector(b, 4)).astype(BF)

        def chunk(i):
            cols = pl.ds(pl.multiple_of(i * 256, 256), 256)
            pre = nn(hq2[b], fc1[b, :, cols]) + vec[b * 8 + 7 : b * 8 + 8, cols]
            for at in range(0, CELLS, 16):
                h, dg = gelu_parts(pre[at : at + 16])
                hid[b, at : at + 16, cols] = h.astype(BF)
                dgelu[b, at : at + 16, cols] = dg.astype(BF)

        pl.loop(0, FF // 512)(chunk)
        hook(0)
        pl.loop(FF // 512, FF // 256)(chunk)

        total = nn(hid[b], fc2[b])
        for at in range(0, CELLS, TILE):
            rows = slice(at, at + TILE)
            out[rows, :] = (x[rows, :].astype(F32) + (total[rows] + vector(b, 5))).astype(BF)

    def norm_backward(b, kind, x, gz, out):
        @pl.loop(0, CELLS // TILE)
        def _(t):
            rows = row_block(t, TILE)
            xhat, rs = standardized(x[rows, :].astype(F32))
            gn = canvf[rows, :]
            gzf = gz[rows, :].astype(F32)
            add_vec(b, kind, by_eights(gn * xhat))
            add_vec(b, kind + 1, by_eights(gn))
            add_vec(b, 5 if kind else 2, by_eights(gzf))
            g = gn * vector(b, kind)
            mg = jnp.mean(g, axis=-1, keepdims=True)
            mgx = jnp.mean(g * xhat, axis=-1, keepdims=True)
            out[rows, :] = (gzf + rs * (g - mg - xhat * mgx)).astype(BF)

    def mlp_backward(b, x, gz, out, free_out, hook):
        hook(0)
        wide_t[0, :, :CELLS] = hq2[b].T
        wide_t[1, :, :CELLS] = gz[...].T

        def chunk(i):
            cols = pl.ds(pl.multiple_of(i * 256, 256), 256)
            gh = nt(gz[...], fc2[b, cols, :])
            sums = jnp.zeros((8, 256), F32)
            for at in range(0, CELLS, 16):
                gp = (gh[at : at + 16] * dgelu[b, at : at + 16, cols].astype(F32)).astype(BF)
                dgelu[b, at : at + 16, cols] = gp
                sums = sums + by_eights(gp.astype(F32))
            g_vec[b, 7, :, cols] += sums
            g_fc1[b, :, cols] += nn(wide_t[0, :, :CELLS], dgelu[b, :, cols])
            g_fc2t[b, :, cols] += nn(wide_t[1, :, :CELLS], hid[b, :, cols])

        pl.loop(0, FF // 512)(chunk)
        hook(1)
        pl.loop(FF // 512, FF // 256)(chunk)
        hook(2)
        canvf[...] = nt(dgelu[b], fc1[b])
        hook(3)
        free_out()
        norm_backward(b, 3, x, gz, out)
        hook(4)

    def attention_backward(b, x, gz, out, free_out, hook):
        lanes = head_of_lane()
        hook(0)

        @pl.loop(0, CELLS // TILE)
        def _(t):
            rows = row_block(t, TILE)
            canvf[rows, :] = gz[rows, :].astype(F32)

        to_windows(canvf, winf, SHIFT * b)

        @pl.loop(0, 4)
        def _(t):
            rows = row_block(t, 256)
            gzw[rows, :] = windowed(rows, 256)

        g_proj[b] += tn(att[b], gzw[...])

        @pl.loop(0, 4)
        def _(t):
            rows = row_block(t, 256)
            att[b, rows, :] = nt(gzw[rows, :], wat[b, :, 3 * D :]).astype(BF)

        hook(1)

        def window(w):
            rows = row_block(w, PLACES)
            for g in range(GROUPS):
                at = [slice(part * D + g * 128, part * D + (g + 1) * 128) for part in range(3)]
                q, k, v = (qkv[b, rows, cols] for cols in at)
                go_wide = by_head(att[b, rows, at[0]], lanes)
                p_low = probs[b, w * GROUPS + g]
                p = p_low.astype(F32)
                pd = p * nt(v, go_wide)
                ds = (pd - p * jnp.sum(pd, axis=0, keepdims=True)).astype(BF)
                g_tab[b, :, g * 256 : (g + 1) * 256] += ds.astype(F32)
                qkv[b, rows, at[0]] = (own_head(tn(ds, k), lanes) * SCALE).astype(BF)
                qkv[b, rows, at[1]] = nn(ds, by_head(q, lanes)).astype(BF)
                qkv[b, rows, at[2]] = nn(p_low, go_wide).astype(BF)

        by_two(0, WINDOWS // 2, window)
        hook(2)
        by_two(WINDOWS // 2, WINDOWS, window)
        hook(3)

        @pl.loop(0, 4)
        def _(t):
            rows = row_block(t, 256)
            gq = qkv[b, rows, :]
            add_vec(b, 6, by_eights(gq.astype(F32)))
            winf[rows, :] = nt(gq, wat[b, :, : 3 * D])

        to_canvas(winf, canvf, SHIFT * b)
        free_out()
        norm_backward(b, 0, x, gz, out)

    def attention_weights(b):
        wide_t[0] = hqw[b].T
        for part in range(3):
            cols = slice(part * D, (part + 1) * D)
            g_qkv[b, :, cols] += nn(wide_t[0], qkv[b, :, cols])

    def push(kind, s, n, start):
        src = buf.at[s]
        dst = (r.act_hbm, r.igrad_hbm)[kind].at[me, n]
        local = pltpu.make_async_copy(src, dst, r.local_sem.at[kind, n])
        away = remote(src, dst, r.send_sem.at[kind, s, n], r.recv_sem.at[kind, me, n], {"pipe": s})

        @pl.when(me == s)
        def _():
            local.start() if start else local.wait()

        @pl.when(me != s)
        def _():
            away.start() if start else away.wait_send()

    def arrived(kind, k, n):
        sender = lax.rem(me + k, 4)
        dst = (r.act_hbm, r.igrad_hbm)[kind].at[sender, n]
        remote(
            buf.at[0], dst, r.send_sem.at[kind, 0, n], r.recv_sem.at[kind, sender, n], {"pipe": sender}
        ).wait_recv()

    steps = (step_1, step_2, step_3, step_4, step_5)
    schedule = {
        (3, 2): ((1, 3),),
        (2, 0): ((2, 3),),
        (2, 4): ((3, 3), (1, 2)),
        (1, 0): ((2, 2),),
        (1, 1): ((4, 3),),
        (1, 2): ((1, 1),),
        (0, 0): ((3, 2), (2, 1)),
        (0, 1): ((5, 3),),
        (0, 2): ((4, 2),),
        (0, 3): ((5, 2), (3, 1)),
        (0, 4): ((4, 1),),
    }

    weight_steps = (weights_1, weights_2, weights_3, weights_4) if linked else ()
    gathering = {
        (0, 1): ((2, 1),),
        (0, 2): ((2, 2), (2, 3)),
        (0, 3): ((3, 1), (4, 1)),
        (1, 0): ((3, 2),),
        (1, 3): ((4, 2),),
        (2, 0): ((3, 3),),
        (2, 3): ((4, 3),),
    }

    @pl.loop(0, canvases)
    def _(n):
        def gather(sec, i):
            todo = gathering.get((sec, i), ())
            if linked and todo:

                @pl.when(n == 0)
                def _():
                    for step, of in todo:
                        weight_steps[step - 1](of)

        def hook(sec, i):
            todo = schedule.get((sec, i), ())
            if linked and todo:

                @pl.when(n == canvases - 1)
                def _():
                    for step, of in todo:
                        steps[step - 1](of)

        loads = [
            pltpu.make_async_copy(r.x_hbm.at[me, n], xin, r.in_sem.at[0]),
            pltpu.make_async_copy(r.cot_hbm.at[me, n], cot, r.in_sem.at[1]),
            pltpu.make_async_copy(r.code_hbm.at[n], code, r.in_sem.at[2]),
        ]
        for load in loads:
            load.start()
        for load in loads:
            load.wait()

        x = xin
        for s in range(4):
            @pl.when(n > 0)
            def _():
                push(1, s, n - 1, False)

            forward = mlp_forward if s % 2 else attention_forward
            forward(s // 2, x, buf.at[s], functools.partial(gather, s))
            x = buf.at[s]
            push(0, s, n, True)
            gather(s, 3)
        gz = cot
        for s in (3, 2, 1, 0):
            x = buf.at[s - 1] if s else xin
            backward = mlp_backward if s % 2 else attention_backward
            backward(
                s // 2, x, gz, buf.at[s], functools.partial(push, 0, s, n, False), functools.partial(hook, s)
            )
            gz = buf.at[s]
            push(1, s, n, True)
            if s % 2 == 0:
                attention_weights(s // 2)
                hook(s, 4)

    if linked:
        step_5(1)
        step_1(0)
        step_2(0)
        smalls_sent(1)
        step_3(0)
        step_4(0)
        step_5(0)
        reductions_done()
        weights_sent()
        for k in range(1, 8):
            pack_copy(k).wait_send()
    for kind in range(2):
        for k in range(1, 4):
            for n in range(canvases):
                arrived(kind, k, n)
    for s in range(4):
        push(1, s, canvases - 1, False)


def compute(linked, operands):
    canvases = operands["x_hbm"].shape[1]
    shape = jax.ShapeDtypeStruct
    hbm = pl.BlockSpec(memory_space=pl.ANY)
    vmem = pl.BlockSpec(memory_space=pltpu.VMEM)
    dma = pltpu.SemaphoreType.DMA
    full = {
        "wat": ((2, D, 4 * D), BF),
        "fc1": ((2, D, FF), BF),
        "fc2": ((2, FF, D), BF),
        "vec": ((16, FF), F32),
    }
    grads = {
        "g_qkv": ((2, D, 3 * D), F32),
        "g_proj": ((2, D, D), F32),
        "g_fc1": ((2, D, FF), F32),
        "g_fc2t": ((2, D, FF), F32),
        "g_vec": ((2, 8, 8, FF), F32),
        "g_tab": ((2, PLACES, GROUPS * 256), F32),
    }
    outs = {"act_hbm": ((4, canvases, CELLS, D), BF), "igrad_hbm": ((4, canvases, CELLS, D), BF)}
    scratch = {
        "xin": ((CELLS, D), BF),
        "cot": ((CELLS, D), BF),
        "code": ((CELLS, 128), jnp.int32),
        "codew": ((WROWS, 128), jnp.int32),
        "buf": ((4, CELLS, D), BF),
        "hqw": ((2, WROWS, D), BF),
        "qkv": ((2, WROWS, 3 * D), BF),
        "probs": ((2, WINDOWS * GROUPS, PLACES, 256), BF),
        "att": ((2, WROWS, D), BF),
        "hq2": ((2, CELLS, D), BF),
        "hid": ((2, CELLS, FF), BF),
        "dgelu": ((2, CELLS, FF), BF),
        "canvf": ((CELLS, D), F32),
        "winf": ((WROWS, D), F32),
        "gzw": ((WROWS, D), BF),
        "wide_t": ((2, D, WROWS), BF),
    }
    sems = {
        "in_sem": (3,),
        "local_sem": (2, canvases),
        "send_sem": (2, 4, canvases),
        "recv_sem": (2, 4, canvases),
    }
    if linked:
        outs |= {
            "o_qkv": ((2, 48, 3 * D), F32),
            "o_proj": ((2, 48, D), F32),
            "o_fc1": ((2, 48, FF), F32),
            "o_fc2": ((2, 192, D), F32),
            "o_small": ((2, 8, 64, D), BF),
        }
        scratch |= full | grads
        scratch["packs"] = ((8, 16, 256), BF)
        for kind, rows in (("m_", MLP_ROWS), ("a_", ATT_ROWS)):
            scratch |= {
                kind + "st_a": ((4, rows, D), BF),
                kind + "rc_a": ((4, rows, D), BF),
                kind + "st_b": ((3, rows, D), BF),
                kind + "rc_b": ((3, rows, D), BF),
                kind + "st_c": ((rows, D), BF),
                kind + "rc_c": ((3, rows // 4, D), BF),
                kind + "fin": ((rows, D), BF),
            }
        sems |= {
            "sh_sem": (4,),
            "os_sem": (2,),
            "go_sem": (4, 2),
            "wz_send": (4, 2, 3),
            "wz_recv": (4, 2, 3),
            "wx_send": (4, 2, 3, 3),
            "wx_recv": (4, 2, 3, 3),
            "ws_send": (4, 2, 4),
            "ws_recv": (4, 2, 4),
            "pk_send": (7,),
            "pk_recv": (7,),
            "ra_send": (4,),
            "ra_recv": (4,),
            "rb_send": (4, 3),
            "rb_recv": (4, 3),
            "rc_send": (4, 3),
            "rc_recv": (4, 3),
            "rf_send": (4, 3),
            "rf_recv": (4, 3),
            "rs_send": (2, 7),
            "rs_recv": (2, 7),
        }
    else:
        outs |= grads
    in_vmem = set(grads) | set(full) | {"bias", "pack"}
    names = tuple(operands) + tuple(outs) + tuple(scratch) + tuple(sems)
    results = pl.pallas_call(
        functools.partial(kernel, names, linked, canvases),
        out_shape=tuple(shape(*o) for o in outs.values()),
        in_specs=[vmem if name in in_vmem else hbm for name in operands],
        out_specs=tuple(vmem if name in in_vmem else hbm for name in outs),
        scratch_shapes=[pltpu.VMEM(*v) for v in scratch.values()] + [dma(v) for v in sems.values()],
        compiler_params=pltpu.CompilerParams(
            vmem_limit_bytes=64 * 1024 * 1024 - 65536, collective_id=0, has_side_effects=True
        ),
    )(*operands.values())
    return dict(zip(outs, results))


def place_pairs():
    place = np.arange(PLACES)
    r, c = place // 8, place % 8
    index = (r[None, :] - r[:, None] + WIN - 1) * (2 * WIN - 1) + c[None, :] - c[:, None] + WIN - 1
    real = (r < WIN) & (c < WIN)
    return index, real[:, None] & real[None, :], real


def pair_onehot():
    index, both, _ = place_pairs()
    table = (2 * WIN - 1) ** 2
    hot = (np.where(both, index, -1).reshape(-1)[None, :] == np.arange(table)[:, None])
    return hot.astype(np.float32)


def body(
    inputs,
    cotangent,
    pad_mask,
    region_ids,
    norm1_gain,
    norm1_bias,
    qkv_weight,
    qv_bias,
    rel_table,
    proj_weight,
    proj_bias,
    norm2_gain,
    norm2_bias,
    fc1_weight,
    fc1_bias,
    fc2_weight,
    fc2_bias,
):
    owners = lax.axis_size("dp")
    linked = owners == 8
    mine = lax.axis_index("pipe")

    def own(a):
        return lax.dynamic_index_in_dim(a, mine, 0, keepdims=False)

    code = own(region_ids) * 2 + own(pad_mask)
    code = jnp.broadcast_to(code[:, :, None], code.shape + (128,))

    hot = pair_onehot()
    _, _, real = place_pairs()
    rel = lax.dot_general(
        rel_table.astype(BF), jnp.asarray(hot, BF), (((1,), (0,)), ((), ())), preferred_element_type=F32
    )
    rel = rel.reshape(2, GROUPS, 4, PLACES, PLACES).transpose(0, 1, 3, 2, 4)
    rel = jnp.where(jnp.asarray(real)[None, None, :, None, None], rel, MASKED)
    rel = rel.reshape(2, GROUPS, PLACES, 256)

    operands = {"x_hbm": inputs, "cot_hbm": cotangent, "code_hbm": code, "bias": rel}
    vectors = (norm1_gain, norm1_bias, proj_bias, norm2_gain, norm2_bias, fc2_bias, qv_bias, fc1_bias)
    sizes = [v.shape[1] for v in vectors]
    ends = np.cumsum([0] + sizes)
    if linked:
        pack = jnp.stack([jnp.pad(v, ((0, 0), (0, 256 - v.shape[1]))) for v in vectors], axis=1)
        operands |= {
            "pack": pack.reshape(16, 256).astype(BF),
            "s_qkv": qkv_weight,
            "s_proj": proj_weight,
            "s_fc1": fc1_weight,
            "s_fc2": fc2_weight,
        }
    else:

        def gathered(a):
            return lax.all_gather(a.astype(BF), "dp", axis=1, tiled=True)

        packed = lax.all_gather(jnp.concatenate(vectors, axis=1).astype(BF), "dp", axis=1)
        parts = [packed[:, :, a:b].reshape(2, -1).astype(F32) for a, b in zip(ends[:-1], ends[1:])]
        qv = parts[6]
        parts[6] = jnp.concatenate([qv[:, :D], jnp.zeros_like(qv[:, :D]), qv[:, D:]], axis=1)
        vec = jnp.stack([jnp.pad(p, ((0, 0), (0, FF - p.shape[1]))) for p in parts], axis=1)
        operands |= {
            "wat": jnp.concatenate([gathered(qkv_weight), gathered(proj_weight)], axis=2),
            "fc1": gathered(fc1_weight),
            "fc2": gathered(fc2_weight),
            "vec": vec.reshape(16, FF),
        }

    out = compute(linked, operands)

    def to_owners(g):
        shared = lax.psum_scatter(g, "dp", scatter_dimension=1, tiled=True)
        return lax.psum(shared, "pipe")

    if linked:
        small = out["o_small"].astype(F32)
        g_tab = jnp.concatenate([small[:, :, :8], small[:, :, 8:16]], axis=3).reshape(2, PLACES, GROUPS * 256)
        g_vec = jnp.concatenate([small[:, :, 16 + 8 * j : 24 + 8 * j] for j in range(4)], axis=3)
    else:
        g_tab, g_vec = out["g_tab"], out["g_vec"]

    g_vec = jnp.sum(g_vec, axis=2)
    kinds = [g_vec[:, i] for i in range(8)]
    qv_sum = jnp.concatenate([kinds[6][:, :D], kinds[6][:, 2 * D : 3 * D]], axis=1)
    rows = [kinds[0], kinds[1], kinds[2], kinds[3], kinds[4], kinds[5], qv_sum, kinds[7]]
    if linked:
        at = lax.axis_index("dp")
        small = [lax.dynamic_slice_in_dim(v, at * n, n, 1) for v, n in zip(rows, sizes)]
    else:
        rows = [v[:, : n * owners].reshape(2, -1, n) for v, n in zip(rows, sizes)]
        g_small = to_owners(jnp.concatenate(rows, axis=2))[:, 0]
        small = [g_small[:, a:b] for a, b in zip(ends[:-1], ends[1:])]

    pairs = g_tab.reshape(2, PLACES, HEADS, PLACES).transpose(0, 2, 1, 3)
    pairs = pairs.reshape(2, HEADS, PLACES * PLACES)
    g_table = lax.dot_general(
        jnp.broadcast_to(jnp.asarray(hot), (2,) + hot.shape),
        pairs,
        (((2,), (2,)), ((0,), (0,))),
        precision=lax.Precision.HIGHEST,
        preferred_element_type=F32,
    )
    if linked:
        big = [out[name] for name in ("o_qkv", "o_proj", "o_fc1", "o_fc2")]
    else:
        g_table = lax.psum(g_table, ("pipe", "dp"))
        big = [to_owners(out[name]) for name in ("g_qkv", "g_proj", "g_fc1")]
        big.append(to_owners(out["g_fc2t"].transpose(0, 2, 1)))

    return (
        out["act_hbm"][None],
        out["igrad_hbm"][None],
        small[0],
        small[1],
        big[0],
        small[6],
        g_table,
        big[1],
        small[2],
        small[3],
        small[4],
        big[2],
        small[7],
        big[3],
        small[5],
    )


def solution(mesh):
    cols = P(None, "dp")
    rows = P(None, "dp", None)
    return jax.shard_map(
        body,
        mesh=mesh,
        in_specs=(
            P(None, "dp", None, None),
            P(None, "dp", None, None),
            rows,
            rows,
            cols,
            cols,
            rows,
            cols,
            P(),
            rows,
            cols,
            cols,
            cols,
            rows,
            cols,
            rows,
            cols,
        ),
        out_specs=(
            P("pipe", None, "dp", None, None),
            P("pipe", None, "dp", None, None),
            cols,
            cols,
            rows,
            cols,
            P(),
            rows,
            cols,
            cols,
            cols,
            rows,
            cols,
            rows,
            cols,
        ),
        check_vma=False,
    )
```

```python
import functools
import types

import jax
import jax.numpy as jnp
import numpy as np
from jax import lax
from jax.experimental import pallas as pl
from jax.experimental.pallas import tpu as pltpu
from jax.sharding import PartitionSpec as P

HEADS = 12
WIN = 7
SHIFT = 3
GRID = 28
CELLS = 784
D = 384
FF = 1536
HEAD = 32
SIDE = 4
WINDOWS = 16
PLACES = 64
WROWS = WINDOWS * PLACES
GROUPS = 3
TILE = 112
SCALE = HEAD**-0.5
NORM_EPS = 1e-05
MASKED = -1e30
BF = jnp.bfloat16
F32 = jnp.float32

ERF_P = 0.3275911 / np.sqrt(2.0)
ERF_A = [0.5 * a for a in (0.254829592, -0.284496736, 1.421413741, -1.453152027, 1.061405429)]
PHI_0 = 1.0 / np.sqrt(2.0 * np.pi)


def nn(a, b):
    return lax.dot_general(a, b, (((1,), (0,)), ((), ())), preferred_element_type=F32)


def nt(a, b):
    return lax.dot_general(a, b, (((1,), (1,)), ((), ())), preferred_element_type=F32)


def tn(a, b):
    return lax.dot_general(a, b, (((0,), (0,)), ((), ())), preferred_element_type=F32)


def segments(shift):
    runs = []
    for wr in range(SIDE):
        for r in range(WIN):
            row = (wr * WIN + r + shift) % GRID
            for wc in range(SIDE):
                col = (wc * WIN + shift) % GRID
                place = (wr * SIDE + wc) * PLACES + r * 8
                first = min(WIN, GRID - col)
                runs.append((row * GRID + col, place, first))
                if first < WIN:
                    runs.append((row * GRID, place + first, WIN - first))
    return runs


def to_windows(src, dst, shift):
    for cell, place, count in segments(shift):
        dst[pl.ds(place, count), :] = src[pl.ds(cell, count), :]


def to_canvas(src, dst, shift):
    for cell, place, count in segments(shift):
        dst[pl.ds(cell, count), :] = src[pl.ds(place, count), :]


def row_block(t, size):
    return pl.ds(pl.multiple_of(t * size, 16), size)


def standardized(v):
    centered = v - jnp.mean(v, axis=-1, keepdims=True)
    spread = jnp.mean(centered * centered, axis=-1, keepdims=True)
    rs = lax.rsqrt(spread + NORM_EPS)
    return centered * rs, rs


def by_eights(v):
    return jnp.sum(v.reshape(v.shape[0] // 8, 8, v.shape[1]), axis=0)


def gelu_parts(x):
    den = 1.0 + ERF_P * jnp.abs(x)
    t = pl.reciprocal(den, approx=True)
    t = t * (2.0 - den * t)
    e = jnp.exp(-0.5 * x * x)
    poly = ERF_A[4]
    for a in ERF_A[3::-1]:
        poly = poly * t + a
    tail = poly * t * e
    cdf = jnp.where(x >= 0.0, 1.0 - tail, tail)
    return x * cdf, cdf + x * (e * PHI_0)


def real_places(rows):
    place = lax.broadcasted_iota(jnp.int32, (rows, 1), 0)
    return ((place & 7) < WIN) & (((place >> 3) & 7) < WIN)


def head_of_lane():
    return lax.broadcasted_iota(jnp.int32, (PLACES, 128), 1) >> 5


def by_head(x, lanes):
    zero = jnp.zeros_like(x)
    return jnp.concatenate([jnp.where(lanes == h, x, zero) for h in range(4)], axis=0)


def own_head(wide, lanes):
    out = wide[3 * PLACES :]
    for h in (2, 1, 0):
        out = jnp.where(lanes == h, wide[h * PLACES : (h + 1) * PLACES], out)
    return out


MESH = pl.DeviceIdType.MESH
ATT_ROWS = 256
MLP_ROWS = 384
SMALL = 192


def kernel(names, linked, canvases, *refs):
    r = types.SimpleNamespace(**dict(zip(names, refs)))
    me = lax.axis_index("pipe")
    xin, cot, code, codew, buf = r.xin, r.cot, r.code, r.codew, r.buf
    hqw, qkv, probs, att = r.hqw, r.qkv, r.probs, r.att
    hq2, hid, dgelu = r.hq2, r.hid, r.dgelu
    canvf, winf, gzw, wide_t, gqkv, go = r.canvf, r.winf, r.gzw, r.wide_t, r.gqkv, r.go
    g_qkv, g_proj, g_fc1, g_fc2t, g_vec, g_tab = r.g_qkv, r.g_proj, r.g_fc1, r.g_fc2t, r.g_vec, r.g_tab
    wat, fc1, fc2, vec, bias = r.wat, r.fc1, r.fc2, r.vec, r.bias
    if linked:
        d = lax.axis_index("dp")
        z, c = d // 2, d % 2
        sibling = {"dp": 2 * z + 1 - c}

    def z_peer(k):
        return {"dp": 2 * lax.rem(z + k, 4) + c}

    def pipe_peer(k):
        return {"pipe": lax.rem(me + k, 4)}

    def dp_peer(k):
        return {"dp": lax.rem(d + k, 8)}

    def remote(src, dst, send, recv, device):
        return pltpu.make_async_remote_copy(
            src_ref=src, dst_ref=dst, send_sem=send, recv_sem=recv, device_id=device, device_id_type=MESH
        )

    barrier = pltpu.get_barrier_semaphore()
    partners = [pipe_peer(k) for k in range(1, 4)]
    if linked:
        partners += [dp_peer(k) for k in range(1, 8)]
    for partner in partners:
        pl.semaphore_signal(barrier, inc=1, device_id=partner, device_id_type=MESH)

    full = ((wat,), (fc1, fc2), (wat,), (fc1, fc2))

    def owner_back(k):
        return 2 * lax.rem(z + 4 - k, 4) + c

    def shard(sec, a, owner):
        h = 192 if a else 48
        return full[sec][a].at[sec // 2, pl.ds(pl.multiple_of(owner * h, 16), h), :]

    def part(sec, a, owner, place):
        if a:
            return fc2.at[sec // 2, pl.ds(pl.multiple_of(owner * 192 + place * 48, 16), 48), :]
        rows = pl.ds(pl.multiple_of(owner * 48, 16), 48)
        return full[sec][0].at[sec // 2, rows, pl.ds(pl.multiple_of(place * D, 128), D)]

    def to_z(sec, a, k):
        own = part(sec, a, d, me)
        return remote(own, own, r.wz_send.at[sec, a, k - 1], r.wz_recv.at[sec, a, k - 1], z_peer(k))

    def to_places(sec, a, k, j):
        got = part(sec, a, owner_back(k), me)
        return remote(
            got, got, r.wx_send.at[sec, a, k - 1, j - 1], r.wx_recv.at[sec, a, k - 1, j - 1], pipe_peer(j)
        )

    def to_sibling(sec, a, k):
        block = shard(sec, a, owner_back(k))
        return remote(block, block, r.ws_send.at[sec, a, k], r.ws_recv.at[sec, a, k], sibling)

    def weights_1(sec):
        for a in range(len(full[sec])):
            for k in range(1, 4):
                to_z(sec, a, k).start()
            to_sibling(sec, a, 0).start()

    def weights_2(sec):
        for k in range(1, 4):
            for a in range(len(full[sec])):
                got = part(sec, a, owner_back(k), me)
                remote(got, got, r.wz_send.at[sec, a, k - 1], r.wz_recv.at[sec, a, k - 1], z_peer(k)).wait_recv()
                for j in range(1, 4):
                    to_places(sec, a, k, j).start()

    def weights_3(sec):
        for k in range(1, 4):
            for a in range(len(full[sec])):
                for j in range(1, 4):
                    got = part(sec, a, owner_back(k), lax.rem(me + 4 - j, 4))
                    remote(
                        got, got, r.wx_send.at[sec, a, k - 1, j - 1], r.wx_recv.at[sec, a, k - 1, j - 1], pipe_peer(j)
                    ).wait_recv()
                to_sibling(sec, a, k).start()

    def weights_4(sec):
        for k in range(4):
            for a in range(len(full[sec])):
                block = shard(sec, a, 2 * lax.rem(z + 4 - k, 4) + 1 - c)
                remote(block, block, r.ws_send.at[sec, a, k], r.ws_recv.at[sec, a, k], sibling).wait_recv()

    def weights_sent():
        for sec in range(4):
            for a in range(len(full[sec])):
                for k in range(4):
                    to_sibling(sec, a, k).wait_send()
                    if k:
                        to_z(sec, a, k).wait_send()
                        for j in range(1, 4):
                            to_places(sec, a, k, j).wait_send()

    def pack_copy(k):
        return remote(
            r.packs.at[d], r.packs.at[d], r.pk_send.at[k - 1], r.pk_recv.at[k - 1], dp_peer(k)
        )

    def pack_arrival(k):
        slot = r.packs.at[lax.rem(d + 8 - k, 8)]
        return remote(slot, slot, r.pk_send.at[k - 1], r.pk_recv.at[k - 1], dp_peer(k))

    def place_vectors():
        kind = lax.broadcasted_iota(jnp.int32, (16, 256), 0) & 7
        lane = lax.broadcasted_iota(jnp.int32, (16, 256), 1)
        vec[...] = jnp.zeros_like(vec)
        for width, kinds in ((48, kind < 6), (96, kind == 6), (192, kind == 7)):
            for owner in range(8):
                at = owner * width
                if width == 96 and owner >= 4:
                    at += D
                start = at // 128 * 128
                part = jnp.where(kinds & (lane < width), r.packs[owner].astype(F32), 0.0)
                if at > start:
                    part = pltpu.roll(part, at - start, 1)
                vec[:, start : start + 256] += part

    def pieces(sec, owner):
        b = sec // 2
        out = []

        def matrix(ref, h):
            for t in range(h // 48):
                rows = pl.ds(pl.multiple_of(owner * h + t * 48, 16), 48)
                for j in range(ref.shape[2] // D):
                    load = functools.partial(lambda ref, rows, j: ref[b, rows, j * D : (j + 1) * D], ref, rows, j)
                    out.append((len(out) * 48, 48, load))

        def small():
            rows = pl.ds(pl.multiple_of(owner * 8, 8), 8)
            parts = [g_tab[b, rows, j * D : (j + 1) * D] for j in range(2)]
            parts += [g_vec[b, owner, :, j * D : (j + 1) * D] for j in range(4)]
            return jnp.concatenate(parts + [jnp.zeros((16, D), F32)], axis=0)

        if sec % 2:
            matrix(g_fc1, 48)
        else:
            matrix(g_qkv, 48)
            matrix(g_proj, 48)
            out.append((SMALL, 64, small))
        return out

    def reduce_refs(sec):
        kind = "m" if sec % 2 else "a"
        return types.SimpleNamespace(
            **{n: getattr(r, kind + "_" + n) for n in ("st_a", "rc_a", "st_b", "rc_b", "st_c", "rc_c", "fin")}
        )

    def step_1(sec):
        q = reduce_refs(sec)
        if sec < 2:
            copy_a(sec + 2).wait_send()
            for k in range(1, 4):
                copy_b(sec + 2, k).wait_send()
                copy_c(sec + 2, k).wait_send()
        for k in range(4):
            i = lax.rem(z + k, 4)
            kept = q.st_b.at[k - 1] if k else q.st_c
            for row, rows, load in pieces(sec, 2 * i + 1 - c):
                q.st_a[i, row : row + rows, :] = load().astype(BF)
            for row, rows, load in pieces(sec, 2 * i + c):
                kept[row : row + rows, :] = load().astype(BF)
            if sec % 2:
                winf[:D, :] = g_fc2t[sec // 2, :, pl.ds(pl.multiple_of(i * D, 128), D)].T
                for t in range(0, 192, 48):
                    at = slice(192 + t, 240 + t)
                    q.st_a[i, at, :] = winf[pl.ds(pl.multiple_of((1 - c) * 192 + t, 16), 48), :].astype(BF)
                    kept[at, :] = winf[pl.ds(pl.multiple_of(c * 192 + t, 16), 48), :].astype(BF)
        copy_a(sec).start()

    def copy_a(sec):
        q = reduce_refs(sec)
        return remote(q.st_a, q.rc_a, r.ra_send.at[sec], r.ra_recv.at[sec], sibling)

    def copy_b(sec, k):
        q = reduce_refs(sec)
        return remote(
            q.st_b.at[k - 1], q.rc_b.at[k - 1], r.rb_send.at[sec, k - 1], r.rb_recv.at[sec, k - 1], z_peer(k)
        )

    def step_2(sec):
        q = reduce_refs(sec)
        copy_a(sec).wait_recv()
        for k in (1, 2, 3, 0):
            i = lax.rem(z + k, 4)
            kept = q.st_b.at[k - 1] if k else q.st_c
            for row in range(0, kept.shape[0], 64):
                at = slice(row, row + 64)
                kept[at, :] = (kept[at, :].astype(F32) + q.rc_a[i, at, :].astype(F32)).astype(BF)
            if k:
                copy_b(sec, k).start()

    def quarter(sec, ref, who):
        rows = (MLP_ROWS if sec % 2 else ATT_ROWS) // 4
        return ref.at[pl.ds(pl.multiple_of(who * rows, 16), rows), :]

    def copy_c(sec, k):
        q = reduce_refs(sec)
        return remote(
            quarter(sec, q.st_c, lax.rem(me + k, 4)),
            q.rc_c.at[k - 1],
            r.rc_send.at[sec, k - 1],
            r.rc_recv.at[sec, k - 1],
            pipe_peer(k),
        )

    def step_3(sec):
        q = reduce_refs(sec)
        for k in range(1, 4):
            copy_b(sec, k).wait_recv()
        for row in range(0, q.st_c.shape[0], 64):
            at = slice(row, row + 64)
            total = q.st_c[at, :].astype(F32)
            for k in range(3):
                total = total + q.rc_b[k, at, :].astype(F32)
            q.st_c[at, :] = total.astype(BF)
        for k in range(1, 4):
            copy_c(sec, k).start()

    def copy_f(sec, k):
        q = reduce_refs(sec)
        own = quarter(sec, q.fin, me)
        return remote(own, own, r.rf_send.at[sec, k - 1], r.rf_recv.at[sec, k - 1], pipe_peer(k))

    def step_4(sec):
        q = reduce_refs(sec)
        for k in range(1, 4):
            copy_c(sec, k).wait_recv()
            if sec < 2:
                copy_f(sec + 2, k).wait_send()
        total = quarter(sec, q.st_c, me)[...].astype(F32)
        for k in range(3):
            total = total + q.rc_c[k].astype(F32)
        quarter(sec, q.fin, me)[...] = total.astype(BF)
        for k in range(1, 4):
            copy_f(sec, k).start()

    def copy_s(b, k):
        rows = pl.ds(SMALL, 64)
        return remote(
            r.a_fin.at[rows, :], r.o_small.at[b, d], r.rs_send.at[b, k - 1], r.rs_recv.at[b, k - 1], dp_peer(k)
        )

    def own_small(b):
        return pltpu.make_async_copy(r.a_fin.at[pl.ds(SMALL, 64), :], r.o_small.at[b, d], r.os_sem.at[b])

    def outputs(sec):
        pairs = ((g_fc1, r.o_fc1, 48), (g_fc2t, r.o_fc2, 192)) if sec % 2 else (
            (g_qkv, r.o_qkv, 48), (g_proj, r.o_proj, 48))
        b = sec // 2
        return [
            pltpu.make_async_copy(ref.at[b, pl.ds(0, h), pl.ds(0, out.shape[2])], out.at[b], r.go_sem.at[sec, i])
            for i, (ref, out, h) in enumerate(pairs)
        ]

    def step_5(sec):
        q = reduce_refs(sec)
        b = sec // 2
        for k in range(1, 4):
            got = quarter(sec, q.fin, lax.rem(me + 4 - k, 4))
            remote(got, got, r.rf_send.at[sec, k - 1], r.rf_recv.at[sec, k - 1], pipe_peer(k)).wait_recv()
        if sec % 2 == 0:
            for k in range(1, 8):
                copy_s(b, k).start()
            own_small(b).start()
        row = 0
        for ref, h, n in ((g_fc1, 48, 4), (g_fc2t, 192, 1)) if sec % 2 else ((g_qkv, 48, 3), (g_proj, 48, 1)):
            for t in range(h // 48):
                for j in range(n):
                    ref[b, t * 48 : (t + 1) * 48, j * D : (j + 1) * D] = q.fin[row : row + 48, :].astype(F32)
                    row += 48
        for out in outputs(sec):
            out.start()

    def smalls_sent(b):
        for k in range(1, 8):
            copy_s(b, k).wait_send()
        own_small(b).wait()

    def reductions_done():
        for sec in (1, 0):
            copy_a(sec).wait_send()
            for k in range(1, 4):
                copy_b(sec, k).wait_send()
                copy_c(sec, k).wait_send()
                copy_f(sec, k).wait_send()
        for sec in range(4):
            for out in outputs(sec):
                out.wait()
        smalls_sent(0)
        for b in range(2):
            for k in range(1, 8):
                rows = pl.ds(SMALL, 64)
                remote(
                    r.a_fin.at[rows, :],
                    r.o_small.at[b, lax.rem(d + 8 - k, 8)],
                    r.rs_send.at[b, k - 1],
                    r.rs_recv.at[b, k - 1],
                    dp_peer(k),
                ).wait_recv()

    if linked:
        lands = ((r.s_qkv, g_qkv, 48, wat, 0), (r.s_proj, g_proj, 48, wat, 3 * D), (r.s_fc1, g_fc1, 48, fc1, 0), (r.s_fc2, g_fc2t, 192, fc2, 0))
        loads = [
            pltpu.make_async_copy(src, dst.at[:, pl.ds(0, h), pl.ds(0, src.shape[2])], r.sh_sem.at[i])
            for i, (src, dst, h, _, _) in enumerate(lands)
        ]
        for load in loads:
            load.start()
        r.packs[d] = r.pack[...]
        for load in loads:
            load.wait()
        for src, wide, h, ref, col in lands:
            n = src.shape[2]
            for b in range(2):
                for t in range(h // 48):
                    rows = pl.ds(pl.multiple_of(d * h + t * 48, 16), 48)
                    ref[b, rows, col : col + n] = wide[b, t * 48 : (t + 1) * 48, :n].astype(BF)
    pl.semaphore_wait(barrier, len(partners))
    if linked:
        for k in range(1, 8):
            pack_copy(k).start()
        weights_1(0)

    for ref in (g_qkv, g_proj, g_fc1, g_fc2t):
        for b in range(2):

            @pl.loop(0, ref.shape[1] // 16)
            def _(i):
                ref[b, row_block(i, 16), :] = jnp.zeros((16, ref.shape[2]), F32)

    g_vec[...] = jnp.zeros_like(g_vec)
    g_tab[...] = jnp.zeros_like(g_tab)
    codew[...] = jnp.zeros_like(codew)

    if linked:
        weights_2(0)
        for sec in range(1, 4):
            weights_1(sec)
        for k in range(1, 8):
            pack_arrival(k).wait_recv()
        place_vectors()
        weights_3(0)
        weights_4(0)

    def vector(b, kind, width=D):
        return vec[b * 8 + kind : b * 8 + kind + 1, :width]

    def add_vec(b, kind, part):
        g_vec[b, kind, :, : part.shape[1]] += part

    def windowed(rows, count):
        return jnp.where(real_places(count), winf[rows, :], 0.0).astype(BF)

    def by_two(start, stop, step):
        @pl.loop(start // 2, stop // 2)
        def _(i):
            step((2 * i, 2 * i + 1))

    def attention_forward(b, x, out, free_out, hook):
        lanes = head_of_lane()

        @pl.loop(0, CELLS // TILE)
        def _(t):
            rows = row_block(t, TILE)
            xhat, _ = standardized(x[rows, :].astype(F32))
            canvf[rows, :] = xhat * vector(b, 0) + vector(b, 1)

        to_windows(canvf, winf, SHIFT * b)
        to_windows(code, codew, SHIFT * b)

        @pl.loop(0, 4)
        def _(t):
            rows = row_block(t, 256)
            hq = windowed(rows, 256)
            hqw[b, rows, :] = hq
            for part in range(3):
                cols = slice(part * D, (part + 1) * D)
                acc = nn(hq, wat[b, :, cols]) + vec[b * 8 + 6 : b * 8 + 7, cols]
                if part == 0:
                    acc = acc * SCALE
                qkv[b, rows, cols] = acc.astype(BF)

        hook(0)

        def windows(pair):
            blocks = [row_block(w, PLACES) for w in pair]
            masks = []
            for rows in blocks:
                cells = codew[rows, :]
                region = (cells >> 1) * b
                pad = (cells & 1).astype(F32)
                lane = lax.broadcasted_iota(jnp.int32, (PLACES, 128), 1)
                same = jnp.where(lane == region, 1.0, 0.0)
                left = jnp.where(lane == 127, 1.0 - pad, same).astype(BF)
                right = jnp.where(lane == 127, -pad, same).astype(BF)
                agree = nt(left, jnp.concatenate([right, right], axis=0))
                mask = jnp.where(agree > 0.5, 0.0, MASKED)
                masks.append(jnp.concatenate([mask, mask], axis=1))
            for g in range(GROUPS):
                for w, rows, mask in zip(pair, blocks, masks):
                    q = qkv[b, rows, g * 128 : (g + 1) * 128]
                    k = qkv[b, rows, D + g * 128 : D + (g + 1) * 128]
                    v = qkv[b, rows, 2 * D + g * 128 : 2 * D + (g + 1) * 128]
                    s = nt(k, by_head(q, lanes)) + bias[b, g] + mask
                    e = jnp.exp(s - jnp.max(s, axis=0, keepdims=True))
                    p = (e * (1.0 / jnp.sum(e, axis=0, keepdims=True))).astype(BF)
                    probs[b, w * GROUPS + g] = p
                    att[b, rows, g * 128 : (g + 1) * 128] = own_head(tn(p, v), lanes).astype(BF)

        by_two(0, WINDOWS // 2, windows)
        hook(1)
        by_two(WINDOWS // 2, WINDOWS, windows)
        hook(2)

        @pl.loop(0, 4)
        def _(t):
            rows = row_block(t, 256)
            winf[rows, :] = nn(att[b, rows, :], wat[b, :, 3 * D :])

        to_canvas(winf, canvf, SHIFT * b)
        free_out()

        @pl.loop(0, CELLS // TILE)
        def _(t):
            rows = row_block(t, TILE)
            out[rows, :] = (x[rows, :].astype(F32) + (canvf[rows, :] + vector(b, 2))).astype(BF)

    def mlp_forward(b, x, out, free_out, hook):
        @pl.loop(0, CELLS // TILE)
        def _(t):
            rows = row_block(t, TILE)
            xhat, _ = standardized(x[rows, :].astype(F32))
            hq2[b, rows, :] = (xhat * vector(b, 3) + vector(b, 4)).astype(BF)

        def chunk(i):
            cols = pl.ds(pl.multiple_of(i * 256, 256), 256)
            pre = nn(hq2[b], fc1[b, :, cols]) + vec[b * 8 + 7 : b * 8 + 8, cols]
            for at in range(0, CELLS, 16):
                h, dg = gelu_parts(pre[at : at + 16])
                hid[b, at : at + 16, cols] = h.astype(BF)
                dgelu[b, at : at + 16, cols] = dg.astype(BF)

        pl.loop(0, FF // 512)(chunk)
        hook(0)
        pl.loop(FF // 512, FF // 256)(chunk)

        free_out()
        total = nn(hid[b], fc2[b])
        for at in range(0, CELLS, TILE):
            rows = slice(at, at + TILE)
            out[rows, :] = (x[rows, :].astype(F32) + (total[rows] + vector(b, 5))).astype(BF)

    def norm_backward(b, kind, x, gz, out):
        @pl.loop(0, CELLS // TILE)
        def _(t):
            rows = row_block(t, TILE)
            xhat, rs = standardized(x[rows, :].astype(F32))
            gn = canvf[rows, :]
            gzf = gz[rows, :].astype(F32)
            add_vec(b, kind, by_eights(gn * xhat))
            add_vec(b, kind + 1, by_eights(gn))
            add_vec(b, 5 if kind else 2, by_eights(gzf))
            g = gn * vector(b, kind)
            mg = jnp.mean(g, axis=-1, keepdims=True)
            mgx = jnp.mean(g * xhat, axis=-1, keepdims=True)
            out[rows, :] = (gzf + rs * (g - mg - xhat * mgx)).astype(BF)

    def mlp_backward(b, x, gz, out, free_out, hook):
        hook(0)
        wide_t[0, :, :CELLS] = hq2[b].T
        wide_t[1, :, :CELLS] = gz[...].T

        def chunk(i):
            cols = pl.ds(pl.multiple_of(i * 256, 256), 256)
            gh = nt(gz[...], fc2[b, cols, :])
            sums = jnp.zeros((8, 256), F32)
            for at in range(0, CELLS, 16):
                gp = (gh[at : at + 16] * dgelu[b, at : at + 16, cols].astype(F32)).astype(BF)
                dgelu[b, at : at + 16, cols] = gp
                sums = sums + by_eights(gp.astype(F32))
            g_vec[b, 7, :, cols] += sums
            g_fc1[b, :, cols] += nn(wide_t[0, :, :CELLS], dgelu[b, :, cols])
            g_fc2t[b, :, cols] += nn(wide_t[1, :, :CELLS], hid[b, :, cols])

        pl.loop(0, FF // 512)(chunk)
        hook(1)
        pl.loop(FF // 512, FF // 256)(chunk)
        hook(2)
        canvf[...] = nt(dgelu[b], fc1[b])
        hook(3)
        free_out()
        norm_backward(b, 3, x, gz, out)
        hook(4)

    def attention_backward(b, x, gz, out, free_out, hook):
        lanes = head_of_lane()
        hook(0)

        @pl.loop(0, CELLS // TILE)
        def _(t):
            rows = row_block(t, TILE)
            canvf[rows, :] = gz[rows, :].astype(F32)

        to_windows(canvf, winf, SHIFT * b)

        @pl.loop(0, 4)
        def _(t):
            rows = row_block(t, 256)
            gzw[rows, :] = windowed(rows, 256)

        g_proj[b] += tn(att[b], gzw[...])

        @pl.loop(0, 4)
        def _(t):
            rows = row_block(t, 256)
            go[rows, :] = nt(gzw[rows, :], wat[b, :, 3 * D :]).astype(BF)

        hook(1)

        def windows(pair):
            blocks = [row_block(w, PLACES) for w in pair]
            for g in range(GROUPS):
                at = [slice(part * D + g * 128, part * D + (g + 1) * 128) for part in range(3)]
                table = jnp.zeros((PLACES, 256), F32)
                for w, rows in zip(pair, blocks):
                    q, k, v = (qkv[b, rows, cols] for cols in at)
                    go_wide = by_head(go[rows, at[0]], lanes)
                    p_low = probs[b, w * GROUPS + g]
                    p = p_low.astype(F32)
                    pd = p * nt(v, go_wide)
                    ds = (pd - p * jnp.sum(pd, axis=0, keepdims=True)).astype(BF)
                    table = table + ds.astype(F32)
                    gqkv[rows, at[0]] = (own_head(tn(ds, k), lanes) * SCALE).astype(BF)
                    gqkv[rows, at[1]] = nn(ds, by_head(q, lanes)).astype(BF)
                    gqkv[rows, at[2]] = nn(p_low, go_wide).astype(BF)
                g_tab[b, :, g * 256 : (g + 1) * 256] += table

        by_two(0, WINDOWS // 2, windows)
        hook(2)
        by_two(WINDOWS // 2, WINDOWS, windows)
        hook(3)

        @pl.loop(0, 4)
        def _(t):
            rows = row_block(t, 256)
            gq = gqkv[rows, :]
            add_vec(b, 6, by_eights(gq.astype(F32)))
            winf[rows, :] = nt(gq, wat[b, :, : 3 * D])

        to_canvas(winf, canvf, SHIFT * b)
        free_out()
        norm_backward(b, 0, x, gz, out)

    def attention_weights(b):
        wide_t[0] = hqw[b].T
        for part in range(3):
            cols = slice(part * D, (part + 1) * D)
            g_qkv[b, :, cols] += nn(wide_t[0], gqkv[:, cols])

    def push(kind, s, n, start):
        src = buf.at[s]
        dst = (r.act_hbm, r.igrad_hbm)[kind].at[me, n]
        local = pltpu.make_async_copy(src, dst, r.local_sem.at[kind, n])
        away = remote(src, dst, r.send_sem.at[kind, s, n], r.recv_sem.at[kind, me, n], {"pipe": s})

        @pl.when(me == s)
        def _():
            local.start() if start else local.wait()

        @pl.when(me != s)
        def _():
            away.start() if start else away.wait_send()

    def arrived(kind, k, n):
        sender = lax.rem(me + k, 4)
        dst = (r.act_hbm, r.igrad_hbm)[kind].at[sender, n]
        remote(
            buf.at[0], dst, r.send_sem.at[kind, 0, n], r.recv_sem.at[kind, sender, n], {"pipe": sender}
        ).wait_recv()

    steps = (step_1, step_2, step_3, step_4, step_5)
    schedule = {
        (3, 2): ((1, 3),),
        (2, 0): ((2, 3),),
        (2, 4): ((3, 3), (1, 2)),
        (1, 0): ((2, 2),),
        (1, 1): ((4, 3),),
        (1, 2): ((1, 1),),
        (0, 0): ((3, 2), (2, 1)),
        (0, 1): ((5, 3),),
        (0, 2): ((4, 2),),
        (0, 3): ((5, 2), (3, 1)),
        (0, 4): ((4, 1),),
    }

    weight_steps = (weights_1, weights_2, weights_3, weights_4) if linked else ()
    gathering = {
        (0, 1): ((2, 1),),
        (0, 2): ((2, 2), (2, 3)),
        (0, 3): ((3, 1), (4, 1)),
        (1, 0): ((3, 2),),
        (1, 3): ((4, 2),),
        (2, 0): ((3, 3),),
        (2, 3): ((4, 3),),
    }

    @pl.loop(0, canvases)
    def _(n):
        def gather(sec, i):
            todo = gathering.get((sec, i), ())
            if linked and todo:

                @pl.when(n == 0)
                def _():
                    for step, of in todo:
                        weight_steps[step - 1](of)

        def hook(sec, i):
            todo = schedule.get((sec, i), ())
            if linked and todo:

                @pl.when(n == canvases - 1)
                def _():
                    for step, of in todo:
                        steps[step - 1](of)

        loads = [
            pltpu.make_async_copy(r.x_hbm.at[me, n], xin, r.in_sem.at[0]),
            pltpu.make_async_copy(r.cot_hbm.at[me, n], cot, r.in_sem.at[1]),
            pltpu.make_async_copy(r.code_hbm.at[n], code, r.in_sem.at[2]),
        ]
        for load in loads:
            load.start()
        for load in loads:
            load.wait()

        x = xin
        for s in range(4):
            def free_out():
                @pl.when(n > 0)
                def _():
                    push(1, s, n - 1, False)

            forward = mlp_forward if s % 2 else attention_forward
            forward(s // 2, x, buf.at[s], free_out, functools.partial(gather, s))
            x = buf.at[s]
            push(0, s, n, True)
            gather(s, 3)
        gz = cot
        for s in (3, 2, 1, 0):
            x = buf.at[s - 1] if s else xin
            backward = mlp_backward if s % 2 else attention_backward
            backward(
                s // 2, x, gz, buf.at[s], functools.partial(push, 0, s, n, False), functools.partial(hook, s)
            )
            gz = buf.at[s]
            push(1, s, n, True)
            if s % 2 == 0:
                attention_weights(s // 2)
                hook(s, 4)

    if linked:
        step_5(1)
        step_1(0)
        step_2(0)
        smalls_sent(1)
        step_3(0)
        step_4(0)
        step_5(0)
        reductions_done()
        weights_sent()
        for k in range(1, 8):
            pack_copy(k).wait_send()
    for kind in range(2):
        for k in range(1, 4):
            for n in range(canvases):
                arrived(kind, k, n)
    for s in range(4):
        push(1, s, canvases - 1, False)


def compute(linked, operands):
    canvases = operands["x_hbm"].shape[1]
    shape = jax.ShapeDtypeStruct
    hbm = pl.BlockSpec(memory_space=pl.ANY)
    vmem = pl.BlockSpec(memory_space=pltpu.VMEM)
    dma = pltpu.SemaphoreType.DMA
    full = {
        "wat": ((2, D, 4 * D), BF),
        "fc1": ((2, D, FF), BF),
        "fc2": ((2, FF, D), BF),
        "vec": ((16, FF), F32),
    }
    grads = {
        "g_qkv": ((2, D, 3 * D), F32),
        "g_proj": ((2, D, D), F32),
        "g_fc1": ((2, D, FF), F32),
        "g_fc2t": ((2, D, FF), F32),
        "g_vec": ((2, 8, 8, FF), F32),
        "g_tab": ((2, PLACES, GROUPS * 256), F32),
    }
    outs = {"act_hbm": ((4, canvases, CELLS, D), BF), "igrad_hbm": ((4, canvases, CELLS, D), BF)}
    scratch = {
        "xin": ((CELLS, D), BF),
        "cot": ((CELLS, D), BF),
        "code": ((CELLS, 128), jnp.int32),
        "codew": ((WROWS, 128), jnp.int32),
        "buf": ((4, CELLS, D), BF),
        "hqw": ((2, WROWS, D), BF),
        "qkv": ((2, WROWS, 3 * D), BF),
        "probs": ((2, WINDOWS * GROUPS, PLACES, 256), BF),
        "att": ((2, WROWS, D), BF),
        "hq2": ((2, CELLS, D), BF),
        "hid": ((2, CELLS, FF), BF),
        "dgelu": ((2, CELLS, FF), BF),
        "canvf": ((CELLS, D), F32),
        "winf": ((WROWS, D), F32),
        "gzw": ((WROWS, D), BF),
        "go": ((WROWS, D), BF),
        "gqkv": ((WROWS, 3 * D), BF),
        "wide_t": ((2, D, WROWS), BF),
    }
    sems = {
        "in_sem": (3,),
        "local_sem": (2, canvases),
        "send_sem": (2, 4, canvases),
        "recv_sem": (2, 4, canvases),
    }
    if linked:
        outs |= {
            "o_qkv": ((2, 48, 3 * D), F32),
            "o_proj": ((2, 48, D), F32),
            "o_fc1": ((2, 48, FF), F32),
            "o_fc2": ((2, 192, D), F32),
            "o_small": ((2, 8, 64, D), BF),
        }
        scratch |= full | grads
        scratch["packs"] = ((8, 16, 256), BF)
        for kind, rows in (("m_", MLP_ROWS), ("a_", ATT_ROWS)):
            scratch |= {
                kind + "st_a": ((4, rows, D), BF),
                kind + "rc_a": ((4, rows, D), BF),
                kind + "st_b": ((3, rows, D), BF),
                kind + "rc_b": ((3, rows, D), BF),
                kind + "st_c": ((rows, D), BF),
                kind + "rc_c": ((3, rows // 4, D), BF),
                kind + "fin": ((rows, D), BF),
            }
        sems |= {
            "sh_sem": (4,),
            "os_sem": (2,),
            "go_sem": (4, 2),
            "wz_send": (4, 2, 3),
            "wz_recv": (4, 2, 3),
            "wx_send": (4, 2, 3, 3),
            "wx_recv": (4, 2, 3, 3),
            "ws_send": (4, 2, 4),
            "ws_recv": (4, 2, 4),
            "pk_send": (7,),
            "pk_recv": (7,),
            "ra_send": (4,),
            "ra_recv": (4,),
            "rb_send": (4, 3),
            "rb_recv": (4, 3),
            "rc_send": (4, 3),
            "rc_recv": (4, 3),
            "rf_send": (4, 3),
            "rf_recv": (4, 3),
            "rs_send": (2, 7),
            "rs_recv": (2, 7),
        }
    else:
        outs |= grads
    in_vmem = set(grads) | set(full) | {"bias", "pack"}
    names = tuple(operands) + tuple(outs) + tuple(scratch) + tuple(sems)
    results = pl.pallas_call(
        functools.partial(kernel, names, linked, canvases),
        out_shape=tuple(shape(*o) for o in outs.values()),
        in_specs=[vmem if name in in_vmem else hbm for name in operands],
        out_specs=tuple(vmem if name in in_vmem else hbm for name in outs),
        scratch_shapes=[pltpu.VMEM(*v) for v in scratch.values()] + [dma(v) for v in sems.values()],
        compiler_params=pltpu.CompilerParams(
            vmem_limit_bytes=64 * 1024 * 1024 - 65536, collective_id=0, has_side_effects=True
        ),
    )(*operands.values())
    return dict(zip(outs, results))


def place_pairs():
    place = np.arange(PLACES)
    r, c = place // 8, place % 8
    index = (r[None, :] - r[:, None] + WIN - 1) * (2 * WIN - 1) + c[None, :] - c[:, None] + WIN - 1
    real = (r < WIN) & (c < WIN)
    return index, real[:, None] & real[None, :], real


def pair_onehot():
    index, both, _ = place_pairs()
    table = (2 * WIN - 1) ** 2
    hot = (np.where(both, index, -1).reshape(-1)[None, :] == np.arange(table)[:, None])
    return hot.astype(np.float32)


def body(
    inputs,
    cotangent,
    pad_mask,
    region_ids,
    norm1_gain,
    norm1_bias,
    qkv_weight,
    qv_bias,
    rel_table,
    proj_weight,
    proj_bias,
    norm2_gain,
    norm2_bias,
    fc1_weight,
    fc1_bias,
    fc2_weight,
    fc2_bias,
):
    owners = lax.axis_size("dp")
    linked = owners == 8
    mine = lax.axis_index("pipe")

    def own(a):
        return lax.dynamic_index_in_dim(a, mine, 0, keepdims=False)

    code = own(region_ids) * 2 + own(pad_mask)
    code = jnp.broadcast_to(code[:, :, None], code.shape + (128,))

    hot = pair_onehot()
    _, _, real = place_pairs()
    rel = lax.dot_general(
        rel_table.astype(BF), jnp.asarray(hot, BF), (((1,), (0,)), ((), ())), preferred_element_type=F32
    )
    rel = rel.reshape(2, GROUPS, 4, PLACES, PLACES).transpose(0, 1, 3, 2, 4)
    rel = jnp.where(jnp.asarray(real)[None, None, :, None, None], rel, MASKED)
    rel = rel.reshape(2, GROUPS, PLACES, 256)

    operands = {"x_hbm": inputs, "cot_hbm": cotangent, "code_hbm": code, "bias": rel}
    vectors = (norm1_gain, norm1_bias, proj_bias, norm2_gain, norm2_bias, fc2_bias, qv_bias, fc1_bias)
    sizes = [v.shape[1] for v in vectors]
    ends = np.cumsum([0] + sizes)
    if linked:
        pack = jnp.stack([jnp.pad(v, ((0, 0), (0, 256 - v.shape[1]))) for v in vectors], axis=1)
        operands |= {
            "pack": pack.reshape(16, 256).astype(BF),
            "s_qkv": qkv_weight,
            "s_proj": proj_weight,
            "s_fc1": fc1_weight,
            "s_fc2": fc2_weight,
        }
    else:

        def gathered(a):
            return lax.all_gather(a.astype(BF), "dp", axis=1, tiled=True)

        packed = lax.all_gather(jnp.concatenate(vectors, axis=1).astype(BF), "dp", axis=1)
        parts = [packed[:, :, a:b].reshape(2, -1).astype(F32) for a, b in zip(ends[:-1], ends[1:])]
        qv = parts[6]
        parts[6] = jnp.concatenate([qv[:, :D], jnp.zeros_like(qv[:, :D]), qv[:, D:]], axis=1)
        vec = jnp.stack([jnp.pad(p, ((0, 0), (0, FF - p.shape[1]))) for p in parts], axis=1)
        operands |= {
            "wat": jnp.concatenate([gathered(qkv_weight), gathered(proj_weight)], axis=2),
            "fc1": gathered(fc1_weight),
            "fc2": gathered(fc2_weight),
            "vec": vec.reshape(16, FF),
        }

    out = compute(linked, operands)

    def to_owners(g):
        shared = lax.psum_scatter(g, "dp", scatter_dimension=1, tiled=True)
        return lax.psum(shared, "pipe")

    if linked:
        small = out["o_small"]
        g_tab = jnp.concatenate([small[:, :, :8], small[:, :, 8:16]], axis=3).reshape(2, PLACES, GROUPS * 256)
        g_vec = jnp.concatenate([small[:, :, 16 + 8 * j : 24 + 8 * j] for j in range(4)], axis=3)
    else:
        g_tab, g_vec = out["g_tab"], out["g_vec"]

    g_vec = jnp.sum(g_vec.astype(F32), axis=2)
    kinds = [g_vec[:, i] for i in range(8)]
    qv_sum = jnp.concatenate([kinds[6][:, :D], kinds[6][:, 2 * D : 3 * D]], axis=1)
    rows = [kinds[0], kinds[1], kinds[2], kinds[3], kinds[4], kinds[5], qv_sum, kinds[7]]
    if linked:
        at = lax.axis_index("dp")
        small = [lax.dynamic_slice_in_dim(v, at * n, n, 1) for v, n in zip(rows, sizes)]
    else:
        rows = [v[:, : n * owners].reshape(2, -1, n) for v, n in zip(rows, sizes)]
        g_small = to_owners(jnp.concatenate(rows, axis=2))[:, 0]
        small = [g_small[:, a:b] for a, b in zip(ends[:-1], ends[1:])]

    pairs = g_tab.reshape(2, PLACES, HEADS, PLACES).transpose(0, 2, 1, 3)
    pairs = pairs.reshape(2, HEADS, PLACES * PLACES)
    g_table = lax.dot_general(
        jnp.broadcast_to(jnp.asarray(hot, pairs.dtype), (2,) + hot.shape),
        pairs,
        (((2,), (2,)), ((0,), (0,))),
        precision=None if linked else lax.Precision.HIGHEST,
        preferred_element_type=F32,
    )
    if linked:
        big = [out[name] for name in ("o_qkv", "o_proj", "o_fc1", "o_fc2")]
    else:
        g_table = lax.psum(g_table, ("pipe", "dp"))
        big = [to_owners(out[name]) for name in ("g_qkv", "g_proj", "g_fc1")]
        big.append(to_owners(out["g_fc2t"].transpose(0, 2, 1)))

    return (
        out["act_hbm"][None],
        out["igrad_hbm"][None],
        small[0],
        small[1],
        big[0],
        small[6],
        g_table,
        big[1],
        small[2],
        small[3],
        small[4],
        big[2],
        small[7],
        big[3],
        small[5],
    )


def solution(mesh):
    cols = P(None, "dp")
    rows = P(None, "dp", None)
    return jax.shard_map(
        body,
        mesh=mesh,
        in_specs=(
            P(None, "dp", None, None),
            P(None, "dp", None, None),
            rows,
            rows,
            cols,
            cols,
            rows,
            cols,
            P(),
            rows,
            cols,
            cols,
            cols,
            rows,
            cols,
            rows,
            cols,
        ),
        out_specs=(
            P("pipe", None, "dp", None, None),
            P("pipe", None, "dp", None, None),
            cols,
            cols,
            rows,
            cols,
            P(),
            rows,
            cols,
            cols,
            cols,
            rows,
            cols,
            rows,
            cols,
        ),
        check_vma=False,
    )
```

```python
import functools
import types

import jax
import jax.numpy as jnp
import numpy as np
from jax import lax
from jax.experimental import pallas as pl
from jax.experimental.pallas import tpu as pltpu
from jax.sharding import PartitionSpec as P

HEADS = 12
WIN = 7
SHIFT = 3
GRID = 28
CELLS = 784
D = 384
FF = 1536
HEAD = 32
SIDE = 4
WINDOWS = 16
PLACES = 64
WROWS = WINDOWS * PLACES
GROUPS = 3
TILE = 112
SCALE = HEAD**-0.5
NORM_EPS = 1e-05
MASKED = -1e30
BF = jnp.bfloat16
F32 = jnp.float32

ERF_P = 0.3275911 / np.sqrt(2.0)
ERF_A = [0.5 * a for a in (0.254829592, -0.284496736, 1.421413741, -1.453152027, 1.061405429)]
PHI_0 = 1.0 / np.sqrt(2.0 * np.pi)


def nn(a, b):
    return lax.dot_general(a, b, (((1,), (0,)), ((), ())), preferred_element_type=F32)


def nt(a, b):
    return lax.dot_general(a, b, (((1,), (1,)), ((), ())), preferred_element_type=F32)


def tn(a, b):
    return lax.dot_general(a, b, (((0,), (0,)), ((), ())), preferred_element_type=F32)


def segments(shift):
    runs = []
    for wr in range(SIDE):
        for r in range(WIN):
            row = (wr * WIN + r + shift) % GRID
            for wc in range(SIDE):
                col = (wc * WIN + shift) % GRID
                place = (wr * SIDE + wc) * PLACES + r * 8
                first = min(WIN, GRID - col)
                runs.append((row * GRID + col, place, first))
                if first < WIN:
                    runs.append((row * GRID, place + first, WIN - first))
    return runs


def to_windows(src, dst, shift):
    for cell, place, count in segments(shift):
        dst[pl.ds(place, count), :] = src[pl.ds(cell, count), :]


def to_canvas(src, dst, shift):
    for cell, place, count in segments(shift):
        dst[pl.ds(cell, count), :] = src[pl.ds(place, count), :]


def row_block(t, size):
    return pl.ds(pl.multiple_of(t * size, 16), size)


def standardized(v):
    centered = v - jnp.mean(v, axis=-1, keepdims=True)
    spread = jnp.mean(centered * centered, axis=-1, keepdims=True)
    rs = lax.rsqrt(spread + NORM_EPS)
    return centered * rs, rs


def by_eights(v):
    return jnp.sum(v.reshape(v.shape[0] // 8, 8, v.shape[1]), axis=0)


def gelu_parts(x):
    den = 1.0 + ERF_P * jnp.abs(x)
    t = pl.reciprocal(den, approx=True)
    t = t * (2.0 - den * t)
    e = jnp.exp(-0.5 * x * x)
    poly = ERF_A[4]
    for a in ERF_A[3::-1]:
        poly = poly * t + a
    tail = poly * t * e
    cdf = jnp.where(x >= 0.0, 1.0 - tail, tail)
    return x * cdf, cdf + x * (e * PHI_0)


def real_places(rows):
    place = lax.broadcasted_iota(jnp.int32, (rows, 1), 0)
    return ((place & 7) < WIN) & (((place >> 3) & 7) < WIN)


def head_of_lane():
    return lax.broadcasted_iota(jnp.int32, (PLACES, 128), 1) >> 5


def by_head(x, lanes):
    zero = jnp.zeros_like(x)
    return jnp.concatenate([jnp.where(lanes == h, x, zero) for h in range(4)], axis=0)


def own_head(wide, lanes):
    out = wide[3 * PLACES :]
    for h in (2, 1, 0):
        out = jnp.where(lanes == h, wide[h * PLACES : (h + 1) * PLACES], out)
    return out


MESH = pl.DeviceIdType.MESH
ATT_ROWS = 256
MLP_ROWS = 384
SMALL = 192


def gather_kernel(names, *refs):
    r = types.SimpleNamespace(**dict(zip(names, refs)))
    me = lax.axis_index("pipe")
    wat, fc1, fc2, vec = r.wat, r.fc1, r.fc2, r.vec
    d = lax.axis_index("dp")
    z, c = d // 2, d % 2
    sibling = {"dp": 2 * z + 1 - c}

    def z_peer(k):
        return {"dp": 2 * lax.rem(z + k, 4) + c}

    def pipe_peer(k):
        return {"pipe": lax.rem(me + k, 4)}

    def dp_peer(k):
        return {"dp": lax.rem(d + k, 8)}

    def remote(src, dst, send, recv, device):
        return pltpu.make_async_remote_copy(
            src_ref=src, dst_ref=dst, send_sem=send, recv_sem=recv, device_id=device, device_id_type=MESH
        )

    barrier = pltpu.get_barrier_semaphore()
    partners = [pipe_peer(k) for k in range(1, 4)] + [dp_peer(k) for k in range(1, 8)]
    for partner in partners:
        pl.semaphore_signal(barrier, inc=1, device_id=partner, device_id_type=MESH)

    full = ((wat,), (fc1, fc2), (wat,), (fc1, fc2))

    def owner_back(k):
        return 2 * lax.rem(z + 4 - k, 4) + c

    def shard(sec, a, owner):
        h = 192 if a else 48
        return full[sec][a].at[sec // 2, pl.ds(pl.multiple_of(owner * h, 16), h), :]

    def part(sec, a, owner, place):
        if a:
            return fc2.at[sec // 2, pl.ds(pl.multiple_of(owner * 192 + place * 48, 16), 48), :]
        rows = pl.ds(pl.multiple_of(owner * 48, 16), 48)
        return full[sec][0].at[sec // 2, rows, pl.ds(pl.multiple_of(place * D, 128), D)]

    def to_z(sec, a, k):
        own = part(sec, a, d, me)
        return remote(own, own, r.wz_send.at[sec, a, k - 1], r.wz_recv.at[sec, a, k - 1], z_peer(k))

    def to_places(sec, a, k, j):
        got = part(sec, a, owner_back(k), me)
        return remote(
            got, got, r.wx_send.at[sec, a, k - 1, j - 1], r.wx_recv.at[sec, a, k - 1, j - 1], pipe_peer(j)
        )

    def to_sibling(sec, a, k):
        block = shard(sec, a, owner_back(k))
        return remote(block, block, r.ws_send.at[sec, a, k], r.ws_recv.at[sec, a, k], sibling)

    def weights_1(sec):
        for a in range(len(full[sec])):
            for k in range(1, 4):
                to_z(sec, a, k).start()
            to_sibling(sec, a, 0).start()

    def weights_2(sec):
        for k in range(1, 4):
            for a in range(len(full[sec])):
                got = part(sec, a, owner_back(k), me)
                remote(got, got, r.wz_send.at[sec, a, k - 1], r.wz_recv.at[sec, a, k - 1], z_peer(k)).wait_recv()
                for j in range(1, 4):
                    to_places(sec, a, k, j).start()

    def weights_3(sec):
        for k in range(1, 4):
            for a in range(len(full[sec])):
                for j in range(1, 4):
                    got = part(sec, a, owner_back(k), lax.rem(me + 4 - j, 4))
                    remote(
                        got, got, r.wx_send.at[sec, a, k - 1, j - 1], r.wx_recv.at[sec, a, k - 1, j - 1], pipe_peer(j)
                    ).wait_recv()
                to_sibling(sec, a, k).start()

    def weights_4(sec):
        for k in range(4):
            for a in range(len(full[sec])):
                block = shard(sec, a, 2 * lax.rem(z + 4 - k, 4) + 1 - c)
                remote(block, block, r.ws_send.at[sec, a, k], r.ws_recv.at[sec, a, k], sibling).wait_recv()

    def weights_sent():
        for sec in range(4):
            for a in range(len(full[sec])):
                for k in range(4):
                    to_sibling(sec, a, k).wait_send()
                    if k:
                        to_z(sec, a, k).wait_send()
                        for j in range(1, 4):
                            to_places(sec, a, k, j).wait_send()

    def pack_copy(k):
        return remote(
            r.packs.at[d], r.packs.at[d], r.pk_send.at[k - 1], r.pk_recv.at[k - 1], dp_peer(k)
        )

    def pack_arrival(k):
        slot = r.packs.at[lax.rem(d + 8 - k, 8)]
        return remote(slot, slot, r.pk_send.at[k - 1], r.pk_recv.at[k - 1], dp_peer(k))

    def place_vectors():
        kind = lax.broadcasted_iota(jnp.int32, (16, 256), 0) & 7
        lane = lax.broadcasted_iota(jnp.int32, (16, 256), 1)
        vec[...] = jnp.zeros_like(vec)
        for width, kinds in ((48, kind < 6), (96, kind == 6), (192, kind == 7)):
            for owner in range(8):
                at = owner * width
                if width == 96 and owner >= 4:
                    at += D
                start = at // 128 * 128
                part = jnp.where(kinds & (lane < width), r.packs[owner].astype(F32), 0.0)
                if at > start:
                    part = pltpu.roll(part, at - start, 1)
                vec[:, start : start + 256] += part

    lands = ((r.s_qkv, 48, wat, 0), (r.s_proj, 48, wat, 3 * D), (r.s_fc1, 48, fc1, 0), (r.s_fc2, 192, fc2, 0))
    r.packs[d] = r.pack[...]
    for src, h, ref, col in lands:
        for b in range(2):
            for t in range(h // 48):
                rows = pl.ds(pl.multiple_of(d * h + t * 48, 16), 48)
                ref[b, rows, col : col + src.shape[2]] = src[b, t * 48 : (t + 1) * 48, :].astype(BF)
    pl.semaphore_wait(barrier, len(partners))
    for k in range(1, 8):
        pack_copy(k).start()
    for step in (weights_1, weights_2, weights_3, weights_4):
        for sec in range(4):
            step(sec)
    for k in range(1, 8):
        pack_arrival(k).wait_recv()
    place_vectors()
    weights_sent()
    for k in range(1, 8):
        pack_copy(k).wait_send()


def gather(operands):
    shape = jax.ShapeDtypeStruct
    vmem = pl.BlockSpec(memory_space=pltpu.VMEM)
    dma = pltpu.SemaphoreType.DMA
    outs = {
        "wat": ((2, D, 4 * D), BF),
        "fc1": ((2, D, FF), BF),
        "fc2": ((2, FF, D), BF),
        "vec": ((16, FF), F32),
    }
    sems = {
        "wz_send": (4, 2, 3),
        "wz_recv": (4, 2, 3),
        "wx_send": (4, 2, 3, 3),
        "wx_recv": (4, 2, 3, 3),
        "ws_send": (4, 2, 4),
        "ws_recv": (4, 2, 4),
        "pk_send": (7,),
        "pk_recv": (7,),
    }
    names = tuple(operands) + tuple(outs) + ("packs",) + tuple(sems)
    results = pl.pallas_call(
        functools.partial(gather_kernel, names),
        out_shape=tuple(shape(*o) for o in outs.values()),
        in_specs=[vmem] * len(operands),
        out_specs=(vmem,) * len(outs),
        scratch_shapes=[pltpu.VMEM((8, 16, 256), BF)] + [dma(v) for v in sems.values()],
        compiler_params=pltpu.CompilerParams(
            vmem_limit_bytes=32 * 1024 * 1024, collective_id=1, has_side_effects=True
        ),
    )(*operands.values())
    return dict(zip(outs, results))


def kernel(names, linked, canvases, *refs):
    r = types.SimpleNamespace(**dict(zip(names, refs)))
    me = lax.axis_index("pipe")
    xin, cot, code, codew, buf = r.xin, r.cot, r.code, r.codew, r.buf
    hqw, qkv, probs, att = r.hqw, r.qkv, r.probs, r.att
    hq2, hid, dgelu = r.hq2, r.hid, r.dgelu
    canvf, winf, gzw, wide_t, gqkv, go = r.canvf, r.winf, r.gzw, r.wide_t, r.gqkv, r.go
    g_qkv, g_proj, g_fc1, g_fc2t, g_vec, g_tab = r.g_qkv, r.g_proj, r.g_fc1, r.g_fc2t, r.g_vec, r.g_tab
    wat, fc1, fc2, vec, bias = r.wat, r.fc1, r.fc2, r.vec, r.bias
    if linked:
        d = lax.axis_index("dp")
        z, c = d // 2, d % 2
        sibling = {"dp": 2 * z + 1 - c}

    def z_peer(k):
        return {"dp": 2 * lax.rem(z + k, 4) + c}

    def pipe_peer(k):
        return {"pipe": lax.rem(me + k, 4)}

    def dp_peer(k):
        return {"dp": lax.rem(d + k, 8)}

    def remote(src, dst, send, recv, device):
        return pltpu.make_async_remote_copy(
            src_ref=src, dst_ref=dst, send_sem=send, recv_sem=recv, device_id=device, device_id_type=MESH
        )

    barrier = pltpu.get_barrier_semaphore()
    partners = [pipe_peer(k) for k in range(1, 4)]
    if linked:
        partners += [dp_peer(k) for k in range(1, 8)]
    for partner in partners:
        pl.semaphore_signal(barrier, inc=1, device_id=partner, device_id_type=MESH)

    def pieces(sec, owner):
        b = sec // 2
        out = []

        def matrix(ref, h):
            for t in range(h // 48):
                rows = pl.ds(pl.multiple_of(owner * h + t * 48, 16), 48)
                for j in range(ref.shape[2] // D):
                    load = functools.partial(lambda ref, rows, j: ref[b, rows, j * D : (j + 1) * D], ref, rows, j)
                    out.append((len(out) * 48, 48, load))

        def small():
            rows = pl.ds(pl.multiple_of(owner * 8, 8), 8)
            parts = [g_tab[b, rows, j * D : (j + 1) * D] for j in range(2)]
            parts += [g_vec[b, owner, :, j * D : (j + 1) * D] for j in range(4)]
            return jnp.concatenate(parts + [jnp.zeros((16, D), F32)], axis=0)

        if sec % 2:
            matrix(g_fc1, 48)
        else:
            matrix(g_qkv, 48)
            matrix(g_proj, 48)
            out.append((SMALL, 64, small))
        return out

    def reduce_refs(sec):
        kind = "m" if sec % 2 else "a"
        return types.SimpleNamespace(
            **{n: getattr(r, kind + "_" + n) for n in ("st_a", "rc_a", "st_b", "rc_b", "st_c", "rc_c", "fin")}
        )

    def step_1(sec):
        q = reduce_refs(sec)
        if sec < 2:
            copy_a(sec + 2).wait_send()
            for k in range(1, 4):
                copy_b(sec + 2, k).wait_send()
                copy_c(sec + 2, k).wait_send()
        for k in range(4):
            i = lax.rem(z + k, 4)
            kept = q.st_b.at[k - 1] if k else q.st_c
            for row, rows, load in pieces(sec, 2 * i + 1 - c):
                q.st_a[i, row : row + rows, :] = load().astype(BF)
            for row, rows, load in pieces(sec, 2 * i + c):
                kept[row : row + rows, :] = load().astype(BF)
            if sec % 2:
                winf[:D, :] = g_fc2t[sec // 2, :, pl.ds(pl.multiple_of(i * D, 128), D)].T
                for t in range(0, 192, 48):
                    at = slice(192 + t, 240 + t)
                    q.st_a[i, at, :] = winf[pl.ds(pl.multiple_of((1 - c) * 192 + t, 16), 48), :].astype(BF)
                    kept[at, :] = winf[pl.ds(pl.multiple_of(c * 192 + t, 16), 48), :].astype(BF)
        copy_a(sec).start()

    def copy_a(sec):
        q = reduce_refs(sec)
        return remote(q.st_a, q.rc_a, r.ra_send.at[sec], r.ra_recv.at[sec], sibling)

    def copy_b(sec, k):
        q = reduce_refs(sec)
        return remote(
            q.st_b.at[k - 1], q.rc_b.at[k - 1], r.rb_send.at[sec, k - 1], r.rb_recv.at[sec, k - 1], z_peer(k)
        )

    def step_2(sec):
        q = reduce_refs(sec)
        copy_a(sec).wait_recv()
        for k in (1, 2, 3, 0):
            i = lax.rem(z + k, 4)
            kept = q.st_b.at[k - 1] if k else q.st_c
            for row in range(0, kept.shape[0], 64):
                at = slice(row, row + 64)
                kept[at, :] = (kept[at, :].astype(F32) + q.rc_a[i, at, :].astype(F32)).astype(BF)
            if k:
                copy_b(sec, k).start()

    def quarter(sec, ref, who):
        rows = (MLP_ROWS if sec % 2 else ATT_ROWS) // 4
        return ref.at[pl.ds(pl.multiple_of(who * rows, 16), rows), :]

    def copy_c(sec, k):
        q = reduce_refs(sec)
        return remote(
            quarter(sec, q.st_c, lax.rem(me + k, 4)),
            q.rc_c.at[k - 1],
            r.rc_send.at[sec, k - 1],
            r.rc_recv.at[sec, k - 1],
            pipe_peer(k),
        )

    def step_3(sec):
        q = reduce_refs(sec)
        for k in range(1, 4):
            copy_b(sec, k).wait_recv()
        for row in range(0, q.st_c.shape[0], 64):
            at = slice(row, row + 64)
            total = q.st_c[at, :].astype(F32)
            for k in range(3):
                total = total + q.rc_b[k, at, :].astype(F32)
            q.st_c[at, :] = total.astype(BF)
        for k in range(1, 4):
            copy_c(sec, k).start()

    def copy_f(sec, k):
        q = reduce_refs(sec)
        own = quarter(sec, q.fin, me)
        return remote(own, own, r.rf_send.at[sec, k - 1], r.rf_recv.at[sec, k - 1], pipe_peer(k))

    def step_4(sec):
        q = reduce_refs(sec)
        for k in range(1, 4):
            copy_c(sec, k).wait_recv()
            if sec < 2:
                copy_f(sec + 2, k).wait_send()
        total = quarter(sec, q.st_c, me)[...].astype(F32)
        for k in range(3):
            total = total + q.rc_c[k].astype(F32)
        quarter(sec, q.fin, me)[...] = total.astype(BF)
        for k in range(1, 4):
            copy_f(sec, k).start()

    def copy_s(b, k):
        rows = pl.ds(SMALL, 64)
        return remote(
            r.a_fin.at[rows, :], r.o_small.at[b, d], r.rs_send.at[b, k - 1], r.rs_recv.at[b, k - 1], dp_peer(k)
        )

    def own_small(b):
        return pltpu.make_async_copy(r.a_fin.at[pl.ds(SMALL, 64), :], r.o_small.at[b, d], r.os_sem.at[b])

    def outputs(sec):
        pairs = ((g_fc1, r.o_fc1, 48), (g_fc2t, r.o_fc2, 192)) if sec % 2 else (
            (g_qkv, r.o_qkv, 48), (g_proj, r.o_proj, 48))
        b = sec // 2
        return [
            pltpu.make_async_copy(ref.at[b, pl.ds(0, h), pl.ds(0, out.shape[2])], out.at[b], r.go_sem.at[sec, i])
            for i, (ref, out, h) in enumerate(pairs)
        ]

    def step_5(sec):
        q = reduce_refs(sec)
        b = sec // 2
        for k in range(1, 4):
            got = quarter(sec, q.fin, lax.rem(me + 4 - k, 4))
            remote(got, got, r.rf_send.at[sec, k - 1], r.rf_recv.at[sec, k - 1], pipe_peer(k)).wait_recv()
        if sec % 2 == 0:
            for k in range(1, 8):
                copy_s(b, k).start()
            own_small(b).start()
        row = 0
        for ref, h, n in ((g_fc1, 48, 4), (g_fc2t, 192, 1)) if sec % 2 else ((g_qkv, 48, 3), (g_proj, 48, 1)):
            for t in range(h // 48):
                for j in range(n):
                    ref[b, t * 48 : (t + 1) * 48, j * D : (j + 1) * D] = q.fin[row : row + 48, :].astype(F32)
                    row += 48
        for out in outputs(sec):
            out.start()

    def smalls_sent(b):
        for k in range(1, 8):
            copy_s(b, k).wait_send()
        own_small(b).wait()

    def reductions_done():
        for sec in (1, 0):
            copy_a(sec).wait_send()
            for k in range(1, 4):
                copy_b(sec, k).wait_send()
                copy_c(sec, k).wait_send()
                copy_f(sec, k).wait_send()
        for sec in range(4):
            for out in outputs(sec):
                out.wait()
        smalls_sent(0)
        for b in range(2):
            for k in range(1, 8):
                rows = pl.ds(SMALL, 64)
                remote(
                    r.a_fin.at[rows, :],
                    r.o_small.at[b, lax.rem(d + 8 - k, 8)],
                    r.rs_send.at[b, k - 1],
                    r.rs_recv.at[b, k - 1],
                    dp_peer(k),
                ).wait_recv()

    pl.semaphore_wait(barrier, len(partners))
    for ref in (g_qkv, g_proj, g_fc1, g_fc2t):
        for b in range(2):

            @pl.loop(0, ref.shape[1] // 16)
            def _(i):
                ref[b, row_block(i, 16), :] = jnp.zeros((16, ref.shape[2]), F32)

    g_vec[...] = jnp.zeros_like(g_vec)
    g_tab[...] = jnp.zeros_like(g_tab)
    codew[...] = jnp.zeros_like(codew)

    def vector(b, kind, width=D):
        return vec[b * 8 + kind : b * 8 + kind + 1, :width]

    def add_vec(b, kind, part):
        g_vec[b, kind, :, : part.shape[1]] += part

    def windowed(rows, count):
        return jnp.where(real_places(count), winf[rows, :], 0.0).astype(BF)

    def by_two(start, stop, step):
        @pl.loop(start // 2, stop // 2)
        def _(i):
            step((2 * i, 2 * i + 1))

    def attention_forward(b, x, out, free_out, hook):
        lanes = head_of_lane()

        @pl.loop(0, CELLS // TILE)
        def _(t):
            rows = row_block(t, TILE)
            xhat, _ = standardized(x[rows, :].astype(F32))
            canvf[rows, :] = xhat * vector(b, 0) + vector(b, 1)

        to_windows(canvf, winf, SHIFT * b)
        to_windows(code, codew, SHIFT * b)

        @pl.loop(0, 4)
        def _(t):
            rows = row_block(t, 256)
            hq = windowed(rows, 256)
            hqw[b, rows, :] = hq
            for part in range(3):
                cols = slice(part * D, (part + 1) * D)
                acc = nn(hq, wat[b, :, cols]) + vec[b * 8 + 6 : b * 8 + 7, cols]
                if part == 0:
                    acc = acc * SCALE
                qkv[b, rows, cols] = acc.astype(BF)

        hook(0)

        def windows(pair):
            blocks = [row_block(w, PLACES) for w in pair]
            masks = []
            for rows in blocks:
                cells = codew[rows, :]
                region = (cells >> 1) * b
                pad = (cells & 1).astype(F32)
                lane = lax.broadcasted_iota(jnp.int32, (PLACES, 128), 1)
                same = jnp.where(lane == region, 1.0, 0.0)
                left = jnp.where(lane == 127, 1.0 - pad, same).astype(BF)
                right = jnp.where(lane == 127, -pad, same).astype(BF)
                agree = nt(left, jnp.concatenate([right, right], axis=0))
                mask = jnp.where(agree > 0.5, 0.0, MASKED)
                masks.append(jnp.concatenate([mask, mask], axis=1))
            for g in range(GROUPS):
                for w, rows, mask in zip(pair, blocks, masks):
                    q = qkv[b, rows, g * 128 : (g + 1) * 128]
                    k = qkv[b, rows, D + g * 128 : D + (g + 1) * 128]
                    v = qkv[b, rows, 2 * D + g * 128 : 2 * D + (g + 1) * 128]
                    s = nt(k, by_head(q, lanes)) + bias[b, g] + mask
                    e = jnp.exp(s - jnp.max(s, axis=0, keepdims=True))
                    p = (e * (1.0 / jnp.sum(e, axis=0, keepdims=True))).astype(BF)
                    probs[b, w * GROUPS + g] = p
                    att[b, rows, g * 128 : (g + 1) * 128] = own_head(tn(p, v), lanes).astype(BF)

        by_two(0, WINDOWS // 2, windows)
        hook(1)
        by_two(WINDOWS // 2, WINDOWS, windows)
        hook(2)

        @pl.loop(0, 4)
        def _(t):
            rows = row_block(t, 256)
            winf[rows, :] = nn(att[b, rows, :], wat[b, :, 3 * D :])

        to_canvas(winf, canvf, SHIFT * b)
        free_out()

        @pl.loop(0, CELLS // TILE)
        def _(t):
            rows = row_block(t, TILE)
            out[rows, :] = (x[rows, :].astype(F32) + (canvf[rows, :] + vector(b, 2))).astype(BF)

    def mlp_forward(b, x, out, free_out, hook):
        @pl.loop(0, CELLS // TILE)
        def _(t):
            rows = row_block(t, TILE)
            xhat, _ = standardized(x[rows, :].astype(F32))
            hq2[b, rows, :] = (xhat * vector(b, 3) + vector(b, 4)).astype(BF)

        def chunk(i):
            cols = pl.ds(pl.multiple_of(i * 256, 256), 256)
            pre = nn(hq2[b], fc1[b, :, cols]) + vec[b * 8 + 7 : b * 8 + 8, cols]
            for at in range(0, CELLS, 16):
                h, dg = gelu_parts(pre[at : at + 16])
                hid[b, at : at + 16, cols] = h.astype(BF)
                dgelu[b, at : at + 16, cols] = dg.astype(BF)

        pl.loop(0, FF // 512)(chunk)
        hook(0)
        pl.loop(FF // 512, FF // 256)(chunk)

        free_out()
        total = nn(hid[b], fc2[b])
        for at in range(0, CELLS, TILE):
            rows = slice(at, at + TILE)
            out[rows, :] = (x[rows, :].astype(F32) + (total[rows] + vector(b, 5))).astype(BF)

    def norm_backward(b, kind, x, gz, out):
        @pl.loop(0, CELLS // TILE)
        def _(t):
            rows = row_block(t, TILE)
            xhat, rs = standardized(x[rows, :].astype(F32))
            gn = canvf[rows, :]
            gzf = gz[rows, :].astype(F32)
            add_vec(b, kind, by_eights(gn * xhat))
            add_vec(b, kind + 1, by_eights(gn))
            add_vec(b, 5 if kind else 2, by_eights(gzf))
            g = gn * vector(b, kind)
            mg = jnp.mean(g, axis=-1, keepdims=True)
            mgx = jnp.mean(g * xhat, axis=-1, keepdims=True)
            out[rows, :] = (gzf + rs * (g - mg - xhat * mgx)).astype(BF)

    def mlp_backward(b, x, gz, out, free_out, hook):
        hook(0)
        wide_t[0, :, :CELLS] = hq2[b].T
        wide_t[1, :, :CELLS] = gz[...].T

        def chunk(i):
            cols = pl.ds(pl.multiple_of(i * 256, 256), 256)
            gh = nt(gz[...], fc2[b, cols, :])
            sums = jnp.zeros((8, 256), F32)
            for at in range(0, CELLS, 16):
                gp = (gh[at : at + 16] * dgelu[b, at : at + 16, cols].astype(F32)).astype(BF)
                dgelu[b, at : at + 16, cols] = gp
                sums = sums + by_eights(gp.astype(F32))
            g_vec[b, 7, :, cols] += sums
            g_fc1[b, :, cols] += nn(wide_t[0, :, :CELLS], dgelu[b, :, cols])
            g_fc2t[b, :, cols] += nn(wide_t[1, :, :CELLS], hid[b, :, cols])

        pl.loop(0, FF // 512)(chunk)
        hook(1)
        pl.loop(FF // 512, FF // 256)(chunk)
        hook(2)
        canvf[...] = nt(dgelu[b], fc1[b])
        hook(3)
        free_out()
        norm_backward(b, 3, x, gz, out)
        hook(4)

    def attention_backward(b, x, gz, out, free_out, hook):
        lanes = head_of_lane()
        hook(0)

        @pl.loop(0, CELLS // TILE)
        def _(t):
            rows = row_block(t, TILE)
            canvf[rows, :] = gz[rows, :].astype(F32)

        to_windows(canvf, winf, SHIFT * b)

        @pl.loop(0, 4)
        def _(t):
            rows = row_block(t, 256)
            gzw[rows, :] = windowed(rows, 256)

        g_proj[b] += tn(att[b], gzw[...])

        @pl.loop(0, 4)
        def _(t):
            rows = row_block(t, 256)
            go[rows, :] = nt(gzw[rows, :], wat[b, :, 3 * D :]).astype(BF)

        hook(1)

        def windows(pair):
            blocks = [row_block(w, PLACES) for w in pair]
            for g in range(GROUPS):
                at = [slice(part * D + g * 128, part * D + (g + 1) * 128) for part in range(3)]
                table = jnp.zeros((PLACES, 256), F32)
                for w, rows in zip(pair, blocks):
                    q, k, v = (qkv[b, rows, cols] for cols in at)
                    go_wide = by_head(go[rows, at[0]], lanes)
                    p_low = probs[b, w * GROUPS + g]
                    p = p_low.astype(F32)
                    pd = p * nt(v, go_wide)
                    ds = (pd - p * jnp.sum(pd, axis=0, keepdims=True)).astype(BF)
                    table = table + ds.astype(F32)
                    gqkv[rows, at[0]] = (own_head(tn(ds, k), lanes) * SCALE).astype(BF)
                    gqkv[rows, at[1]] = nn(ds, by_head(q, lanes)).astype(BF)
                    gqkv[rows, at[2]] = nn(p_low, go_wide).astype(BF)
                g_tab[b, :, g * 256 : (g + 1) * 256] += table

        by_two(0, WINDOWS // 2, windows)
        hook(2)
        by_two(WINDOWS // 2, WINDOWS, windows)
        hook(3)

        @pl.loop(0, 4)
        def _(t):
            rows = row_block(t, 256)
            gq = gqkv[rows, :]
            add_vec(b, 6, by_eights(gq.astype(F32)))
            winf[rows, :] = nt(gq, wat[b, :, : 3 * D])

        to_canvas(winf, canvf, SHIFT * b)
        free_out()
        norm_backward(b, 0, x, gz, out)

    def attention_weights(b):
        wide_t[0] = hqw[b].T
        for part in range(3):
            cols = slice(part * D, (part + 1) * D)
            g_qkv[b, :, cols] += nn(wide_t[0], gqkv[:, cols])

    def push(kind, s, n, start):
        src = buf.at[s]
        dst = (r.act_hbm, r.igrad_hbm)[kind].at[me, n]
        local = pltpu.make_async_copy(src, dst, r.local_sem.at[kind, n])
        away = remote(src, dst, r.send_sem.at[kind, s, n], r.recv_sem.at[kind, me, n], {"pipe": s})

        @pl.when(me == s)
        def _():
            local.start() if start else local.wait()

        @pl.when(me != s)
        def _():
            away.start() if start else away.wait_send()

    def arrived(kind, k, n):
        sender = lax.rem(me + k, 4)
        dst = (r.act_hbm, r.igrad_hbm)[kind].at[sender, n]
        remote(
            buf.at[0], dst, r.send_sem.at[kind, 0, n], r.recv_sem.at[kind, sender, n], {"pipe": sender}
        ).wait_recv()

    steps = (step_1, step_2, step_3, step_4, step_5)
    schedule = {
        (3, 2): ((1, 3),),
        (2, 0): ((2, 3),),
        (2, 4): ((3, 3), (1, 2)),
        (1, 0): ((2, 2),),
        (1, 1): ((4, 3),),
        (1, 2): ((1, 1),),
        (0, 0): ((3, 2), (2, 1)),
        (0, 1): ((5, 3),),
        (0, 2): ((4, 2),),
        (0, 3): ((5, 2), (3, 1)),
        (0, 4): ((4, 1),),
    }

    @pl.loop(0, canvases)
    def _(n):
        def hook(sec, i):
            todo = schedule.get((sec, i), ())
            if linked and todo:

                @pl.when(n == canvases - 1)
                def _():
                    for step, of in todo:
                        steps[step - 1](of)

        loads = [
            pltpu.make_async_copy(r.x_hbm.at[me, n], xin, r.in_sem.at[0]),
            pltpu.make_async_copy(r.cot_hbm.at[me, n], cot, r.in_sem.at[1]),
            pltpu.make_async_copy(r.code_hbm.at[n], code, r.in_sem.at[2]),
        ]
        for load in loads:
            load.start()
        for load in loads:
            load.wait()

        x = xin
        for s in range(4):
            def free_out():
                @pl.when(n > 0)
                def _():
                    push(1, s, n - 1, False)

            forward = mlp_forward if s % 2 else attention_forward
            forward(s // 2, x, buf.at[s], free_out, lambda i: None)
            x = buf.at[s]
            push(0, s, n, True)
        gz = cot
        for s in (3, 2, 1, 0):
            x = buf.at[s - 1] if s else xin
            backward = mlp_backward if s % 2 else attention_backward
            backward(
                s // 2, x, gz, buf.at[s], functools.partial(push, 0, s, n, False), functools.partial(hook, s)
            )
            gz = buf.at[s]
            push(1, s, n, True)
            if s % 2 == 0:
                attention_weights(s // 2)
                hook(s, 4)

    if linked:
        step_5(1)
        step_1(0)
        step_2(0)
        smalls_sent(1)
        step_3(0)
        step_4(0)
        step_5(0)
        reductions_done()
    for kind in range(2):
        for k in range(1, 4):
            for n in range(canvases):
                arrived(kind, k, n)
    for s in range(4):
        push(1, s, canvases - 1, False)


def compute(linked, operands):
    canvases = operands["x_hbm"].shape[1]
    shape = jax.ShapeDtypeStruct
    hbm = pl.BlockSpec(memory_space=pl.ANY)
    vmem = pl.BlockSpec(memory_space=pltpu.VMEM)
    dma = pltpu.SemaphoreType.DMA
    full = {
        "wat": ((2, D, 4 * D), BF),
        "fc1": ((2, D, FF), BF),
        "fc2": ((2, FF, D), BF),
        "vec": ((16, FF), F32),
    }
    grads = {
        "g_qkv": ((2, D, 3 * D), F32),
        "g_proj": ((2, D, D), F32),
        "g_fc1": ((2, D, FF), F32),
        "g_fc2t": ((2, D, FF), F32),
        "g_vec": ((2, 8, 8, FF), F32),
        "g_tab": ((2, PLACES, GROUPS * 256), F32),
    }
    outs = {"act_hbm": ((4, canvases, CELLS, D), BF), "igrad_hbm": ((4, canvases, CELLS, D), BF)}
    scratch = {
        "xin": ((CELLS, D), BF),
        "cot": ((CELLS, D), BF),
        "code": ((CELLS, 128), jnp.int32),
        "codew": ((WROWS, 128), jnp.int32),
        "buf": ((4, CELLS, D), BF),
        "hqw": ((2, WROWS, D), BF),
        "qkv": ((2, WROWS, 3 * D), BF),
        "probs": ((2, WINDOWS * GROUPS, PLACES, 256), BF),
        "att": ((2, WROWS, D), BF),
        "hq2": ((2, CELLS, D), BF),
        "hid": ((2, CELLS, FF), BF),
        "dgelu": ((2, CELLS, FF), BF),
        "canvf": ((CELLS, D), F32),
        "winf": ((WROWS, D), F32),
        "gzw": ((WROWS, D), BF),
        "go": ((WROWS, D), BF),
        "gqkv": ((WROWS, 3 * D), BF),
        "wide_t": ((2, D, WROWS), BF),
    }
    sems = {
        "in_sem": (3,),
        "local_sem": (2, canvases),
        "send_sem": (2, 4, canvases),
        "recv_sem": (2, 4, canvases),
    }
    if linked:
        outs |= {
            "o_qkv": ((2, 48, 3 * D), F32),
            "o_proj": ((2, 48, D), F32),
            "o_fc1": ((2, 48, FF), F32),
            "o_fc2": ((2, 192, D), F32),
            "o_small": ((2, 8, 64, D), BF),
        }
        scratch |= grads
        for kind, rows in (("m_", MLP_ROWS), ("a_", ATT_ROWS)):
            scratch |= {
                kind + "st_a": ((4, rows, D), BF),
                kind + "rc_a": ((4, rows, D), BF),
                kind + "st_b": ((3, rows, D), BF),
                kind + "rc_b": ((3, rows, D), BF),
                kind + "st_c": ((rows, D), BF),
                kind + "rc_c": ((3, rows // 4, D), BF),
                kind + "fin": ((rows, D), BF),
            }
        sems |= {
            "os_sem": (2,),
            "go_sem": (4, 2),
            "ra_send": (4,),
            "ra_recv": (4,),
            "rb_send": (4, 3),
            "rb_recv": (4, 3),
            "rc_send": (4, 3),
            "rc_recv": (4, 3),
            "rf_send": (4, 3),
            "rf_recv": (4, 3),
            "rs_send": (2, 7),
            "rs_recv": (2, 7),
        }
    else:
        outs |= grads
    in_vmem = set(grads) | set(full) | {"bias"}
    names = tuple(operands) + tuple(outs) + tuple(scratch) + tuple(sems)
    results = pl.pallas_call(
        functools.partial(kernel, names, linked, canvases),
        out_shape=tuple(shape(*o) for o in outs.values()),
        in_specs=[vmem if name in in_vmem else hbm for name in operands],
        out_specs=tuple(vmem if name in in_vmem else hbm for name in outs),
        scratch_shapes=[pltpu.VMEM(*v) for v in scratch.values()] + [dma(v) for v in sems.values()],
        compiler_params=pltpu.CompilerParams(
            vmem_limit_bytes=64 * 1024 * 1024 - 65536, collective_id=0, has_side_effects=True
        ),
    )(*operands.values())
    return dict(zip(outs, results))


def place_pairs():
    place = np.arange(PLACES)
    r, c = place // 8, place % 8
    index = (r[None, :] - r[:, None] + WIN - 1) * (2 * WIN - 1) + c[None, :] - c[:, None] + WIN - 1
    real = (r < WIN) & (c < WIN)
    return index, real[:, None] & real[None, :], real


def pair_onehot():
    index, both, _ = place_pairs()
    table = (2 * WIN - 1) ** 2
    hot = (np.where(both, index, -1).reshape(-1)[None, :] == np.arange(table)[:, None])
    return hot.astype(np.float32)


def body(
    inputs,
    cotangent,
    pad_mask,
    region_ids,
    norm1_gain,
    norm1_bias,
    qkv_weight,
    qv_bias,
    rel_table,
    proj_weight,
    proj_bias,
    norm2_gain,
    norm2_bias,
    fc1_weight,
    fc1_bias,
    fc2_weight,
    fc2_bias,
):
    owners = lax.axis_size("dp")
    linked = owners == 8
    mine = lax.axis_index("pipe")

    def own(a):
        return lax.dynamic_index_in_dim(a, mine, 0, keepdims=False)

    code = own(region_ids) * 2 + own(pad_mask)
    code = jnp.broadcast_to(code[:, :, None], code.shape + (128,))

    hot = pair_onehot()
    _, _, real = place_pairs()
    rel = lax.dot_general(
        rel_table.astype(BF), jnp.asarray(hot, BF), (((1,), (0,)), ((), ())), preferred_element_type=F32
    )
    rel = rel.reshape(2, GROUPS, 4, PLACES, PLACES).transpose(0, 1, 3, 2, 4)
    rel = jnp.where(jnp.asarray(real)[None, None, :, None, None], rel, MASKED)
    rel = rel.reshape(2, GROUPS, PLACES, 256)

    operands = {"x_hbm": inputs, "cot_hbm": cotangent, "code_hbm": code, "bias": rel}
    vectors = (norm1_gain, norm1_bias, proj_bias, norm2_gain, norm2_bias, fc2_bias, qv_bias, fc1_bias)
    sizes = [v.shape[1] for v in vectors]
    ends = np.cumsum([0] + sizes)
    if linked:
        pack = jnp.stack([jnp.pad(v, ((0, 0), (0, 256 - v.shape[1]))) for v in vectors], axis=1)
        operands |= gather(
            {
                "pack": pack.reshape(16, 256).astype(BF),
                "s_qkv": qkv_weight,
                "s_proj": proj_weight,
                "s_fc1": fc1_weight,
                "s_fc2": fc2_weight,
            }
        )
    else:

        def gathered(a):
            return lax.all_gather(a.astype(BF), "dp", axis=1, tiled=True)

        packed = lax.all_gather(jnp.concatenate(vectors, axis=1).astype(BF), "dp", axis=1)
        parts = [packed[:, :, a:b].reshape(2, -1).astype(F32) for a, b in zip(ends[:-1], ends[1:])]
        qv = parts[6]
        parts[6] = jnp.concatenate([qv[:, :D], jnp.zeros_like(qv[:, :D]), qv[:, D:]], axis=1)
        vec = jnp.stack([jnp.pad(p, ((0, 0), (0, FF - p.shape[1]))) for p in parts], axis=1)
        operands |= {
            "wat": jnp.concatenate([gathered(qkv_weight), gathered(proj_weight)], axis=2),
            "fc1": gathered(fc1_weight),
            "fc2": gathered(fc2_weight),
            "vec": vec.reshape(16, FF),
        }

    out = compute(linked, operands)

    def to_owners(g):
        shared = lax.psum_scatter(g, "dp", scatter_dimension=1, tiled=True)
        return lax.psum(shared, "pipe")

    if linked:
        small = out["o_small"]
        g_tab = jnp.concatenate([small[:, :, :8], small[:, :, 8:16]], axis=3).reshape(2, PLACES, GROUPS * 256)
        g_vec = jnp.concatenate([small[:, :, 16 + 8 * j : 24 + 8 * j] for j in range(4)], axis=3)
    else:
        g_tab, g_vec = out["g_tab"], out["g_vec"]

    g_vec = jnp.sum(g_vec.astype(F32), axis=2)
    kinds = [g_vec[:, i] for i in range(8)]
    qv_sum = jnp.concatenate([kinds[6][:, :D], kinds[6][:, 2 * D : 3 * D]], axis=1)
    rows = [kinds[0], kinds[1], kinds[2], kinds[3], kinds[4], kinds[5], qv_sum, kinds[7]]
    if linked:
        at = lax.axis_index("dp")
        small = [lax.dynamic_slice_in_dim(v, at * n, n, 1) for v, n in zip(rows, sizes)]
    else:
        rows = [v[:, : n * owners].reshape(2, -1, n) for v, n in zip(rows, sizes)]
        g_small = to_owners(jnp.concatenate(rows, axis=2))[:, 0]
        small = [g_small[:, a:b] for a, b in zip(ends[:-1], ends[1:])]

    pairs = g_tab.reshape(2, PLACES, HEADS, PLACES).transpose(0, 2, 1, 3)
    pairs = pairs.reshape(2, HEADS, PLACES * PLACES)
    g_table = lax.dot_general(
        jnp.broadcast_to(jnp.asarray(hot, pairs.dtype), (2,) + hot.shape),
        pairs,
        (((2,), (2,)), ((0,), (0,))),
        precision=None if linked else lax.Precision.HIGHEST,
        preferred_element_type=F32,
    )
    if linked:
        big = [out[name] for name in ("o_qkv", "o_proj", "o_fc1", "o_fc2")]
    else:
        g_table = lax.psum(g_table, ("pipe", "dp"))
        big = [to_owners(out[name]) for name in ("g_qkv", "g_proj", "g_fc1")]
        big.append(to_owners(out["g_fc2t"].transpose(0, 2, 1)))

    return (
        out["act_hbm"][None],
        out["igrad_hbm"][None],
        small[0],
        small[1],
        big[0],
        small[6],
        g_table,
        big[1],
        small[2],
        small[3],
        small[4],
        big[2],
        small[7],
        big[3],
        small[5],
    )


def solution(mesh):
    cols = P(None, "dp")
    rows = P(None, "dp", None)
    return jax.shard_map(
        body,
        mesh=mesh,
        in_specs=(
            P(None, "dp", None, None),
            P(None, "dp", None, None),
            rows,
            rows,
            cols,
            cols,
            rows,
            cols,
            P(),
            rows,
            cols,
            cols,
            cols,
            rows,
            cols,
            rows,
            cols,
        ),
        out_specs=(
            P("pipe", None, "dp", None, None),
            P("pipe", None, "dp", None, None),
            cols,
            cols,
            rows,
            cols,
            P(),
            rows,
            cols,
            cols,
            cols,
            rows,
            cols,
            rows,
            cols,
        ),
        check_vma=False,
    )
```

```python
import functools
import types

import jax
import jax.numpy as jnp
import numpy as np
from jax import lax
from jax.experimental import pallas as pl
from jax.experimental.pallas import tpu as pltpu
from jax.sharding import PartitionSpec as P

HEADS = 12
WIN = 7
SHIFT = 3
GRID = 28
CELLS = 784
D = 384
FF = 1536
HEAD = 32
SIDE = 4
WINDOWS = 16
PLACES = 64
WROWS = WINDOWS * PLACES
GROUPS = 3
TILE = 112
SCALE = HEAD**-0.5
NORM_EPS = 1e-05
MASKED = -1e30
BF = jnp.bfloat16
F32 = jnp.float32

ERF_P = 0.3275911 / np.sqrt(2.0)
ERF_A = [0.5 * a for a in (0.254829592, -0.284496736, 1.421413741, -1.453152027, 1.061405429)]
PHI_0 = 1.0 / np.sqrt(2.0 * np.pi)


def nn(a, b):
    return lax.dot_general(a, b, (((1,), (0,)), ((), ())), preferred_element_type=F32)


def nt(a, b):
    return lax.dot_general(a, b, (((1,), (1,)), ((), ())), preferred_element_type=F32)


def tn(a, b):
    return lax.dot_general(a, b, (((0,), (0,)), ((), ())), preferred_element_type=F32)


def segments(shift):
    runs = []
    for wr in range(SIDE):
        for r in range(WIN):
            row = (wr * WIN + r + shift) % GRID
            for wc in range(SIDE):
                col = (wc * WIN + shift) % GRID
                place = (wr * SIDE + wc) * PLACES + r * 8
                first = min(WIN, GRID - col)
                runs.append((row * GRID + col, place, first))
                if first < WIN:
                    runs.append((row * GRID, place + first, WIN - first))
    return runs


def to_windows(src, dst, shift):
    for cell, place, count in segments(shift):
        dst[pl.ds(place, count), :] = src[pl.ds(cell, count), :]


def to_canvas(src, dst, shift):
    for cell, place, count in segments(shift):
        dst[pl.ds(cell, count), :] = src[pl.ds(place, count), :]


def row_block(t, size):
    return pl.ds(pl.multiple_of(t * size, 16), size)


def standardized(v):
    centered = v - jnp.mean(v, axis=-1, keepdims=True)
    spread = jnp.mean(centered * centered, axis=-1, keepdims=True)
    rs = lax.rsqrt(spread + NORM_EPS)
    return centered * rs, rs


def by_eights(v):
    return jnp.sum(v.reshape(v.shape[0] // 8, 8, v.shape[1]), axis=0)


def gelu_parts(x):
    den = 1.0 + ERF_P * jnp.abs(x)
    t = pl.reciprocal(den, approx=True)
    t = t * (2.0 - den * t)
    e = jnp.exp(-0.5 * x * x)
    poly = ERF_A[4]
    for a in ERF_A[3::-1]:
        poly = poly * t + a
    tail = poly * t * e
    cdf = jnp.where(x >= 0.0, 1.0 - tail, tail)
    return x * cdf, cdf + x * (e * PHI_0)


def real_places(rows):
    place = lax.broadcasted_iota(jnp.int32, (rows, 1), 0)
    return ((place & 7) < WIN) & (((place >> 3) & 7) < WIN)


def head_of_lane():
    return lax.broadcasted_iota(jnp.int32, (PLACES, 128), 1) >> 5


def by_head(x, lanes):
    zero = jnp.zeros_like(x)
    return jnp.concatenate([jnp.where(lanes == h, x, zero) for h in range(4)], axis=0)


def own_head(wide, lanes):
    out = wide[3 * PLACES :]
    for h in (2, 1, 0):
        out = jnp.where(lanes == h, wide[h * PLACES : (h + 1) * PLACES], out)
    return out


MESH = pl.DeviceIdType.MESH
ATT_ROWS = 256
MLP_ROWS = 384
SMALL = 192


def gather_kernel(names, *refs):
    r = types.SimpleNamespace(**dict(zip(names, refs)))
    me = lax.axis_index("pipe")
    wat, fc1, fc2, vec = r.wat, r.fc1, r.fc2, r.vec
    d = lax.axis_index("dp")
    z, c = d // 2, d % 2
    sibling = {"dp": 2 * z + 1 - c}

    def z_peer(k):
        return {"dp": 2 * lax.rem(z + k, 4) + c}

    def pipe_peer(k):
        return {"pipe": lax.rem(me + k, 4)}

    def dp_peer(k):
        return {"dp": lax.rem(d + k, 8)}

    def remote(src, dst, send, recv, device):
        return pltpu.make_async_remote_copy(
            src_ref=src, dst_ref=dst, send_sem=send, recv_sem=recv, device_id=device, device_id_type=MESH
        )

    barrier = pltpu.get_barrier_semaphore()
    partners = [pipe_peer(k) for k in range(1, 4)] + [dp_peer(k) for k in range(1, 8)]
    for partner in partners:
        pl.semaphore_signal(barrier, inc=1, device_id=partner, device_id_type=MESH)

    full = ((wat,), (fc1, fc2), (wat,), (fc1, fc2))

    def owner_back(k):
        return 2 * lax.rem(z + 4 - k, 4) + c

    def shard(sec, a, owner):
        h = 192 if a else 48
        return full[sec][a].at[sec // 2, pl.ds(pl.multiple_of(owner * h, 16), h), :]

    def part(sec, a, owner, place):
        if a:
            return fc2.at[sec // 2, pl.ds(pl.multiple_of(owner * 192 + place * 48, 16), 48), :]
        rows = pl.ds(pl.multiple_of(owner * 48, 16), 48)
        return full[sec][0].at[sec // 2, rows, pl.ds(pl.multiple_of(place * D, 128), D)]

    def to_z(sec, a, k):
        own = part(sec, a, d, me)
        return remote(own, own, r.wz_send.at[sec, a, k - 1], r.wz_recv.at[sec, a, k - 1], z_peer(k))

    def to_places(sec, a, k, j):
        got = part(sec, a, owner_back(k), me)
        return remote(
            got, got, r.wx_send.at[sec, a, k - 1, j - 1], r.wx_recv.at[sec, a, k - 1, j - 1], pipe_peer(j)
        )

    def to_sibling(sec, a, k):
        block = shard(sec, a, owner_back(k))
        return remote(block, block, r.ws_send.at[sec, a, k], r.ws_recv.at[sec, a, k], sibling)

    def weights_1(sec):
        for a in range(len(full[sec])):
            for k in range(1, 4):
                to_z(sec, a, k).start()
            to_sibling(sec, a, 0).start()

    def weights_2(sec):
        for k in range(1, 4):
            for a in range(len(full[sec])):
                got = part(sec, a, owner_back(k), me)
                remote(got, got, r.wz_send.at[sec, a, k - 1], r.wz_recv.at[sec, a, k - 1], z_peer(k)).wait_recv()
                for j in range(1, 4):
                    to_places(sec, a, k, j).start()

    def weights_3(sec):
        for k in range(1, 4):
            for a in range(len(full[sec])):
                for j in range(1, 4):
                    got = part(sec, a, owner_back(k), lax.rem(me + 4 - j, 4))
                    remote(
                        got, got, r.wx_send.at[sec, a, k - 1, j - 1], r.wx_recv.at[sec, a, k - 1, j - 1], pipe_peer(j)
                    ).wait_recv()
                to_sibling(sec, a, k).start()

    def weights_4(sec):
        for k in range(4):
            for a in range(len(full[sec])):
                block = shard(sec, a, 2 * lax.rem(z + 4 - k, 4) + 1 - c)
                remote(block, block, r.ws_send.at[sec, a, k], r.ws_recv.at[sec, a, k], sibling).wait_recv()

    def weights_sent():
        for sec in range(4):
            for a in range(len(full[sec])):
                for k in range(4):
                    to_sibling(sec, a, k).wait_send()
                    if k:
                        to_z(sec, a, k).wait_send()
                        for j in range(1, 4):
                            to_places(sec, a, k, j).wait_send()

    def pack_copy(k):
        return remote(
            r.packs.at[d], r.packs.at[d], r.pk_send.at[k - 1], r.pk_recv.at[k - 1], dp_peer(k)
        )

    def pack_arrival(k):
        slot = r.packs.at[lax.rem(d + 8 - k, 8)]
        return remote(slot, slot, r.pk_send.at[k - 1], r.pk_recv.at[k - 1], dp_peer(k))

    def place_vectors():
        kind = lax.broadcasted_iota(jnp.int32, (16, 256), 0) & 7
        lane = lax.broadcasted_iota(jnp.int32, (16, 256), 1)
        vec[...] = jnp.zeros_like(vec)
        for width, kinds in ((48, kind < 6), (96, kind == 6), (192, kind == 7)):
            for owner in range(8):
                at = owner * width
                if width == 96 and owner >= 4:
                    at += D
                start = at // 128 * 128
                part = jnp.where(kinds & (lane < width), r.packs[owner].astype(F32), 0.0)
                if at > start:
                    part = pltpu.roll(part, at - start, 1)
                vec[:, start : start + 256] += part

    lands = ((r.s_qkv, 48, wat, 0), (r.s_proj, 48, wat, 3 * D), (r.s_fc1, 48, fc1, 0), (r.s_fc2, 192, fc2, 0))
    r.packs[d] = r.pack[...]
    for src, h, ref, col in lands:
        for b in range(2):
            for t in range(h // 48):
                rows = pl.ds(pl.multiple_of(d * h + t * 48, 16), 48)
                ref[b, rows, col : col + src.shape[2]] = src[b, t * 48 : (t + 1) * 48, :].astype(BF)
    pl.semaphore_wait(barrier, len(partners))
    for k in range(1, 8):
        pack_copy(k).start()
    for step in (weights_1, weights_2, weights_3, weights_4):
        for sec in range(4):
            step(sec)
    for k in range(1, 8):
        pack_arrival(k).wait_recv()
    place_vectors()
    weights_sent()
    for k in range(1, 8):
        pack_copy(k).wait_send()


def gather(operands):
    shape = jax.ShapeDtypeStruct
    vmem = pl.BlockSpec(memory_space=pltpu.VMEM)
    dma = pltpu.SemaphoreType.DMA
    outs = {
        "wat": ((2, D, 4 * D), BF),
        "fc1": ((2, D, FF), BF),
        "fc2": ((2, FF, D), BF),
        "vec": ((16, FF), F32),
    }
    sems = {
        "wz_send": (4, 2, 3),
        "wz_recv": (4, 2, 3),
        "wx_send": (4, 2, 3, 3),
        "wx_recv": (4, 2, 3, 3),
        "ws_send": (4, 2, 4),
        "ws_recv": (4, 2, 4),
        "pk_send": (7,),
        "pk_recv": (7,),
    }
    names = tuple(operands) + tuple(outs) + ("packs",) + tuple(sems)
    results = pl.pallas_call(
        functools.partial(gather_kernel, names),
        out_shape=tuple(shape(*o) for o in outs.values()),
        in_specs=[vmem] * len(operands),
        out_specs=(vmem,) * len(outs),
        scratch_shapes=[pltpu.VMEM((8, 16, 256), BF)] + [dma(v) for v in sems.values()],
        compiler_params=pltpu.CompilerParams(
            vmem_limit_bytes=32 * 1024 * 1024, collective_id=1, has_side_effects=True
        ),
    )(*operands.values())
    return dict(zip(outs, results))


def reduce_kernel(names, *refs):
    r = types.SimpleNamespace(**dict(zip(names, refs)))
    me = lax.axis_index("pipe")
    g_qkv, g_proj, g_fc1, g_fc2t, g_vec, g_tab = r.g_qkv, r.g_proj, r.g_fc1, r.g_fc2t, r.g_vec, r.g_tab
    d = lax.axis_index("dp")
    z, c = d // 2, d % 2
    sibling = {"dp": 2 * z + 1 - c}

    def z_peer(k):
        return {"dp": 2 * lax.rem(z + k, 4) + c}

    def pipe_peer(k):
        return {"pipe": lax.rem(me + k, 4)}

    def dp_peer(k):
        return {"dp": lax.rem(d + k, 8)}

    def remote(src, dst, send, recv, device):
        return pltpu.make_async_remote_copy(
            src_ref=src, dst_ref=dst, send_sem=send, recv_sem=recv, device_id=device, device_id_type=MESH
        )

    barrier = pltpu.get_barrier_semaphore()
    partners = [pipe_peer(k) for k in range(1, 4)] + [dp_peer(k) for k in range(1, 8)]
    for partner in partners:
        pl.semaphore_signal(barrier, inc=1, device_id=partner, device_id_type=MESH)

    def pieces(sec, owner):
        b = sec // 2
        out = []

        def matrix(ref, h):
            for t in range(h // 48):
                rows = pl.ds(pl.multiple_of(owner * h + t * 48, 16), 48)
                for j in range(ref.shape[2] // D):
                    load = functools.partial(lambda ref, rows, j: ref[b, rows, j * D : (j + 1) * D], ref, rows, j)
                    out.append((len(out) * 48, 48, load))

        def small():
            rows = pl.ds(pl.multiple_of(owner * 8, 8), 8)
            parts = [g_tab[b, rows, j * D : (j + 1) * D] for j in range(2)]
            parts += [g_vec[b, owner, :, j * D : (j + 1) * D] for j in range(4)]
            return jnp.concatenate(parts + [jnp.zeros((16, D), F32)], axis=0)

        if sec % 2:
            matrix(g_fc1, 48)
        else:
            matrix(g_qkv, 48)
            matrix(g_proj, 48)
            out.append((SMALL, 64, small))
        return out

    def reduce_refs(sec):
        return types.SimpleNamespace(
            **{n: getattr(r, f"s{sec}_{n}") for n in ("st_a", "rc_a", "st_b", "rc_b", "st_c", "rc_c", "fin")}
        )

    def step_1(sec):
        q = reduce_refs(sec)
        for k in range(4):
            i = lax.rem(z + k, 4)
            kept = q.st_b.at[k - 1] if k else q.st_c
            for row, rows, load in pieces(sec, 2 * i + 1 - c):
                q.st_a[i, row : row + rows, :] = load().astype(BF)
            for row, rows, load in pieces(sec, 2 * i + c):
                kept[row : row + rows, :] = load().astype(BF)
            if sec % 2:
                r.turned[...] = g_fc2t[sec // 2, :, pl.ds(pl.multiple_of(i * D, 128), D)].T
                for t in range(0, 192, 48):
                    at = slice(192 + t, 240 + t)
                    q.st_a[i, at, :] = r.turned[pl.ds(pl.multiple_of((1 - c) * 192 + t, 16), 48), :].astype(BF)
                    kept[at, :] = r.turned[pl.ds(pl.multiple_of(c * 192 + t, 16), 48), :].astype(BF)

    def copy_a(sec):
        q = reduce_refs(sec)
        return remote(q.st_a, q.rc_a, r.ra_send.at[sec], r.ra_recv.at[sec], sibling)

    def copy_b(sec, k):
        q = reduce_refs(sec)
        return remote(
            q.st_b.at[k - 1], q.rc_b.at[k - 1], r.rb_send.at[sec, k - 1], r.rb_recv.at[sec, k - 1], z_peer(k)
        )

    def step_2(sec):
        q = reduce_refs(sec)
        copy_a(sec).wait_recv()
        for k in (1, 2, 3, 0):
            i = lax.rem(z + k, 4)
            kept = q.st_b.at[k - 1] if k else q.st_c
            for row in range(0, kept.shape[0], 64):
                at = slice(row, row + 64)
                kept[at, :] = (kept[at, :].astype(F32) + q.rc_a[i, at, :].astype(F32)).astype(BF)
            if k:
                copy_b(sec, k).start()

    def quarter(sec, ref, who):
        rows = (MLP_ROWS if sec % 2 else ATT_ROWS) // 4
        return ref.at[pl.ds(pl.multiple_of(who * rows, 16), rows), :]

    def copy_c(sec, k):
        q = reduce_refs(sec)
        return remote(
            quarter(sec, q.st_c, lax.rem(me + k, 4)),
            q.rc_c.at[k - 1],
            r.rc_send.at[sec, k - 1],
            r.rc_recv.at[sec, k - 1],
            pipe_peer(k),
        )

    def step_3(sec):
        q = reduce_refs(sec)
        for k in range(1, 4):
            copy_b(sec, k).wait_recv()
        for row in range(0, q.st_c.shape[0], 64):
            at = slice(row, row + 64)
            total = q.st_c[at, :].astype(F32)
            for k in range(3):
                total = total + q.rc_b[k, at, :].astype(F32)
            q.st_c[at, :] = total.astype(BF)
        for k in range(1, 4):
            copy_c(sec, k).start()

    def copy_f(sec, k):
        q = reduce_refs(sec)
        own = quarter(sec, q.fin, me)
        return remote(own, own, r.rf_send.at[sec, k - 1], r.rf_recv.at[sec, k - 1], pipe_peer(k))

    def step_4(sec):
        q = reduce_refs(sec)
        for k in range(1, 4):
            copy_c(sec, k).wait_recv()
        total = quarter(sec, q.st_c, me)[...].astype(F32)
        for k in range(3):
            total = total + q.rc_c[k].astype(F32)
        quarter(sec, q.fin, me)[...] = total.astype(BF)
        for k in range(1, 4):
            copy_f(sec, k).start()

    def copy_s(b, k):
        rows = pl.ds(SMALL, 64)
        return remote(
            getattr(r, f"s{2 * b}_fin").at[rows, :], r.o_small.at[b, d], r.rs_send.at[b, k - 1], r.rs_recv.at[b, k - 1], dp_peer(k)
        )

    def own_small(b):
        return pltpu.make_async_copy(getattr(r, f"s{2 * b}_fin").at[pl.ds(SMALL, 64), :], r.o_small.at[b, d], r.os_sem.at[b])

    def step_5(sec):
        q = reduce_refs(sec)
        b = sec // 2
        for k in range(1, 4):
            got = quarter(sec, q.fin, lax.rem(me + 4 - k, 4))
            remote(got, got, r.rf_send.at[sec, k - 1], r.rf_recv.at[sec, k - 1], pipe_peer(k)).wait_recv()
        if sec % 2 == 0:
            for k in range(1, 8):
                copy_s(b, k).start()
            own_small(b).start()
        row = 0
        for ref, h, n in ((r.o_fc1, 48, 4), (r.o_fc2, 192, 1)) if sec % 2 else ((r.o_qkv, 48, 3), (r.o_proj, 48, 1)):
            for t in range(h // 48):
                for j in range(n):
                    ref[b, t * 48 : (t + 1) * 48, j * D : (j + 1) * D] = q.fin[row : row + 48, :].astype(F32)
                    row += 48

    def smalls_sent(b):
        for k in range(1, 8):
            copy_s(b, k).wait_send()
        own_small(b).wait()

    order = (3, 1, 2, 0)
    for sec in order:
        step_1(sec)
        if sec == 3:
            pl.semaphore_wait(barrier, len(partners))
        copy_a(sec).start()
    for step in (step_2, step_3, step_4, step_5):
        for sec in order:
            step(sec)
    for sec in order:
        copy_a(sec).wait_send()
        for k in range(1, 4):
            copy_b(sec, k).wait_send()
            copy_c(sec, k).wait_send()
            copy_f(sec, k).wait_send()
    for b in range(2):
        smalls_sent(b)
        for k in range(1, 8):
            slot = r.o_small.at[b, lax.rem(d + 8 - k, 8)]
            remote(slot, slot, r.rs_send.at[b, k - 1], r.rs_recv.at[b, k - 1], dp_peer(k)).wait_recv()


def reduce(operands):
    shape = jax.ShapeDtypeStruct
    vmem = pl.BlockSpec(memory_space=pltpu.VMEM)
    dma = pltpu.SemaphoreType.DMA
    outs = {
        "o_qkv": ((2, 48, 3 * D), F32),
        "o_proj": ((2, 48, D), F32),
        "o_fc1": ((2, 48, FF), F32),
        "o_fc2": ((2, 192, D), F32),
        "o_small": ((2, 8, 64, D), BF),
    }
    scratch = {"turned": ((D, D), F32)}
    for sec in range(4):
        rows = MLP_ROWS if sec % 2 else ATT_ROWS
        kind = f"s{sec}_"
        scratch |= {
            kind + "st_a": ((4, rows, D), BF),
            kind + "rc_a": ((4, rows, D), BF),
            kind + "st_b": ((3, rows, D), BF),
            kind + "rc_b": ((3, rows, D), BF),
            kind + "st_c": ((rows, D), BF),
            kind + "rc_c": ((3, rows // 4, D), BF),
            kind + "fin": ((rows, D), BF),
        }
    sems = {
        "os_sem": (2,),
        "ra_send": (4,),
        "ra_recv": (4,),
        "rb_send": (4, 3),
        "rb_recv": (4, 3),
        "rc_send": (4, 3),
        "rc_recv": (4, 3),
        "rf_send": (4, 3),
        "rf_recv": (4, 3),
        "rs_send": (2, 7),
        "rs_recv": (2, 7),
    }
    names = tuple(operands) + tuple(outs) + tuple(scratch) + tuple(sems)
    results = pl.pallas_call(
        functools.partial(reduce_kernel, names),
        out_shape=tuple(shape(*o) for o in outs.values()),
        in_specs=[vmem] * len(operands),
        out_specs=(vmem,) * len(outs),
        scratch_shapes=[pltpu.VMEM(*v) for v in scratch.values()] + [dma(v) for v in sems.values()],
        compiler_params=pltpu.CompilerParams(
            vmem_limit_bytes=48 * 1024 * 1024, collective_id=2, has_side_effects=True
        ),
    )(*operands.values())
    return dict(zip(outs, results))


def kernel(names, linked, canvases, *refs):
    r = types.SimpleNamespace(**dict(zip(names, refs)))
    me = lax.axis_index("pipe")
    xin, cot, code, codew, buf = r.xin, r.cot, r.code, r.codew, r.buf
    hqw, qkv, probs, att = r.hqw, r.qkv, r.probs, r.att
    hq2, hid, dgelu = r.hq2, r.hid, r.dgelu
    canvf, winf, gzw, wide_t, gqkv, go = r.canvf, r.winf, r.gzw, r.wide_t, r.gqkv, r.go
    g_qkv, g_proj, g_fc1, g_fc2t, g_vec, g_tab = r.g_qkv, r.g_proj, r.g_fc1, r.g_fc2t, r.g_vec, r.g_tab
    wat, fc1, fc2, vec, bias = r.wat, r.fc1, r.fc2, r.vec, r.bias
    if linked:
        d = lax.axis_index("dp")
        z, c = d // 2, d % 2
        sibling = {"dp": 2 * z + 1 - c}

    def z_peer(k):
        return {"dp": 2 * lax.rem(z + k, 4) + c}

    def pipe_peer(k):
        return {"pipe": lax.rem(me + k, 4)}

    def dp_peer(k):
        return {"dp": lax.rem(d + k, 8)}

    def remote(src, dst, send, recv, device):
        return pltpu.make_async_remote_copy(
            src_ref=src, dst_ref=dst, send_sem=send, recv_sem=recv, device_id=device, device_id_type=MESH
        )

    barrier = pltpu.get_barrier_semaphore()
    partners = [pipe_peer(k) for k in range(1, 4)]
    if linked:
        partners += [dp_peer(k) for k in range(1, 8)]
    for partner in partners:
        pl.semaphore_signal(barrier, inc=1, device_id=partner, device_id_type=MESH)

    pl.semaphore_wait(barrier, len(partners))

    for ref in (g_qkv, g_proj, g_fc1, g_fc2t):
        for b in range(2):

            @pl.loop(0, ref.shape[1] // 16)
            def _(i):
                ref[b, row_block(i, 16), :] = jnp.zeros((16, ref.shape[2]), F32)

    g_vec[...] = jnp.zeros_like(g_vec)
    g_tab[...] = jnp.zeros_like(g_tab)
    codew[...] = jnp.zeros_like(codew)

    def vector(b, kind, width=D):
        return vec[b * 8 + kind : b * 8 + kind + 1, :width]

    def add_vec(b, kind, part):
        g_vec[b, kind, :, : part.shape[1]] += part

    def windowed(rows, count):
        return jnp.where(real_places(count), winf[rows, :], 0.0).astype(BF)

    def by_two(start, stop, step):
        @pl.loop(start // 2, stop // 2)
        def _(i):
            step((2 * i, 2 * i + 1))

    def attention_forward(b, x, out, free_out, hook):
        lanes = head_of_lane()

        @pl.loop(0, CELLS // TILE)
        def _(t):
            rows = row_block(t, TILE)
            xhat, _ = standardized(x[rows, :].astype(F32))
            canvf[rows, :] = xhat * vector(b, 0) + vector(b, 1)

        to_windows(canvf, winf, SHIFT * b)
        to_windows(code, codew, SHIFT * b)

        @pl.loop(0, 4)
        def _(t):
            rows = row_block(t, 256)
            hq = windowed(rows, 256)
            hqw[b, rows, :] = hq
            for part in range(3):
                cols = slice(part * D, (part + 1) * D)
                acc = nn(hq, wat[b, :, cols]) + vec[b * 8 + 6 : b * 8 + 7, cols]
                if part == 0:
                    acc = acc * SCALE
                qkv[b, rows, cols] = acc.astype(BF)

        hook(0)

        def windows(pair):
            blocks = [row_block(w, PLACES) for w in pair]
            masks = []
            for rows in blocks:
                cells = codew[rows, :]
                region = (cells >> 1) * b
                pad = (cells & 1).astype(F32)
                lane = lax.broadcasted_iota(jnp.int32, (PLACES, 128), 1)
                same = jnp.where(lane == region, 1.0, 0.0)
                left = jnp.where(lane == 127, 1.0 - pad, same).astype(BF)
                right = jnp.where(lane == 127, -pad, same).astype(BF)
                agree = nt(left, jnp.concatenate([right, right], axis=0))
                mask = jnp.where(agree > 0.5, 0.0, MASKED)
                masks.append(jnp.concatenate([mask, mask], axis=1))
            for g in range(GROUPS):
                for w, rows, mask in zip(pair, blocks, masks):
                    q = qkv[b, rows, g * 128 : (g + 1) * 128]
                    k = qkv[b, rows, D + g * 128 : D + (g + 1) * 128]
                    v = qkv[b, rows, 2 * D + g * 128 : 2 * D + (g + 1) * 128]
                    s = nt(k, by_head(q, lanes)) + bias[b, g] + mask
                    e = jnp.exp(s - jnp.max(s, axis=0, keepdims=True))
                    p = (e * (1.0 / jnp.sum(e, axis=0, keepdims=True))).astype(BF)
                    probs[b, w * GROUPS + g] = p
                    att[b, rows, g * 128 : (g + 1) * 128] = own_head(tn(p, v), lanes).astype(BF)

        by_two(0, WINDOWS // 2, windows)
        hook(1)
        by_two(WINDOWS // 2, WINDOWS, windows)
        hook(2)

        @pl.loop(0, 4)
        def _(t):
            rows = row_block(t, 256)
            winf[rows, :] = nn(att[b, rows, :], wat[b, :, 3 * D :])

        to_canvas(winf, canvf, SHIFT * b)
        free_out()

        @pl.loop(0, CELLS // TILE)
        def _(t):
            rows = row_block(t, TILE)
            out[rows, :] = (x[rows, :].astype(F32) + (canvf[rows, :] + vector(b, 2))).astype(BF)

    def mlp_forward(b, x, out, free_out, hook):
        @pl.loop(0, CELLS // TILE)
        def _(t):
            rows = row_block(t, TILE)
            xhat, _ = standardized(x[rows, :].astype(F32))
            hq2[b, rows, :] = (xhat * vector(b, 3) + vector(b, 4)).astype(BF)

        def chunk(i):
            cols = pl.ds(pl.multiple_of(i * 256, 256), 256)
            pre = nn(hq2[b], fc1[b, :, cols]) + vec[b * 8 + 7 : b * 8 + 8, cols]
            for at in range(0, CELLS, 16):
                h, dg = gelu_parts(pre[at : at + 16])
                hid[b, at : at + 16, cols] = h.astype(BF)
                dgelu[b, at : at + 16, cols] = dg.astype(BF)

        pl.loop(0, FF // 512)(chunk)
        hook(0)
        pl.loop(FF // 512, FF // 256)(chunk)

        free_out()
        total = nn(hid[b], fc2[b])
        for at in range(0, CELLS, TILE):
            rows = slice(at, at + TILE)
            out[rows, :] = (x[rows, :].astype(F32) + (total[rows] + vector(b, 5))).astype(BF)

    def norm_backward(b, kind, x, gz, out):
        @pl.loop(0, CELLS // TILE)
        def _(t):
            rows = row_block(t, TILE)
            xhat, rs = standardized(x[rows, :].astype(F32))
            gn = canvf[rows, :]
            gzf = gz[rows, :].astype(F32)
            add_vec(b, kind, by_eights(gn * xhat))
            add_vec(b, kind + 1, by_eights(gn))
            add_vec(b, 5 if kind else 2, by_eights(gzf))
            g = gn * vector(b, kind)
            mg = jnp.mean(g, axis=-1, keepdims=True)
            mgx = jnp.mean(g * xhat, axis=-1, keepdims=True)
            out[rows, :] = (gzf + rs * (g - mg - xhat * mgx)).astype(BF)

    def mlp_backward(b, x, gz, out, free_out, hook):
        hook(0)
        wide_t[0, :, :CELLS] = hq2[b].T
        wide_t[1, :, :CELLS] = gz[...].T

        def chunk(i):
            cols = pl.ds(pl.multiple_of(i * 256, 256), 256)
            gh = nt(gz[...], fc2[b, cols, :])
            sums = jnp.zeros((8, 256), F32)
            for at in range(0, CELLS, 16):
                gp = (gh[at : at + 16] * dgelu[b, at : at + 16, cols].astype(F32)).astype(BF)
                dgelu[b, at : at + 16, cols] = gp
                sums = sums + by_eights(gp.astype(F32))
            g_vec[b, 7, :, cols] += sums
            g_fc1[b, :, cols] += nn(wide_t[0, :, :CELLS], dgelu[b, :, cols])
            g_fc2t[b, :, cols] += nn(wide_t[1, :, :CELLS], hid[b, :, cols])

        pl.loop(0, FF // 512)(chunk)
        hook(1)
        pl.loop(FF // 512, FF // 256)(chunk)
        hook(2)
        canvf[...] = nt(dgelu[b], fc1[b])
        hook(3)
        free_out()
        norm_backward(b, 3, x, gz, out)
        hook(4)

    def attention_backward(b, x, gz, out, free_out, hook):
        lanes = head_of_lane()
        hook(0)

        @pl.loop(0, CELLS // TILE)
        def _(t):
            rows = row_block(t, TILE)
            canvf[rows, :] = gz[rows, :].astype(F32)

        to_windows(canvf, winf, SHIFT * b)

        @pl.loop(0, 4)
        def _(t):
            rows = row_block(t, 256)
            gzw[rows, :] = windowed(rows, 256)

        g_proj[b] += tn(att[b], gzw[...])

        @pl.loop(0, 4)
        def _(t):
            rows = row_block(t, 256)
            go[rows, :] = nt(gzw[rows, :], wat[b, :, 3 * D :]).astype(BF)

        hook(1)

        def windows(pair):
            blocks = [row_block(w, PLACES) for w in pair]
            for g in range(GROUPS):
                at = [slice(part * D + g * 128, part * D + (g + 1) * 128) for part in range(3)]
                table = jnp.zeros((PLACES, 256), F32)
                for w, rows in zip(pair, blocks):
                    q, k, v = (qkv[b, rows, cols] for cols in at)
                    go_wide = by_head(go[rows, at[0]], lanes)
                    p_low = probs[b, w * GROUPS + g]
                    p = p_low.astype(F32)
                    pd = p * nt(v, go_wide)
                    ds = (pd - p * jnp.sum(pd, axis=0, keepdims=True)).astype(BF)
                    table = table + ds.astype(F32)
                    gqkv[rows, at[0]] = (own_head(tn(ds, k), lanes) * SCALE).astype(BF)
                    gqkv[rows, at[1]] = nn(ds, by_head(q, lanes)).astype(BF)
                    gqkv[rows, at[2]] = nn(p_low, go_wide).astype(BF)
                g_tab[b, :, g * 256 : (g + 1) * 256] += table

        by_two(0, WINDOWS // 2, windows)
        hook(2)
        by_two(WINDOWS // 2, WINDOWS, windows)
        hook(3)

        @pl.loop(0, 4)
        def _(t):
            rows = row_block(t, 256)
            gq = gqkv[rows, :]
            add_vec(b, 6, by_eights(gq.astype(F32)))
            winf[rows, :] = nt(gq, wat[b, :, : 3 * D])

        to_canvas(winf, canvf, SHIFT * b)
        free_out()
        norm_backward(b, 0, x, gz, out)

    def attention_weights(b):
        wide_t[0] = hqw[b].T
        for part in range(3):
            cols = slice(part * D, (part + 1) * D)
            g_qkv[b, :, cols] += nn(wide_t[0], gqkv[:, cols])

    def push(kind, s, n, start):
        src = buf.at[s]
        dst = (r.act_hbm, r.igrad_hbm)[kind].at[me, n]
        local = pltpu.make_async_copy(src, dst, r.local_sem.at[kind, n])
        away = remote(src, dst, r.send_sem.at[kind, s, n], r.recv_sem.at[kind, me, n], {"pipe": s})

        @pl.when(me == s)
        def _():
            local.start() if start else local.wait()

        @pl.when(me != s)
        def _():
            away.start() if start else away.wait_send()

    def arrived(kind, k, n):
        sender = lax.rem(me + k, 4)
        dst = (r.act_hbm, r.igrad_hbm)[kind].at[sender, n]
        remote(
            buf.at[0], dst, r.send_sem.at[kind, 0, n], r.recv_sem.at[kind, sender, n], {"pipe": sender}
        ).wait_recv()

    @pl.loop(0, canvases)
    def _(n):
        def hook(sec, i):
            pass

        loads = [
            pltpu.make_async_copy(r.x_hbm.at[me, n], xin, r.in_sem.at[0]),
            pltpu.make_async_copy(r.cot_hbm.at[me, n], cot, r.in_sem.at[1]),
            pltpu.make_async_copy(r.code_hbm.at[n], code, r.in_sem.at[2]),
        ]
        for load in loads:
            load.start()
        for load in loads:
            load.wait()

        x = xin
        for s in range(4):
            def free_out():
                @pl.when(n > 0)
                def _():
                    push(1, s, n - 1, False)

            forward = mlp_forward if s % 2 else attention_forward
            forward(s // 2, x, buf.at[s], free_out, lambda i: None)
            x = buf.at[s]
            push(0, s, n, True)
        gz = cot
        for s in (3, 2, 1, 0):
            x = buf.at[s - 1] if s else xin
            backward = mlp_backward if s % 2 else attention_backward
            backward(
                s // 2, x, gz, buf.at[s], functools.partial(push, 0, s, n, False), functools.partial(hook, s)
            )
            gz = buf.at[s]
            push(1, s, n, True)
            if s % 2 == 0:
                attention_weights(s // 2)
                hook(s, 4)

    for kind in range(2):
        for k in range(1, 4):
            for n in range(canvases):
                arrived(kind, k, n)
    for s in range(4):
        push(1, s, canvases - 1, False)


def compute(linked, operands):
    canvases = operands["x_hbm"].shape[1]
    shape = jax.ShapeDtypeStruct
    hbm = pl.BlockSpec(memory_space=pl.ANY)
    vmem = pl.BlockSpec(memory_space=pltpu.VMEM)
    dma = pltpu.SemaphoreType.DMA
    full = {
        "wat": ((2, D, 4 * D), BF),
        "fc1": ((2, D, FF), BF),
        "fc2": ((2, FF, D), BF),
        "vec": ((16, FF), F32),
    }
    grads = {
        "g_qkv": ((2, D, 3 * D), F32),
        "g_proj": ((2, D, D), F32),
        "g_fc1": ((2, D, FF), F32),
        "g_fc2t": ((2, D, FF), F32),
        "g_vec": ((2, 8, 8, FF), F32),
        "g_tab": ((2, PLACES, GROUPS * 256), F32),
    }
    outs = {"act_hbm": ((4, canvases, CELLS, D), BF), "igrad_hbm": ((4, canvases, CELLS, D), BF)}
    scratch = {
        "xin": ((CELLS, D), BF),
        "cot": ((CELLS, D), BF),
        "code": ((CELLS, 128), jnp.int32),
        "codew": ((WROWS, 128), jnp.int32),
        "buf": ((4, CELLS, D), BF),
        "hqw": ((2, WROWS, D), BF),
        "qkv": ((2, WROWS, 3 * D), BF),
        "probs": ((2, WINDOWS * GROUPS, PLACES, 256), BF),
        "att": ((2, WROWS, D), BF),
        "hq2": ((2, CELLS, D), BF),
        "hid": ((2, CELLS, FF), BF),
        "dgelu": ((2, CELLS, FF), BF),
        "canvf": ((CELLS, D), F32),
        "winf": ((WROWS, D), F32),
        "gzw": ((WROWS, D), BF),
        "go": ((WROWS, D), BF),
        "gqkv": ((WROWS, 3 * D), BF),
        "wide_t": ((2, D, WROWS), BF),
    }
    sems = {
        "in_sem": (3,),
        "local_sem": (2, canvases),
        "send_sem": (2, 4, canvases),
        "recv_sem": (2, 4, canvases),
    }
    if linked:
        outs |= {
            "o_qkv": ((2, 48, 3 * D), F32),
            "o_proj": ((2, 48, D), F32),
            "o_fc1": ((2, 48, FF), F32),
            "o_fc2": ((2, 192, D), F32),
            "o_small": ((2, 8, 64, D), BF),
        }
        scratch |= grads
        for kind, rows in (("m_", MLP_ROWS), ("a_", ATT_ROWS)):
            scratch |= {
                kind + "st_a": ((4, rows, D), BF),
                kind + "rc_a": ((4, rows, D), BF),
                kind + "st_b": ((3, rows, D), BF),
                kind + "rc_b": ((3, rows, D), BF),
                kind + "st_c": ((rows, D), BF),
                kind + "rc_c": ((3, rows // 4, D), BF),
                kind + "fin": ((rows, D), BF),
            }
        sems |= {
            "os_sem": (2,),
            "go_sem": (4, 2),
            "ra_send": (4,),
            "ra_recv": (4,),
            "rb_send": (4, 3),
            "rb_recv": (4, 3),
            "rc_send": (4, 3),
            "rc_recv": (4, 3),
            "rf_send": (4, 3),
            "rf_recv": (4, 3),
            "rs_send": (2, 7),
            "rs_recv": (2, 7),
        }
    else:
        outs |= grads
    in_vmem = set(grads) | set(full) | {"bias"}
    names = tuple(operands) + tuple(outs) + tuple(scratch) + tuple(sems)
    results = pl.pallas_call(
        functools.partial(kernel, names, linked, canvases),
        out_shape=tuple(shape(*o) for o in outs.values()),
        in_specs=[vmem if name in in_vmem else hbm for name in operands],
        out_specs=tuple(vmem if name in in_vmem else hbm for name in outs),
        scratch_shapes=[pltpu.VMEM(*v) for v in scratch.values()] + [dma(v) for v in sems.values()],
        compiler_params=pltpu.CompilerParams(
            vmem_limit_bytes=64 * 1024 * 1024 - 65536, collective_id=0, has_side_effects=True
        ),
    )(*operands.values())
    return dict(zip(outs, results))


def place_pairs():
    place = np.arange(PLACES)
    r, c = place // 8, place % 8
    index = (r[None, :] - r[:, None] + WIN - 1) * (2 * WIN - 1) + c[None, :] - c[:, None] + WIN - 1
    real = (r < WIN) & (c < WIN)
    return index, real[:, None] & real[None, :], real


def pair_onehot():
    index, both, _ = place_pairs()
    table = (2 * WIN - 1) ** 2
    hot = (np.where(both, index, -1).reshape(-1)[None, :] == np.arange(table)[:, None])
    return hot.astype(np.float32)


def body(
    inputs,
    cotangent,
    pad_mask,
    region_ids,
    norm1_gain,
    norm1_bias,
    qkv_weight,
    qv_bias,
    rel_table,
    proj_weight,
    proj_bias,
    norm2_gain,
    norm2_bias,
    fc1_weight,
    fc1_bias,
    fc2_weight,
    fc2_bias,
):
    owners = lax.axis_size("dp")
    linked = owners == 8
    mine = lax.axis_index("pipe")

    def own(a):
        return lax.dynamic_index_in_dim(a, mine, 0, keepdims=False)

    code = own(region_ids) * 2 + own(pad_mask)
    code = jnp.broadcast_to(code[:, :, None], code.shape + (128,))

    hot = pair_onehot()
    _, _, real = place_pairs()
    rel = lax.dot_general(
        rel_table.astype(BF), jnp.asarray(hot, BF), (((1,), (0,)), ((), ())), preferred_element_type=F32
    )
    rel = rel.reshape(2, GROUPS, 4, PLACES, PLACES).transpose(0, 1, 3, 2, 4)
    rel = jnp.where(jnp.asarray(real)[None, None, :, None, None], rel, MASKED)
    rel = rel.reshape(2, GROUPS, PLACES, 256)

    operands = {"x_hbm": inputs, "cot_hbm": cotangent, "code_hbm": code, "bias": rel}
    vectors = (norm1_gain, norm1_bias, proj_bias, norm2_gain, norm2_bias, fc2_bias, qv_bias, fc1_bias)
    sizes = [v.shape[1] for v in vectors]
    ends = np.cumsum([0] + sizes)
    if linked:
        pack = jnp.stack([jnp.pad(v, ((0, 0), (0, 256 - v.shape[1]))) for v in vectors], axis=1)
        operands |= gather(
            {
                "pack": pack.reshape(16, 256).astype(BF),
                "s_qkv": qkv_weight,
                "s_proj": proj_weight,
                "s_fc1": fc1_weight,
                "s_fc2": fc2_weight,
            }
        )
    else:

        def gathered(a):
            return lax.all_gather(a.astype(BF), "dp", axis=1, tiled=True)

        packed = lax.all_gather(jnp.concatenate(vectors, axis=1).astype(BF), "dp", axis=1)
        parts = [packed[:, :, a:b].reshape(2, -1).astype(F32) for a, b in zip(ends[:-1], ends[1:])]
        qv = parts[6]
        parts[6] = jnp.concatenate([qv[:, :D], jnp.zeros_like(qv[:, :D]), qv[:, D:]], axis=1)
        vec = jnp.stack([jnp.pad(p, ((0, 0), (0, FF - p.shape[1]))) for p in parts], axis=1)
        operands |= {
            "wat": jnp.concatenate([gathered(qkv_weight), gathered(proj_weight)], axis=2),
            "fc1": gathered(fc1_weight),
            "fc2": gathered(fc2_weight),
            "vec": vec.reshape(16, FF),
        }

    out = compute(False, operands)
    if linked:
        out |= reduce({name: out[name] for name in ("g_qkv", "g_proj", "g_fc1", "g_fc2t", "g_vec", "g_tab")})

    def to_owners(g):
        shared = lax.psum_scatter(g, "dp", scatter_dimension=1, tiled=True)
        return lax.psum(shared, "pipe")

    if linked:
        small = out["o_small"]
        g_tab = jnp.concatenate([small[:, :, :8], small[:, :, 8:16]], axis=3).reshape(2, PLACES, GROUPS * 256)
        g_vec = jnp.concatenate([small[:, :, 16 + 8 * j : 24 + 8 * j] for j in range(4)], axis=3)
    else:
        g_tab, g_vec = out["g_tab"], out["g_vec"]

    g_vec = jnp.sum(g_vec.astype(F32), axis=2)
    kinds = [g_vec[:, i] for i in range(8)]
    qv_sum = jnp.concatenate([kinds[6][:, :D], kinds[6][:, 2 * D : 3 * D]], axis=1)
    rows = [kinds[0], kinds[1], kinds[2], kinds[3], kinds[4], kinds[5], qv_sum, kinds[7]]
    if linked:
        at = lax.axis_index("dp")
        small = [lax.dynamic_slice_in_dim(v, at * n, n, 1) for v, n in zip(rows, sizes)]
    else:
        rows = [v[:, : n * owners].reshape(2, -1, n) for v, n in zip(rows, sizes)]
        g_small = to_owners(jnp.concatenate(rows, axis=2))[:, 0]
        small = [g_small[:, a:b] for a, b in zip(ends[:-1], ends[1:])]

    pairs = g_tab.reshape(2, PLACES, HEADS, PLACES).transpose(0, 2, 1, 3)
    pairs = pairs.reshape(2, HEADS, PLACES * PLACES)
    g_table = lax.dot_general(
        jnp.broadcast_to(jnp.asarray(hot, pairs.dtype), (2,) + hot.shape),
        pairs,
        (((2,), (2,)), ((0,), (0,))),
        precision=None if linked else lax.Precision.HIGHEST,
        preferred_element_type=F32,
    )
    if linked:
        big = [out[name] for name in ("o_qkv", "o_proj", "o_fc1", "o_fc2")]
    else:
        g_table = lax.psum(g_table, ("pipe", "dp"))
        big = [to_owners(out[name]) for name in ("g_qkv", "g_proj", "g_fc1")]
        big.append(to_owners(out["g_fc2t"].transpose(0, 2, 1)))

    return (
        out["act_hbm"][None],
        out["igrad_hbm"][None],
        small[0],
        small[1],
        big[0],
        small[6],
        g_table,
        big[1],
        small[2],
        small[3],
        small[4],
        big[2],
        small[7],
        big[3],
        small[5],
    )


def solution(mesh):
    cols = P(None, "dp")
    rows = P(None, "dp", None)
    return jax.shard_map(
        body,
        mesh=mesh,
        in_specs=(
            P(None, "dp", None, None),
            P(None, "dp", None, None),
            rows,
            rows,
            cols,
            cols,
            rows,
            cols,
            P(),
            rows,
            cols,
            cols,
            cols,
            rows,
            cols,
            rows,
            cols,
        ),
        out_specs=(
            P("pipe", None, "dp", None, None),
            P("pipe", None, "dp", None, None),
            cols,
            cols,
            rows,
            cols,
            P(),
            rows,
            cols,
            cols,
            cols,
            rows,
            cols,
            rows,
            cols,
        ),
        check_vma=False,
    )
```

```python
import functools
import types

import jax
import jax.numpy as jnp
import numpy as np
from jax import lax
from jax.experimental import pallas as pl
from jax.experimental.pallas import tpu as pltpu
from jax.sharding import PartitionSpec as P

HEADS = 12
WIN = 7
SHIFT = 3
GRID = 28
CELLS = 784
D = 384
FF = 1536
HEAD = 32
SIDE = 4
WINDOWS = 16
PLACES = 64
WROWS = WINDOWS * PLACES
GROUPS = 3
TILE = 112
SCALE = HEAD**-0.5
NORM_EPS = 1e-05
MASKED = -1e30
BF = jnp.bfloat16
F32 = jnp.float32

ERF_P = 0.3275911 / np.sqrt(2.0)
ERF_A = [0.5 * a for a in (0.254829592, -0.284496736, 1.421413741, -1.453152027, 1.061405429)]
PHI_0 = 1.0 / np.sqrt(2.0 * np.pi)


def nn(a, b):
    return lax.dot_general(a, b, (((1,), (0,)), ((), ())), preferred_element_type=F32)


def nt(a, b):
    return lax.dot_general(a, b, (((1,), (1,)), ((), ())), preferred_element_type=F32)


def tn(a, b):
    return lax.dot_general(a, b, (((0,), (0,)), ((), ())), preferred_element_type=F32)


def segments(shift):
    runs = []
    for wr in range(SIDE):
        for r in range(WIN):
            row = (wr * WIN + r + shift) % GRID
            for wc in range(SIDE):
                col = (wc * WIN + shift) % GRID
                place = (wr * SIDE + wc) * PLACES + r * 8
                first = min(WIN, GRID - col)
                runs.append((row * GRID + col, place, first))
                if first < WIN:
                    runs.append((row * GRID, place + first, WIN - first))
    return runs


def to_windows(src, dst, shift):
    for cell, place, count in segments(shift):
        dst[pl.ds(place, count), :] = src[pl.ds(cell, count), :]


def to_canvas(src, dst, shift):
    for cell, place, count in segments(shift):
        dst[pl.ds(cell, count), :] = src[pl.ds(place, count), :]


def row_block(t, size):
    return pl.ds(pl.multiple_of(t * size, 16), size)


def standardized(v):
    centered = v - jnp.mean(v, axis=-1, keepdims=True)
    spread = jnp.mean(centered * centered, axis=-1, keepdims=True)
    rs = lax.rsqrt(spread + NORM_EPS)
    return centered * rs, rs


def by_eights(v):
    return jnp.sum(v.reshape(v.shape[0] // 8, 8, v.shape[1]), axis=0)


def gelu_parts(x):
    den = 1.0 + ERF_P * jnp.abs(x)
    t = pl.reciprocal(den, approx=True)
    t = t * (2.0 - den * t)
    e = jnp.exp(-0.5 * x * x)
    poly = ERF_A[4]
    for a in ERF_A[3::-1]:
        poly = poly * t + a
    tail = poly * t * e
    cdf = jnp.where(x >= 0.0, 1.0 - tail, tail)
    return x * cdf, cdf + x * (e * PHI_0)


def real_places(rows):
    place = lax.broadcasted_iota(jnp.int32, (rows, 1), 0)
    return ((place & 7) < WIN) & (((place >> 3) & 7) < WIN)


def head_of_lane():
    return lax.broadcasted_iota(jnp.int32, (PLACES, 128), 1) >> 5


def by_head(x, lanes):
    zero = jnp.zeros_like(x)
    return jnp.concatenate([jnp.where(lanes == h, x, zero) for h in range(4)], axis=0)


def own_head(wide, lanes):
    out = wide[3 * PLACES :]
    for h in (2, 1, 0):
        out = jnp.where(lanes == h, wide[h * PLACES : (h + 1) * PLACES], out)
    return out


MESH = pl.DeviceIdType.MESH
ATT_ROWS = 256
MLP_ROWS = 384
SMALL = 192


def kernel(names, linked, canvases, *refs):
    r = types.SimpleNamespace(**dict(zip(names, refs)))
    me = lax.axis_index("pipe")
    inb, code, codew, buf = r.inb, r.code, r.codew, r.buf
    hqw, qkv, probs, att = r.hqw, r.qkv, r.probs, r.att
    hq2, hid, dgelu = r.hq2, r.hid, r.dgelu
    canvf, winf, gzw, wide_t, gqkv, go = r.canvf, r.winf, r.gzw, r.wide_t, r.gqkv, r.go
    g_qkv, g_proj, g_fc1, g_fc2t, g_vec, g_tab = r.g_qkv, r.g_proj, r.g_fc1, r.g_fc2t, r.g_vec, r.g_tab
    wat, fc1, fc2, vec, bias = r.wat, r.fc1, r.fc2, r.vec, r.bias
    if linked:
        d = lax.axis_index("dp")
        z, c = d // 2, d % 2
        sibling = {"dp": 2 * z + 1 - c}

    def z_peer(k):
        return {"dp": 2 * lax.rem(z + k, 4) + c}

    def pipe_peer(k):
        return {"pipe": lax.rem(me + k, 4)}

    def dp_peer(k):
        return {"dp": lax.rem(d + k, 8)}

    def remote(src, dst, send, recv, device):
        return pltpu.make_async_remote_copy(
            src_ref=src, dst_ref=dst, send_sem=send, recv_sem=recv, device_id=device, device_id_type=MESH
        )

    barrier = pltpu.get_barrier_semaphore()
    partners = [pipe_peer(k) for k in range(1, 4)]
    if linked:
        partners += [dp_peer(k) for k in range(1, 8)]
    for partner in partners:
        pl.semaphore_signal(barrier, inc=1, device_id=partner, device_id_type=MESH)

    full = ((wat,), (fc1, fc2), (wat,), (fc1, fc2))

    def owner_back(k):
        return 2 * lax.rem(z + 4 - k, 4) + c

    def shard(sec, a, owner):
        h = 192 if a else 48
        return full[sec][a].at[sec // 2, pl.ds(pl.multiple_of(owner * h, 16), h), :]

    def part(sec, a, owner, place):
        if a:
            return fc2.at[sec // 2, pl.ds(pl.multiple_of(owner * 192 + place * 48, 16), 48), :]
        rows = pl.ds(pl.multiple_of(owner * 48, 16), 48)
        return full[sec][0].at[sec // 2, rows, pl.ds(pl.multiple_of(place * D, 128), D)]

    def to_z(sec, a, k):
        own = part(sec, a, d, me)
        return remote(own, own, r.wz_send.at[sec, a, k - 1], r.wz_recv.at[sec, a, k - 1], z_peer(k))

    def to_places(sec, a, k, j):
        got = part(sec, a, owner_back(k), me)
        return remote(
            got, got, r.wx_send.at[sec, a, k - 1, j - 1], r.wx_recv.at[sec, a, k - 1, j - 1], pipe_peer(j)
        )

    def to_sibling(sec, a, k):
        block = shard(sec, a, owner_back(k))
        return remote(block, block, r.ws_send.at[sec, a, k], r.ws_recv.at[sec, a, k], sibling)

    def weights_1(sec):
        for a in range(len(full[sec])):
            for k in range(1, 4):
                to_z(sec, a, k).start()
            to_sibling(sec, a, 0).start()

    def weights_2(sec):
        for k in range(1, 4):
            for a in range(len(full[sec])):
                got = part(sec, a, owner_back(k), me)
                remote(got, got, r.wz_send.at[sec, a, k - 1], r.wz_recv.at[sec, a, k - 1], z_peer(k)).wait_recv()
                for j in range(1, 4):
                    to_places(sec, a, k, j).start()

    def weights_3(sec):
        for k in range(1, 4):
            for a in range(len(full[sec])):
                for j in range(1, 4):
                    got = part(sec, a, owner_back(k), lax.rem(me + 4 - j, 4))
                    remote(
                        got, got, r.wx_send.at[sec, a, k - 1, j - 1], r.wx_recv.at[sec, a, k - 1, j - 1], pipe_peer(j)
                    ).wait_recv()
                to_sibling(sec, a, k).start()

    def weights_4(sec):
        for k in range(4):
            for a in range(len(full[sec])):
                block = shard(sec, a, 2 * lax.rem(z + 4 - k, 4) + 1 - c)
                remote(block, block, r.ws_send.at[sec, a, k], r.ws_recv.at[sec, a, k], sibling).wait_recv()

    def weights_sent():
        for sec in range(4):
            for a in range(len(full[sec])):
                for k in range(4):
                    to_sibling(sec, a, k).wait_send()
                    if k:
                        to_z(sec, a, k).wait_send()
                        for j in range(1, 4):
                            to_places(sec, a, k, j).wait_send()

    def pack_copy(k):
        return remote(
            r.packs.at[d], r.packs.at[d], r.pk_send.at[k - 1], r.pk_recv.at[k - 1], dp_peer(k)
        )

    def pack_arrival(k):
        slot = r.packs.at[lax.rem(d + 8 - k, 8)]
        return remote(slot, slot, r.pk_send.at[k - 1], r.pk_recv.at[k - 1], dp_peer(k))

    def place_vectors():
        kind = lax.broadcasted_iota(jnp.int32, (16, 256), 0) & 7
        lane = lax.broadcasted_iota(jnp.int32, (16, 256), 1)
        vec[...] = jnp.zeros_like(vec)
        for width, kinds in ((48, kind < 6), (96, kind == 6), (192, kind == 7)):
            for owner in range(8):
                at = owner * width
                if width == 96 and owner >= 4:
                    at += D
                start = at // 128 * 128
                part = jnp.where(kinds & (lane < width), r.packs[owner].astype(F32), 0.0)
                if at > start:
                    part = pltpu.roll(part, at - start, 1)
                vec[:, start : start + 256] += part

    def pieces(sec, owner):
        b = sec // 2
        out = []

        def matrix(ref, h):
            for t in range(h // 48):
                rows = pl.ds(pl.multiple_of(owner * h + t * 48, 16), 48)
                for j in range(ref.shape[1] // D):
                    load = functools.partial(lambda ref, rows, j: ref[rows, j * D : (j + 1) * D], ref, rows, j)
                    out.append((len(out) * 48, 48, load))

        def small():
            rows = pl.ds(pl.multiple_of(owner * 8, 8), 8)
            parts = [g_tab[b, rows, j * D : (j + 1) * D] for j in range(2)]
            parts += [g_vec[b, owner, :, j * D : (j + 1) * D] for j in range(4)]
            return jnp.concatenate(parts + [jnp.zeros((16, D), F32)], axis=0)

        if sec % 2:
            matrix(g_fc1, 48)
        else:
            matrix(g_qkv, 48)
            matrix(g_proj, 48)
            out.append((SMALL, 64, small))
        return out

    def reduce_refs(sec):
        kind = "m" if sec % 2 else "a"
        return types.SimpleNamespace(
            **{n: getattr(r, kind + "_" + n) for n in ("st_a", "rc_a", "st_b", "rc_b", "st_c", "rc_c", "fin")}
        )

    def step_1(sec):
        q = reduce_refs(sec)
        if sec < 2:
            copy_a(sec + 2).wait_send()
            for k in range(1, 4):
                copy_b(sec + 2, k).wait_send()
                copy_c(sec + 2, k).wait_send()
        for k in range(4):
            i = lax.rem(z + k, 4)
            kept = q.st_b.at[k - 1] if k else q.st_c
            for row, rows, load in pieces(sec, 2 * i + 1 - c):
                q.st_a[i, row : row + rows, :] = load().astype(BF)
            for row, rows, load in pieces(sec, 2 * i + c):
                kept[row : row + rows, :] = load().astype(BF)
            if sec % 2:
                winf[:D, :] = g_fc2t[:, pl.ds(pl.multiple_of(i * D, 128), D)].T
                for t in range(0, 192, 48):
                    at = slice(192 + t, 240 + t)
                    q.st_a[i, at, :] = winf[pl.ds(pl.multiple_of((1 - c) * 192 + t, 16), 48), :].astype(BF)
                    kept[at, :] = winf[pl.ds(pl.multiple_of(c * 192 + t, 16), 48), :].astype(BF)
        copy_a(sec).start()

    def copy_a(sec):
        q = reduce_refs(sec)
        return remote(q.st_a, q.rc_a, r.ra_send.at[sec], r.ra_recv.at[sec], sibling)

    def copy_b(sec, k):
        q = reduce_refs(sec)
        return remote(
            q.st_b.at[k - 1], q.rc_b.at[k - 1], r.rb_send.at[sec, k - 1], r.rb_recv.at[sec, k - 1], z_peer(k)
        )

    def step_2(sec):
        q = reduce_refs(sec)
        copy_a(sec).wait_recv()
        for k in (1, 2, 3, 0):
            i = lax.rem(z + k, 4)
            kept = q.st_b.at[k - 1] if k else q.st_c
            for row in range(0, kept.shape[0], 64):
                at = slice(row, row + 64)
                kept[at, :] = (kept[at, :].astype(F32) + q.rc_a[i, at, :].astype(F32)).astype(BF)
            if k:
                copy_b(sec, k).start()

    def quarter(sec, ref, who):
        rows = (MLP_ROWS if sec % 2 else ATT_ROWS) // 4
        return ref.at[pl.ds(pl.multiple_of(who * rows, 16), rows), :]

    def copy_c(sec, k):
        q = reduce_refs(sec)
        return remote(
            quarter(sec, q.st_c, lax.rem(me + k, 4)),
            q.rc_c.at[k - 1],
            r.rc_send.at[sec, k - 1],
            r.rc_recv.at[sec, k - 1],
            pipe_peer(k),
        )

    def step_3(sec):
        q = reduce_refs(sec)
        for k in range(1, 4):
            copy_b(sec, k).wait_recv()
        for row in range(0, q.st_c.shape[0], 64):
            at = slice(row, row + 64)
            total = q.st_c[at, :].astype(F32)
            for k in range(3):
                total = total + q.rc_b[k, at, :].astype(F32)
            q.st_c[at, :] = total.astype(BF)
        for k in range(1, 4):
            copy_c(sec, k).start()

    def copy_f(sec, k):
        q = reduce_refs(sec)
        own = quarter(sec, q.fin, me)
        return remote(own, own, r.rf_send.at[sec, k - 1], r.rf_recv.at[sec, k - 1], pipe_peer(k))

    def step_4(sec):
        q = reduce_refs(sec)
        for k in range(1, 4):
            copy_c(sec, k).wait_recv()
            if sec < 2:
                copy_f(sec + 2, k).wait_send()
        total = quarter(sec, q.st_c, me)[...].astype(F32)
        for k in range(3):
            total = total + q.rc_c[k].astype(F32)
        quarter(sec, q.fin, me)[...] = total.astype(BF)
        for k in range(1, 4):
            copy_f(sec, k).start()

    def copy_s(b, k):
        rows = pl.ds(SMALL, 64)
        return remote(
            r.a_fin.at[rows, :], r.o_small.at[b, d], r.rs_send.at[b, k - 1], r.rs_recv.at[b, k - 1], dp_peer(k)
        )

    def own_small(b):
        return pltpu.make_async_copy(r.a_fin.at[pl.ds(SMALL, 64), :], r.o_small.at[b, d], r.os_sem.at[b])

    def outputs(sec):
        pairs = ((r.l_fc1, r.o_fc1), (r.l_fc2, r.o_fc2)) if sec % 2 else ((r.l_qkv, r.o_qkv), (r.l_proj, r.o_proj))
        return [
            pltpu.make_async_copy(ref, out.at[sec // 2], r.go_sem.at[sec, i]) for i, (ref, out) in enumerate(pairs)
        ]

    def step_5(sec):
        q = reduce_refs(sec)
        b = sec // 2
        for k in range(1, 4):
            got = quarter(sec, q.fin, lax.rem(me + 4 - k, 4))
            remote(got, got, r.rf_send.at[sec, k - 1], r.rf_recv.at[sec, k - 1], pipe_peer(k)).wait_recv()
        if sec % 2 == 0:
            for k in range(1, 8):
                copy_s(b, k).start()
            own_small(b).start()
        if sec < 2:
            for out in outputs(sec + 2):
                out.wait()
        row = 0
        for ref in (r.l_fc1, r.l_fc2) if sec % 2 else (r.l_qkv, r.l_proj):
            for t in range(ref.shape[0] // 48):
                for j in range(ref.shape[1] // D):
                    ref[t * 48 : (t + 1) * 48, j * D : (j + 1) * D] = q.fin[row : row + 48, :].astype(F32)
                    row += 48
        for out in outputs(sec):
            out.start()

    def smalls_sent(b):
        for k in range(1, 8):
            copy_s(b, k).wait_send()
        own_small(b).wait()

    def reductions_done():
        for sec in (1, 0):
            copy_a(sec).wait_send()
            for k in range(1, 4):
                copy_b(sec, k).wait_send()
                copy_c(sec, k).wait_send()
                copy_f(sec, k).wait_send()
        for sec in range(2):
            for out in outputs(sec):
                out.wait()
        smalls_sent(0)
        for b in range(2):
            for k in range(1, 8):
                rows = pl.ds(SMALL, 64)
                remote(
                    r.a_fin.at[rows, :],
                    r.o_small.at[b, lax.rem(d + 8 - k, 8)],
                    r.rs_send.at[b, k - 1],
                    r.rs_recv.at[b, k - 1],
                    dp_peer(k),
                ).wait_recv()

    if linked:
        lands = ((r.s_qkv, g_qkv, wat, 0), (r.s_proj, g_proj, wat, 3 * D), (r.s_fc1, g_fc1, fc1, 0), (r.s_fc2, g_fc2t, fc2, 0))

        def landing(i, b):
            src, dst, _, _ = lands[i]
            h, n = src.shape[1:]
            return pltpu.make_async_copy(
                src.at[b], dst.at[pl.ds(192 * b, h), pl.ds(0, n)], r.sh_sem.at[i, b]
            )

        for i in range(4):
            for b in range(2):
                landing(i, b).start()
        r.packs[d] = r.pack[...]
        for i, (src, dst, ref, col) in enumerate(lands):
            h, n = src.shape[1:]
            for b in range(2):
                landing(i, b).wait()
                for t in range(0, h, 48):
                    rows = pl.ds(pl.multiple_of(d * h + t, 16), 48)
                    ref[b, rows, col : col + n] = dst[192 * b + t : 192 * b + t + 48, :n].astype(BF)
    pl.semaphore_wait(barrier, len(partners))
    if linked:
        for k in range(1, 8):
            pack_copy(k).start()
        weights_1(0)

    def cleared(*refs):
        for ref in refs:

            @pl.loop(0, ref.shape[0] // 16)
            def _(i):
                ref[row_block(i, 16), :] = jnp.zeros((16, ref.shape[1]), F32)

    g_vec[...] = jnp.zeros_like(g_vec)
    g_tab[...] = jnp.zeros_like(g_tab)
    codew[...] = jnp.zeros_like(codew)

    if linked:
        weights_2(0)
        for sec in range(1, 4):
            weights_1(sec)
        for k in range(1, 8):
            pack_arrival(k).wait_recv()
        place_vectors()
        weights_3(0)
        weights_4(0)

    def vector(b, kind, width=D):
        return vec[b * 8 + kind : b * 8 + kind + 1, :width]

    def add_vec(b, kind, part):
        g_vec[b, kind, :, : part.shape[1]] += part

    def windowed(rows, count):
        return jnp.where(real_places(count), winf[rows, :], 0.0).astype(BF)

    def attention_forward(b, n, x, out, hook):
        lanes = head_of_lane()

        @pl.loop(0, CELLS // TILE)
        def _(t):
            rows = row_block(t, TILE)
            xhat, _ = standardized(x[rows, :].astype(F32))
            canvf[rows, :] = xhat * vector(b, 0) + vector(b, 1)

        to_windows(canvf, winf, SHIFT * b)
        to_windows(code.at[n], codew, SHIFT * b)

        @pl.loop(0, 4)
        def _(t):
            rows = row_block(t, 256)
            hq = windowed(rows, 256)
            hqw[n, rows, :] = hq
            for part in range(3):
                cols = slice(part * D, (part + 1) * D)
                acc = nn(hq, wat[b, :, cols]) + vec[b * 8 + 6 : b * 8 + 7, cols]
                if part == 0:
                    acc = acc * SCALE
                qkv[n, rows, cols] = acc.astype(BF)

        hook(0)

        @pl.loop(0, WINDOWS)
        def _(w):
            rows = row_block(w, PLACES)
            cells = codew[rows, :]
            region = (cells >> 1) * b
            pad = (cells & 1).astype(F32)
            lane = lax.broadcasted_iota(jnp.int32, (PLACES, 128), 1)
            same = jnp.where(lane == region, 1.0, 0.0)
            left = jnp.where(lane == 127, 1.0 - pad, same).astype(BF)
            right = jnp.where(lane == 127, -pad, same).astype(BF)
            agree = nt(left, jnp.concatenate([right, right], axis=0))
            mask = jnp.where(agree > 0.5, 0.0, MASKED)
            mask = jnp.concatenate([mask, mask], axis=1)
            for g in range(GROUPS):
                q = qkv[n, rows, g * 128 : (g + 1) * 128]
                k = qkv[n, rows, D + g * 128 : D + (g + 1) * 128]
                v = qkv[n, rows, 2 * D + g * 128 : 2 * D + (g + 1) * 128]
                s = nt(k, by_head(q, lanes)) + bias[b, g] + mask
                e = jnp.exp(s - jnp.max(s, axis=0, keepdims=True))
                p = (e * (1.0 / jnp.sum(e, axis=0, keepdims=True))).astype(BF)
                probs[n, w * GROUPS + g] = p
                att[n, rows, g * 128 : (g + 1) * 128] = own_head(tn(p, v), lanes).astype(BF)

        hook(1)

        @pl.loop(0, 4)
        def _(t):
            rows = row_block(t, 256)
            winf[rows, :] = nn(att[n, rows, :], wat[b, :, 3 * D :])

        to_canvas(winf, canvf, SHIFT * b)

        @pl.loop(0, CELLS // TILE)
        def _(t):
            rows = row_block(t, TILE)
            out[rows, :] = (x[rows, :].astype(F32) + (canvf[rows, :] + vector(b, 2))).astype(BF)

    def mlp_forward(b, n, x, out, hook):
        @pl.loop(0, CELLS // TILE)
        def _(t):
            rows = row_block(t, TILE)
            xhat, _ = standardized(x[rows, :].astype(F32))
            hq2[n, rows, :] = (xhat * vector(b, 3) + vector(b, 4)).astype(BF)

        @pl.loop(0, FF // 256)
        def _(i):
            cols = pl.ds(pl.multiple_of(i * 256, 256), 256)
            pre = nn(hq2[n], fc1[b, :, cols]) + vec[b * 8 + 7 : b * 8 + 8, cols]
            for at in range(0, CELLS, 16):
                h, dg = gelu_parts(pre[at : at + 16])
                hid[n, at : at + 16, cols] = h.astype(BF)
                dgelu[n, at : at + 16, cols] = dg.astype(BF)

        hook(0)
        total = nn(hid[n], fc2[b])
        for at in range(0, CELLS, TILE):
            rows = slice(at, at + TILE)
            out[rows, :] = (x[rows, :].astype(F32) + (total[rows] + vector(b, 5))).astype(BF)

    def norm_backward(b, kind, x, gz, out):
        @pl.loop(0, CELLS // TILE)
        def _(t):
            rows = row_block(t, TILE)
            xhat, rs = standardized(x[rows, :].astype(F32))
            gn = canvf[rows, :]
            gzf = gz[rows, :].astype(F32)
            add_vec(b, kind, by_eights(gn * xhat))
            add_vec(b, kind + 1, by_eights(gn))
            add_vec(b, 5 if kind else 2, by_eights(gzf))
            g = gn * vector(b, kind)
            mg = jnp.mean(g, axis=-1, keepdims=True)
            mgx = jnp.mean(g * xhat, axis=-1, keepdims=True)
            out[rows, :] = (gzf + rs * (g - mg - xhat * mgx)).astype(BF)

    def mlp_backward(b, n, x, gz, out, free_out, hook):
        wide_t[0, :, :CELLS] = hq2[n].T
        wide_t[1, :, :CELLS] = gz[...].T

        @pl.loop(0, FF // 256)
        def _(i):
            cols = pl.ds(pl.multiple_of(i * 256, 256), 256)
            gh = nt(gz[...], fc2[b, cols, :])
            sums = jnp.zeros((8, 256), F32)
            for at in range(0, CELLS, 16):
                gp = (gh[at : at + 16] * dgelu[n, at : at + 16, cols].astype(F32)).astype(BF)
                dgelu[n, at : at + 16, cols] = gp
                sums = sums + by_eights(gp.astype(F32))
            g_vec[b, 7, :, cols] += sums
            g_fc1[:, cols] += nn(wide_t[0, :, :CELLS], dgelu[n, :, cols])
            g_fc2t[:, cols] += nn(wide_t[1, :, :CELLS], hid[n, :, cols])

        hook(0)
        canvf[...] = nt(dgelu[n], fc1[b])
        free_out()
        norm_backward(b, 3, x, gz, out)

    def attention_backward(b, n, x, gz, out, free_out, hook):
        lanes = head_of_lane()

        @pl.loop(0, CELLS // TILE)
        def _(t):
            rows = row_block(t, TILE)
            canvf[rows, :] = gz[rows, :].astype(F32)

        to_windows(canvf, winf, SHIFT * b)

        @pl.loop(0, 4)
        def _(t):
            rows = row_block(t, 256)
            gzw[rows, :] = windowed(rows, 256)

        g_proj[...] += tn(att[n], gzw[...])

        @pl.loop(0, 4)
        def _(t):
            rows = row_block(t, 256)
            go[rows, :] = nt(gzw[rows, :], wat[b, :, 3 * D :]).astype(BF)

        hook(0)

        @pl.loop(0, WINDOWS)
        def _(w):
            rows = row_block(w, PLACES)
            for g in range(GROUPS):
                at = [slice(part * D + g * 128, part * D + (g + 1) * 128) for part in range(3)]
                q, k, v = (qkv[n, rows, cols] for cols in at)
                go_wide = by_head(go[rows, at[0]], lanes)
                p_low = probs[n, w * GROUPS + g]
                p = p_low.astype(F32)
                pd = p * nt(v, go_wide)
                ds = (pd - p * jnp.sum(pd, axis=0, keepdims=True)).astype(BF)
                g_tab[b, :, g * 256 : (g + 1) * 256] += ds.astype(F32)
                gqkv[rows, at[0]] = (own_head(tn(ds, k), lanes) * SCALE).astype(BF)
                gqkv[rows, at[1]] = nn(ds, by_head(q, lanes)).astype(BF)
                gqkv[rows, at[2]] = nn(p_low, go_wide).astype(BF)

        hook(1)

        @pl.loop(0, 4)
        def _(t):
            rows = row_block(t, 256)
            gq = gqkv[rows, :]
            add_vec(b, 6, by_eights(gq.astype(F32)))
            winf[rows, :] = nt(gq, wat[b, :, : 3 * D])

        to_canvas(winf, canvf, SHIFT * b)
        free_out()
        norm_backward(b, 0, x, gz, out)

    def attention_weights(n):
        wide_t[0] = hqw[n].T
        for part in range(3):
            cols = slice(part * D, (part + 1) * D)
            g_qkv[:, cols] += nn(wide_t[0], gqkv[:, cols])

    def push(kind, s, n, start):
        src = buf.at[s, n]
        dst = (r.act_hbm, r.igrad_hbm)[kind].at[me, n]
        local = pltpu.make_async_copy(src, dst, r.local_sem.at[kind, n])
        away = remote(src, dst, r.send_sem.at[kind, s, n], r.recv_sem.at[kind, me, n], {"pipe": s})

        @pl.when(me == s)
        def _():
            local.start() if start else local.wait()

        @pl.when(me != s)
        def _():
            away.start() if start else away.wait_send()

    def arrived(kind, k, n):
        sender = lax.rem(me + k, 4)
        dst = (r.act_hbm, r.igrad_hbm)[kind].at[sender, n]
        remote(
            buf.at[0, 0], dst, r.send_sem.at[kind, 0, n], r.recv_sem.at[kind, sender, n], {"pipe": sender}
        ).wait_recv()

    attention_stash = ((hqw, r.h_hqw), (qkv, r.h_qkv), (probs, r.h_probs), (att, r.h_att))
    mlp_stash = ((hq2, r.h_hq2), (hid, r.h_hid), (dgelu, r.h_dgelu))

    def stash(sec, n, back):
        pairs = mlp_stash if sec else attention_stash
        return [
            pltpu.make_async_copy(*((far.at[n], near.at[n]) if back else (near.at[n], far.at[n])), r.st_sem.at[sec, n, i])
            for i, (near, far) in enumerate(pairs)
        ]

    def load(src, n):
        return pltpu.make_async_copy(src.at[me, n], inb.at[n], r.in_sem.at[n])

    def start(copies):
        for copy in copies:
            copy.start()

    def wait(copies):
        for copy in copies:
            copy.wait()

    steps = (step_1, step_2, step_3, step_4, step_5)
    schedule = {
        (2, 0, 0): ((2, 3),),
        (2, 1, 1): ((3, 3),),
        (1, 0, 0): ((2, 2), (5, 3)),
        (0, 0, 0): ((2, 1), (4, 2)),
        (0, 0, 1): ((5, 2),),
        (0, 1, 1): ((3, 1),),
    }
    after = {3: ((1, 3),), 2: ((1, 2), (4, 3)), 1: ((1, 1), (3, 2)), 0: ((4, 1),)}
    weight_steps = (weights_1, weights_2, weights_3, weights_4) if linked else ()
    gathering = {
        (0, 0): ((2, 1),),
        (0, 1): ((2, 2), (2, 3), (3, 1)),
        (0, 3): ((4, 1), (3, 2)),
        (1, 3): ((4, 2),),
        (2, 0): ((3, 3),),
        (2, 3): ((4, 3),),
    }

    codes = [pltpu.make_async_copy(r.code_hbm, code, r.code_sem.at[0])]
    start(codes)
    start([load(r.x_hbm, n) for n in range(canvases)])
    wait(codes)

    @pl.loop(0, canvases)
    def _(n):
        def gather(sec, i):
            todo = gathering.get((sec, i), ())
            if linked and todo:

                @pl.when(n == 0)
                def _():
                    for step, of in todo:
                        weight_steps[step - 1](of)

        load(r.x_hbm, n).wait()
        x = inb.at[n]
        for s in range(4):
            if s >= 2:
                wait(stash(s - 2, n, False))
            forward = mlp_forward if s % 2 else attention_forward
            forward(s // 2, n, x, buf.at[s, n], functools.partial(gather, s))
            x = buf.at[s, n]
            push(0, s, n, True)
            if s < 2:
                start(stash(s, n, False))
            if s == 0:
                load(r.cot_hbm, n).start()
            gather(s, 3)

    for s in (3, 2, 1, 0):
        cleared(*((g_fc1, g_fc2t) if s % 2 else (g_qkv, g_proj)))

        @pl.loop(0, canvases)
        def _(n):
            def hook(i):
                for at in range(2):
                    todo = schedule.get((s, at, i), ())
                    if linked and todo:

                        @pl.when(n == (canvases - 1 if at else 0))
                        def _():
                            for step, of in todo:
                                steps[step - 1](of)

            if s == 3:
                load(r.cot_hbm, n).wait()
            if s == 0:
                load(r.x_hbm, n).wait()
            if s < 2:
                wait(stash(s, n, True))
            x = buf.at[s - 1, n] if s else inb.at[n]
            gz = inb.at[n] if s == 3 else buf.at[s + 1, n]
            backward = mlp_backward if s % 2 else attention_backward
            backward(s // 2, n, x, gz, buf.at[s, n], functools.partial(push, 0, s, n, False), hook)
            push(1, s, n, True)
            if s % 2 == 0:
                attention_weights(n)
            if s == 3:
                load(r.x_hbm, n).start()
            if s >= 2:
                start(stash(s - 2, n, True))

        if linked:
            for step, of in after[s]:
                steps[step - 1](of)
        else:
            whole = ((g_fc1, r.f_fc1), (g_fc2t, r.f_fc2t)) if s % 2 else ((g_qkv, r.f_qkv), (g_proj, r.f_proj))
            copies = [pltpu.make_async_copy(a, o.at[s // 2], r.go_sem.at[s, i]) for i, (a, o) in enumerate(whole)]
            start(copies)
            wait(copies)

    if linked:
        step_1(0)
        step_5(1)
        step_2(0)
        smalls_sent(1)
        step_3(0)
        step_4(0)
        step_5(0)
        reductions_done()
        weights_sent()
        for k in range(1, 8):
            pack_copy(k).wait_send()
    for kind in range(2):
        for k in range(1, 4):
            for n in range(canvases):
                arrived(kind, k, n)
    for s in range(4):
        for n in range(canvases):
            push(1, s, n, False)


def compute(linked, operands):
    canvases = operands["x_hbm"].shape[1]
    shape = jax.ShapeDtypeStruct
    hbm = pl.BlockSpec(memory_space=pl.ANY)
    vmem = pl.BlockSpec(memory_space=pltpu.VMEM)
    dma = pltpu.SemaphoreType.DMA
    full = {
        "wat": ((2, D, 4 * D), BF),
        "fc1": ((2, D, FF), BF),
        "fc2": ((2, FF, D), BF),
        "vec": ((16, FF), F32),
    }
    grads = {
        "g_qkv": ((D, 3 * D), F32),
        "g_proj": ((D, D), F32),
        "g_fc1": ((D, FF), F32),
        "g_fc2t": ((D, FF), F32),
        "g_vec": ((2, 8, 8, FF), F32),
        "g_tab": ((2, PLACES, GROUPS * 256), F32),
    }
    outs = {"act_hbm": ((4, canvases, CELLS, D), BF), "igrad_hbm": ((4, canvases, CELLS, D), BF)}
    kept = {
        "hqw": ((canvases, WROWS, D), BF),
        "qkv": ((canvases, WROWS, 3 * D), BF),
        "probs": ((canvases, WINDOWS * GROUPS, PLACES, 256), BF),
        "att": ((canvases, WROWS, D), BF),
        "hq2": ((canvases, CELLS, D), BF),
        "hid": ((canvases, CELLS, FF), BF),
        "dgelu": ((canvases, CELLS, FF), BF),
    }
    outs |= {"h_" + name: kind for name, kind in kept.items()}
    scratch = kept | {
        "inb": ((canvases, CELLS, D), BF),
        "code": ((canvases, CELLS, 128), jnp.int32),
        "codew": ((WROWS, 128), jnp.int32),
        "buf": ((4, canvases, CELLS, D), BF),
        "canvf": ((CELLS, D), F32),
        "winf": ((WROWS, D), F32),
        "gzw": ((WROWS, D), BF),
        "go": ((WROWS, D), BF),
        "gqkv": ((WROWS, 3 * D), BF),
        "wide_t": ((2, D, WROWS), BF),
    }
    sems = {
        "in_sem": (canvases,),
        "code_sem": (1,),
        "st_sem": (2, canvases, 4),
        "local_sem": (2, canvases),
        "send_sem": (2, 4, canvases),
        "recv_sem": (2, 4, canvases),
    }
    if linked:
        outs |= {
            "o_qkv": ((2, 48, 3 * D), F32),
            "o_proj": ((2, 48, D), F32),
            "o_fc1": ((2, 48, FF), F32),
            "o_fc2": ((2, 192, D), F32),
            "o_small": ((2, 8, 64, D), BF),
        }
        scratch |= full | grads
        scratch |= {
            "packs": ((8, 16, 256), BF),
            "l_qkv": ((48, 3 * D), F32),
            "l_proj": ((48, D), F32),
            "l_fc1": ((48, FF), F32),
            "l_fc2": ((192, D), F32),
        }
        for kind, rows in (("m_", MLP_ROWS), ("a_", ATT_ROWS)):
            scratch |= {
                kind + "st_a": ((4, rows, D), BF),
                kind + "rc_a": ((4, rows, D), BF),
                kind + "st_b": ((3, rows, D), BF),
                kind + "rc_b": ((3, rows, D), BF),
                kind + "st_c": ((rows, D), BF),
                kind + "rc_c": ((3, rows // 4, D), BF),
                kind + "fin": ((rows, D), BF),
            }
        sems |= {
            "sh_sem": (4, 2),
            "os_sem": (2,),
            "go_sem": (4, 2),
            "wz_send": (4, 2, 3),
            "wz_recv": (4, 2, 3),
            "wx_send": (4, 2, 3, 3),
            "wx_recv": (4, 2, 3, 3),
            "ws_send": (4, 2, 4),
            "ws_recv": (4, 2, 4),
            "pk_send": (7,),
            "pk_recv": (7,),
            "ra_send": (4,),
            "ra_recv": (4,),
            "rb_send": (4, 3),
            "rb_recv": (4, 3),
            "rc_send": (4, 3),
            "rc_recv": (4, 3),
            "rf_send": (4, 3),
            "rf_recv": (4, 3),
            "rs_send": (2, 7),
            "rs_recv": (2, 7),
        }
    else:
        for name in ("g_vec", "g_tab"):
            outs[name] = grads.pop(name)
        outs |= {name.replace("g_", "f_"): ((2,) + dims, F32) for name, (dims, _) in grads.items()}
        scratch |= grads
        sems["go_sem"] = (4, 2)
    in_vmem = set(full) | {"bias", "pack", "g_vec", "g_tab"}
    names = tuple(operands) + tuple(outs) + tuple(scratch) + tuple(sems)
    results = pl.pallas_call(
        functools.partial(kernel, names, linked, canvases),
        out_shape=tuple(shape(*o) for o in outs.values()),
        in_specs=[vmem if name in in_vmem else hbm for name in operands],
        out_specs=tuple(vmem if name in in_vmem else hbm for name in outs),
        scratch_shapes=[pltpu.VMEM(*v) for v in scratch.values()] + [dma(v) for v in sems.values()],
        compiler_params=pltpu.CompilerParams(
            vmem_limit_bytes=64 * 1024 * 1024 - 65536, collective_id=0, has_side_effects=True
        ),
    )(*operands.values())
    return dict(zip(outs, results))


def place_pairs():
    place = np.arange(PLACES)
    r, c = place // 8, place % 8
    index = (r[None, :] - r[:, None] + WIN - 1) * (2 * WIN - 1) + c[None, :] - c[:, None] + WIN - 1
    real = (r < WIN) & (c < WIN)
    return index, real[:, None] & real[None, :], real


def pair_onehot():
    index, both, _ = place_pairs()
    table = (2 * WIN - 1) ** 2
    hot = (np.where(both, index, -1).reshape(-1)[None, :] == np.arange(table)[:, None])
    return hot.astype(np.float32)


def body(
    inputs,
    cotangent,
    pad_mask,
    region_ids,
    norm1_gain,
    norm1_bias,
    qkv_weight,
    qv_bias,
    rel_table,
    proj_weight,
    proj_bias,
    norm2_gain,
    norm2_bias,
    fc1_weight,
    fc1_bias,
    fc2_weight,
    fc2_bias,
):
    owners = lax.axis_size("dp")
    linked = owners == 8
    mine = lax.axis_index("pipe")

    def own(a):
        return lax.dynamic_index_in_dim(a, mine, 0, keepdims=False)

    code = own(region_ids) * 2 + own(pad_mask)
    code = jnp.broadcast_to(code[:, :, None], code.shape + (128,))

    hot = pair_onehot()
    _, _, real = place_pairs()
    rel = lax.dot_general(
        rel_table.astype(BF), jnp.asarray(hot, BF), (((1,), (0,)), ((), ())), preferred_element_type=F32
    )
    rel = rel.reshape(2, GROUPS, 4, PLACES, PLACES).transpose(0, 1, 3, 2, 4)
    rel = jnp.where(jnp.asarray(real)[None, None, :, None, None], rel, MASKED)
    rel = rel.reshape(2, GROUPS, PLACES, 256)

    operands = {"x_hbm": inputs, "cot_hbm": cotangent, "code_hbm": code, "bias": rel}
    vectors = (norm1_gain, norm1_bias, proj_bias, norm2_gain, norm2_bias, fc2_bias, qv_bias, fc1_bias)
    sizes = [v.shape[1] for v in vectors]
    ends = np.cumsum([0] + sizes)
    if linked:
        pack = jnp.stack([jnp.pad(v, ((0, 0), (0, 256 - v.shape[1]))) for v in vectors], axis=1)
        operands |= {
            "pack": pack.reshape(16, 256).astype(BF),
            "s_qkv": qkv_weight,
            "s_proj": proj_weight,
            "s_fc1": fc1_weight,
            "s_fc2": fc2_weight,
        }
    else:

        def gathered(a):
            return lax.all_gather(a.astype(BF), "dp", axis=1, tiled=True)

        packed = lax.all_gather(jnp.concatenate(vectors, axis=1).astype(BF), "dp", axis=1)
        parts = [packed[:, :, a:b].reshape(2, -1).astype(F32) for a, b in zip(ends[:-1], ends[1:])]
        qv = parts[6]
        parts[6] = jnp.concatenate([qv[:, :D], jnp.zeros_like(qv[:, :D]), qv[:, D:]], axis=1)
        vec = jnp.stack([jnp.pad(p, ((0, 0), (0, FF - p.shape[1]))) for p in parts], axis=1)
        operands |= {
            "wat": jnp.concatenate([gathered(qkv_weight), gathered(proj_weight)], axis=2),
            "fc1": gathered(fc1_weight),
            "fc2": gathered(fc2_weight),
            "vec": vec.reshape(16, FF),
        }

    out = compute(linked, operands)

    def to_owners(g):
        shared = lax.psum_scatter(g, "dp", scatter_dimension=1, tiled=True)
        return lax.psum(shared, "pipe")

    if linked:
        small = out["o_small"]
        g_tab = jnp.concatenate([small[:, :, :8], small[:, :, 8:16]], axis=3).reshape(2, PLACES, GROUPS * 256)
        g_vec = jnp.concatenate([small[:, :, 16 + 8 * j : 24 + 8 * j] for j in range(4)], axis=3)
    else:
        g_tab, g_vec = out["g_tab"], out["g_vec"]

    g_vec = jnp.sum(g_vec.astype(F32), axis=2)
    kinds = [g_vec[:, i] for i in range(8)]
    qv_sum = jnp.concatenate([kinds[6][:, :D], kinds[6][:, 2 * D : 3 * D]], axis=1)
    rows = [kinds[0], kinds[1], kinds[2], kinds[3], kinds[4], kinds[5], qv_sum, kinds[7]]
    if linked:
        at = lax.axis_index("dp")
        small = [lax.dynamic_slice_in_dim(v, at * n, n, 1) for v, n in zip(rows, sizes)]
    else:
        rows = [v[:, : n * owners].reshape(2, -1, n) for v, n in zip(rows, sizes)]
        g_small = to_owners(jnp.concatenate(rows, axis=2))[:, 0]
        small = [g_small[:, a:b] for a, b in zip(ends[:-1], ends[1:])]

    pairs = g_tab.reshape(2, PLACES, HEADS, PLACES).transpose(0, 2, 1, 3)
    pairs = pairs.reshape(2, HEADS, PLACES * PLACES)
    g_table = lax.dot_general(
        jnp.broadcast_to(jnp.asarray(hot, pairs.dtype), (2,) + hot.shape),
        pairs,
        (((2,), (2,)), ((0,), (0,))),
        precision=None if linked else lax.Precision.HIGHEST,
        preferred_element_type=F32,
    )
    if linked:
        big = [out[name] for name in ("o_qkv", "o_proj", "o_fc1", "o_fc2")]
    else:
        g_table = lax.psum(g_table, ("pipe", "dp"))
        big = [to_owners(out[name]) for name in ("f_qkv", "f_proj", "f_fc1")]
        big.append(to_owners(out["f_fc2t"].transpose(0, 2, 1)))

    return (
        out["act_hbm"][None],
        out["igrad_hbm"][None],
        small[0],
        small[1],
        big[0],
        small[6],
        g_table,
        big[1],
        small[2],
        small[3],
        small[4],
        big[2],
        small[7],
        big[3],
        small[5],
    )


def solution(mesh):
    cols = P(None, "dp")
    rows = P(None, "dp", None)
    return jax.shard_map(
        body,
        mesh=mesh,
        in_specs=(
            P(None, "dp", None, None),
            P(None, "dp", None, None),
            rows,
            rows,
            cols,
            cols,
            rows,
            cols,
            P(),
            rows,
            cols,
            cols,
            cols,
            rows,
            cols,
            rows,
            cols,
        ),
        out_specs=(
            P("pipe", None, "dp", None, None),
            P("pipe", None, "dp", None, None),
            cols,
            cols,
            rows,
            cols,
            P(),
            rows,
            cols,
            cols,
            cols,
            rows,
            cols,
            rows,
            cols,
        ),
        check_vma=False,
    )
```

```python
import functools
import types

import jax
import jax.numpy as jnp
import numpy as np
from jax import lax
from jax.experimental import pallas as pl
from jax.experimental.pallas import tpu as pltpu
from jax.sharding import PartitionSpec as P

HEADS = 12
WIN = 7
SHIFT = 3
GRID = 28
CELLS = 784
D = 384
FF = 1536
HEAD = 32
SIDE = 4
WINDOWS = 16
PLACES = 64
WROWS = WINDOWS * PLACES
GROUPS = 3
TILE = 112
SCALE = HEAD**-0.5
NORM_EPS = 1e-05
MASKED = -1e30
BF = jnp.bfloat16
F32 = jnp.float32

ERF_P = 0.3275911 / np.sqrt(2.0)
ERF_A = [0.5 * a for a in (0.254829592, -0.284496736, 1.421413741, -1.453152027, 1.061405429)]
PHI_0 = 1.0 / np.sqrt(2.0 * np.pi)


def nn(a, b):
    return lax.dot_general(a, b, (((1,), (0,)), ((), ())), preferred_element_type=F32)


def nt(a, b):
    return lax.dot_general(a, b, (((1,), (1,)), ((), ())), preferred_element_type=F32)


def tn(a, b):
    return lax.dot_general(a, b, (((0,), (0,)), ((), ())), preferred_element_type=F32)


def segments(shift):
    runs = []
    for wr in range(SIDE):
        for r in range(WIN):
            row = (wr * WIN + r + shift) % GRID
            for wc in range(SIDE):
                col = (wc * WIN + shift) % GRID
                place = (wr * SIDE + wc) * PLACES + r * 8
                first = min(WIN, GRID - col)
                runs.append((row * GRID + col, place, first))
                if first < WIN:
                    runs.append((row * GRID, place + first, WIN - first))
    return runs


def to_windows(src, dst, shift):
    for cell, place, count in segments(shift):
        dst[pl.ds(place, count), :] = src[pl.ds(cell, count), :]


def to_canvas(src, dst, shift):
    for cell, place, count in segments(shift):
        dst[pl.ds(cell, count), :] = src[pl.ds(place, count), :]


def row_block(t, size):
    return pl.ds(pl.multiple_of(t * size, 16), size)


def standardized(v):
    centered = v - jnp.mean(v, axis=-1, keepdims=True)
    spread = jnp.mean(centered * centered, axis=-1, keepdims=True)
    rs = lax.rsqrt(spread + NORM_EPS)
    return centered * rs, rs


def by_eights(v):
    return jnp.sum(v.reshape(v.shape[0] // 8, 8, v.shape[1]), axis=0)


def gelu_parts(x):
    den = 1.0 + ERF_P * jnp.abs(x)
    t = pl.reciprocal(den, approx=True)
    t = t * (2.0 - den * t)
    e = jnp.exp(-0.5 * x * x)
    poly = ERF_A[4]
    for a in ERF_A[3::-1]:
        poly = poly * t + a
    tail = poly * t * e
    cdf = jnp.where(x >= 0.0, 1.0 - tail, tail)
    return x * cdf, cdf + x * (e * PHI_0)


def real_places(rows):
    place = lax.broadcasted_iota(jnp.int32, (rows, 1), 0)
    return ((place & 7) < WIN) & (((place >> 3) & 7) < WIN)


def head_of_lane():
    return lax.broadcasted_iota(jnp.int32, (PLACES, 128), 1) >> 5


def by_head(x, lanes):
    zero = jnp.zeros_like(x)
    return jnp.concatenate([jnp.where(lanes == h, x, zero) for h in range(4)], axis=0)


def own_head(wide, lanes):
    out = wide[3 * PLACES :]
    for h in (2, 1, 0):
        out = jnp.where(lanes == h, wide[h * PLACES : (h + 1) * PLACES], out)
    return out


MESH = pl.DeviceIdType.MESH
ATT_ROWS = 256
MLP_ROWS = 384
SMALL = 192


def kernel(names, linked, canvases, *refs):
    r = types.SimpleNamespace(**dict(zip(names, refs)))
    me = lax.axis_index("pipe")
    inb, code, codew, buf = r.inb, r.code, r.codew, r.buf
    hqw, qkv, probs, att = r.hqw, r.qkv, r.probs, r.att
    hq2, hid, dgelu = r.hq2, r.hid, r.dgelu
    canvf, winf, gzw, wide_t, gqkv, go = r.canvf, r.winf, r.gzw, r.wide_t, r.gqkv, r.go
    g_qkv, g_proj, g_fc1, g_fc2t, g_vec, g_tab = r.g_qkv, r.g_proj, r.g_fc1, r.g_fc2t, r.g_vec, r.g_tab
    wat, fc1, fc2, vec, bias = r.wat, r.fc1, r.fc2, r.vec, r.bias
    if linked:
        d = lax.axis_index("dp")
        z, c = d // 2, d % 2
        sibling = {"dp": 2 * z + 1 - c}

    def z_peer(k):
        return {"dp": 2 * lax.rem(z + k, 4) + c}

    def pipe_peer(k):
        return {"pipe": lax.rem(me + k, 4)}

    def dp_peer(k):
        return {"dp": lax.rem(d + k, 8)}

    def remote(src, dst, send, recv, device):
        return pltpu.make_async_remote_copy(
            src_ref=src, dst_ref=dst, send_sem=send, recv_sem=recv, device_id=device, device_id_type=MESH
        )

    barrier = pltpu.get_barrier_semaphore()
    partners = [pipe_peer(k) for k in range(1, 4)]
    if linked:
        partners += [dp_peer(k) for k in range(1, 8)]
    for partner in partners:
        pl.semaphore_signal(barrier, inc=1, device_id=partner, device_id_type=MESH)

    full = ((wat,), (fc1, fc2), (wat,), (fc1, fc2))

    def owner_back(k):
        return 2 * lax.rem(z + 4 - k, 4) + c

    def shard(sec, a, owner):
        h = 192 if a else 48
        return full[sec][a].at[sec // 2, pl.ds(pl.multiple_of(owner * h, 16), h), :]

    def part(sec, a, owner, place):
        if a:
            return fc2.at[sec // 2, pl.ds(pl.multiple_of(owner * 192 + place * 48, 16), 48), :]
        rows = pl.ds(pl.multiple_of(owner * 48, 16), 48)
        return full[sec][0].at[sec // 2, rows, pl.ds(pl.multiple_of(place * D, 128), D)]

    def to_z(sec, a, k):
        own = part(sec, a, d, me)
        return remote(own, own, r.wz_send.at[sec, a, k - 1], r.wz_recv.at[sec, a, k - 1], z_peer(k))

    def to_places(sec, a, k, j):
        got = part(sec, a, owner_back(k), me)
        return remote(
            got, got, r.wx_send.at[sec, a, k - 1, j - 1], r.wx_recv.at[sec, a, k - 1, j - 1], pipe_peer(j)
        )

    def to_sibling(sec, a, k):
        block = shard(sec, a, owner_back(k))
        return remote(block, block, r.ws_send.at[sec, a, k], r.ws_recv.at[sec, a, k], sibling)

    def weights_1(sec):
        for a in range(len(full[sec])):
            for k in range(1, 4):
                to_z(sec, a, k).start()
            to_sibling(sec, a, 0).start()

    def weights_2(sec):
        for k in range(1, 4):
            for a in range(len(full[sec])):
                got = part(sec, a, owner_back(k), me)
                remote(got, got, r.wz_send.at[sec, a, k - 1], r.wz_recv.at[sec, a, k - 1], z_peer(k)).wait_recv()
                for j in range(1, 4):
                    to_places(sec, a, k, j).start()

    def weights_3(sec):
        for k in range(1, 4):
            for a in range(len(full[sec])):
                for j in range(1, 4):
                    got = part(sec, a, owner_back(k), lax.rem(me + 4 - j, 4))
                    remote(
                        got, got, r.wx_send.at[sec, a, k - 1, j - 1], r.wx_recv.at[sec, a, k - 1, j - 1], pipe_peer(j)
                    ).wait_recv()
                to_sibling(sec, a, k).start()

    def weights_4(sec):
        for k in range(4):
            for a in range(len(full[sec])):
                block = shard(sec, a, 2 * lax.rem(z + 4 - k, 4) + 1 - c)
                remote(block, block, r.ws_send.at[sec, a, k], r.ws_recv.at[sec, a, k], sibling).wait_recv()

    def weights_sent():
        for sec in range(4):
            for a in range(len(full[sec])):
                for k in range(4):
                    to_sibling(sec, a, k).wait_send()
                    if k:
                        to_z(sec, a, k).wait_send()
                        for j in range(1, 4):
                            to_places(sec, a, k, j).wait_send()

    def pack_copy(k):
        return remote(
            r.packs.at[d], r.packs.at[d], r.pk_send.at[k - 1], r.pk_recv.at[k - 1], dp_peer(k)
        )

    def pack_arrival(k):
        slot = r.packs.at[lax.rem(d + 8 - k, 8)]
        return remote(slot, slot, r.pk_send.at[k - 1], r.pk_recv.at[k - 1], dp_peer(k))

    def place_vectors():
        kind = lax.broadcasted_iota(jnp.int32, (16, 256), 0) & 7
        lane = lax.broadcasted_iota(jnp.int32, (16, 256), 1)
        vec[...] = jnp.zeros_like(vec)
        for width, kinds in ((48, kind < 6), (96, kind == 6), (192, kind == 7)):
            for owner in range(8):
                at = owner * width
                if width == 96 and owner >= 4:
                    at += D
                start = at // 128 * 128
                part = jnp.where(kinds & (lane < width), r.packs[owner].astype(F32), 0.0)
                if at > start:
                    part = pltpu.roll(part, at - start, 1)
                vec[:, start : start + 256] += part

    def pieces(sec, owner):
        b = sec // 2
        out = []

        def matrix(ref, h):
            for t in range(h // 48):
                rows = pl.ds(pl.multiple_of(owner * h + t * 48, 16), 48)
                for j in range(ref.shape[1] // D):
                    load = functools.partial(lambda ref, rows, j: ref[rows, j * D : (j + 1) * D], ref, rows, j)
                    out.append((len(out) * 48, 48, load))

        def small():
            rows = pl.ds(pl.multiple_of(owner * 8, 8), 8)
            parts = [g_tab[b, rows, j * D : (j + 1) * D] for j in range(2)]
            parts += [g_vec[b, owner, :, j * D : (j + 1) * D] for j in range(4)]
            return jnp.concatenate(parts + [jnp.zeros((16, D), F32)], axis=0)

        if sec % 2:
            matrix(g_fc1, 48)
        else:
            matrix(g_qkv, 48)
            matrix(g_proj, 48)
            out.append((SMALL, 64, small))
        return out

    def reduce_refs(sec):
        kind = "m" if sec % 2 else "a"
        return types.SimpleNamespace(
            **{n: getattr(r, kind + "_" + n) for n in ("st_a", "rc_a", "st_b", "rc_b", "st_c", "rc_c", "fin")}
        )

    def step_1(sec):
        q = reduce_refs(sec)
        if sec < 2:
            copy_a(sec + 2).wait_send()
            for k in range(1, 4):
                copy_b(sec + 2, k).wait_send()
                copy_c(sec + 2, k).wait_send()
        for k in range(4):
            i = lax.rem(z + k, 4)
            kept = q.st_b.at[k - 1] if k else q.st_c
            for row, rows, load in pieces(sec, 2 * i + 1 - c):
                q.st_a[i, row : row + rows, :] = load().astype(BF)
            for row, rows, load in pieces(sec, 2 * i + c):
                kept[row : row + rows, :] = load().astype(BF)
            if sec % 2:
                winf[:D, :] = g_fc2t[:, pl.ds(pl.multiple_of(i * D, 128), D)].T
                for t in range(0, 192, 48):
                    at = slice(192 + t, 240 + t)
                    q.st_a[i, at, :] = winf[pl.ds(pl.multiple_of((1 - c) * 192 + t, 16), 48), :].astype(BF)
                    kept[at, :] = winf[pl.ds(pl.multiple_of(c * 192 + t, 16), 48), :].astype(BF)
        copy_a(sec).start()

    def copy_a(sec):
        q = reduce_refs(sec)
        return remote(q.st_a, q.rc_a, r.ra_send.at[sec], r.ra_recv.at[sec], sibling)

    def copy_b(sec, k):
        q = reduce_refs(sec)
        return remote(
            q.st_b.at[k - 1], q.rc_b.at[k - 1], r.rb_send.at[sec, k - 1], r.rb_recv.at[sec, k - 1], z_peer(k)
        )

    def step_2(sec):
        q = reduce_refs(sec)
        copy_a(sec).wait_recv()
        for k in (1, 2, 3, 0):
            i = lax.rem(z + k, 4)
            kept = q.st_b.at[k - 1] if k else q.st_c
            for row in range(0, kept.shape[0], 64):
                at = slice(row, row + 64)
                kept[at, :] = (kept[at, :].astype(F32) + q.rc_a[i, at, :].astype(F32)).astype(BF)
            if k:
                copy_b(sec, k).start()

    def quarter(sec, ref, who):
        rows = (MLP_ROWS if sec % 2 else ATT_ROWS) // 4
        return ref.at[pl.ds(pl.multiple_of(who * rows, 16), rows), :]

    def copy_c(sec, k):
        q = reduce_refs(sec)
        return remote(
            quarter(sec, q.st_c, lax.rem(me + k, 4)),
            q.rc_c.at[k - 1],
            r.rc_send.at[sec, k - 1],
            r.rc_recv.at[sec, k - 1],
            pipe_peer(k),
        )

    def step_3(sec):
        q = reduce_refs(sec)
        for k in range(1, 4):
            copy_b(sec, k).wait_recv()
        for row in range(0, q.st_c.shape[0], 64):
            at = slice(row, row + 64)
            total = q.st_c[at, :].astype(F32)
            for k in range(3):
                total = total + q.rc_b[k, at, :].astype(F32)
            q.st_c[at, :] = total.astype(BF)
        for k in range(1, 4):
            copy_c(sec, k).start()

    def copy_f(sec, k):
        q = reduce_refs(sec)
        own = quarter(sec, q.fin, me)
        return remote(own, own, r.rf_send.at[sec, k - 1], r.rf_recv.at[sec, k - 1], pipe_peer(k))

    def step_4(sec):
        q = reduce_refs(sec)
        for k in range(1, 4):
            copy_c(sec, k).wait_recv()
            if sec < 2:
                copy_f(sec + 2, k).wait_send()
        total = quarter(sec, q.st_c, me)[...].astype(F32)
        for k in range(3):
            total = total + q.rc_c[k].astype(F32)
        quarter(sec, q.fin, me)[...] = total.astype(BF)
        for k in range(1, 4):
            copy_f(sec, k).start()

    def copy_s(b, k):
        rows = pl.ds(SMALL, 64)
        return remote(
            r.a_fin.at[rows, :], r.o_small.at[b, d], r.rs_send.at[b, k - 1], r.rs_recv.at[b, k - 1], dp_peer(k)
        )

    def own_small(b):
        return pltpu.make_async_copy(r.a_fin.at[pl.ds(SMALL, 64), :], r.o_small.at[b, d], r.os_sem.at[b])

    def outputs(sec):
        pairs = ((r.l_fc1, r.o_fc1), (r.l_fc2, r.o_fc2)) if sec % 2 else ((r.l_qkv, r.o_qkv), (r.l_proj, r.o_proj))
        return [
            pltpu.make_async_copy(ref, out.at[sec // 2], r.go_sem.at[sec, i]) for i, (ref, out) in enumerate(pairs)
        ]

    def step_5(sec):
        q = reduce_refs(sec)
        b = sec // 2
        for k in range(1, 4):
            got = quarter(sec, q.fin, lax.rem(me + 4 - k, 4))
            remote(got, got, r.rf_send.at[sec, k - 1], r.rf_recv.at[sec, k - 1], pipe_peer(k)).wait_recv()
        if sec % 2 == 0:
            for k in range(1, 8):
                copy_s(b, k).start()
            own_small(b).start()
        if sec < 2:
            for out in outputs(sec + 2):
                out.wait()
        row = 0
        for ref in (r.l_fc1, r.l_fc2) if sec % 2 else (r.l_qkv, r.l_proj):
            for t in range(ref.shape[0] // 48):
                for j in range(ref.shape[1] // D):
                    ref[t * 48 : (t + 1) * 48, j * D : (j + 1) * D] = q.fin[row : row + 48, :].astype(F32)
                    row += 48
        for out in outputs(sec):
            out.start()

    def smalls_sent(b):
        for k in range(1, 8):
            copy_s(b, k).wait_send()
        own_small(b).wait()

    def reductions_done():
        for sec in (1, 0):
            copy_a(sec).wait_send()
            for k in range(1, 4):
                copy_b(sec, k).wait_send()
                copy_c(sec, k).wait_send()
                copy_f(sec, k).wait_send()
        for sec in range(2):
            for out in outputs(sec):
                out.wait()
        smalls_sent(0)
        for b in range(2):
            for k in range(1, 8):
                rows = pl.ds(SMALL, 64)
                remote(
                    r.a_fin.at[rows, :],
                    r.o_small.at[b, lax.rem(d + 8 - k, 8)],
                    r.rs_send.at[b, k - 1],
                    r.rs_recv.at[b, k - 1],
                    dp_peer(k),
                ).wait_recv()

    if linked:
        lands = ((r.s_qkv, g_qkv, wat, 0), (r.s_proj, g_proj, wat, 3 * D), (r.s_fc1, g_fc1, fc1, 0), (r.s_fc2, g_fc2t, fc2, 0))

        def landing(i, b):
            src, dst, _, _ = lands[i]
            h, n = src.shape[1:]
            return pltpu.make_async_copy(
                src.at[b], dst.at[pl.ds(192 * b, h), pl.ds(0, n)], r.sh_sem.at[i, b]
            )

        for i in range(4):
            for b in range(2):
                landing(i, b).start()
        r.packs[d] = r.pack[...]
        for i, (src, dst, ref, col) in enumerate(lands):
            h, n = src.shape[1:]
            for b in range(2):
                landing(i, b).wait()
                for t in range(0, h, 48):
                    rows = pl.ds(pl.multiple_of(d * h + t, 16), 48)
                    ref[b, rows, col : col + n] = dst[192 * b + t : 192 * b + t + 48, :n].astype(BF)
    pl.semaphore_wait(barrier, len(partners))
    if linked:
        for k in range(1, 8):
            pack_copy(k).start()
        weights_1(0)

    def cleared(*refs):
        for ref in refs:

            @pl.loop(0, ref.shape[0] // 16)
            def _(i):
                ref[row_block(i, 16), :] = jnp.zeros((16, ref.shape[1]), F32)

    g_vec[...] = jnp.zeros_like(g_vec)
    g_tab[...] = jnp.zeros_like(g_tab)
    codew[...] = jnp.zeros_like(codew)

    if linked:
        weights_2(0)
        for sec in range(1, 4):
            weights_1(sec)
        for k in range(1, 8):
            pack_arrival(k).wait_recv()
        place_vectors()
        weights_3(0)
        weights_4(0)

    def vector(b, kind, width=D):
        return vec[b * 8 + kind : b * 8 + kind + 1, :width]

    def add_vec(b, kind, part):
        g_vec[b, kind, :, : part.shape[1]] += part

    def windowed(rows, count):
        return jnp.where(real_places(count), winf[rows, :], 0.0).astype(BF)

    def attention_forward(b, n, x, out, hook):
        lanes = head_of_lane()

        @pl.loop(0, CELLS // TILE)
        def _(t):
            rows = row_block(t, TILE)
            xhat, _ = standardized(x[rows, :].astype(F32))
            canvf[rows, :] = xhat * vector(b, 0) + vector(b, 1)

        to_windows(canvf, winf, SHIFT * b)
        to_windows(code.at[n], codew, SHIFT * b)

        @pl.loop(0, 4)
        def _(t):
            rows = row_block(t, 256)
            hq = windowed(rows, 256)
            hqw[n, rows, :] = hq
            for part in range(3):
                cols = slice(part * D, (part + 1) * D)
                acc = nn(hq, wat[b, :, cols]) + vec[b * 8 + 6 : b * 8 + 7, cols]
                if part == 0:
                    acc = acc * SCALE
                qkv[n, rows, cols] = acc.astype(BF)

        hook(0)

        @pl.loop(0, WINDOWS)
        def _(w):
            rows = row_block(w, PLACES)
            cells = codew[rows, :]
            region = (cells >> 1) * b
            pad = (cells & 1).astype(F32)
            lane = lax.broadcasted_iota(jnp.int32, (PLACES, 128), 1)
            same = jnp.where(lane == region, 1.0, 0.0)
            left = jnp.where(lane == 127, 1.0 - pad, same).astype(BF)
            right = jnp.where(lane == 127, -pad, same).astype(BF)
            agree = nt(left, jnp.concatenate([right, right], axis=0))
            mask = jnp.where(agree > 0.5, 0.0, MASKED)
            mask = jnp.concatenate([mask, mask], axis=1)
            for g in range(GROUPS):
                q = qkv[n, rows, g * 128 : (g + 1) * 128]
                k = qkv[n, rows, D + g * 128 : D + (g + 1) * 128]
                v = qkv[n, rows, 2 * D + g * 128 : 2 * D + (g + 1) * 128]
                s = nt(k, by_head(q, lanes)) + bias[b, g] + mask
                e = jnp.exp(s - jnp.max(s, axis=0, keepdims=True))
                p = (e * (1.0 / jnp.sum(e, axis=0, keepdims=True))).astype(BF)
                probs[n, w * GROUPS + g] = p
                att[n, rows, g * 128 : (g + 1) * 128] = own_head(tn(p, v), lanes).astype(BF)

        hook(1)

        @pl.loop(0, 4)
        def _(t):
            rows = row_block(t, 256)
            winf[rows, :] = nn(att[n, rows, :], wat[b, :, 3 * D :])

        to_canvas(winf, canvf, SHIFT * b)

        @pl.loop(0, CELLS // TILE)
        def _(t):
            rows = row_block(t, TILE)
            out[rows, :] = (x[rows, :].astype(F32) + (canvf[rows, :] + vector(b, 2))).astype(BF)

    def mlp_forward(b, n, x, out, hook):
        @pl.loop(0, CELLS // TILE)
        def _(t):
            rows = row_block(t, TILE)
            xhat, _ = standardized(x[rows, :].astype(F32))
            hq2[n, rows, :] = (xhat * vector(b, 3) + vector(b, 4)).astype(BF)

        @pl.loop(0, FF // 256)
        def _(i):
            cols = pl.ds(pl.multiple_of(i * 256, 256), 256)
            pre = nn(hq2[n], fc1[b, :, cols]) + vec[b * 8 + 7 : b * 8 + 8, cols]
            for at in range(0, CELLS, 16):
                h, dg = gelu_parts(pre[at : at + 16])
                hid[n, at : at + 16, cols] = h.astype(BF)
                dgelu[n, at : at + 16, cols] = dg.astype(BF)

        hook(0)
        total = nn(hid[n], fc2[b])
        for at in range(0, CELLS, TILE):
            rows = slice(at, at + TILE)
            out[rows, :] = (x[rows, :].astype(F32) + (total[rows] + vector(b, 5))).astype(BF)

    def norm_backward(b, kind, x, gz, out):
        @pl.loop(0, CELLS // TILE)
        def _(t):
            rows = row_block(t, TILE)
            xhat, rs = standardized(x[rows, :].astype(F32))
            gn = canvf[rows, :]
            gzf = gz[rows, :].astype(F32)
            add_vec(b, kind, by_eights(gn * xhat))
            add_vec(b, kind + 1, by_eights(gn))
            add_vec(b, 5 if kind else 2, by_eights(gzf))
            g = gn * vector(b, kind)
            mg = jnp.mean(g, axis=-1, keepdims=True)
            mgx = jnp.mean(g * xhat, axis=-1, keepdims=True)
            out[rows, :] = (gzf + rs * (g - mg - xhat * mgx)).astype(BF)

    def mlp_backward(b, n, x, gz, out, free_out, hook):
        wide_t[0, :, :CELLS] = hq2[n].T
        wide_t[1, :, :CELLS] = gz[...].T

        @pl.loop(0, FF // 256)
        def _(i):
            cols = pl.ds(pl.multiple_of(i * 256, 256), 256)
            gh = nt(gz[...], fc2[b, cols, :])
            sums = jnp.zeros((8, 256), F32)
            for at in range(0, CELLS, 16):
                gp = (gh[at : at + 16] * dgelu[n, at : at + 16, cols].astype(F32)).astype(BF)
                dgelu[n, at : at + 16, cols] = gp
                sums = sums + by_eights(gp.astype(F32))
            g_vec[b, 7, :, cols] += sums
            g_fc1[:, cols] += nn(wide_t[0, :, :CELLS], dgelu[n, :, cols])
            g_fc2t[:, cols] += nn(wide_t[1, :, :CELLS], hid[n, :, cols])

        hook(0)
        canvf[...] = nt(dgelu[n], fc1[b])
        free_out()
        norm_backward(b, 3, x, gz, out)

    def attention_backward(b, n, x, gz, out, free_out, hook):
        lanes = head_of_lane()

        @pl.loop(0, CELLS // TILE)
        def _(t):
            rows = row_block(t, TILE)
            canvf[rows, :] = gz[rows, :].astype(F32)

        to_windows(canvf, winf, SHIFT * b)

        @pl.loop(0, 4)
        def _(t):
            rows = row_block(t, 256)
            gzw[rows, :] = windowed(rows, 256)

        g_proj[...] += tn(att[n], gzw[...])

        @pl.loop(0, 4)
        def _(t):
            rows = row_block(t, 256)
            go[rows, :] = nt(gzw[rows, :], wat[b, :, 3 * D :]).astype(BF)

        hook(0)

        @pl.loop(0, WINDOWS)
        def _(w):
            rows = row_block(w, PLACES)
            for g in range(GROUPS):
                at = [slice(part * D + g * 128, part * D + (g + 1) * 128) for part in range(3)]
                q, k, v = (qkv[n, rows, cols] for cols in at)
                go_wide = by_head(go[rows, at[0]], lanes)
                p_low = probs[n, w * GROUPS + g]
                p = p_low.astype(F32)
                pd = p * nt(v, go_wide)
                ds = (pd - p * jnp.sum(pd, axis=0, keepdims=True)).astype(BF)
                g_tab[b, :, g * 256 : (g + 1) * 256] += ds.astype(F32)
                gqkv[rows, at[0]] = (own_head(tn(ds, k), lanes) * SCALE).astype(BF)
                gqkv[rows, at[1]] = nn(ds, by_head(q, lanes)).astype(BF)
                gqkv[rows, at[2]] = nn(p_low, go_wide).astype(BF)

        hook(1)

        @pl.loop(0, 4)
        def _(t):
            rows = row_block(t, 256)
            gq = gqkv[rows, :]
            add_vec(b, 6, by_eights(gq.astype(F32)))
            winf[rows, :] = nt(gq, wat[b, :, : 3 * D])

        to_canvas(winf, canvf, SHIFT * b)
        free_out()
        norm_backward(b, 0, x, gz, out)

    def attention_weights(n):
        wide_t[0] = hqw[n].T
        for part in range(3):
            cols = slice(part * D, (part + 1) * D)
            g_qkv[:, cols] += nn(wide_t[0], gqkv[:, cols])

    def partner(k):
        x, y = me % 2, me // 2
        return 2 * (1 - y if k & 2 else y) + (1 - x if k & 1 else x)

    def act_copies(n):
        away = [
            remote(
                buf.at[partner(k), n],
                r.act_hbm.at[me, n],
                r.act_send.at[k - 1, n],
                r.act_recv.at[k - 1, n],
                {"pipe": partner(k)},
            )
            for k in (2, 1, 3)
        ]
        return away, pltpu.make_async_copy(buf.at[me, n], r.act_hbm.at[me, n], r.local_sem.at[0, n])

    def send_acts(n):
        away, local = act_copies(n)
        for copy in away:
            copy.start()
        local.start()

    def acts_sent(n):
        away, local = act_copies(n)
        for copy in away:
            copy.wait_send()
        local.wait()

    def push(s, n, start):
        src = buf.at[s, n]
        dst = r.igrad_hbm.at[me, n]
        local = pltpu.make_async_copy(src, dst, r.local_sem.at[1, n])
        away = remote(src, dst, r.send_sem.at[s, n], r.recv_sem.at[me, n], {"pipe": s})

        @pl.when(me == s)
        def _():
            local.start() if start else local.wait()

        @pl.when(me != s)
        def _():
            away.start() if start else away.wait_send()

    def arrived(k, n):
        sender = partner(k)
        got = r.act_hbm.at[sender, n]
        remote(got, got, r.act_send.at[k - 1, n], r.act_recv.at[k - 1, n], {"pipe": sender}).wait_recv()
        got = r.igrad_hbm.at[sender, n]
        remote(got, got, r.send_sem.at[0, n], r.recv_sem.at[sender, n], {"pipe": sender}).wait_recv()

    attention_stash = ((hqw, r.h_hqw), (qkv, r.h_qkv), (probs, r.h_probs), (att, r.h_att))
    mlp_stash = ((hq2, r.h_hq2), (hid, r.h_hid), (dgelu, r.h_dgelu))

    def stash(sec, n, back):
        pairs = mlp_stash if sec else attention_stash
        return [
            pltpu.make_async_copy(*((far.at[n], near.at[n]) if back else (near.at[n], far.at[n])), r.st_sem.at[sec, n, i])
            for i, (near, far) in enumerate(pairs)
        ]

    def load(src, n):
        return pltpu.make_async_copy(src.at[me, n], inb.at[n], r.in_sem.at[n])

    def start(copies):
        for copy in copies:
            copy.start()

    def wait(copies):
        for copy in copies:
            copy.wait()

    steps = (step_1, step_2, step_3, step_4, step_5)
    schedule = {
        (2, 0, 0): ((2, 3),),
        (2, 1, 1): ((3, 3),),
        (1, 0, 0): ((2, 2),),
        (1, 1, 0): ((4, 3),),
        (0, 0, 0): ((3, 2), (2, 1), (5, 3)),
        (0, 0, 1): ((4, 2),),
        (0, 1, 0): ((5, 2),),
        (0, 1, 1): ((3, 1),),
    }
    after = {3: ((1, 3),), 2: ((1, 2),), 1: ((1, 1),), 0: ()}
    weight_steps = (weights_1, weights_2, weights_3, weights_4) if linked else ()
    gathering = {
        (0, 0): ((2, 1),),
        (0, 1): ((2, 2), (2, 3), (3, 1)),
        (0, 3): ((4, 1), (3, 2)),
        (1, 3): ((4, 2),),
        (2, 0): ((3, 3),),
        (2, 3): ((4, 3),),
    }

    codes = [pltpu.make_async_copy(r.code_hbm, code, r.code_sem.at[0])]
    start(codes)
    start([load(r.x_hbm, n) for n in range(canvases)])
    wait(codes)

    @pl.loop(0, canvases)
    def _(n):
        def gather(sec, i):
            todo = gathering.get((sec, i), ())
            if linked and todo:

                @pl.when(n == 0)
                def _():
                    for step, of in todo:
                        weight_steps[step - 1](of)

        load(r.x_hbm, n).wait()
        x = inb.at[n]
        for s in range(4):
            if s >= 2:
                wait(stash(s - 2, n, False))
            forward = mlp_forward if s % 2 else attention_forward
            forward(s // 2, n, x, buf.at[s, n], functools.partial(gather, s))
            x = buf.at[s, n]
            if s == 3:
                send_acts(n)
            if s < 2:
                start(stash(s, n, False))
            if s == 0:
                load(r.cot_hbm, n).start()
            gather(s, 3)

    for s in (3, 2, 1, 0):
        cleared(*((g_fc1, g_fc2t) if s % 2 else (g_qkv, g_proj)))

        @pl.loop(0, canvases)
        def _(n):
            def hook(i):
                for at in range(2):
                    todo = schedule.get((s, at, i), ())
                    if linked and todo:

                        @pl.when(n == (canvases - 1 if at else 0))
                        def _():
                            for step, of in todo:
                                steps[step - 1](of)

            if s == 3:
                load(r.cot_hbm, n).wait()
            if s == 0:
                load(r.x_hbm, n).wait()
            if s < 2:
                wait(stash(s, n, True))
            x = buf.at[s - 1, n] if s else inb.at[n]
            gz = inb.at[n] if s == 3 else buf.at[s + 1, n]
            backward = mlp_backward if s % 2 else attention_backward
            free_out = functools.partial(acts_sent, n) if s == 3 else lambda: None
            backward(s // 2, n, x, gz, buf.at[s, n], free_out, hook)
            if s % 2 == 0:
                attention_weights(n)
            if s == 2:
                push(3, n, True)
            if s:
                if s < 3:
                    push(s, n, True)
            else:

                @pl.when(n < canvases - 1)
                def _():
                    push(0, n, True)

            if s == 3:
                load(r.x_hbm, n).start()
            if s >= 2:
                start(stash(s - 2, n, True))

        if linked:
            for step, of in after[s]:
                steps[step - 1](of)
        else:
            whole = ((g_fc1, r.f_fc1), (g_fc2t, r.f_fc2t)) if s % 2 else ((g_qkv, r.f_qkv), (g_proj, r.f_proj))
            copies = [pltpu.make_async_copy(a, o.at[s // 2], r.go_sem.at[s, i]) for i, (a, o) in enumerate(whole)]
            start(copies)
            wait(copies)

    if linked:
        step_1(0)
        step_4(1)
        step_2(0)
    push(0, canvases - 1, True)
    if linked:
        step_5(1)
        smalls_sent(1)
        step_3(0)
        step_4(0)
        step_5(0)
        reductions_done()
        weights_sent()
        for k in range(1, 8):
            pack_copy(k).wait_send()
    for k in range(1, 4):
        for n in range(canvases):
            arrived(k, n)
    for s in range(4):
        for n in range(canvases):
            push(s, n, False)


def compute(linked, operands):
    canvases = operands["x_hbm"].shape[1]
    shape = jax.ShapeDtypeStruct
    hbm = pl.BlockSpec(memory_space=pl.ANY)
    vmem = pl.BlockSpec(memory_space=pltpu.VMEM)
    dma = pltpu.SemaphoreType.DMA
    full = {
        "wat": ((2, D, 4 * D), BF),
        "fc1": ((2, D, FF), BF),
        "fc2": ((2, FF, D), BF),
        "vec": ((16, FF), F32),
    }
    grads = {
        "g_qkv": ((D, 3 * D), F32),
        "g_proj": ((D, D), F32),
        "g_fc1": ((D, FF), F32),
        "g_fc2t": ((D, FF), F32),
        "g_vec": ((2, 8, 8, FF), F32),
        "g_tab": ((2, PLACES, GROUPS * 256), F32),
    }
    outs = {"act_hbm": ((4, canvases, CELLS, D), BF), "igrad_hbm": ((4, canvases, CELLS, D), BF)}
    kept = {
        "hqw": ((canvases, WROWS, D), BF),
        "qkv": ((canvases, WROWS, 3 * D), BF),
        "probs": ((canvases, WINDOWS * GROUPS, PLACES, 256), BF),
        "att": ((canvases, WROWS, D), BF),
        "hq2": ((canvases, CELLS, D), BF),
        "hid": ((canvases, CELLS, FF), BF),
        "dgelu": ((canvases, CELLS, FF), BF),
    }
    outs |= {"h_" + name: kind for name, kind in kept.items()}
    scratch = kept | {
        "inb": ((canvases, CELLS, D), BF),
        "code": ((canvases, CELLS, 128), jnp.int32),
        "codew": ((WROWS, 128), jnp.int32),
        "buf": ((4, canvases, CELLS, D), BF),
        "canvf": ((CELLS, D), F32),
        "winf": ((WROWS, D), F32),
        "gzw": ((WROWS, D), BF),
        "go": ((WROWS, D), BF),
        "gqkv": ((WROWS, 3 * D), BF),
        "wide_t": ((2, D, WROWS), BF),
    }
    sems = {
        "in_sem": (canvases,),
        "code_sem": (1,),
        "st_sem": (2, canvases, 4),
        "local_sem": (2, canvases),
        "act_send": (3, canvases),
        "act_recv": (3, canvases),
        "send_sem": (4, canvases),
        "recv_sem": (4, canvases),
    }
    if linked:
        outs |= {
            "o_qkv": ((2, 48, 3 * D), F32),
            "o_proj": ((2, 48, D), F32),
            "o_fc1": ((2, 48, FF), F32),
            "o_fc2": ((2, 192, D), F32),
            "o_small": ((2, 8, 64, D), BF),
        }
        scratch |= full | grads
        scratch |= {
            "packs": ((8, 16, 256), BF),
            "l_qkv": ((48, 3 * D), F32),
            "l_proj": ((48, D), F32),
            "l_fc1": ((48, FF), F32),
            "l_fc2": ((192, D), F32),
        }
        for kind, rows in (("m_", MLP_ROWS), ("a_", ATT_ROWS)):
            scratch |= {
                kind + "st_a": ((4, rows, D), BF),
                kind + "rc_a": ((4, rows, D), BF),
                kind + "st_b": ((3, rows, D), BF),
                kind + "rc_b": ((3, rows, D), BF),
                kind + "st_c": ((rows, D), BF),
                kind + "rc_c": ((3, rows // 4, D), BF),
                kind + "fin": ((rows, D), BF),
            }
        sems |= {
            "sh_sem": (4, 2),
            "os_sem": (2,),
            "go_sem": (4, 2),
            "wz_send": (4, 2, 3),
            "wz_recv": (4, 2, 3),
            "wx_send": (4, 2, 3, 3),
            "wx_recv": (4, 2, 3, 3),
            "ws_send": (4, 2, 4),
            "ws_recv": (4, 2, 4),
            "pk_send": (7,),
            "pk_recv": (7,),
            "ra_send": (4,),
            "ra_recv": (4,),
            "rb_send": (4, 3),
            "rb_recv": (4, 3),
            "rc_send": (4, 3),
            "rc_recv": (4, 3),
            "rf_send": (4, 3),
            "rf_recv": (4, 3),
            "rs_send": (2, 7),
            "rs_recv": (2, 7),
        }
    else:
        for name in ("g_vec", "g_tab"):
            outs[name] = grads.pop(name)
        outs |= {name.replace("g_", "f_"): ((2,) + dims, F32) for name, (dims, _) in grads.items()}
        scratch |= grads
        sems["go_sem"] = (4, 2)
    in_vmem = set(full) | {"bias", "pack", "g_vec", "g_tab"}
    names = tuple(operands) + tuple(outs) + tuple(scratch) + tuple(sems)
    results = pl.pallas_call(
        functools.partial(kernel, names, linked, canvases),
        out_shape=tuple(shape(*o) for o in outs.values()),
        in_specs=[vmem if name in in_vmem else hbm for name in operands],
        out_specs=tuple(vmem if name in in_vmem else hbm for name in outs),
        scratch_shapes=[pltpu.VMEM(*v) for v in scratch.values()] + [dma(v) for v in sems.values()],
        compiler_params=pltpu.CompilerParams(
            vmem_limit_bytes=64 * 1024 * 1024 - 65536, collective_id=0, has_side_effects=True
        ),
    )(*operands.values())
    return dict(zip(outs, results))


def place_pairs():
    place = np.arange(PLACES)
    r, c = place // 8, place % 8
    index = (r[None, :] - r[:, None] + WIN - 1) * (2 * WIN - 1) + c[None, :] - c[:, None] + WIN - 1
    real = (r < WIN) & (c < WIN)
    return index, real[:, None] & real[None, :], real


def pair_onehot():
    index, both, _ = place_pairs()
    table = (2 * WIN - 1) ** 2
    hot = (np.where(both, index, -1).reshape(-1)[None, :] == np.arange(table)[:, None])
    return hot.astype(np.float32)


def body(
    inputs,
    cotangent,
    pad_mask,
    region_ids,
    norm1_gain,
    norm1_bias,
    qkv_weight,
    qv_bias,
    rel_table,
    proj_weight,
    proj_bias,
    norm2_gain,
    norm2_bias,
    fc1_weight,
    fc1_bias,
    fc2_weight,
    fc2_bias,
):
    owners = lax.axis_size("dp")
    linked = owners == 8
    mine = lax.axis_index("pipe")

    def own(a):
        return lax.dynamic_index_in_dim(a, mine, 0, keepdims=False)

    code = own(region_ids) * 2 + own(pad_mask)
    code = jnp.broadcast_to(code[:, :, None], code.shape + (128,))

    hot = pair_onehot()
    _, _, real = place_pairs()
    rel = lax.dot_general(
        rel_table.astype(BF), jnp.asarray(hot, BF), (((1,), (0,)), ((), ())), preferred_element_type=F32
    )
    rel = rel.reshape(2, GROUPS, 4, PLACES, PLACES).transpose(0, 1, 3, 2, 4)
    rel = jnp.where(jnp.asarray(real)[None, None, :, None, None], rel, MASKED)
    rel = rel.reshape(2, GROUPS, PLACES, 256)

    operands = {"x_hbm": inputs, "cot_hbm": cotangent, "code_hbm": code, "bias": rel}
    vectors = (norm1_gain, norm1_bias, proj_bias, norm2_gain, norm2_bias, fc2_bias, qv_bias, fc1_bias)
    sizes = [v.shape[1] for v in vectors]
    ends = np.cumsum([0] + sizes)
    if linked:
        pack = jnp.stack([jnp.pad(v, ((0, 0), (0, 256 - v.shape[1]))) for v in vectors], axis=1)
        operands |= {
            "pack": pack.reshape(16, 256).astype(BF),
            "s_qkv": qkv_weight,
            "s_proj": proj_weight,
            "s_fc1": fc1_weight,
            "s_fc2": fc2_weight,
        }
    else:

        def gathered(a):
            return lax.all_gather(a.astype(BF), "dp", axis=1, tiled=True)

        packed = lax.all_gather(jnp.concatenate(vectors, axis=1).astype(BF), "dp", axis=1)
        parts = [packed[:, :, a:b].reshape(2, -1).astype(F32) for a, b in zip(ends[:-1], ends[1:])]
        qv = parts[6]
        parts[6] = jnp.concatenate([qv[:, :D], jnp.zeros_like(qv[:, :D]), qv[:, D:]], axis=1)
        vec = jnp.stack([jnp.pad(p, ((0, 0), (0, FF - p.shape[1]))) for p in parts], axis=1)
        operands |= {
            "wat": jnp.concatenate([gathered(qkv_weight), gathered(proj_weight)], axis=2),
            "fc1": gathered(fc1_weight),
            "fc2": gathered(fc2_weight),
            "vec": vec.reshape(16, FF),
        }

    out = compute(linked, operands)

    def to_owners(g):
        shared = lax.psum_scatter(g, "dp", scatter_dimension=1, tiled=True)
        return lax.psum(shared, "pipe")

    if linked:
        small = out["o_small"]
        g_tab = jnp.concatenate([small[:, :, :8], small[:, :, 8:16]], axis=3).reshape(2, PLACES, GROUPS * 256)
        g_vec = jnp.concatenate([small[:, :, 16 + 8 * j : 24 + 8 * j] for j in range(4)], axis=3)
    else:
        g_tab, g_vec = out["g_tab"], out["g_vec"]

    g_vec = jnp.sum(g_vec.astype(F32), axis=2)
    kinds = [g_vec[:, i] for i in range(8)]
    qv_sum = jnp.concatenate([kinds[6][:, :D], kinds[6][:, 2 * D : 3 * D]], axis=1)
    rows = [kinds[0], kinds[1], kinds[2], kinds[3], kinds[4], kinds[5], qv_sum, kinds[7]]
    if linked:
        at = lax.axis_index("dp")
        small = [lax.dynamic_slice_in_dim(v, at * n, n, 1) for v, n in zip(rows, sizes)]
    else:
        rows = [v[:, : n * owners].reshape(2, -1, n) for v, n in zip(rows, sizes)]
        g_small = to_owners(jnp.concatenate(rows, axis=2))[:, 0]
        small = [g_small[:, a:b] for a, b in zip(ends[:-1], ends[1:])]

    pairs = g_tab.reshape(2, PLACES, HEADS, PLACES).transpose(0, 2, 1, 3)
    pairs = pairs.reshape(2, HEADS, PLACES * PLACES)
    g_table = lax.dot_general(
        jnp.broadcast_to(jnp.asarray(hot, pairs.dtype), (2,) + hot.shape),
        pairs,
        (((2,), (2,)), ((0,), (0,))),
        precision=None if linked else lax.Precision.HIGHEST,
        preferred_element_type=F32,
    )
    if linked:
        big = [out[name] for name in ("o_qkv", "o_proj", "o_fc1", "o_fc2")]
    else:
        g_table = lax.psum(g_table, ("pipe", "dp"))
        big = [to_owners(out[name]) for name in ("f_qkv", "f_proj", "f_fc1")]
        big.append(to_owners(out["f_fc2t"].transpose(0, 2, 1)))

    return (
        out["act_hbm"][None],
        out["igrad_hbm"][None],
        small[0],
        small[1],
        big[0],
        small[6],
        g_table,
        big[1],
        small[2],
        small[3],
        small[4],
        big[2],
        small[7],
        big[3],
        small[5],
    )


def solution(mesh):
    cols = P(None, "dp")
    rows = P(None, "dp", None)
    return jax.shard_map(
        body,
        mesh=mesh,
        in_specs=(
            P(None, "dp", None, None),
            P(None, "dp", None, None),
            rows,
            rows,
            cols,
            cols,
            rows,
            cols,
            P(),
            rows,
            cols,
            cols,
            cols,
            rows,
            cols,
            rows,
            cols,
        ),
        out_specs=(
            P("pipe", None, "dp", None, None),
            P("pipe", None, "dp", None, None),
            cols,
            cols,
            rows,
            cols,
            P(),
            rows,
            cols,
            cols,
            cols,
            rows,
            cols,
            rows,
            cols,
        ),
        check_vma=False,
    )
```

```python
import functools
import types

import jax
import jax.numpy as jnp
import numpy as np
from jax import lax
from jax.experimental import pallas as pl
from jax.experimental.pallas import tpu as pltpu
from jax.sharding import PartitionSpec as P

HEADS = 12
WIN = 7
SHIFT = 3
GRID = 28
CELLS = 784
D = 384
FF = 1536
HEAD = 32
SIDE = 4
WINDOWS = 16
PLACES = 64
WROWS = WINDOWS * PLACES
GROUPS = 3
TILE = 112
SCALE = HEAD**-0.5
NORM_EPS = 1e-05
MASKED = -1e30
BF = jnp.bfloat16
F32 = jnp.float32

RSQRT_2 = 1.0 / np.sqrt(2.0)
PHI_0 = 1.0 / np.sqrt(2.0 * np.pi)


def nn(a, b):
    return lax.dot_general(a, b, (((1,), (0,)), ((), ())), preferred_element_type=F32)


def nt(a, b):
    return lax.dot_general(a, b, (((1,), (1,)), ((), ())), preferred_element_type=F32)


def tn(a, b):
    return lax.dot_general(a, b, (((0,), (0,)), ((), ())), preferred_element_type=F32)


def segments(shift):
    runs = []
    for wr in range(SIDE):
        for r in range(WIN):
            row = (wr * WIN + r + shift) % GRID
            for wc in range(SIDE):
                col = (wc * WIN + shift) % GRID
                place = (wr * SIDE + wc) * PLACES + r * 8
                first = min(WIN, GRID - col)
                runs.append((row * GRID + col, place, first))
                if first < WIN:
                    runs.append((row * GRID, place + first, WIN - first))
    return runs


def to_windows(src, dst, shift):
    for cell, place, count in segments(shift):
        dst[pl.ds(place, count), :] = src[pl.ds(cell, count), :]


def to_canvas(src, dst, shift):
    for cell, place, count in segments(shift):
        dst[pl.ds(cell, count), :] = src[pl.ds(place, count), :]


def row_block(t, size):
    return pl.ds(pl.multiple_of(t * size, 16), size)


def standardized(v):
    centered = v - jnp.mean(v, axis=-1, keepdims=True)
    spread = jnp.mean(centered * centered, axis=-1, keepdims=True)
    rs = lax.rsqrt(spread + NORM_EPS)
    return centered * rs, rs


def by_eights(v):
    return jnp.sum(v.reshape(v.shape[0] // 8, 8, v.shape[1]), axis=0)


def gelu_parts(x):
    cdf = 0.5 + 0.5 * lax.erf(x * RSQRT_2)
    return x * cdf, cdf + x * (jnp.exp(-0.5 * x * x) * PHI_0)


def real_places(rows):
    place = lax.broadcasted_iota(jnp.int32, (rows, 1), 0)
    return ((place & 7) < WIN) & (((place >> 3) & 7) < WIN)


def head_of_lane():
    return lax.broadcasted_iota(jnp.int32, (PLACES, 128), 1) >> 5


def by_low(x, lanes):
    zero = jnp.zeros_like(x)
    return jnp.concatenate([jnp.where((lanes & 1) == h, x, zero) for h in range(2)], axis=0)


def by_high(x, lanes):
    zero = jnp.zeros_like(x)
    return jnp.concatenate([jnp.where((lanes >> 1) == h, x, zero) for h in range(2)], axis=0)


def own_low(wide, lanes):
    return jnp.where((lanes & 1) == 0, wide[:PLACES], wide[PLACES:])


def own_high(wide, lanes):
    return jnp.where((lanes >> 1) == 0, wide[:PLACES], wide[PLACES:])


MESH = pl.DeviceIdType.MESH
ATT_ROWS = 256
MLP_ROWS = 384
SMALL = 192


def kernel(names, linked, canvases, *refs):
    r = types.SimpleNamespace(**dict(zip(names, refs)))
    me = lax.axis_index("pipe")
    inb, code, codew, buf = r.inb, r.code, r.codew, r.buf
    hqw, qkv, probs, att = r.hqw, r.qkv, r.probs, r.att
    hq2, hid, dgelu = r.hq2, r.hid, r.dgelu
    canvf, winf, gzw, gqkv, go = r.canvf, r.winf, r.gzw, r.gqkv, r.go
    g_qkv, g_proj, g_fc1, g_fc2, g_vec, g_tab = r.g_qkv, r.g_proj, r.g_fc1, r.g_fc2, r.g_vec, r.g_tab
    wat, fc1, fc2, vec, bias = r.wat, r.fc1, r.fc2, r.vec, r.bias
    if linked:
        d = lax.axis_index("dp")
        z, c = d // 2, d % 2
        sibling = {"dp": 2 * z + 1 - c}

    def z_peer(k):
        return {"dp": 2 * lax.rem(z + k, 4) + c}

    def pipe_peer(k):
        return {"pipe": lax.rem(me + k, 4)}

    def dp_peer(k):
        return {"dp": lax.rem(d + k, 8)}

    def remote(src, dst, send, recv, device):
        return pltpu.make_async_remote_copy(
            src_ref=src, dst_ref=dst, send_sem=send, recv_sem=recv, device_id=device, device_id_type=MESH
        )

    barrier = pltpu.get_barrier_semaphore()
    partners = [pipe_peer(k) for k in range(1, 4)]
    if linked:
        partners += [dp_peer(k) for k in range(1, 8)]
    for partner in partners:
        pl.semaphore_signal(barrier, inc=1, device_id=partner, device_id_type=MESH)

    full = ((wat,), (fc1, fc2), (wat,), (fc1, fc2))

    def owner_back(k):
        return 2 * lax.rem(z + 4 - k, 4) + c

    def shard(sec, a, owner):
        h = 192 if a else 48
        return full[sec][a].at[sec // 2, pl.ds(pl.multiple_of(owner * h, 16), h), :]

    def part(sec, a, owner, place):
        if a:
            return fc2.at[sec // 2, pl.ds(pl.multiple_of(owner * 192 + place * 48, 16), 48), :]
        rows = pl.ds(pl.multiple_of(owner * 48, 16), 48)
        return full[sec][0].at[sec // 2, rows, pl.ds(pl.multiple_of(place * D, 128), D)]

    def to_z(sec, a, k):
        own = part(sec, a, d, me)
        return remote(own, own, r.wz_send.at[sec, a, k - 1], r.wz_recv.at[sec, a, k - 1], z_peer(k))

    def to_places(sec, a, k, j):
        got = part(sec, a, owner_back(k), me)
        return remote(
            got, got, r.wx_send.at[sec, a, k - 1, j - 1], r.wx_recv.at[sec, a, k - 1, j - 1], pipe_peer(j)
        )

    def to_sibling(sec, a, k):
        block = shard(sec, a, owner_back(k))
        return remote(block, block, r.ws_send.at[sec, a, k], r.ws_recv.at[sec, a, k], sibling)

    def weights_1(sec):
        for a in range(len(full[sec])):
            for k in range(1, 4):
                to_z(sec, a, k).start()
            to_sibling(sec, a, 0).start()

    def weights_2(sec):
        for k in range(1, 4):
            for a in range(len(full[sec])):
                got = part(sec, a, owner_back(k), me)
                remote(got, got, r.wz_send.at[sec, a, k - 1], r.wz_recv.at[sec, a, k - 1], z_peer(k)).wait_recv()
                for j in range(1, 4):
                    to_places(sec, a, k, j).start()

    def weights_3(sec):
        for k in range(1, 4):
            for a in range(len(full[sec])):
                for j in range(1, 4):
                    got = part(sec, a, owner_back(k), lax.rem(me + 4 - j, 4))
                    remote(
                        got, got, r.wx_send.at[sec, a, k - 1, j - 1], r.wx_recv.at[sec, a, k - 1, j - 1], pipe_peer(j)
                    ).wait_recv()
                to_sibling(sec, a, k).start()

    def weights_4(sec):
        for k in range(4):
            for a in range(len(full[sec])):
                block = shard(sec, a, 2 * lax.rem(z + 4 - k, 4) + 1 - c)
                remote(block, block, r.ws_send.at[sec, a, k], r.ws_recv.at[sec, a, k], sibling).wait_recv()

    def weights_sent():
        for sec in range(4):
            for a in range(len(full[sec])):
                for k in range(4):
                    to_sibling(sec, a, k).wait_send()
                    if k:
                        to_z(sec, a, k).wait_send()
                        for j in range(1, 4):
                            to_places(sec, a, k, j).wait_send()

    def pack_copy(k):
        return remote(
            r.packs.at[d], r.packs.at[d], r.pk_send.at[k - 1], r.pk_recv.at[k - 1], dp_peer(k)
        )

    def pack_arrival(k):
        slot = r.packs.at[lax.rem(d + 8 - k, 8)]
        return remote(slot, slot, r.pk_send.at[k - 1], r.pk_recv.at[k - 1], dp_peer(k))

    def place_vectors():
        kind = lax.broadcasted_iota(jnp.int32, (16, 256), 0) & 7
        lane = lax.broadcasted_iota(jnp.int32, (16, 256), 1)
        vec[...] = jnp.zeros_like(vec)
        for width, kinds in ((48, kind < 6), (96, kind == 6), (192, kind == 7)):
            for owner in range(8):
                at = owner * width
                if width == 96 and owner >= 4:
                    at += D
                start = at // 128 * 128
                part = jnp.where(kinds & (lane < width), r.packs[owner].astype(F32), 0.0)
                if at > start:
                    part = pltpu.roll(part, at - start, 1)
                vec[:, start : start + 256] += part

    def pieces(sec, owner):
        b = sec // 2
        out = []

        def matrix(ref, h):
            for t in range(h // 48):
                rows = pl.ds(pl.multiple_of(owner * h + t * 48, 16), 48)
                for j in range(ref.shape[1] // D):
                    load = functools.partial(lambda ref, rows, j: ref[rows, j * D : (j + 1) * D], ref, rows, j)
                    out.append((len(out) * 48, 48, load))

        def small():
            parts = [g_tab[b, pl.ds(pl.multiple_of(owner * 16, 16), 16), :]]
            parts += [g_vec[b, owner, :, j * D : (j + 1) * D] for j in range(4)]
            return jnp.concatenate(parts + [jnp.zeros((16, D), F32)], axis=0)

        if sec % 2:
            matrix(g_fc1, 48)
            matrix(g_fc2, 192)
        else:
            matrix(g_qkv, 48)
            matrix(g_proj, 48)
            out.append((SMALL, 64, small))
        return out

    def reduce_refs(sec):
        kind = "m" if sec % 2 else "a"
        return types.SimpleNamespace(
            **{n: getattr(r, kind + "_" + n) for n in ("st_a", "rc_a", "st_b", "rc_b", "st_c", "rc_c", "fin")}
        )

    def step_1(sec):
        q = reduce_refs(sec)
        if sec < 2:
            copy_a(sec + 2).wait_send()
            for k in range(1, 4):
                copy_b(sec + 2, k).wait_send()
                copy_c(sec + 2, k).wait_send()
        for k in range(4):
            i = lax.rem(z + k, 4)
            kept = q.st_b.at[k - 1] if k else q.st_c
            for row, rows, load in pieces(sec, 2 * i + 1 - c):
                q.st_a[i, row : row + rows, :] = load().astype(BF)
            for row, rows, load in pieces(sec, 2 * i + c):
                kept[row : row + rows, :] = load().astype(BF)
        copy_a(sec).start()

    def copy_a(sec):
        q = reduce_refs(sec)
        return remote(q.st_a, q.rc_a, r.ra_send.at[sec], r.ra_recv.at[sec], sibling)

    def copy_b(sec, k):
        q = reduce_refs(sec)
        return remote(
            q.st_b.at[k - 1], q.rc_b.at[k - 1], r.rb_send.at[sec, k - 1], r.rb_recv.at[sec, k - 1], z_peer(k)
        )

    def step_2(sec):
        q = reduce_refs(sec)
        copy_a(sec).wait_recv()
        for k in (1, 2, 3, 0):
            i = lax.rem(z + k, 4)
            kept = q.st_b.at[k - 1] if k else q.st_c
            for row in range(0, kept.shape[0], 64):
                at = slice(row, row + 64)
                kept[at, :] = (kept[at, :].astype(F32) + q.rc_a[i, at, :].astype(F32)).astype(BF)
            if k:
                copy_b(sec, k).start()

    def quarter(sec, ref, who):
        rows = (MLP_ROWS if sec % 2 else ATT_ROWS) // 4
        return ref.at[pl.ds(pl.multiple_of(who * rows, 16), rows), :]

    def copy_c(sec, k):
        q = reduce_refs(sec)
        return remote(
            quarter(sec, q.st_c, lax.rem(me + k, 4)),
            q.rc_c.at[k - 1],
            r.rc_send.at[sec, k - 1],
            r.rc_recv.at[sec, k - 1],
            pipe_peer(k),
        )

    def step_3(sec):
        q = reduce_refs(sec)
        for k in range(1, 4):
            copy_b(sec, k).wait_recv()
        for row in range(0, q.st_c.shape[0], 64):
            at = slice(row, row + 64)
            total = q.st_c[at, :].astype(F32)
            for k in range(3):
                total = total + q.rc_b[k, at, :].astype(F32)
            q.st_c[at, :] = total.astype(BF)
        for k in range(1, 4):
            copy_c(sec, k).start()

    def copy_f(sec, k):
        q = reduce_refs(sec)
        own = quarter(sec, q.fin, me)
        return remote(own, own, r.rf_send.at[sec, k - 1], r.rf_recv.at[sec, k - 1], pipe_peer(k))

    def step_4(sec):
        q = reduce_refs(sec)
        for k in range(1, 4):
            copy_c(sec, k).wait_recv()
            if sec < 2:
                copy_f(sec + 2, k).wait_send()
        total = quarter(sec, q.st_c, me)[...].astype(F32)
        for k in range(3):
            total = total + q.rc_c[k].astype(F32)
        quarter(sec, q.fin, me)[...] = total.astype(BF)
        for k in range(1, 4):
            copy_f(sec, k).start()

    def copy_s(b, k):
        rows = pl.ds(SMALL, 64)
        return remote(
            r.a_fin.at[rows, :], r.o_small.at[b, d], r.rs_send.at[b, k - 1], r.rs_recv.at[b, k - 1], dp_peer(k)
        )

    def own_small(b):
        return pltpu.make_async_copy(r.a_fin.at[pl.ds(SMALL, 64), :], r.o_small.at[b, d], r.os_sem.at[b])

    def outputs(sec):
        pairs = ((r.l_fc1, r.o_fc1), (r.l_fc2, r.o_fc2)) if sec % 2 else ((r.l_qkv, r.o_qkv), (r.l_proj, r.o_proj))
        return [
            pltpu.make_async_copy(ref, out.at[sec // 2], r.go_sem.at[sec, i]) for i, (ref, out) in enumerate(pairs)
        ]

    def step_5(sec):
        q = reduce_refs(sec)
        b = sec // 2
        for k in range(1, 4):
            got = quarter(sec, q.fin, lax.rem(me + 4 - k, 4))
            remote(got, got, r.rf_send.at[sec, k - 1], r.rf_recv.at[sec, k - 1], pipe_peer(k)).wait_recv()
        if sec % 2 == 0:
            for k in range(1, 8):
                copy_s(b, k).start()
            own_small(b).start()
        if sec < 2:
            for out in outputs(sec + 2):
                out.wait()
        row = 0
        for ref in (r.l_fc1, r.l_fc2) if sec % 2 else (r.l_qkv, r.l_proj):
            for t in range(ref.shape[0] // 48):
                for j in range(ref.shape[1] // D):
                    ref[t * 48 : (t + 1) * 48, j * D : (j + 1) * D] = q.fin[row : row + 48, :].astype(F32)
                    row += 48
        for out in outputs(sec):
            out.start()

    def smalls_sent(b):
        for k in range(1, 8):
            copy_s(b, k).wait_send()
        own_small(b).wait()

    def reductions_done():
        for sec in (1, 0):
            copy_a(sec).wait_send()
            for k in range(1, 4):
                copy_b(sec, k).wait_send()
                copy_c(sec, k).wait_send()
                copy_f(sec, k).wait_send()
        for sec in range(2):
            for out in outputs(sec):
                out.wait()
        smalls_sent(0)
        for b in range(2):
            for k in range(1, 8):
                rows = pl.ds(SMALL, 64)
                remote(
                    r.a_fin.at[rows, :],
                    r.o_small.at[b, lax.rem(d + 8 - k, 8)],
                    r.rs_send.at[b, k - 1],
                    r.rs_recv.at[b, k - 1],
                    dp_peer(k),
                ).wait_recv()

    if linked:
        lands = ((r.s_qkv, g_qkv, wat, 0), (r.s_proj, g_proj, wat, 3 * D), (r.s_fc1, g_fc1, fc1, 0), (r.s_fc2, g_fc2, fc2, 0))

        def landing(i, b):
            src, dst, _, _ = lands[i]
            h, n = src.shape[1:]
            return pltpu.make_async_copy(
                src.at[b], dst.at[pl.ds(192 * b, h), pl.ds(0, n)], r.sh_sem.at[i, b]
            )

        for i in range(4):
            for b in range(2):
                landing(i, b).start()
        r.packs[d] = r.pack[...]
        for i, (src, dst, ref, col) in enumerate(lands):
            h, n = src.shape[1:]
            for b in range(2):
                landing(i, b).wait()
                for t in range(0, h, 48):
                    rows = pl.ds(pl.multiple_of(d * h + t, 16), 48)
                    ref[b, rows, col : col + n] = dst[192 * b + t : 192 * b + t + 48, :n].astype(BF)
    pl.semaphore_wait(barrier, len(partners))
    if linked:
        for k in range(1, 8):
            pack_copy(k).start()
        weights_1(0)

    def cleared(*refs):
        for ref in refs:

            @pl.loop(0, ref.shape[0] // 16)
            def _(i):
                ref[row_block(i, 16), :] = jnp.zeros((16, ref.shape[1]), F32)

    g_vec[...] = jnp.zeros_like(g_vec)
    g_tab[...] = jnp.zeros_like(g_tab)
    codew[...] = jnp.zeros_like(codew)

    if linked:
        weights_2(0)
        for sec in range(1, 4):
            weights_1(sec)
        for k in range(1, 8):
            pack_arrival(k).wait_recv()
        place_vectors()

    def vector(b, kind, width=D):
        return vec[b * 8 + kind : b * 8 + kind + 1, :width]

    def add_vec(b, kind, part):
        g_vec[b, kind, :, : part.shape[1]] += part

    def windowed(rows, count):
        return jnp.where(real_places(count), winf[rows, :], 0.0).astype(BF)

    def attention_forward(b, n, x, out, hook):
        lanes = head_of_lane()

        @pl.loop(0, CELLS // TILE)
        def _(t):
            rows = row_block(t, TILE)
            xhat, _ = standardized(x[rows, :].astype(F32))
            canvf[rows, :] = xhat * vector(b, 0) + vector(b, 1)

        to_windows(canvf, winf, SHIFT * b)
        to_windows(code.at[n], codew, SHIFT * b)
        hook(4)

        @pl.loop(0, 4)
        def _(t):
            rows = row_block(t, 256)
            hq = windowed(rows, 256)
            hqw[n, rows, :] = hq
            for part in range(3):
                cols = slice(part * D, (part + 1) * D)
                acc = nn(hq, wat[b, :, cols]) + vec[b * 8 + 6 : b * 8 + 7, cols]
                if part == 0:
                    acc = acc * SCALE
                qkv[n, rows, cols] = acc.astype(BF)

        hook(0)

        @pl.loop(0, WINDOWS)
        def _(w):
            rows = row_block(w, PLACES)
            cells = codew[rows, :]
            region = (cells >> 1) * b
            pad = (cells & 1).astype(F32)
            lane = lax.broadcasted_iota(jnp.int32, (PLACES, 128), 1)
            same = jnp.where(lane == region, 1.0, 0.0)
            left = jnp.where(lane == 127, 1.0 - pad, same).astype(BF)
            right = jnp.where(lane == 127, -pad, same).astype(BF)
            agree = nt(left, jnp.concatenate([right, right], axis=0))
            mask = jnp.where(agree > 0.5, 0.0, MASKED)
            for g in range(GROUPS):
                q = qkv[n, rows, g * 128 : (g + 1) * 128]
                k = qkv[n, rows, D + g * 128 : D + (g + 1) * 128]
                v = qkv[n, rows, 2 * D + g * 128 : 2 * D + (g + 1) * 128]
                scores = nt(by_low(k, lanes), by_high(q, lanes)) + bias[b, g]
                halves = []
                for h in range(2):
                    s = scores[h * PLACES : (h + 1) * PLACES] + mask
                    e = jnp.exp(s - jnp.max(s, axis=0, keepdims=True))
                    halves.append((e * (1.0 / jnp.sum(e, axis=0, keepdims=True))).astype(BF))
                p = jnp.concatenate(halves, axis=0)
                probs[n, w * GROUPS + g] = p
                att[n, rows, g * 128 : (g + 1) * 128] = own_high(tn(p, by_low(v, lanes)), lanes).astype(BF)

        hook(1)

        @pl.loop(0, 4)
        def _(t):
            rows = row_block(t, 256)
            winf[rows, :] = nn(att[n, rows, :], wat[b, :, 3 * D :])

        to_canvas(winf, canvf, SHIFT * b)

        @pl.loop(0, CELLS // TILE)
        def _(t):
            rows = row_block(t, TILE)
            out[rows, :] = (x[rows, :].astype(F32) + (canvf[rows, :] + vector(b, 2))).astype(BF)

    def mlp_forward(b, n, x, out, hook):
        @pl.loop(0, CELLS // TILE)
        def _(t):
            rows = row_block(t, TILE)
            xhat, _ = standardized(x[rows, :].astype(F32))
            hq2[n, rows, :] = (xhat * vector(b, 3) + vector(b, 4)).astype(BF)

        @pl.loop(0, FF // 256)
        def _(i):
            cols = pl.ds(pl.multiple_of(i * 256, 256), 256)
            pre = nn(hq2[n], fc1[b, :, cols]) + vec[b * 8 + 7 : b * 8 + 8, cols]
            for at in range(0, CELLS, 16):
                h, dg = gelu_parts(pre[at : at + 16])
                hid[n, at : at + 16, cols] = h.astype(BF)
                dgelu[n, at : at + 16, cols] = dg.astype(BF)

        hook(0)
        total = nn(hid[n], fc2[b])
        for at in range(0, CELLS, TILE):
            rows = slice(at, at + TILE)
            out[rows, :] = (x[rows, :].astype(F32) + (total[rows] + vector(b, 5))).astype(BF)

    def norm_backward(b, kind, x, gz, out):
        @pl.loop(0, CELLS // TILE)
        def _(t):
            rows = row_block(t, TILE)
            xhat, rs = standardized(x[rows, :].astype(F32))
            gn = canvf[rows, :]
            gzf = gz[rows, :].astype(F32)
            add_vec(b, kind, by_eights(gn * xhat))
            add_vec(b, kind + 1, by_eights(gn))
            add_vec(b, 5 if kind else 2, by_eights(gzf))
            g = gn * vector(b, kind)
            mg = jnp.mean(g, axis=-1, keepdims=True)
            mgx = jnp.mean(g * xhat, axis=-1, keepdims=True)
            out[rows, :] = (gzf + rs * (g - mg - xhat * mgx)).astype(BF)

    def mlp_backward(b, n, x, gz, out, free_out, hook):
        @pl.loop(0, FF // 256)
        def _(i):
            cols = pl.ds(pl.multiple_of(i * 256, 256), 256)
            gh = nt(gz[...], fc2[b, cols, :])
            sums = jnp.zeros((8, 256), F32)
            for at in range(0, CELLS, 16):
                gp = (gh[at : at + 16] * dgelu[n, at : at + 16, cols].astype(F32)).astype(BF)
                dgelu[n, at : at + 16, cols] = gp
                sums = sums + by_eights(gp.astype(F32))
            g_vec[b, 7, :, cols] += sums
            g_fc1[:, cols] += tn(hq2[n], dgelu[n, :, cols])
            g_fc2[cols, :] += tn(hid[n, :, cols], gz[...])

        hook(0)
        canvf[...] = nt(dgelu[n], fc1[b])
        free_out()
        norm_backward(b, 3, x, gz, out)

    def attention_backward(b, n, x, gz, out, free_out, hook):
        lanes = head_of_lane()

        @pl.loop(0, CELLS // TILE)
        def _(t):
            rows = row_block(t, TILE)
            canvf[rows, :] = gz[rows, :].astype(F32)

        to_windows(canvf, winf, SHIFT * b)

        @pl.loop(0, 4)
        def _(t):
            rows = row_block(t, 256)
            gzw[rows, :] = windowed(rows, 256)

        g_proj[...] += tn(att[n], gzw[...])

        @pl.loop(0, 4)
        def _(t):
            rows = row_block(t, 256)
            go[rows, :] = nt(gzw[rows, :], wat[b, :, 3 * D :]).astype(BF)

        hook(0)

        @pl.loop(0, WINDOWS)
        def _(w):
            rows = row_block(w, PLACES)
            for g in range(GROUPS):
                at = [slice(part * D + g * 128, part * D + (g + 1) * 128) for part in range(3)]
                q, k, v = (qkv[n, rows, cols] for cols in at)
                go_wide = by_high(go[rows, at[0]], lanes)
                p_low = probs[n, w * GROUPS + g]
                p = p_low.astype(F32)
                pd = p * nt(by_low(v, lanes), go_wide)
                halves = []
                for h in range(2):
                    half = slice(h * PLACES, (h + 1) * PLACES)
                    halves.append((pd[half] - p[half] * jnp.sum(pd[half], axis=0, keepdims=True)).astype(BF))
                ds = jnp.concatenate(halves, axis=0)
                g_tab[b, :, g * 128 : (g + 1) * 128] += ds.astype(F32)
                gqkv[rows, at[0]] = (own_high(tn(ds, by_low(k, lanes)), lanes) * SCALE).astype(BF)
                gqkv[rows, at[1]] = own_low(nn(ds, by_high(q, lanes)), lanes).astype(BF)
                gqkv[rows, at[2]] = own_low(nn(p_low, go_wide), lanes).astype(BF)

        hook(1)

        @pl.loop(0, 4)
        def _(t):
            rows = row_block(t, 256)
            gq = gqkv[rows, :]
            add_vec(b, 6, by_eights(gq.astype(F32)))
            winf[rows, :] = nt(gq, wat[b, :, : 3 * D])

        to_canvas(winf, canvf, SHIFT * b)
        free_out()
        norm_backward(b, 0, x, gz, out)

    def attention_weights(n):
        for part in range(3):
            cols = slice(part * D, (part + 1) * D)
            g_qkv[:, cols] += tn(hqw[n], gqkv[:, cols])

    def partner(k):
        x, y = me % 2, me // 2
        return 2 * (1 - y if k & 2 else y) + (1 - x if k & 1 else x)

    def act_copies(n):
        away = [
            remote(
                buf.at[partner(k), n],
                r.act_hbm.at[me, n],
                r.act_send.at[k - 1, n],
                r.act_recv.at[k - 1, n],
                {"pipe": partner(k)},
            )
            for k in (2, 1, 3)
        ]
        return away, pltpu.make_async_copy(buf.at[me, n], r.act_hbm.at[me, n], r.local_sem.at[0, n])

    def send_acts(n):
        away, local = act_copies(n)
        for copy in away:
            copy.start()
        local.start()

    def acts_sent(n):
        away, local = act_copies(n)
        for copy in away:
            copy.wait_send()
        local.wait()

    def push(s, n, start):
        src = buf.at[s, n]
        dst = r.igrad_hbm.at[me, n]
        local = pltpu.make_async_copy(src, dst, r.local_sem.at[1, n])
        away = remote(src, dst, r.send_sem.at[s, n], r.recv_sem.at[me, n], {"pipe": s})

        @pl.when(me == s)
        def _():
            local.start() if start else local.wait()

        @pl.when(me != s)
        def _():
            away.start() if start else away.wait_send()

    def arrived(k, n):
        sender = partner(k)
        got = r.act_hbm.at[sender, n]
        remote(got, got, r.act_send.at[k - 1, n], r.act_recv.at[k - 1, n], {"pipe": sender}).wait_recv()
        got = r.igrad_hbm.at[sender, n]
        remote(got, got, r.send_sem.at[0, n], r.recv_sem.at[sender, n], {"pipe": sender}).wait_recv()

    attention_stash = ((hqw, r.h_hqw), (qkv, r.h_qkv), (probs, r.h_probs), (att, r.h_att))
    mlp_stash = ((hq2, r.h_hq2), (hid, r.h_hid), (dgelu, r.h_dgelu))

    def stash(sec, n, back):
        pairs = mlp_stash if sec else attention_stash
        return [
            pltpu.make_async_copy(*((far.at[n], near.at[n]) if back else (near.at[n], far.at[n])), r.st_sem.at[sec, n, i])
            for i, (near, far) in enumerate(pairs)
        ]

    def load(src, n):
        return pltpu.make_async_copy(src.at[me, n], inb.at[n], r.in_sem.at[n])

    def start(copies):
        for copy in copies:
            copy.start()

    def wait(copies):
        for copy in copies:
            copy.wait()

    steps = (step_1, step_2, step_3, step_4, step_5)
    schedule = {
        (2, 0, 0): ((2, 3),),
        (2, 1, 1): ((3, 3),),
        (1, 0, 0): ((2, 2),),
        (1, 1, 0): ((4, 3),),
        (0, 0, 0): ((3, 2), (2, 1), (5, 3)),
        (0, 0, 1): ((4, 2),),
        (0, 1, 0): ((5, 2),),
        (0, 1, 1): ((3, 1),),
    }
    after = {3: ((1, 3),), 2: ((1, 2),), 1: ((1, 1),), 0: ()}
    weight_steps = (weights_1, weights_2, weights_3, weights_4) if linked else ()
    gathering = {
        (0, 4): ((3, 0), (4, 0)),
        (0, 0): ((2, 1),),
        (0, 1): ((2, 2), (2, 3), (3, 1)),
        (0, 3): ((4, 1), (3, 2)),
        (1, 3): ((4, 2),),
        (2, 0): ((3, 3),),
        (2, 3): ((4, 3),),
    }

    codes = [pltpu.make_async_copy(r.code_hbm, code, r.code_sem.at[0])]
    start(codes)
    start([load(r.x_hbm, n) for n in range(canvases)])
    wait(codes)

    @pl.loop(0, canvases)
    def _(n):
        def gather(sec, i):
            todo = gathering.get((sec, i), ())
            if linked and todo:

                @pl.when(n == 0)
                def _():
                    for step, of in todo:
                        weight_steps[step - 1](of)

        load(r.x_hbm, n).wait()
        x = inb.at[n]
        for s in range(4):
            if s >= 2:
                wait(stash(s - 2, n, False))
            forward = mlp_forward if s % 2 else attention_forward
            forward(s // 2, n, x, buf.at[s, n], functools.partial(gather, s))
            x = buf.at[s, n]
            if s == 3:
                send_acts(n)
            if s < 2:
                start(stash(s, n, False))
            if s == 0:
                load(r.cot_hbm, n).start()
            gather(s, 3)

    for s in (3, 2, 1, 0):
        cleared(*((g_fc1, g_fc2) if s % 2 else (g_qkv, g_proj)))

        @pl.loop(0, canvases)
        def _(n):
            def hook(i):
                for at in range(2):
                    todo = schedule.get((s, at, i), ())
                    if linked and todo:

                        @pl.when(n == (canvases - 1 if at else 0))
                        def _():
                            for step, of in todo:
                                steps[step - 1](of)

            if s == 3:
                load(r.cot_hbm, n).wait()
            if s == 0:
                load(r.x_hbm, n).wait()
            if s < 2:
                wait(stash(s, n, True))
            x = buf.at[s - 1, n] if s else inb.at[n]
            gz = inb.at[n] if s == 3 else buf.at[s + 1, n]
            backward = mlp_backward if s % 2 else attention_backward
            free_out = functools.partial(acts_sent, n) if s == 3 else lambda: None
            backward(s // 2, n, x, gz, buf.at[s, n], free_out, hook)
            if s % 2 == 0:
                attention_weights(n)
            if s == 2:
                push(3, n, True)
                push(2, n, True)
            if s == 0:

                @pl.when(n < canvases - 1)
                def _():
                    push(1, n, True)
                    push(0, n, True)

            if s == 3:
                load(r.x_hbm, n).start()
            if s >= 2:
                start(stash(s - 2, n, True))

        if linked:
            for step, of in after[s]:
                steps[step - 1](of)
        else:
            whole = ((g_fc1, r.f_fc1), (g_fc2, r.f_fc2)) if s % 2 else ((g_qkv, r.f_qkv), (g_proj, r.f_proj))
            copies = [pltpu.make_async_copy(a, o.at[s // 2], r.go_sem.at[s, i]) for i, (a, o) in enumerate(whole)]
            start(copies)
            wait(copies)

    if linked:
        step_1(0)
        step_4(1)
        step_2(0)
    push(1, canvases - 1, True)
    push(0, canvases - 1, True)
    if linked:
        step_5(1)
        smalls_sent(1)
        step_3(0)
        step_4(0)
        step_5(0)
        reductions_done()
        weights_sent()
        for k in range(1, 8):
            pack_copy(k).wait_send()
    for k in range(1, 4):
        for n in range(canvases):
            arrived(k, n)
    for s in range(4):
        for n in range(canvases):
            push(s, n, False)


def compute(linked, operands):
    canvases = operands["x_hbm"].shape[1]
    shape = jax.ShapeDtypeStruct
    hbm = pl.BlockSpec(memory_space=pl.ANY)
    vmem = pl.BlockSpec(memory_space=pltpu.VMEM)
    dma = pltpu.SemaphoreType.DMA
    full = {
        "wat": ((2, D, 4 * D), BF),
        "fc1": ((2, D, FF), BF),
        "fc2": ((2, FF, D), BF),
        "vec": ((16, FF), F32),
    }
    grads = {
        "g_qkv": ((D, 3 * D), F32),
        "g_proj": ((D, D), F32),
        "g_fc1": ((D, FF), F32),
        "g_fc2": ((FF, D), F32),
        "g_vec": ((2, 8, 8, FF), F32),
        "g_tab": ((2, 2 * PLACES, GROUPS * 128), F32),
    }
    outs = {"act_hbm": ((4, canvases, CELLS, D), BF), "igrad_hbm": ((4, canvases, CELLS, D), BF)}
    kept = {
        "hqw": ((canvases, WROWS, D), BF),
        "qkv": ((canvases, WROWS, 3 * D), BF),
        "probs": ((canvases, WINDOWS * GROUPS, 128, 128), BF),
        "att": ((canvases, WROWS, D), BF),
        "hq2": ((canvases, CELLS, D), BF),
        "hid": ((canvases, CELLS, FF), BF),
        "dgelu": ((canvases, CELLS, FF), BF),
    }
    outs |= {"h_" + name: kind for name, kind in kept.items()}
    scratch = kept | {
        "inb": ((canvases, CELLS, D), BF),
        "code": ((canvases, CELLS, 128), jnp.int32),
        "codew": ((WROWS, 128), jnp.int32),
        "buf": ((4, canvases, CELLS, D), BF),
        "canvf": ((CELLS, D), F32),
        "winf": ((WROWS, D), F32),
        "gzw": ((WROWS, D), BF),
        "go": ((WROWS, D), BF),
        "gqkv": ((WROWS, 3 * D), BF),
    }
    sems = {
        "in_sem": (canvases,),
        "code_sem": (1,),
        "st_sem": (2, canvases, 4),
        "local_sem": (2, canvases),
        "act_send": (3, canvases),
        "act_recv": (3, canvases),
        "send_sem": (4, canvases),
        "recv_sem": (4, canvases),
    }
    if linked:
        outs |= {
            "o_qkv": ((2, 48, 3 * D), F32),
            "o_proj": ((2, 48, D), F32),
            "o_fc1": ((2, 48, FF), F32),
            "o_fc2": ((2, 192, D), F32),
            "o_small": ((2, 8, 64, D), BF),
        }
        scratch |= full | grads
        scratch |= {
            "packs": ((8, 16, 256), BF),
            "l_qkv": ((48, 3 * D), F32),
            "l_proj": ((48, D), F32),
            "l_fc1": ((48, FF), F32),
            "l_fc2": ((192, D), F32),
        }
        for kind, rows in (("m_", MLP_ROWS), ("a_", ATT_ROWS)):
            scratch |= {
                kind + "st_a": ((4, rows, D), BF),
                kind + "rc_a": ((4, rows, D), BF),
                kind + "st_b": ((3, rows, D), BF),
                kind + "rc_b": ((3, rows, D), BF),
                kind + "st_c": ((rows, D), BF),
                kind + "rc_c": ((3, rows // 4, D), BF),
                kind + "fin": ((rows, D), BF),
            }
        sems |= {
            "sh_sem": (4, 2),
            "os_sem": (2,),
            "go_sem": (4, 2),
            "wz_send": (4, 2, 3),
            "wz_recv": (4, 2, 3),
            "wx_send": (4, 2, 3, 3),
            "wx_recv": (4, 2, 3, 3),
            "ws_send": (4, 2, 4),
            "ws_recv": (4, 2, 4),
            "pk_send": (7,),
            "pk_recv": (7,),
            "ra_send": (4,),
            "ra_recv": (4,),
            "rb_send": (4, 3),
            "rb_recv": (4, 3),
            "rc_send": (4, 3),
            "rc_recv": (4, 3),
            "rf_send": (4, 3),
            "rf_recv": (4, 3),
            "rs_send": (2, 7),
            "rs_recv": (2, 7),
        }
    else:
        for name in ("g_vec", "g_tab"):
            outs[name] = grads.pop(name)
        outs |= {name.replace("g_", "f_"): ((2,) + dims, F32) for name, (dims, _) in grads.items()}
        scratch |= grads
        sems["go_sem"] = (4, 2)
    in_vmem = set(full) | {"bias", "pack", "g_vec", "g_tab"}
    names = tuple(operands) + tuple(outs) + tuple(scratch) + tuple(sems)
    results = pl.pallas_call(
        functools.partial(kernel, names, linked, canvases),
        out_shape=tuple(shape(*o) for o in outs.values()),
        in_specs=[vmem if name in in_vmem else hbm for name in operands],
        out_specs=tuple(vmem if name in in_vmem else hbm for name in outs),
        scratch_shapes=[pltpu.VMEM(*v) for v in scratch.values()] + [dma(v) for v in sems.values()],
        compiler_params=pltpu.CompilerParams(
            vmem_limit_bytes=64 * 1024 * 1024 - 65536, collective_id=0, has_side_effects=True
        ),
    )(*operands.values())
    return dict(zip(outs, results))


def place_pairs():
    place = np.arange(PLACES)
    r, c = place // 8, place % 8
    index = (r[None, :] - r[:, None] + WIN - 1) * (2 * WIN - 1) + c[None, :] - c[:, None] + WIN - 1
    real = (r < WIN) & (c < WIN)
    return index, real[:, None] & real[None, :], real


def pair_onehot():
    index, both, _ = place_pairs()
    table = (2 * WIN - 1) ** 2
    hot = (np.where(both, index, -1).reshape(-1)[None, :] == np.arange(table)[:, None])
    return hot.astype(np.float32)


def body(
    inputs,
    cotangent,
    pad_mask,
    region_ids,
    norm1_gain,
    norm1_bias,
    qkv_weight,
    qv_bias,
    rel_table,
    proj_weight,
    proj_bias,
    norm2_gain,
    norm2_bias,
    fc1_weight,
    fc1_bias,
    fc2_weight,
    fc2_bias,
):
    owners = lax.axis_size("dp")
    linked = owners == 8
    mine = lax.axis_index("pipe")

    def own(a):
        return lax.dynamic_index_in_dim(a, mine, 0, keepdims=False)

    code = own(region_ids) * 2 + own(pad_mask)
    code = jnp.broadcast_to(code[:, :, None], code.shape + (128,))

    hot = pair_onehot()
    _, _, real = place_pairs()
    rel = lax.dot_general(
        rel_table.astype(BF), jnp.asarray(hot, BF), (((1,), (0,)), ((), ())), preferred_element_type=F32
    )
    rel = rel.reshape(2, GROUPS, 2, 2, PLACES, PLACES)
    rel = jnp.where(jnp.asarray(real)[None, None, None, None, :, None], rel, MASKED)
    rel = rel.transpose(0, 1, 3, 4, 2, 5).reshape(2, GROUPS, 128, 128)

    operands = {"x_hbm": inputs, "cot_hbm": cotangent, "code_hbm": code, "bias": rel}
    vectors = (norm1_gain, norm1_bias, proj_bias, norm2_gain, norm2_bias, fc2_bias, qv_bias, fc1_bias)
    sizes = [v.shape[1] for v in vectors]
    ends = np.cumsum([0] + sizes)
    if linked:
        pack = jnp.stack([jnp.pad(v, ((0, 0), (0, 256 - v.shape[1]))) for v in vectors], axis=1)
        operands |= {
            "pack": pack.reshape(16, 256).astype(BF),
            "s_qkv": qkv_weight,
            "s_proj": proj_weight,
            "s_fc1": fc1_weight,
            "s_fc2": fc2_weight,
        }
    else:

        def gathered(a):
            return lax.all_gather(a.astype(BF), "dp", axis=1, tiled=True)

        packed = lax.all_gather(jnp.concatenate(vectors, axis=1).astype(BF), "dp", axis=1)
        parts = [packed[:, :, a:b].reshape(2, -1).astype(F32) for a, b in zip(ends[:-1], ends[1:])]
        qv = parts[6]
        parts[6] = jnp.concatenate([qv[:, :D], jnp.zeros_like(qv[:, :D]), qv[:, D:]], axis=1)
        vec = jnp.stack([jnp.pad(p, ((0, 0), (0, FF - p.shape[1]))) for p in parts], axis=1)
        operands |= {
            "wat": jnp.concatenate([gathered(qkv_weight), gathered(proj_weight)], axis=2),
            "fc1": gathered(fc1_weight),
            "fc2": gathered(fc2_weight),
            "vec": vec.reshape(16, FF),
        }

    out = compute(linked, operands)

    def to_owners(g):
        shared = lax.psum_scatter(g, "dp", scatter_dimension=1, tiled=True)
        return lax.psum(shared, "pipe")

    if linked:
        small = out["o_small"]
        g_tab = small[:, :, :16].reshape(2, 128, GROUPS * 128)
        g_vec = jnp.concatenate([small[:, :, 16 + 8 * j : 24 + 8 * j] for j in range(4)], axis=3)
    else:
        g_tab, g_vec = out["g_tab"], out["g_vec"]

    g_vec = jnp.sum(g_vec.astype(F32), axis=2)
    kinds = [g_vec[:, i] for i in range(8)]
    qv_sum = jnp.concatenate([kinds[6][:, :D], kinds[6][:, 2 * D : 3 * D]], axis=1)
    rows = [kinds[0], kinds[1], kinds[2], kinds[3], kinds[4], kinds[5], qv_sum, kinds[7]]
    if linked:
        at = lax.axis_index("dp")
        small = [lax.dynamic_slice_in_dim(v, at * n, n, 1) for v, n in zip(rows, sizes)]
    else:
        rows = [v[:, : n * owners].reshape(2, -1, n) for v, n in zip(rows, sizes)]
        g_small = to_owners(jnp.concatenate(rows, axis=2))[:, 0]
        small = [g_small[:, a:b] for a, b in zip(ends[:-1], ends[1:])]

    pairs = g_tab.reshape(2, 2, PLACES, GROUPS, 2, PLACES).transpose(0, 3, 4, 1, 2, 5)
    pairs = pairs.reshape(2, HEADS, PLACES * PLACES)
    g_table = lax.dot_general(
        jnp.broadcast_to(jnp.asarray(hot, pairs.dtype), (2,) + hot.shape),
        pairs,
        (((2,), (2,)), ((0,), (0,))),
        precision=None if linked else lax.Precision.HIGHEST,
        preferred_element_type=F32,
    )
    if linked:
        big = [out[name] for name in ("o_qkv", "o_proj", "o_fc1", "o_fc2")]
    else:
        g_table = lax.psum(g_table, ("pipe", "dp"))
        big = [to_owners(out[name]) for name in ("f_qkv", "f_proj", "f_fc1", "f_fc2")]

    return (
        out["act_hbm"][None],
        out["igrad_hbm"][None],
        small[0],
        small[1],
        big[0],
        small[6],
        g_table,
        big[1],
        small[2],
        small[3],
        small[4],
        big[2],
        small[7],
        big[3],
        small[5],
    )


def solution(mesh):
    cols = P(None, "dp")
    rows = P(None, "dp", None)
    return jax.shard_map(
        body,
        mesh=mesh,
        in_specs=(
            P(None, "dp", None, None),
            P(None, "dp", None, None),
            rows,
            rows,
            cols,
            cols,
            rows,
            cols,
            P(),
            rows,
            cols,
            cols,
            cols,
            rows,
            cols,
            rows,
            cols,
        ),
        out_specs=(
            P("pipe", None, "dp", None, None),
            P("pipe", None, "dp", None, None),
            cols,
            cols,
            rows,
            cols,
            P(),
            rows,
            cols,
            cols,
            cols,
            rows,
            cols,
            rows,
            cols,
        ),
        check_vma=False,
    )
```

```python
import functools
import types

import jax
import jax.numpy as jnp
import numpy as np
from jax import lax
from jax.experimental import pallas as pl
from jax.experimental.pallas import tpu as pltpu
from jax.sharding import PartitionSpec as P

HEADS = 12
WIN = 7
SHIFT = 3
GRID = 28
CELLS = 784
D = 384
FF = 1536
HEAD = 32
SIDE = 4
WINDOWS = 16
PLACES = 64
WROWS = WINDOWS * PLACES
GROUPS = 3
TILE = 112
SCALE = HEAD**-0.5
NORM_EPS = 1e-05
MASKED = -1e30
BF = jnp.bfloat16
F32 = jnp.float32

RSQRT_2 = 1.0 / np.sqrt(2.0)
PHI_0 = 1.0 / np.sqrt(2.0 * np.pi)


def nn(a, b):
    return lax.dot_general(a, b, (((1,), (0,)), ((), ())), preferred_element_type=F32)


def nt(a, b):
    return lax.dot_general(a, b, (((1,), (1,)), ((), ())), preferred_element_type=F32)


def tn(a, b):
    return lax.dot_general(a, b, (((0,), (0,)), ((), ())), preferred_element_type=F32)


def segments(shift):
    runs = []
    for wr in range(SIDE):
        for r in range(WIN):
            row = (wr * WIN + r + shift) % GRID
            for wc in range(SIDE):
                col = (wc * WIN + shift) % GRID
                place = (wr * SIDE + wc) * PLACES + r * 8
                first = min(WIN, GRID - col)
                runs.append((row * GRID + col, place, first))
                if first < WIN:
                    runs.append((row * GRID, place + first, WIN - first))
    return runs


def to_windows(src, dst, shift):
    for cell, place, count in segments(shift):
        dst[pl.ds(place, count), :] = src[pl.ds(cell, count), :]


def to_canvas(src, dst, shift):
    for cell, place, count in segments(shift):
        dst[pl.ds(cell, count), :] = src[pl.ds(place, count), :]


def row_block(t, size):
    return pl.ds(pl.multiple_of(t * size, 16), size)


def standardized(v):
    centered = v - jnp.mean(v, axis=-1, keepdims=True)
    spread = jnp.mean(centered * centered, axis=-1, keepdims=True)
    rs = lax.rsqrt(spread + NORM_EPS)
    return centered * rs, rs


def by_eights(v):
    return jnp.sum(v.reshape(v.shape[0] // 8, 8, v.shape[1]), axis=0)


def gelu_parts(x):
    cdf = 0.5 + 0.5 * lax.erf(x * RSQRT_2)
    return x * cdf, cdf + x * (jnp.exp(-0.5 * x * x) * PHI_0)


def real_places(rows):
    place = lax.broadcasted_iota(jnp.int32, (rows, 1), 0)
    return ((place & 7) < WIN) & (((place >> 3) & 7) < WIN)


def head_of_lane():
    return lax.broadcasted_iota(jnp.int32, (PLACES, 128), 1) >> 5


def by_low(x, lanes):
    zero = jnp.zeros_like(x)
    return jnp.concatenate([jnp.where((lanes & 1) == h, x, zero) for h in range(2)], axis=0)


def by_high(x, lanes):
    zero = jnp.zeros_like(x)
    return jnp.concatenate([jnp.where((lanes >> 1) == h, x, zero) for h in range(2)], axis=0)


def own_low(wide, lanes):
    return jnp.where((lanes & 1) == 0, wide[:PLACES], wide[PLACES:])


def own_high(wide, lanes):
    return jnp.where((lanes >> 1) == 0, wide[:PLACES], wide[PLACES:])


MESH = pl.DeviceIdType.MESH
ATT_ROWS = 256
MLP_ROWS = 384
SMALL = 192


def kernel(names, linked, canvases, *refs):
    r = types.SimpleNamespace(**dict(zip(names, refs)))
    me = lax.axis_index("pipe")
    inb, code, codew, buf = r.inb, r.code, r.codew, r.buf
    hqw, qkv, probs, att = r.hqw, r.qkv, r.probs, r.att
    hq2, hid, dgelu = r.hq2, r.hid, r.dgelu
    canvf, winf, gzw, gqkv, go = r.canvf, r.winf, r.gzw, r.gqkv, r.go
    g_qkv, g_proj, g_fc1, g_fc2, g_vec, g_tab = r.g_qkv, r.g_proj, r.g_fc1, r.g_fc2, r.g_vec, r.g_tab
    wat, fc1, fc2, vec, bias = r.wat, r.fc1, r.fc2, r.vec, r.bias
    if linked:
        d = lax.axis_index("dp")
        z, c = d // 2, d % 2
        sibling = {"dp": 2 * z + 1 - c}

    def z_peer(k):
        return {"dp": 2 * lax.rem(z + k, 4) + c}

    def pipe_peer(k):
        return {"pipe": lax.rem(me + k, 4)}

    def dp_peer(k):
        return {"dp": lax.rem(d + k, 8)}

    def remote(src, dst, send, recv, device):
        return pltpu.make_async_remote_copy(
            src_ref=src, dst_ref=dst, send_sem=send, recv_sem=recv, device_id=device, device_id_type=MESH
        )

    barrier = pltpu.get_barrier_semaphore()
    partners = [pipe_peer(k) for k in range(1, 4)]
    if linked:
        partners += [dp_peer(k) for k in range(1, 8)]
    for partner in partners:
        pl.semaphore_signal(barrier, inc=1, device_id=partner, device_id_type=MESH)

    full = ((wat,), (fc1, fc2), (wat,), (fc1, fc2))

    def owner_back(k):
        return 2 * lax.rem(z + 4 - k, 4) + c

    def shard(sec, a, owner):
        h = 192 if a else 48
        return full[sec][a].at[sec // 2, pl.ds(pl.multiple_of(owner * h, 16), h), :]

    def part(sec, a, owner, place):
        if a:
            return fc2.at[sec // 2, pl.ds(pl.multiple_of(owner * 192 + place * 48, 16), 48), :]
        rows = pl.ds(pl.multiple_of(owner * 48, 16), 48)
        return full[sec][0].at[sec // 2, rows, pl.ds(pl.multiple_of(place * D, 128), D)]

    def to_z(sec, a, k):
        own = part(sec, a, d, me)
        return remote(own, own, r.wz_send.at[sec, a, k - 1], r.wz_recv.at[sec, a, k - 1], z_peer(k))

    def to_places(sec, a, k, j):
        got = part(sec, a, owner_back(k), me)
        return remote(
            got, got, r.wx_send.at[sec, a, k - 1, j - 1], r.wx_recv.at[sec, a, k - 1, j - 1], pipe_peer(j)
        )

    def to_sibling(sec, a, k):
        block = shard(sec, a, owner_back(k))
        return remote(block, block, r.ws_send.at[sec, a, k], r.ws_recv.at[sec, a, k], sibling)

    def weights_1(sec):
        for a in range(len(full[sec])):
            for k in range(1, 4):
                to_z(sec, a, k).start()
            to_sibling(sec, a, 0).start()

    def weights_2(sec):
        for k in range(1, 4):
            for a in range(len(full[sec])):
                got = part(sec, a, owner_back(k), me)
                remote(got, got, r.wz_send.at[sec, a, k - 1], r.wz_recv.at[sec, a, k - 1], z_peer(k)).wait_recv()
                for j in range(1, 4):
                    to_places(sec, a, k, j).start()

    def weights_3(sec):
        for k in range(1, 4):
            for a in range(len(full[sec])):
                for j in range(1, 4):
                    got = part(sec, a, owner_back(k), lax.rem(me + 4 - j, 4))
                    remote(
                        got, got, r.wx_send.at[sec, a, k - 1, j - 1], r.wx_recv.at[sec, a, k - 1, j - 1], pipe_peer(j)
                    ).wait_recv()
                to_sibling(sec, a, k).start()

    def weights_4(sec):
        for k in range(4):
            for a in range(len(full[sec])):
                block = shard(sec, a, 2 * lax.rem(z + 4 - k, 4) + 1 - c)
                remote(block, block, r.ws_send.at[sec, a, k], r.ws_recv.at[sec, a, k], sibling).wait_recv()

    def weights_sent():
        for sec in range(4):
            for a in range(len(full[sec])):
                for k in range(4):
                    to_sibling(sec, a, k).wait_send()
                    if k:
                        to_z(sec, a, k).wait_send()
                        for j in range(1, 4):
                            to_places(sec, a, k, j).wait_send()

    def pack_copy(k):
        return remote(
            r.packs.at[d], r.packs.at[d], r.pk_send.at[k - 1], r.pk_recv.at[k - 1], dp_peer(k)
        )

    def pack_arrival(k):
        slot = r.packs.at[lax.rem(d + 8 - k, 8)]
        return remote(slot, slot, r.pk_send.at[k - 1], r.pk_recv.at[k - 1], dp_peer(k))

    def place_vectors():
        kind = lax.broadcasted_iota(jnp.int32, (16, 256), 0) & 7
        lane = lax.broadcasted_iota(jnp.int32, (16, 256), 1)
        vec[...] = jnp.zeros_like(vec)
        for width, kinds in ((48, kind < 6), (96, kind == 6), (192, kind == 7)):
            for owner in range(8):
                at = owner * width
                if width == 96 and owner >= 4:
                    at += D
                start = at // 128 * 128
                part = jnp.where(kinds & (lane < width), r.packs[owner].astype(F32), 0.0)
                if at > start:
                    part = pltpu.roll(part, at - start, 1)
                vec[:, start : start + 256] += part

    def pieces(sec, owner):
        b = sec // 2
        out = []

        def matrix(ref, h):
            for t in range(h // 48):
                rows = pl.ds(pl.multiple_of(owner * h + t * 48, 16), 48)
                for j in range(ref.shape[1] // D):
                    load = functools.partial(lambda ref, rows, j: ref[rows, j * D : (j + 1) * D], ref, rows, j)
                    out.append((len(out) * 48, 48, load))

        def small():
            parts = [g_tab[b, pl.ds(pl.multiple_of(owner * 16, 16), 16), :]]
            parts += [g_vec[b, owner, :, j * D : (j + 1) * D] for j in range(4)]
            return jnp.concatenate(parts + [jnp.zeros((16, D), F32)], axis=0)

        if sec % 2:
            matrix(g_fc1, 48)
            matrix(g_fc2, 192)
        else:
            matrix(g_qkv, 48)
            matrix(g_proj, 48)
            out.append((SMALL, 64, small))
        return out

    def reduce_refs(sec):
        kind = "m" if sec % 2 else "a"
        return types.SimpleNamespace(
            **{n: getattr(r, kind + "_" + n) for n in ("st_a", "rc_a", "st_b", "rc_b", "st_c", "rc_c", "fin")}
        )

    def step_1(sec):
        q = reduce_refs(sec)
        if sec < 2:
            copy_a(sec + 2).wait_send()
            for k in range(1, 4):
                copy_b(sec + 2, k).wait_send()
                copy_c(sec + 2, k).wait_send()
        for k in range(4):
            i = lax.rem(z + k, 4)
            kept = q.st_b.at[k]
            for row, rows, load in pieces(sec, 2 * i + 1 - c):
                q.st_a[i, row : row + rows, :] = load().astype(BF)
            for row, rows, load in pieces(sec, 2 * i + c):
                kept[row : row + rows, :] = load().astype(BF)
        copy_a(sec).start()

    def copy_a(sec):
        q = reduce_refs(sec)
        return remote(q.st_a, q.rc_a, r.ra_send.at[sec], r.ra_recv.at[sec], sibling)

    def quarter_rows(sec, who):
        rows = (MLP_ROWS if sec % 2 else ATT_ROWS) // 4
        return pl.ds(pl.multiple_of(who * rows, 16), rows)

    def quarter(sec, ref, who):
        return ref.at[quarter_rows(sec, who), :]

    def copy_b(sec, k):
        q = reduce_refs(sec)
        return remote(
            q.st_b.at[:, quarter_rows(sec, lax.rem(me + k, 4)), :],
            q.rc_b.at[k - 1],
            r.rb_send.at[sec, k - 1],
            r.rb_recv.at[sec, k - 1],
            pipe_peer(k),
        )

    def step_2(sec):
        q = reduce_refs(sec)
        copy_a(sec).wait_recv()
        for k in range(4):
            i = lax.rem(z + k, 4)
            kept = q.st_b.at[k]
            for row in range(0, kept.shape[0], 64):
                at = slice(row, row + 64)
                kept[at, :] = (kept[at, :].astype(F32) + q.rc_a[i, at, :].astype(F32)).astype(BF)
        for k in range(1, 4):
            copy_b(sec, k).start()

    def copy_c(sec, k):
        q = reduce_refs(sec)
        return remote(
            q.st_c.at[k], q.rc_c.at[k - 1], r.rc_send.at[sec, k - 1], r.rc_recv.at[sec, k - 1], z_peer(k)
        )

    def step_3(sec):
        q = reduce_refs(sec)
        for k in range(1, 4):
            copy_b(sec, k).wait_recv()
        for k in (1, 2, 3, 0):
            total = q.st_b[k, quarter_rows(sec, me), :].astype(F32)
            for j in range(3):
                total = total + q.rc_b[j, k].astype(F32)
            q.st_c[k] = total.astype(BF)
            if k:
                copy_c(sec, k).start()

    def copy_f(sec, k):
        q = reduce_refs(sec)
        own = quarter(sec, q.fin, me)
        return remote(own, own, r.rf_send.at[sec, k - 1], r.rf_recv.at[sec, k - 1], pipe_peer(k))

    def step_4(sec):
        q = reduce_refs(sec)
        for k in range(1, 4):
            copy_c(sec, k).wait_recv()
            if sec < 2:
                copy_f(sec + 2, k).wait_send()
        total = q.st_c[0].astype(F32)
        for k in range(3):
            total = total + q.rc_c[k].astype(F32)
        quarter(sec, q.fin, me)[...] = total.astype(BF)
        for k in range(1, 4):
            copy_f(sec, k).start()

    def copy_s(b, k):
        rows = pl.ds(SMALL, 64)
        return remote(
            r.a_fin.at[rows, :], r.o_small.at[b, d], r.rs_send.at[b, k - 1], r.rs_recv.at[b, k - 1], dp_peer(k)
        )

    def own_small(b):
        return pltpu.make_async_copy(r.a_fin.at[pl.ds(SMALL, 64), :], r.o_small.at[b, d], r.os_sem.at[b])

    def outputs(sec):
        pairs = ((r.l_fc1, r.o_fc1), (r.l_fc2, r.o_fc2)) if sec % 2 else ((r.l_qkv, r.o_qkv), (r.l_proj, r.o_proj))
        return [
            pltpu.make_async_copy(ref, out.at[sec // 2], r.go_sem.at[sec, i]) for i, (ref, out) in enumerate(pairs)
        ]

    def step_5(sec):
        q = reduce_refs(sec)
        b = sec // 2
        for k in range(1, 4):
            got = quarter(sec, q.fin, lax.rem(me + 4 - k, 4))
            remote(got, got, r.rf_send.at[sec, k - 1], r.rf_recv.at[sec, k - 1], pipe_peer(k)).wait_recv()
        if sec % 2 == 0:
            for k in range(1, 8):
                copy_s(b, k).start()
            own_small(b).start()
        if sec < 2:
            for out in outputs(sec + 2):
                out.wait()
        row = 0
        for ref in (r.l_fc1, r.l_fc2) if sec % 2 else (r.l_qkv, r.l_proj):
            for t in range(ref.shape[0] // 48):
                for j in range(ref.shape[1] // D):
                    ref[t * 48 : (t + 1) * 48, j * D : (j + 1) * D] = q.fin[row : row + 48, :].astype(F32)
                    row += 48
        for out in outputs(sec):
            out.start()

    def smalls_sent(b):
        for k in range(1, 8):
            copy_s(b, k).wait_send()
        own_small(b).wait()

    def reductions_done():
        for sec in (1, 0):
            copy_a(sec).wait_send()
            for k in range(1, 4):
                copy_b(sec, k).wait_send()
                copy_c(sec, k).wait_send()
                copy_f(sec, k).wait_send()
        for sec in range(2):
            for out in outputs(sec):
                out.wait()
        smalls_sent(0)
        for b in range(2):
            for k in range(1, 8):
                rows = pl.ds(SMALL, 64)
                remote(
                    r.a_fin.at[rows, :],
                    r.o_small.at[b, lax.rem(d + 8 - k, 8)],
                    r.rs_send.at[b, k - 1],
                    r.rs_recv.at[b, k - 1],
                    dp_peer(k),
                ).wait_recv()

    if linked:
        lands = ((r.s_qkv, g_qkv, wat, 0), (r.s_proj, g_proj, wat, 3 * D), (r.s_fc1, g_fc1, fc1, 0), (r.s_fc2, g_fc2, fc2, 0))

        def landing(i, b):
            src, dst, _, _ = lands[i]
            h, n = src.shape[1:]
            return pltpu.make_async_copy(
                src.at[b], dst.at[pl.ds(192 * b, h), pl.ds(0, n)], r.sh_sem.at[i, b]
            )

        for i in range(4):
            for b in range(2):
                landing(i, b).start()
        r.packs[d] = r.pack[...]
        for i, (src, dst, ref, col) in enumerate(lands):
            h, n = src.shape[1:]
            for b in range(2):
                landing(i, b).wait()
                for t in range(0, h, 48):
                    rows = pl.ds(pl.multiple_of(d * h + t, 16), 48)
                    ref[b, rows, col : col + n] = dst[192 * b + t : 192 * b + t + 48, :n].astype(BF)
    pl.semaphore_wait(barrier, len(partners))
    if linked:
        for k in range(1, 8):
            pack_copy(k).start()
        weights_1(0)

    def cleared(*refs):
        for ref in refs:

            @pl.loop(0, ref.shape[0] // 16)
            def _(i):
                ref[row_block(i, 16), :] = jnp.zeros((16, ref.shape[1]), F32)

    g_vec[...] = jnp.zeros_like(g_vec)
    g_tab[...] = jnp.zeros_like(g_tab)
    codew[...] = jnp.zeros_like(codew)

    if linked:
        weights_2(0)
        for sec in range(1, 4):
            weights_1(sec)
        for k in range(1, 8):
            pack_arrival(k).wait_recv()
        place_vectors()

    def vector(b, kind, width=D):
        return vec[b * 8 + kind : b * 8 + kind + 1, :width]

    def add_vec(b, kind, part):
        g_vec[b, kind, :, : part.shape[1]] += part

    def windowed(rows, count):
        return jnp.where(real_places(count), winf[rows, :], 0.0).astype(BF)

    def attention_forward(b, n, x, out, hook):
        lanes = head_of_lane()

        @pl.loop(0, CELLS // TILE)
        def _(t):
            rows = row_block(t, TILE)
            xhat, _ = standardized(x[rows, :].astype(F32))
            canvf[rows, :] = xhat * vector(b, 0) + vector(b, 1)

        to_windows(canvf, winf, SHIFT * b)
        to_windows(code.at[n], codew, SHIFT * b)
        hook(4)

        @pl.loop(0, 4)
        def _(t):
            rows = row_block(t, 256)
            hq = windowed(rows, 256)
            hqw[n, rows, :] = hq
            for part in range(3):
                cols = slice(part * D, (part + 1) * D)
                acc = nn(hq, wat[b, :, cols]) + vec[b * 8 + 6 : b * 8 + 7, cols]
                if part == 0:
                    acc = acc * SCALE
                qkv[n, rows, cols] = acc.astype(BF)

        hook(0)

        @pl.loop(0, WINDOWS)
        def _(w):
            rows = row_block(w, PLACES)
            cells = codew[rows, :]
            region = (cells >> 1) * b
            pad = (cells & 1).astype(F32)
            lane = lax.broadcasted_iota(jnp.int32, (PLACES, 128), 1)
            same = jnp.where(lane == region, 1.0, 0.0)
            left = jnp.where(lane == 127, 1.0 - pad, same).astype(BF)
            right = jnp.where(lane == 127, -pad, same).astype(BF)
            agree = nt(left, jnp.concatenate([right, right], axis=0))
            mask = jnp.where(agree > 0.5, 0.0, MASKED)
            for g in range(GROUPS):
                q = qkv[n, rows, g * 128 : (g + 1) * 128]
                k = qkv[n, rows, D + g * 128 : D + (g + 1) * 128]
                v = qkv[n, rows, 2 * D + g * 128 : 2 * D + (g + 1) * 128]
                scores = nt(by_low(k, lanes), by_high(q, lanes)) + bias[b, g]
                halves = []
                for h in range(2):
                    s = scores[h * PLACES : (h + 1) * PLACES] + mask
                    e = jnp.exp(s - jnp.max(s, axis=0, keepdims=True))
                    halves.append((e * (1.0 / jnp.sum(e, axis=0, keepdims=True))).astype(BF))
                p = jnp.concatenate(halves, axis=0)
                probs[n, w * GROUPS + g] = p
                att[n, rows, g * 128 : (g + 1) * 128] = own_high(tn(p, by_low(v, lanes)), lanes).astype(BF)

        hook(1)

        @pl.loop(0, 4)
        def _(t):
            rows = row_block(t, 256)
            winf[rows, :] = nn(att[n, rows, :], wat[b, :, 3 * D :])

        to_canvas(winf, canvf, SHIFT * b)

        @pl.loop(0, CELLS // TILE)
        def _(t):
            rows = row_block(t, TILE)
            out[rows, :] = (x[rows, :].astype(F32) + (canvf[rows, :] + vector(b, 2))).astype(BF)

    def mlp_forward(b, n, x, out, hook):
        @pl.loop(0, CELLS // TILE)
        def _(t):
            rows = row_block(t, TILE)
            xhat, _ = standardized(x[rows, :].astype(F32))
            hq2[n, rows, :] = (xhat * vector(b, 3) + vector(b, 4)).astype(BF)

        @pl.loop(0, FF // 256)
        def _(i):
            cols = pl.ds(pl.multiple_of(i * 256, 256), 256)
            pre = nn(hq2[n], fc1[b, :, cols]) + vec[b * 8 + 7 : b * 8 + 8, cols]
            for at in range(0, CELLS, 16):
                h, dg = gelu_parts(pre[at : at + 16])
                hid[n, at : at + 16, cols] = h.astype(BF)
                dgelu[n, at : at + 16, cols] = dg.astype(BF)

        hook(0)
        total = nn(hid[n], fc2[b])
        for at in range(0, CELLS, TILE):
            rows = slice(at, at + TILE)
            out[rows, :] = (x[rows, :].astype(F32) + (total[rows] + vector(b, 5))).astype(BF)

    def norm_backward(b, kind, x, gz, out):
        @pl.loop(0, CELLS // TILE)
        def _(t):
            rows = row_block(t, TILE)
            xhat, rs = standardized(x[rows, :].astype(F32))
            gn = canvf[rows, :]
            gzf = gz[rows, :].astype(F32)
            add_vec(b, kind, by_eights(gn * xhat))
            add_vec(b, kind + 1, by_eights(gn))
            add_vec(b, 5 if kind else 2, by_eights(gzf))
            g = gn * vector(b, kind)
            mg = jnp.mean(g, axis=-1, keepdims=True)
            mgx = jnp.mean(g * xhat, axis=-1, keepdims=True)
            out[rows, :] = (gzf + rs * (g - mg - xhat * mgx)).astype(BF)

    def mlp_backward(b, n, x, gz, out, free_out, hook):
        @pl.loop(0, FF // 256)
        def _(i):
            cols = pl.ds(pl.multiple_of(i * 256, 256), 256)
            gh = nt(gz[...], fc2[b, cols, :])
            sums = jnp.zeros((8, 256), F32)
            for at in range(0, CELLS, 16):
                gp = (gh[at : at + 16] * dgelu[n, at : at + 16, cols].astype(F32)).astype(BF)
                dgelu[n, at : at + 16, cols] = gp
                sums = sums + by_eights(gp.astype(F32))
            g_vec[b, 7, :, cols] += sums
            g_fc1[:, cols] += tn(hq2[n], dgelu[n, :, cols])
            g_fc2[cols, :] += tn(hid[n, :, cols], gz[...])

        hook(0)
        canvf[...] = nt(dgelu[n], fc1[b])
        free_out()
        norm_backward(b, 3, x, gz, out)

    def attention_backward(b, n, x, gz, out, free_out, hook):
        lanes = head_of_lane()

        @pl.loop(0, CELLS // TILE)
        def _(t):
            rows = row_block(t, TILE)
            canvf[rows, :] = gz[rows, :].astype(F32)

        to_windows(canvf, winf, SHIFT * b)

        @pl.loop(0, 4)
        def _(t):
            rows = row_block(t, 256)
            gzw[rows, :] = windowed(rows, 256)

        g_proj[...] += tn(att[n], gzw[...])

        @pl.loop(0, 4)
        def _(t):
            rows = row_block(t, 256)
            go[rows, :] = nt(gzw[rows, :], wat[b, :, 3 * D :]).astype(BF)

        hook(0)

        @pl.loop(0, WINDOWS)
        def _(w):
            rows = row_block(w, PLACES)
            for g in range(GROUPS):
                at = [slice(part * D + g * 128, part * D + (g + 1) * 128) for part in range(3)]
                q, k, v = (qkv[n, rows, cols] for cols in at)
                go_wide = by_high(go[rows, at[0]], lanes)
                p_low = probs[n, w * GROUPS + g]
                p = p_low.astype(F32)
                pd = p * nt(by_low(v, lanes), go_wide)
                halves = []
                for h in range(2):
                    half = slice(h * PLACES, (h + 1) * PLACES)
                    halves.append((pd[half] - p[half] * jnp.sum(pd[half], axis=0, keepdims=True)).astype(BF))
                ds = jnp.concatenate(halves, axis=0)
                g_tab[b, :, g * 128 : (g + 1) * 128] += ds.astype(F32)
                gqkv[rows, at[0]] = (own_high(tn(ds, by_low(k, lanes)), lanes) * SCALE).astype(BF)
                gqkv[rows, at[1]] = own_low(nn(ds, by_high(q, lanes)), lanes).astype(BF)
                gqkv[rows, at[2]] = own_low(nn(p_low, go_wide), lanes).astype(BF)

        hook(1)

        @pl.loop(0, 4)
        def _(t):
            rows = row_block(t, 256)
            gq = gqkv[rows, :]
            add_vec(b, 6, by_eights(gq.astype(F32)))
            winf[rows, :] = nt(gq, wat[b, :, : 3 * D])

        to_canvas(winf, canvf, SHIFT * b)
        free_out()
        norm_backward(b, 0, x, gz, out)

    def attention_weights(n):
        for part in range(3):
            cols = slice(part * D, (part + 1) * D)
            g_qkv[:, cols] += tn(hqw[n], gqkv[:, cols])

    def partner(k):
        x, y = me % 2, me // 2
        return 2 * (1 - y if k & 2 else y) + (1 - x if k & 1 else x)

    def act_copies(n):
        away = [
            remote(
                buf.at[partner(k), n],
                r.act_hbm.at[me, n],
                r.act_send.at[k - 1, n],
                r.act_recv.at[k - 1, n],
                {"pipe": partner(k)},
            )
            for k in (2, 1, 3)
        ]
        return away, pltpu.make_async_copy(buf.at[me, n], r.act_hbm.at[me, n], r.local_sem.at[0, n])

    def send_acts(n):
        away, local = act_copies(n)
        for copy in away:
            copy.start()
        local.start()

    def acts_sent(n):
        away, local = act_copies(n)
        for copy in away:
            copy.wait_send()
        local.wait()

    def push(s, n, start):
        src = buf.at[s, n]
        dst = r.igrad_hbm.at[me, n]
        local = pltpu.make_async_copy(src, dst, r.local_sem.at[1, n])
        away = remote(src, dst, r.send_sem.at[s, n], r.recv_sem.at[me, n], {"pipe": s})

        @pl.when(me == s)
        def _():
            local.start() if start else local.wait()

        @pl.when(me != s)
        def _():
            away.start() if start else away.wait_send()

    def arrived(k, n):
        sender = partner(k)
        got = r.act_hbm.at[sender, n]
        remote(got, got, r.act_send.at[k - 1, n], r.act_recv.at[k - 1, n], {"pipe": sender}).wait_recv()
        got = r.igrad_hbm.at[sender, n]
        remote(got, got, r.send_sem.at[0, n], r.recv_sem.at[sender, n], {"pipe": sender}).wait_recv()

    attention_stash = ((hqw, r.h_hqw), (qkv, r.h_qkv), (probs, r.h_probs), (att, r.h_att))
    mlp_stash = ((hq2, r.h_hq2), (hid, r.h_hid), (dgelu, r.h_dgelu))

    def stash(sec, n, back):
        pairs = mlp_stash if sec else attention_stash
        return [
            pltpu.make_async_copy(*((far.at[n], near.at[n]) if back else (near.at[n], far.at[n])), r.st_sem.at[sec, n, i])
            for i, (near, far) in enumerate(pairs)
        ]

    def load(src, n):
        return pltpu.make_async_copy(src.at[me, n], inb.at[n], r.in_sem.at[n])

    def start(copies):
        for copy in copies:
            copy.start()

    def wait(copies):
        for copy in copies:
            copy.wait()

    steps = (step_1, step_2, step_3, step_4, step_5)
    schedule = {
        (2, 0, 0): ((2, 3),),
        (2, 0, 1): ((3, 3),),
        (2, 1, 1): ((4, 3),),
        (1, 0, 0): ((2, 2), (5, 3)),
        (1, 1, 0): ((3, 2),),
        (0, 0, 0): ((2, 1), (5, 2)),
        (0, 1, 0): ((3, 1),),
        (0, 1, 1): ((4, 1),),
    }
    after = {3: ((1, 3),), 2: ((1, 2),), 1: ((1, 1), (4, 2)), 0: ()}
    weight_steps = (weights_1, weights_2, weights_3, weights_4) if linked else ()
    gathering = {
        (0, 4): ((3, 0), (4, 0)),
        (0, 0): ((2, 1),),
        (0, 1): ((2, 2), (2, 3), (3, 1)),
        (0, 3): ((4, 1), (3, 2)),
        (1, 3): ((4, 2),),
        (2, 0): ((3, 3),),
        (2, 3): ((4, 3),),
    }

    codes = [pltpu.make_async_copy(r.code_hbm, code, r.code_sem.at[0])]
    start(codes)
    start([load(r.x_hbm, n) for n in range(canvases)])
    wait(codes)

    @pl.loop(0, canvases)
    def _(n):
        def gather(sec, i):
            todo = gathering.get((sec, i), ())
            if linked and todo:

                @pl.when(n == 0)
                def _():
                    for step, of in todo:
                        weight_steps[step - 1](of)

        load(r.x_hbm, n).wait()
        x = inb.at[n]
        for s in range(4):
            if s >= 2:
                wait(stash(s - 2, n, False))
            forward = mlp_forward if s % 2 else attention_forward
            forward(s // 2, n, x, buf.at[s, n], functools.partial(gather, s))
            x = buf.at[s, n]
            if s == 3:
                send_acts(n)
            if s < 2:
                start(stash(s, n, False))
            if s == 0:
                load(r.cot_hbm, n).start()
            gather(s, 3)

    for s in (3, 2, 1, 0):
        cleared(*((g_fc1, g_fc2) if s % 2 else (g_qkv, g_proj)))

        @pl.loop(0, canvases)
        def _(n):
            def hook(i):
                for at in range(2):
                    todo = schedule.get((s, at, i), ())
                    if linked and todo:

                        @pl.when(n == (canvases - 1 if at else 0))
                        def _():
                            for step, of in todo:
                                steps[step - 1](of)

            if s == 3:
                load(r.cot_hbm, n).wait()
            if s == 0:
                load(r.x_hbm, n).wait()
            if s < 2:
                wait(stash(s, n, True))
            x = buf.at[s - 1, n] if s else inb.at[n]
            gz = inb.at[n] if s == 3 else buf.at[s + 1, n]
            backward = mlp_backward if s % 2 else attention_backward
            free_out = functools.partial(acts_sent, n) if s == 3 else lambda: None
            backward(s // 2, n, x, gz, buf.at[s, n], free_out, hook)
            if s % 2 == 0:
                attention_weights(n)
            if s == 2:
                push(3, n, True)
                push(2, n, True)
            if s == 0:

                @pl.when(n == 0)
                def _():
                    for i in range(canvases):
                        push(1, i, True)

                @pl.when(n < canvases - 1)
                def _():
                    push(0, n, True)

            if s == 3:
                load(r.x_hbm, n).start()
            if s >= 2:
                start(stash(s - 2, n, True))

        if linked:
            for step, of in after[s]:
                steps[step - 1](of)
        else:
            whole = ((g_fc1, r.f_fc1), (g_fc2, r.f_fc2)) if s % 2 else ((g_qkv, r.f_qkv), (g_proj, r.f_proj))
            copies = [pltpu.make_async_copy(a, o.at[s // 2], r.go_sem.at[s, i]) for i, (a, o) in enumerate(whole)]
            start(copies)
            wait(copies)

    if linked:
        step_1(0)
        step_5(1)
        smalls_sent(1)
        step_2(0)
    push(0, canvases - 1, True)
    if linked:
        step_3(0)
        step_4(0)
        step_5(0)
        reductions_done()
        weights_sent()
        for k in range(1, 8):
            pack_copy(k).wait_send()
    for k in range(1, 4):
        for n in range(canvases):
            arrived(k, n)
    for s in range(4):
        for n in range(canvases):
            push(s, n, False)


def compute(linked, operands):
    canvases = operands["x_hbm"].shape[1]
    shape = jax.ShapeDtypeStruct
    hbm = pl.BlockSpec(memory_space=pl.ANY)
    vmem = pl.BlockSpec(memory_space=pltpu.VMEM)
    dma = pltpu.SemaphoreType.DMA
    full = {
        "wat": ((2, D, 4 * D), BF),
        "fc1": ((2, D, FF), BF),
        "fc2": ((2, FF, D), BF),
        "vec": ((16, FF), F32),
    }
    grads = {
        "g_qkv": ((D, 3 * D), F32),
        "g_proj": ((D, D), F32),
        "g_fc1": ((D, FF), F32),
        "g_fc2": ((FF, D), F32),
        "g_vec": ((2, 8, 8, FF), F32),
        "g_tab": ((2, 2 * PLACES, GROUPS * 128), F32),
    }
    outs = {"act_hbm": ((4, canvases, CELLS, D), BF), "igrad_hbm": ((4, canvases, CELLS, D), BF)}
    kept = {
        "hqw": ((canvases, WROWS, D), BF),
        "qkv": ((canvases, WROWS, 3 * D), BF),
        "probs": ((canvases, WINDOWS * GROUPS, 128, 128), BF),
        "att": ((canvases, WROWS, D), BF),
        "hq2": ((canvases, CELLS, D), BF),
        "hid": ((canvases, CELLS, FF), BF),
        "dgelu": ((canvases, CELLS, FF), BF),
    }
    outs |= {"h_" + name: kind for name, kind in kept.items()}
    scratch = kept | {
        "inb": ((canvases, CELLS, D), BF),
        "code": ((canvases, CELLS, 128), jnp.int32),
        "codew": ((WROWS, 128), jnp.int32),
        "buf": ((4, canvases, CELLS, D), BF),
        "canvf": ((CELLS, D), F32),
        "winf": ((WROWS, D), F32),
        "gzw": ((WROWS, D), BF),
        "go": ((WROWS, D), BF),
        "gqkv": ((WROWS, 3 * D), BF),
    }
    sems = {
        "in_sem": (canvases,),
        "code_sem": (1,),
        "st_sem": (2, canvases, 4),
        "local_sem": (2, canvases),
        "act_send": (3, canvases),
        "act_recv": (3, canvases),
        "send_sem": (4, canvases),
        "recv_sem": (4, canvases),
    }
    if linked:
        outs |= {
            "o_qkv": ((2, 48, 3 * D), F32),
            "o_proj": ((2, 48, D), F32),
            "o_fc1": ((2, 48, FF), F32),
            "o_fc2": ((2, 192, D), F32),
            "o_small": ((2, 8, 64, D), BF),
        }
        scratch |= full | grads
        scratch |= {
            "packs": ((8, 16, 256), BF),
            "l_qkv": ((48, 3 * D), F32),
            "l_proj": ((48, D), F32),
            "l_fc1": ((48, FF), F32),
            "l_fc2": ((192, D), F32),
        }
        for kind, rows in (("m_", MLP_ROWS), ("a_", ATT_ROWS)):
            scratch |= {
                kind + "st_a": ((4, rows, D), BF),
                kind + "rc_a": ((4, rows, D), BF),
                kind + "st_b": ((4, rows, D), BF),
                kind + "rc_b": ((3, 4, rows // 4, D), BF),
                kind + "st_c": ((4, rows // 4, D), BF),
                kind + "rc_c": ((3, rows // 4, D), BF),
                kind + "fin": ((rows, D), BF),
            }
        sems |= {
            "sh_sem": (4, 2),
            "os_sem": (2,),
            "go_sem": (4, 2),
            "wz_send": (4, 2, 3),
            "wz_recv": (4, 2, 3),
            "wx_send": (4, 2, 3, 3),
            "wx_recv": (4, 2, 3, 3),
            "ws_send": (4, 2, 4),
            "ws_recv": (4, 2, 4),
            "pk_send": (7,),
            "pk_recv": (7,),
            "ra_send": (4,),
            "ra_recv": (4,),
            "rb_send": (4, 3),
            "rb_recv": (4, 3),
            "rc_send": (4, 3),
            "rc_recv": (4, 3),
            "rf_send": (4, 3),
            "rf_recv": (4, 3),
            "rs_send": (2, 7),
            "rs_recv": (2, 7),
        }
    else:
        for name in ("g_vec", "g_tab"):
            outs[name] = grads.pop(name)
        outs |= {name.replace("g_", "f_"): ((2,) + dims, F32) for name, (dims, _) in grads.items()}
        scratch |= grads
        sems["go_sem"] = (4, 2)
    in_vmem = set(full) | {"bias", "pack", "g_vec", "g_tab"}
    names = tuple(operands) + tuple(outs) + tuple(scratch) + tuple(sems)
    results = pl.pallas_call(
        functools.partial(kernel, names, linked, canvases),
        out_shape=tuple(shape(*o) for o in outs.values()),
        in_specs=[vmem if name in in_vmem else hbm for name in operands],
        out_specs=tuple(vmem if name in in_vmem else hbm for name in outs),
        scratch_shapes=[pltpu.VMEM(*v) for v in scratch.values()] + [dma(v) for v in sems.values()],
        compiler_params=pltpu.CompilerParams(
            vmem_limit_bytes=64 * 1024 * 1024 - 65536, collective_id=0, has_side_effects=True
        ),
    )(*operands.values())
    return dict(zip(outs, results))


def place_pairs():
    place = np.arange(PLACES)
    r, c = place // 8, place % 8
    index = (r[None, :] - r[:, None] + WIN - 1) * (2 * WIN - 1) + c[None, :] - c[:, None] + WIN - 1
    real = (r < WIN) & (c < WIN)
    return index, real[:, None] & real[None, :], real


def pair_onehot():
    index, both, _ = place_pairs()
    table = (2 * WIN - 1) ** 2
    hot = (np.where(both, index, -1).reshape(-1)[None, :] == np.arange(table)[:, None])
    return hot.astype(np.float32)


def body(
    inputs,
    cotangent,
    pad_mask,
    region_ids,
    norm1_gain,
    norm1_bias,
    qkv_weight,
    qv_bias,
    rel_table,
    proj_weight,
    proj_bias,
    norm2_gain,
    norm2_bias,
    fc1_weight,
    fc1_bias,
    fc2_weight,
    fc2_bias,
):
    owners = lax.axis_size("dp")
    linked = owners == 8
    mine = lax.axis_index("pipe")

    def own(a):
        return lax.dynamic_index_in_dim(a, mine, 0, keepdims=False)

    code = own(region_ids) * 2 + own(pad_mask)
    code = jnp.broadcast_to(code[:, :, None], code.shape + (128,))

    hot = pair_onehot()
    _, _, real = place_pairs()
    rel = lax.dot_general(
        rel_table.astype(BF), jnp.asarray(hot, BF), (((1,), (0,)), ((), ())), preferred_element_type=F32
    )
    rel = rel.reshape(2, GROUPS, 2, 2, PLACES, PLACES)
    rel = jnp.where(jnp.asarray(real)[None, None, None, None, :, None], rel, MASKED)
    rel = rel.transpose(0, 1, 3, 4, 2, 5).reshape(2, GROUPS, 128, 128)

    operands = {"x_hbm": inputs, "cot_hbm": cotangent, "code_hbm": code, "bias": rel}
    vectors = (norm1_gain, norm1_bias, proj_bias, norm2_gain, norm2_bias, fc2_bias, qv_bias, fc1_bias)
    sizes = [v.shape[1] for v in vectors]
    ends = np.cumsum([0] + sizes)
    if linked:
        pack = jnp.stack([jnp.pad(v, ((0, 0), (0, 256 - v.shape[1]))) for v in vectors], axis=1)
        operands |= {
            "pack": pack.reshape(16, 256).astype(BF),
            "s_qkv": qkv_weight,
            "s_proj": proj_weight,
            "s_fc1": fc1_weight,
            "s_fc2": fc2_weight,
        }
    else:

        def gathered(a):
            return lax.all_gather(a.astype(BF), "dp", axis=1, tiled=True)

        packed = lax.all_gather(jnp.concatenate(vectors, axis=1).astype(BF), "dp", axis=1)
        parts = [packed[:, :, a:b].reshape(2, -1).astype(F32) for a, b in zip(ends[:-1], ends[1:])]
        qv = parts[6]
        parts[6] = jnp.concatenate([qv[:, :D], jnp.zeros_like(qv[:, :D]), qv[:, D:]], axis=1)
        vec = jnp.stack([jnp.pad(p, ((0, 0), (0, FF - p.shape[1]))) for p in parts], axis=1)
        operands |= {
            "wat": jnp.concatenate([gathered(qkv_weight), gathered(proj_weight)], axis=2),
            "fc1": gathered(fc1_weight),
            "fc2": gathered(fc2_weight),
            "vec": vec.reshape(16, FF),
        }

    out = compute(linked, operands)

    def to_owners(g):
        shared = lax.psum_scatter(g, "dp", scatter_dimension=1, tiled=True)
        return lax.psum(shared, "pipe")

    if linked:
        small = out["o_small"]
        g_tab = small[:, :, :16].reshape(2, 128, GROUPS * 128)
        g_vec = jnp.concatenate([small[:, :, 16 + 8 * j : 24 + 8 * j] for j in range(4)], axis=3)
    else:
        g_tab, g_vec = out["g_tab"], out["g_vec"]

    g_vec = jnp.sum(g_vec.astype(F32), axis=2)
    kinds = [g_vec[:, i] for i in range(8)]
    qv_sum = jnp.concatenate([kinds[6][:, :D], kinds[6][:, 2 * D : 3 * D]], axis=1)
    rows = [kinds[0], kinds[1], kinds[2], kinds[3], kinds[4], kinds[5], qv_sum, kinds[7]]
    if linked:
        at = lax.axis_index("dp")
        small = [lax.dynamic_slice_in_dim(v, at * n, n, 1) for v, n in zip(rows, sizes)]
    else:
        rows = [v[:, : n * owners].reshape(2, -1, n) for v, n in zip(rows, sizes)]
        g_small = to_owners(jnp.concatenate(rows, axis=2))[:, 0]
        small = [g_small[:, a:b] for a, b in zip(ends[:-1], ends[1:])]

    pairs = g_tab.reshape(2, 2, PLACES, GROUPS, 2, PLACES).transpose(0, 3, 4, 1, 2, 5)
    pairs = pairs.reshape(2, HEADS, PLACES * PLACES)
    g_table = lax.dot_general(
        jnp.broadcast_to(jnp.asarray(hot, pairs.dtype), (2,) + hot.shape),
        pairs,
        (((2,), (2,)), ((0,), (0,))),
        precision=None if linked else lax.Precision.HIGHEST,
        preferred_element_type=F32,
    )
    if linked:
        big = [out[name] for name in ("o_qkv", "o_proj", "o_fc1", "o_fc2")]
    else:
        g_table = lax.psum(g_table, ("pipe", "dp"))
        big = [to_owners(out[name]) for name in ("f_qkv", "f_proj", "f_fc1", "f_fc2")]

    return (
        out["act_hbm"][None],
        out["igrad_hbm"][None],
        small[0],
        small[1],
        big[0],
        small[6],
        g_table,
        big[1],
        small[2],
        small[3],
        small[4],
        big[2],
        small[7],
        big[3],
        small[5],
    )


def solution(mesh):
    cols = P(None, "dp")
    rows = P(None, "dp", None)
    return jax.shard_map(
        body,
        mesh=mesh,
        in_specs=(
            P(None, "dp", None, None),
            P(None, "dp", None, None),
            rows,
            rows,
            cols,
            cols,
            rows,
            cols,
            P(),
            rows,
            cols,
            cols,
            cols,
            rows,
            cols,
            rows,
            cols,
        ),
        out_specs=(
            P("pipe", None, "dp", None, None),
            P("pipe", None, "dp", None, None),
            cols,
            cols,
            rows,
            cols,
            P(),
            rows,
            cols,
            cols,
            cols,
            rows,
            cols,
            rows,
            cols,
        ),
        check_vma=False,
    )
```

```python
import functools
import types

import jax
import jax.numpy as jnp
import numpy as np
from jax import lax
from jax.experimental import pallas as pl
from jax.experimental.pallas import tpu as pltpu
from jax.sharding import PartitionSpec as P

HEADS = 12
WIN = 7
SHIFT = 3
GRID = 28
CELLS = 784
D = 384
FF = 1536
HEAD = 32
SIDE = 4
WINDOWS = 16
PLACES = 64
WROWS = WINDOWS * PLACES
GROUPS = 3
TILE = 112
SCALE = HEAD**-0.5
NORM_EPS = 1e-05
MASKED = -1e30
BF = jnp.bfloat16
F32 = jnp.float32

RSQRT_2 = 1.0 / np.sqrt(2.0)
PHI_0 = 1.0 / np.sqrt(2.0 * np.pi)


def nn(a, b):
    return lax.dot_general(a, b, (((1,), (0,)), ((), ())), preferred_element_type=F32)


def nt(a, b):
    return lax.dot_general(a, b, (((1,), (1,)), ((), ())), preferred_element_type=F32)


def tn(a, b):
    return lax.dot_general(a, b, (((0,), (0,)), ((), ())), preferred_element_type=F32)


def segments(shift):
    runs = []
    for wr in range(SIDE):
        for r in range(WIN):
            row = (wr * WIN + r + shift) % GRID
            for wc in range(SIDE):
                col = (wc * WIN + shift) % GRID
                place = (wr * SIDE + wc) * PLACES + r * 8
                first = min(WIN, GRID - col)
                runs.append((row * GRID + col, place, first))
                if first < WIN:
                    runs.append((row * GRID, place + first, WIN - first))
    return runs


def to_windows(src, dst, shift):
    for cell, place, count in segments(shift):
        dst[pl.ds(place, count), :] = src[pl.ds(cell, count), :]


def to_canvas(src, dst, shift):
    for cell, place, count in segments(shift):
        dst[pl.ds(cell, count), :] = src[pl.ds(place, count), :]


def row_block(t, size):
    return pl.ds(pl.multiple_of(t * size, 16), size)


def standardized(v):
    centered = v - jnp.mean(v, axis=-1, keepdims=True)
    spread = jnp.mean(centered * centered, axis=-1, keepdims=True)
    rs = lax.rsqrt(spread + NORM_EPS)
    return centered * rs, rs


def by_eights(v):
    return jnp.sum(v.reshape(v.shape[0] // 8, 8, v.shape[1]), axis=0)


def gelu_parts(x):
    cdf = 0.5 + 0.5 * lax.erf(x * RSQRT_2)
    return x * cdf, cdf + x * (jnp.exp(-0.5 * x * x) * PHI_0)


def real_places(rows):
    place = lax.broadcasted_iota(jnp.int32, (rows, 1), 0)
    return ((place & 7) < WIN) & (((place >> 3) & 7) < WIN)


def head_of_lane():
    return lax.broadcasted_iota(jnp.int32, (PLACES, 128), 1) >> 5


def by_low(x, lanes):
    zero = jnp.zeros_like(x)
    return jnp.concatenate([jnp.where((lanes & 1) == h, x, zero) for h in range(2)], axis=0)


def by_high(x, lanes):
    zero = jnp.zeros_like(x)
    return jnp.concatenate([jnp.where((lanes >> 1) == h, x, zero) for h in range(2)], axis=0)


def own_low(wide, lanes):
    return jnp.where((lanes & 1) == 0, wide[:PLACES], wide[PLACES:])


def own_high(wide, lanes):
    return jnp.where((lanes >> 1) == 0, wide[:PLACES], wide[PLACES:])


MESH = pl.DeviceIdType.MESH
ATT_ROWS = 256
MLP_ROWS = 384
SMALL = 192


def kernel(names, linked, canvases, *refs):
    r = types.SimpleNamespace(**dict(zip(names, refs)))
    me = lax.axis_index("pipe")
    inb, code, codew, buf = r.inb, r.code, r.codew, r.buf
    hqw, qkv, probs, att = r.hqw, r.qkv, r.probs, r.att
    hq2, hid, dgelu = r.hq2, r.hid, r.dgelu
    canvf, winf, gzw, gqkv, go = r.canvf, r.winf, r.gzw, r.gqkv, r.go
    g_qkv, g_proj, g_fc1, g_fc2, g_vec, g_tab = r.g_qkv, r.g_proj, r.g_fc1, r.g_fc2, r.g_vec, r.g_tab
    wat, fc1, fc2, vec, bias = r.wat, r.fc1, r.fc2, r.vec, r.bias
    if linked:
        d = lax.axis_index("dp")
        z, c = d // 2, d % 2
        sibling = {"dp": 2 * z + 1 - c}

    def z_peer(k):
        return {"dp": 2 * lax.rem(z + k, 4) + c}

    def pipe_peer(k):
        return {"pipe": lax.rem(me + k, 4)}

    def dp_peer(k):
        return {"dp": lax.rem(d + k, 8)}

    def remote(src, dst, send, recv, device):
        return pltpu.make_async_remote_copy(
            src_ref=src, dst_ref=dst, send_sem=send, recv_sem=recv, device_id=device, device_id_type=MESH
        )

    barrier = pltpu.get_barrier_semaphore()
    partners = [pipe_peer(k) for k in range(1, 4)]
    if linked:
        partners += [dp_peer(k) for k in range(1, 8)]
    for partner in partners:
        pl.semaphore_signal(barrier, inc=1, device_id=partner, device_id_type=MESH)

    full = ((wat,), (fc1, fc2), (wat,), (fc1, fc2))

    def owner_back(k):
        return 2 * lax.rem(z + 4 - k, 4) + c

    def shard(sec, a, owner):
        h = 192 if a else 48
        return full[sec][a].at[sec // 2, pl.ds(pl.multiple_of(owner * h, 16), h), :]

    def part(sec, a, owner, place):
        if a:
            return fc2.at[sec // 2, pl.ds(pl.multiple_of(owner * 192 + place * 48, 16), 48), :]
        rows = pl.ds(pl.multiple_of(owner * 48, 16), 48)
        return full[sec][0].at[sec // 2, rows, pl.ds(pl.multiple_of(place * D, 128), D)]

    def to_z(sec, a, k):
        own = part(sec, a, d, me)
        return remote(own, own, r.wz_send.at[sec, a, k - 1], r.wz_recv.at[sec, a, k - 1], z_peer(k))

    def to_places(sec, a, k, j):
        got = part(sec, a, owner_back(k), me)
        return remote(
            got, got, r.wx_send.at[sec, a, k - 1, j - 1], r.wx_recv.at[sec, a, k - 1, j - 1], pipe_peer(j)
        )

    def to_sibling(sec, a, k):
        block = shard(sec, a, owner_back(k))
        return remote(block, block, r.ws_send.at[sec, a, k], r.ws_recv.at[sec, a, k], sibling)

    def weights_1(sec):
        for a in range(len(full[sec])):
            for k in range(1, 4):
                to_z(sec, a, k).start()
            to_sibling(sec, a, 0).start()

    def weights_2(sec):
        for k in range(1, 4):
            for a in range(len(full[sec])):
                got = part(sec, a, owner_back(k), me)
                remote(got, got, r.wz_send.at[sec, a, k - 1], r.wz_recv.at[sec, a, k - 1], z_peer(k)).wait_recv()
                for j in range(1, 4):
                    to_places(sec, a, k, j).start()

    def weights_3(sec):
        for k in range(1, 4):
            for a in range(len(full[sec])):
                for j in range(1, 4):
                    got = part(sec, a, owner_back(k), lax.rem(me + 4 - j, 4))
                    remote(
                        got, got, r.wx_send.at[sec, a, k - 1, j - 1], r.wx_recv.at[sec, a, k - 1, j - 1], pipe_peer(j)
                    ).wait_recv()
                to_sibling(sec, a, k).start()

    def weights_4(sec):
        for k in range(4):
            for a in range(len(full[sec])):
                block = shard(sec, a, 2 * lax.rem(z + 4 - k, 4) + 1 - c)
                remote(block, block, r.ws_send.at[sec, a, k], r.ws_recv.at[sec, a, k], sibling).wait_recv()

    def weights_sent():
        for sec in range(4):
            for a in range(len(full[sec])):
                for k in range(4):
                    to_sibling(sec, a, k).wait_send()
                    if k:
                        to_z(sec, a, k).wait_send()
                        for j in range(1, 4):
                            to_places(sec, a, k, j).wait_send()

    def pack_copy(k):
        return remote(
            r.packs.at[d], r.packs.at[d], r.pk_send.at[k - 1], r.pk_recv.at[k - 1], dp_peer(k)
        )

    def pack_arrival(k):
        slot = r.packs.at[lax.rem(d + 8 - k, 8)]
        return remote(slot, slot, r.pk_send.at[k - 1], r.pk_recv.at[k - 1], dp_peer(k))

    def place_vectors():
        kind = lax.broadcasted_iota(jnp.int32, (16, 256), 0) & 7
        lane = lax.broadcasted_iota(jnp.int32, (16, 256), 1)
        vec[...] = jnp.zeros_like(vec)
        for width, kinds in ((48, kind < 6), (96, kind == 6), (192, kind == 7)):
            for owner in range(8):
                at = owner * width
                if width == 96 and owner >= 4:
                    at += D
                start = at // 128 * 128
                part = jnp.where(kinds & (lane < width), r.packs[owner].astype(F32), 0.0)
                if at > start:
                    part = pltpu.roll(part, at - start, 1)
                vec[:, start : start + 256] += part

    def pieces(sec, owner):
        b = sec // 2
        out = []

        def matrix(ref, h):
            for t in range(h // 48):
                rows = pl.ds(pl.multiple_of(owner * h + t * 48, 16), 48)
                for j in range(ref.shape[1] // D):
                    load = functools.partial(lambda ref, rows, j: ref[rows, j * D : (j + 1) * D], ref, rows, j)
                    out.append((len(out) * 48, 48, load))

        def small():
            parts = [g_tab[b, pl.ds(pl.multiple_of(owner * 16, 16), 16), :]]
            parts += [g_vec[b, owner, :, j * D : (j + 1) * D] for j in range(4)]
            return jnp.concatenate(parts + [jnp.zeros((16, D), F32)], axis=0)

        if sec % 2:
            matrix(g_fc1, 48)
            matrix(g_fc2, 192)
        else:
            matrix(g_qkv, 48)
            matrix(g_proj, 48)
            out.append((SMALL, 64, small))
        return out

    def reduce_refs(sec):
        kind = "m" if sec % 2 else "a"
        return types.SimpleNamespace(
            **{n: getattr(r, kind + "_" + n) for n in ("st_a", "rc_a", "st_b", "rc_b", "st_c", "rc_c", "fin")}
        )

    def step_1(sec):
        q = reduce_refs(sec)
        if sec < 2:
            copy_a(sec + 2).wait_send()
            for k in range(1, 4):
                copy_b(sec + 2, k).wait_send()
                copy_c(sec + 2, k).wait_send()
        for k in range(4):
            i = lax.rem(z + k, 4)
            kept = q.st_b.at[k - 1] if k else q.st_c
            for row, rows, load in pieces(sec, 2 * i + 1 - c):
                q.st_a[i, row : row + rows, :] = load().astype(BF)
            for row, rows, load in pieces(sec, 2 * i + c):
                kept[row : row + rows, :] = load().astype(BF)
        copy_a(sec).start()

    def copy_a(sec):
        q = reduce_refs(sec)
        return remote(q.st_a, q.rc_a, r.ra_send.at[sec], r.ra_recv.at[sec], sibling)

    def copy_b(sec, k):
        q = reduce_refs(sec)
        return remote(
            q.st_b.at[k - 1], q.rc_b.at[k - 1], r.rb_send.at[sec, k - 1], r.rb_recv.at[sec, k - 1], z_peer(k)
        )

    def step_2(sec):
        q = reduce_refs(sec)
        copy_a(sec).wait_recv()
        for k in (1, 2, 3, 0):
            i = lax.rem(z + k, 4)
            kept = q.st_b.at[k - 1] if k else q.st_c
            for row in range(0, kept.shape[0], 64):
                at = slice(row, row + 64)
                kept[at, :] = (kept[at, :].astype(F32) + q.rc_a[i, at, :].astype(F32)).astype(BF)
            if k:
                copy_b(sec, k).start()

    def quarter(sec, ref, who):
        rows = (MLP_ROWS if sec % 2 else ATT_ROWS) // 4
        return ref.at[pl.ds(pl.multiple_of(who * rows, 16), rows), :]

    def copy_c(sec, k):
        q = reduce_refs(sec)
        return remote(
            quarter(sec, q.st_c, lax.rem(me + k, 4)),
            q.rc_c.at[k - 1],
            r.rc_send.at[sec, k - 1],
            r.rc_recv.at[sec, k - 1],
            pipe_peer(k),
        )

    def step_3(sec):
        q = reduce_refs(sec)
        for k in range(1, 4):
            copy_b(sec, k).wait_recv()
        for row in range(0, q.st_c.shape[0], 64):
            at = slice(row, row + 64)
            total = q.st_c[at, :].astype(F32)
            for k in range(3):
                total = total + q.rc_b[k, at, :].astype(F32)
            q.st_c[at, :] = total.astype(BF)
        for k in range(1, 4):
            copy_c(sec, k).start()

    def copy_f(sec, k):
        q = reduce_refs(sec)
        own = quarter(sec, q.fin, me)
        return remote(own, own, r.rf_send.at[sec, k - 1], r.rf_recv.at[sec, k - 1], pipe_peer(k))

    def step_4(sec):
        q = reduce_refs(sec)
        for k in range(1, 4):
            copy_c(sec, k).wait_recv()
            if sec < 2:
                copy_f(sec + 2, k).wait_send()
        total = quarter(sec, q.st_c, me)[...].astype(F32)
        for k in range(3):
            total = total + q.rc_c[k].astype(F32)
        quarter(sec, q.fin, me)[...] = total.astype(BF)
        for k in range(1, 4):
            copy_f(sec, k).start()

    def copy_s(b, k):
        rows = pl.ds(SMALL, 64)
        return remote(
            r.a_fin.at[rows, :], r.o_small.at[b, d], r.rs_send.at[b, k - 1], r.rs_recv.at[b, k - 1], dp_peer(k)
        )

    def own_small(b):
        return pltpu.make_async_copy(r.a_fin.at[pl.ds(SMALL, 64), :], r.o_small.at[b, d], r.os_sem.at[b])

    def outputs(sec):
        pairs = ((r.l_fc1, r.o_fc1), (r.l_fc2, r.o_fc2)) if sec % 2 else ((r.l_qkv, r.o_qkv), (r.l_proj, r.o_proj))
        return [
            pltpu.make_async_copy(ref, out.at[sec // 2], r.go_sem.at[sec, i]) for i, (ref, out) in enumerate(pairs)
        ]

    def step_5(sec):
        q = reduce_refs(sec)
        b = sec // 2
        for k in range(1, 4):
            got = quarter(sec, q.fin, lax.rem(me + 4 - k, 4))
            remote(got, got, r.rf_send.at[sec, k - 1], r.rf_recv.at[sec, k - 1], pipe_peer(k)).wait_recv()
        if sec % 2 == 0:
            for k in range(1, 8):
                copy_s(b, k).start()
            own_small(b).start()
        if sec < 2:
            for out in outputs(sec + 2):
                out.wait()
        row = 0
        for ref in (r.l_fc1, r.l_fc2) if sec % 2 else (r.l_qkv, r.l_proj):
            for t in range(ref.shape[0] // 48):
                for j in range(ref.shape[1] // D):
                    ref[t * 48 : (t + 1) * 48, j * D : (j + 1) * D] = q.fin[row : row + 48, :].astype(F32)
                    row += 48
        for out in outputs(sec):
            out.start()

    def smalls_sent(b):
        for k in range(1, 8):
            copy_s(b, k).wait_send()
        own_small(b).wait()

    def reductions_done():
        for sec in (1, 0):
            copy_a(sec).wait_send()
            for k in range(1, 4):
                copy_b(sec, k).wait_send()
                copy_c(sec, k).wait_send()
                copy_f(sec, k).wait_send()
        for sec in range(2):
            for out in outputs(sec):
                out.wait()
        smalls_sent(0)
        for b in range(2):
            for k in range(1, 8):
                rows = pl.ds(SMALL, 64)
                remote(
                    r.a_fin.at[rows, :],
                    r.o_small.at[b, lax.rem(d + 8 - k, 8)],
                    r.rs_send.at[b, k - 1],
                    r.rs_recv.at[b, k - 1],
                    dp_peer(k),
                ).wait_recv()

    if linked:
        lands = ((r.s_qkv, g_qkv, wat, 0), (r.s_proj, g_proj, wat, 3 * D), (r.s_fc1, g_fc1, fc1, 0), (r.s_fc2, g_fc2, fc2, 0))

        def landing(i, b):
            src, dst, _, _ = lands[i]
            h, n = src.shape[1:]
            return pltpu.make_async_copy(
                src.at[b], dst.at[pl.ds(192 * b, h), pl.ds(0, n)], r.sh_sem.at[i, b]
            )

        for i in range(4):
            for b in range(2):
                landing(i, b).start()
        r.packs[d] = r.pack[...]
        for i, (src, dst, ref, col) in enumerate(lands):
            h, n = src.shape[1:]
            for b in range(2):
                landing(i, b).wait()
                for t in range(0, h, 48):
                    rows = pl.ds(pl.multiple_of(d * h + t, 16), 48)
                    ref[b, rows, col : col + n] = dst[192 * b + t : 192 * b + t + 48, :n].astype(BF)
    pl.semaphore_wait(barrier, len(partners))
    if linked:
        for k in range(1, 8):
            pack_copy(k).start()
        weights_1(0)

    def cleared(*refs):
        for ref in refs:

            @pl.loop(0, ref.shape[0] // 16)
            def _(i):
                ref[row_block(i, 16), :] = jnp.zeros((16, ref.shape[1]), F32)

    g_vec[...] = jnp.zeros_like(g_vec)
    g_tab[...] = jnp.zeros_like(g_tab)
    codew[...] = jnp.zeros_like(codew)

    if linked:
        weights_2(0)
        for sec in range(1, 4):
            weights_1(sec)
        for k in range(1, 8):
            pack_arrival(k).wait_recv()
        place_vectors()

    def vector(b, kind, width=D):
        return vec[b * 8 + kind : b * 8 + kind + 1, :width]

    def add_vec(b, kind, part):
        g_vec[b, kind, :, : part.shape[1]] += part

    def windowed(rows, count):
        return jnp.where(real_places(count), winf[rows, :], 0.0).astype(BF)

    def attention_forward(b, n, x, out, hook):
        lanes = head_of_lane()

        @pl.loop(0, CELLS // TILE)
        def _(t):
            rows = row_block(t, TILE)
            xhat, _ = standardized(x[rows, :].astype(F32))
            canvf[rows, :] = xhat * vector(b, 0) + vector(b, 1)

        to_windows(canvf, winf, SHIFT * b)
        to_windows(code.at[n], codew, SHIFT * b)
        hook(4)

        @pl.loop(0, 4)
        def _(t):
            rows = row_block(t, 256)
            hq = windowed(rows, 256)
            hqw[n, rows, :] = hq
            for part in range(3):
                cols = slice(part * D, (part + 1) * D)
                acc = nn(hq, wat[b, :, cols]) + vec[b * 8 + 6 : b * 8 + 7, cols]
                if part == 0:
                    acc = acc * SCALE
                qkv[n, rows, cols] = acc.astype(BF)

        hook(0)

        @pl.loop(0, WINDOWS)
        def _(w):
            rows = row_block(w, PLACES)
            cells = codew[rows, :]
            region = (cells >> 1) * b
            pad = (cells & 1).astype(F32)
            lane = lax.broadcasted_iota(jnp.int32, (PLACES, 128), 1)
            same = jnp.where(lane == region, 1.0, 0.0)
            left = jnp.where(lane == 127, 1.0 - pad, same).astype(BF)
            right = jnp.where(lane == 127, -pad, same).astype(BF)
            agree = nt(left, jnp.concatenate([right, right], axis=0))
            mask = jnp.where(agree > 0.5, 0.0, MASKED)
            for g in range(GROUPS):
                q = qkv[n, rows, g * 128 : (g + 1) * 128]
                k = qkv[n, rows, D + g * 128 : D + (g + 1) * 128]
                v = qkv[n, rows, 2 * D + g * 128 : 2 * D + (g + 1) * 128]
                scores = nt(by_low(k, lanes), by_high(q, lanes)) + bias[b, g]
                halves = []
                for h in range(2):
                    s = scores[h * PLACES : (h + 1) * PLACES] + mask
                    e = jnp.exp(s - jnp.max(s, axis=0, keepdims=True))
                    halves.append((e * (1.0 / jnp.sum(e, axis=0, keepdims=True))).astype(BF))
                p = jnp.concatenate(halves, axis=0)
                probs[n, w * GROUPS + g] = p
                att[n, rows, g * 128 : (g + 1) * 128] = own_high(tn(p, by_low(v, lanes)), lanes).astype(BF)

        hook(1)

        @pl.loop(0, 4)
        def _(t):
            rows = row_block(t, 256)
            winf[rows, :] = nn(att[n, rows, :], wat[b, :, 3 * D :])

        to_canvas(winf, canvf, SHIFT * b)

        @pl.loop(0, CELLS // TILE)
        def _(t):
            rows = row_block(t, TILE)
            out[rows, :] = (x[rows, :].astype(F32) + (canvf[rows, :] + vector(b, 2))).astype(BF)

    def mlp_forward(b, n, x, out, hook):
        @pl.loop(0, CELLS // TILE)
        def _(t):
            rows = row_block(t, TILE)
            xhat, _ = standardized(x[rows, :].astype(F32))
            hq2[n, rows, :] = (xhat * vector(b, 3) + vector(b, 4)).astype(BF)

        @pl.loop(0, FF // 256)
        def _(i):
            cols = pl.ds(pl.multiple_of(i * 256, 256), 256)
            pre = nn(hq2[n], fc1[b, :, cols]) + vec[b * 8 + 7 : b * 8 + 8, cols]
            for at in range(0, CELLS, 16):
                h, dg = gelu_parts(pre[at : at + 16])
                hid[n, at : at + 16, cols] = h.astype(BF)
                dgelu[n, at : at + 16, cols] = dg.astype(BF)

        hook(0)
        total = nn(hid[n], fc2[b])
        for at in range(0, CELLS, TILE):
            rows = slice(at, at + TILE)
            out[rows, :] = (x[rows, :].astype(F32) + (total[rows] + vector(b, 5))).astype(BF)

    def norm_backward(b, kind, x, gz, out):
        @pl.loop(0, CELLS // TILE)
        def _(t):
            rows = row_block(t, TILE)
            xhat, rs = standardized(x[rows, :].astype(F32))
            gn = canvf[rows, :]
            gzf = gz[rows, :].astype(F32)
            add_vec(b, kind, by_eights(gn * xhat))
            add_vec(b, kind + 1, by_eights(gn))
            add_vec(b, 5 if kind else 2, by_eights(gzf))
            g = gn * vector(b, kind)
            mg = jnp.mean(g, axis=-1, keepdims=True)
            mgx = jnp.mean(g * xhat, axis=-1, keepdims=True)
            out[rows, :] = (gzf + rs * (g - mg - xhat * mgx)).astype(BF)

    def mlp_backward(b, n, x, gz, out, free_out, hook):
        @pl.loop(0, FF // 256)
        def _(i):
            cols = pl.ds(pl.multiple_of(i * 256, 256), 256)
            gh = nt(gz[...], fc2[b, cols, :])
            sums = jnp.zeros((8, 256), F32)
            for at in range(0, CELLS, 16):
                gp = (gh[at : at + 16] * dgelu[n, at : at + 16, cols].astype(F32)).astype(BF)
                dgelu[n, at : at + 16, cols] = gp
                sums = sums + by_eights(gp.astype(F32))
            g_vec[b, 7, :, cols] += sums
            g_fc1[:, cols] += tn(hq2[n], dgelu[n, :, cols])
            g_fc2[cols, :] += tn(hid[n, :, cols], gz[...])

        hook(0)
        canvf[...] = nt(dgelu[n], fc1[b])
        free_out()
        norm_backward(b, 3, x, gz, out)

    def attention_backward(b, n, x, gz, out, free_out, hook):
        lanes = head_of_lane()

        @pl.loop(0, CELLS // TILE)
        def _(t):
            rows = row_block(t, TILE)
            canvf[rows, :] = gz[rows, :].astype(F32)

        to_windows(canvf, winf, SHIFT * b)

        @pl.loop(0, 4)
        def _(t):
            rows = row_block(t, 256)
            gzw[rows, :] = windowed(rows, 256)

        g_proj[...] += tn(att[n], gzw[...])

        @pl.loop(0, 4)
        def _(t):
            rows = row_block(t, 256)
            go[rows, :] = nt(gzw[rows, :], wat[b, :, 3 * D :]).astype(BF)

        hook(0)

        @pl.loop(0, WINDOWS)
        def _(w):
            rows = row_block(w, PLACES)
            for g in range(GROUPS):
                at = [slice(part * D + g * 128, part * D + (g + 1) * 128) for part in range(3)]
                q, k, v = (qkv[n, rows, cols] for cols in at)
                go_wide = by_high(go[rows, at[0]], lanes)
                p_low = probs[n, w * GROUPS + g]
                p = p_low.astype(F32)
                pd = p * nt(by_low(v, lanes), go_wide)
                halves = []
                for h in range(2):
                    half = slice(h * PLACES, (h + 1) * PLACES)
                    halves.append((pd[half] - p[half] * jnp.sum(pd[half], axis=0, keepdims=True)).astype(BF))
                ds = jnp.concatenate(halves, axis=0)
                g_tab[b, :, g * 128 : (g + 1) * 128] += ds.astype(F32)
                gqkv[rows, at[0]] = (own_high(tn(ds, by_low(k, lanes)), lanes) * SCALE).astype(BF)
                gqkv[rows, at[1]] = own_low(nn(ds, by_high(q, lanes)), lanes).astype(BF)
                gqkv[rows, at[2]] = own_low(nn(p_low, go_wide), lanes).astype(BF)

        hook(1)

        @pl.loop(0, 4)
        def _(t):
            rows = row_block(t, 256)
            gq = gqkv[rows, :]
            add_vec(b, 6, by_eights(gq.astype(F32)))
            winf[rows, :] = nt(gq, wat[b, :, : 3 * D])

        to_canvas(winf, canvf, SHIFT * b)
        free_out()
        norm_backward(b, 0, x, gz, out)

    def attention_weights(n):
        for part in range(3):
            cols = slice(part * D, (part + 1) * D)
            g_qkv[:, cols] += tn(hqw[n], gqkv[:, cols])

    def partner(k):
        x, y = me % 2, me // 2
        return 2 * (1 - y if k & 2 else y) + (1 - x if k & 1 else x)

    def away(kind, k, n):
        dst, send, recv = ((r.act_hbm, r.act_send, r.act_recv), (r.igrad_hbm, r.ig_send, r.ig_recv))[kind]
        return remote(
            buf.at[partner(k), n], dst.at[me, n], send.at[k - 1, n], recv.at[k - 1, n], {"pipe": partner(k)}
        )

    def at_home(kind, n):
        dst = (r.act_hbm, r.igrad_hbm)[kind]
        return pltpu.make_async_copy(buf.at[me, n], dst.at[me, n], r.local_sem.at[kind, n])

    def send_acts(n):
        first = lax.axis_index("dp") % 2

        @pl.when(first == 0)
        def _():
            away(0, 1, n).start()
            away(0, 2, n).start()

        @pl.when(first == 1)
        def _():
            away(0, 2, n).start()
            away(0, 1, n).start()

        away(0, 3, n).start()
        at_home(0, n).start()

    def acts_sent(n):
        for k in (1, 2, 3):
            away(0, k, n).wait_send()
        at_home(0, n).wait()

    def push_row(row, n):
        @pl.when(me // 2 == row)
        def _():
            away(1, 1, n).start()
            at_home(1, n).start()

        @pl.when(me // 2 != row)
        def _():
            away(1, 2, n).start()
            away(1, 3, n).start()

    def pushed(n):
        for k in (1, 2, 3):
            away(1, k, n).wait_send()
        at_home(1, n).wait()

    def arrived(k, n):
        for dst, send, recv in ((r.act_hbm, r.act_send, r.act_recv), (r.igrad_hbm, r.ig_send, r.ig_recv)):
            got = dst.at[partner(k), n]
            remote(got, got, send.at[k - 1, n], recv.at[k - 1, n], {"pipe": partner(k)}).wait_recv()

    attention_stash = ((hqw, r.h_hqw), (qkv, r.h_qkv), (probs, r.h_probs), (att, r.h_att))
    mlp_stash = ((hq2, r.h_hq2), (hid, r.h_hid), (dgelu, r.h_dgelu))

    def stash(sec, n, back):
        pairs = mlp_stash if sec else attention_stash
        return [
            pltpu.make_async_copy(*((far.at[n], near.at[n]) if back else (near.at[n], far.at[n])), r.st_sem.at[sec, n, i])
            for i, (near, far) in enumerate(pairs)
        ]

    def load(src, n):
        return pltpu.make_async_copy(src.at[me, n], inb.at[n], r.in_sem.at[n])

    def start(copies):
        for copy in copies:
            copy.start()

    def wait(copies):
        for copy in copies:
            copy.wait()

    steps = (step_1, step_2, step_3, step_4, step_5)
    schedule = {
        (2, 0, 0): ((2, 3),),
        (2, 1, 1): ((3, 3),),
        (1, 0, 0): ((2, 2),),
        (1, 1, 0): ((4, 3),),
        (0, 0, 0): ((3, 2), (2, 1), (5, 3)),
        (0, 0, 1): ((4, 2),),
        (0, 1, 0): ((5, 2),),
        (0, 1, 1): ((3, 1),),
    }
    after = {3: ((1, 3),), 2: ((1, 2),), 1: ((1, 1),), 0: ()}
    weight_steps = (weights_1, weights_2, weights_3, weights_4) if linked else ()
    gathering = {
        (0, 4): ((3, 0), (4, 0)),
        (0, 0): ((2, 1),),
        (0, 1): ((2, 2), (2, 3), (3, 1)),
        (0, 3): ((4, 1), (3, 2)),
        (1, 3): ((4, 2),),
        (2, 0): ((3, 3),),
        (2, 3): ((4, 3),),
    }

    codes = [pltpu.make_async_copy(r.code_hbm, code, r.code_sem.at[0])]
    start(codes)
    start([load(r.x_hbm, n) for n in range(canvases)])
    wait(codes)

    @pl.loop(0, canvases)
    def _(n):
        def gather(sec, i):
            todo = gathering.get((sec, i), ())
            if linked and todo:

                @pl.when(n == 0)
                def _():
                    for step, of in todo:
                        weight_steps[step - 1](of)

        load(r.x_hbm, n).wait()
        x = inb.at[n]
        for s in range(4):
            if s >= 2:
                wait(stash(s - 2, n, False))
            forward = mlp_forward if s % 2 else attention_forward
            forward(s // 2, n, x, buf.at[s, n], functools.partial(gather, s))
            x = buf.at[s, n]
            if s == 3:
                send_acts(n)
            if s < 2:
                start(stash(s, n, False))
            if s == 0:
                load(r.cot_hbm, n).start()
            gather(s, 3)

    for s in (3, 2, 1, 0):
        cleared(*((g_fc1, g_fc2) if s % 2 else (g_qkv, g_proj)))

        @pl.loop(0, canvases)
        def _(n):
            def hook(i):
                for at in range(2):
                    todo = schedule.get((s, at, i), ())
                    if linked and todo:

                        @pl.when(n == (canvases - 1 if at else 0))
                        def _():
                            for step, of in todo:
                                steps[step - 1](of)

            if s == 3:
                load(r.cot_hbm, n).wait()
            if s == 0:
                load(r.x_hbm, n).wait()
            if s < 2:
                wait(stash(s, n, True))
            x = buf.at[s - 1, n] if s else inb.at[n]
            gz = inb.at[n] if s == 3 else buf.at[s + 1, n]
            backward = mlp_backward if s % 2 else attention_backward
            free_out = functools.partial(acts_sent, n) if s == 3 else lambda: None
            backward(s // 2, n, x, gz, buf.at[s, n], free_out, hook)
            if s % 2 == 0:
                attention_weights(n)
            if s == 2:
                push_row(1, n)
            if s == 0:

                @pl.when(n < canvases - 1)
                def _():
                    push_row(0, n)

            if s == 3:
                load(r.x_hbm, n).start()
            if s >= 2:
                start(stash(s - 2, n, True))

        if linked:
            for step, of in after[s]:
                steps[step - 1](of)
        else:
            whole = ((g_fc1, r.f_fc1), (g_fc2, r.f_fc2)) if s % 2 else ((g_qkv, r.f_qkv), (g_proj, r.f_proj))
            copies = [pltpu.make_async_copy(a, o.at[s // 2], r.go_sem.at[s, i]) for i, (a, o) in enumerate(whole)]
            start(copies)
            wait(copies)

    if linked:
        step_1(0)
        step_4(1)
        step_2(0)
    push_row(0, canvases - 1)
    if linked:
        step_5(1)
        smalls_sent(1)
        step_3(0)
        step_4(0)
        step_5(0)
        reductions_done()
        weights_sent()
        for k in range(1, 8):
            pack_copy(k).wait_send()
    for k in range(1, 4):
        for n in range(canvases):
            arrived(k, n)
    for n in range(canvases):
        pushed(n)


def compute(linked, operands):
    canvases = operands["x_hbm"].shape[1]
    shape = jax.ShapeDtypeStruct
    hbm = pl.BlockSpec(memory_space=pl.ANY)
    vmem = pl.BlockSpec(memory_space=pltpu.VMEM)
    dma = pltpu.SemaphoreType.DMA
    full = {
        "wat": ((2, D, 4 * D), BF),
        "fc1": ((2, D, FF), BF),
        "fc2": ((2, FF, D), BF),
        "vec": ((16, FF), F32),
    }
    grads = {
        "g_qkv": ((D, 3 * D), F32),
        "g_proj": ((D, D), F32),
        "g_fc1": ((D, FF), F32),
        "g_fc2": ((FF, D), F32),
        "g_vec": ((2, 8, 8, FF), F32),
        "g_tab": ((2, 2 * PLACES, GROUPS * 128), F32),
    }
    outs = {"act_hbm": ((4, canvases, CELLS, D), BF), "igrad_hbm": ((4, canvases, CELLS, D), BF)}
    kept = {
        "hqw": ((canvases, WROWS, D), BF),
        "qkv": ((canvases, WROWS, 3 * D), BF),
        "probs": ((canvases, WINDOWS * GROUPS, 128, 128), BF),
        "att": ((canvases, WROWS, D), BF),
        "hq2": ((canvases, CELLS, D), BF),
        "hid": ((canvases, CELLS, FF), BF),
        "dgelu": ((canvases, CELLS, FF), BF),
    }
    outs |= {"h_" + name: kind for name, kind in kept.items()}
    scratch = kept | {
        "inb": ((canvases, CELLS, D), BF),
        "code": ((canvases, CELLS, 128), jnp.int32),
        "codew": ((WROWS, 128), jnp.int32),
        "buf": ((4, canvases, CELLS, D), BF),
        "canvf": ((CELLS, D), F32),
        "winf": ((WROWS, D), F32),
        "gzw": ((WROWS, D), BF),
        "go": ((WROWS, D), BF),
        "gqkv": ((WROWS, 3 * D), BF),
    }
    sems = {
        "in_sem": (canvases,),
        "code_sem": (1,),
        "st_sem": (2, canvases, 4),
        "local_sem": (2, canvases),
        "act_send": (3, canvases),
        "act_recv": (3, canvases),
        "ig_send": (3, canvases),
        "ig_recv": (3, canvases),
    }
    if linked:
        outs |= {
            "o_qkv": ((2, 48, 3 * D), F32),
            "o_proj": ((2, 48, D), F32),
            "o_fc1": ((2, 48, FF), F32),
            "o_fc2": ((2, 192, D), F32),
            "o_small": ((2, 8, 64, D), BF),
        }
        scratch |= full | grads
        scratch |= {
            "packs": ((8, 16, 256), BF),
            "l_qkv": ((48, 3 * D), F32),
            "l_proj": ((48, D), F32),
            "l_fc1": ((48, FF), F32),
            "l_fc2": ((192, D), F32),
        }
        for kind, rows in (("m_", MLP_ROWS), ("a_", ATT_ROWS)):
            scratch |= {
                kind + "st_a": ((4, rows, D), BF),
                kind + "rc_a": ((4, rows, D), BF),
                kind + "st_b": ((3, rows, D), BF),
                kind + "rc_b": ((3, rows, D), BF),
                kind + "st_c": ((rows, D), BF),
                kind + "rc_c": ((3, rows // 4, D), BF),
                kind + "fin": ((rows, D), BF),
            }
        sems |= {
            "sh_sem": (4, 2),
            "os_sem": (2,),
            "go_sem": (4, 2),
            "wz_send": (4, 2, 3),
            "wz_recv": (4, 2, 3),
            "wx_send": (4, 2, 3, 3),
            "wx_recv": (4, 2, 3, 3),
            "ws_send": (4, 2, 4),
            "ws_recv": (4, 2, 4),
            "pk_send": (7,),
            "pk_recv": (7,),
            "ra_send": (4,),
            "ra_recv": (4,),
            "rb_send": (4, 3),
            "rb_recv": (4, 3),
            "rc_send": (4, 3),
            "rc_recv": (4, 3),
            "rf_send": (4, 3),
            "rf_recv": (4, 3),
            "rs_send": (2, 7),
            "rs_recv": (2, 7),
        }
    else:
        for name in ("g_vec", "g_tab"):
            outs[name] = grads.pop(name)
        outs |= {name.replace("g_", "f_"): ((2,) + dims, F32) for name, (dims, _) in grads.items()}
        scratch |= grads
        sems["go_sem"] = (4, 2)
    in_vmem = set(full) | {"bias", "pack", "g_vec", "g_tab"}
    names = tuple(operands) + tuple(outs) + tuple(scratch) + tuple(sems)
    results = pl.pallas_call(
        functools.partial(kernel, names, linked, canvases),
        out_shape=tuple(shape(*o) for o in outs.values()),
        in_specs=[vmem if name in in_vmem else hbm for name in operands],
        out_specs=tuple(vmem if name in in_vmem else hbm for name in outs),
        scratch_shapes=[pltpu.VMEM(*v) for v in scratch.values()] + [dma(v) for v in sems.values()],
        compiler_params=pltpu.CompilerParams(
            vmem_limit_bytes=64 * 1024 * 1024 - 65536, collective_id=0, has_side_effects=True
        ),
    )(*operands.values())
    return dict(zip(outs, results))


def place_pairs():
    place = np.arange(PLACES)
    r, c = place // 8, place % 8
    index = (r[None, :] - r[:, None] + WIN - 1) * (2 * WIN - 1) + c[None, :] - c[:, None] + WIN - 1
    real = (r < WIN) & (c < WIN)
    return index, real[:, None] & real[None, :], real


def pair_onehot():
    index, both, _ = place_pairs()
    table = (2 * WIN - 1) ** 2
    hot = (np.where(both, index, -1).reshape(-1)[None, :] == np.arange(table)[:, None])
    return hot.astype(np.float32)


def body(
    inputs,
    cotangent,
    pad_mask,
    region_ids,
    norm1_gain,
    norm1_bias,
    qkv_weight,
    qv_bias,
    rel_table,
    proj_weight,
    proj_bias,
    norm2_gain,
    norm2_bias,
    fc1_weight,
    fc1_bias,
    fc2_weight,
    fc2_bias,
):
    owners = lax.axis_size("dp")
    linked = owners == 8
    mine = lax.axis_index("pipe")

    def own(a):
        return lax.dynamic_index_in_dim(a, mine, 0, keepdims=False)

    code = own(region_ids) * 2 + own(pad_mask)
    code = jnp.broadcast_to(code[:, :, None], code.shape + (128,))

    hot = pair_onehot()
    _, _, real = place_pairs()
    rel = lax.dot_general(
        rel_table.astype(BF), jnp.asarray(hot, BF), (((1,), (0,)), ((), ())), preferred_element_type=F32
    )
    rel = rel.reshape(2, GROUPS, 2, 2, PLACES, PLACES)
    rel = jnp.where(jnp.asarray(real)[None, None, None, None, :, None], rel, MASKED)
    rel = rel.transpose(0, 1, 3, 4, 2, 5).reshape(2, GROUPS, 128, 128)

    operands = {"x_hbm": inputs, "cot_hbm": cotangent, "code_hbm": code, "bias": rel}
    vectors = (norm1_gain, norm1_bias, proj_bias, norm2_gain, norm2_bias, fc2_bias, qv_bias, fc1_bias)
    sizes = [v.shape[1] for v in vectors]
    ends = np.cumsum([0] + sizes)
    if linked:
        pack = jnp.stack([jnp.pad(v, ((0, 0), (0, 256 - v.shape[1]))) for v in vectors], axis=1)
        operands |= {
            "pack": pack.reshape(16, 256).astype(BF),
            "s_qkv": qkv_weight,
            "s_proj": proj_weight,
            "s_fc1": fc1_weight,
            "s_fc2": fc2_weight,
        }
    else:

        def gathered(a):
            return lax.all_gather(a.astype(BF), "dp", axis=1, tiled=True)

        packed = lax.all_gather(jnp.concatenate(vectors, axis=1).astype(BF), "dp", axis=1)
        parts = [packed[:, :, a:b].reshape(2, -1).astype(F32) for a, b in zip(ends[:-1], ends[1:])]
        qv = parts[6]
        parts[6] = jnp.concatenate([qv[:, :D], jnp.zeros_like(qv[:, :D]), qv[:, D:]], axis=1)
        vec = jnp.stack([jnp.pad(p, ((0, 0), (0, FF - p.shape[1]))) for p in parts], axis=1)
        operands |= {
            "wat": jnp.concatenate([gathered(qkv_weight), gathered(proj_weight)], axis=2),
            "fc1": gathered(fc1_weight),
            "fc2": gathered(fc2_weight),
            "vec": vec.reshape(16, FF),
        }

    out = compute(linked, operands)

    def to_owners(g):
        shared = lax.psum_scatter(g, "dp", scatter_dimension=1, tiled=True)
        return lax.psum(shared, "pipe")

    if linked:
        small = out["o_small"]
        g_tab = small[:, :, :16].reshape(2, 128, GROUPS * 128)
        g_vec = jnp.concatenate([small[:, :, 16 + 8 * j : 24 + 8 * j] for j in range(4)], axis=3)
    else:
        g_tab, g_vec = out["g_tab"], out["g_vec"]

    g_vec = jnp.sum(g_vec.astype(F32), axis=2)
    kinds = [g_vec[:, i] for i in range(8)]
    qv_sum = jnp.concatenate([kinds[6][:, :D], kinds[6][:, 2 * D : 3 * D]], axis=1)
    rows = [kinds[0], kinds[1], kinds[2], kinds[3], kinds[4], kinds[5], qv_sum, kinds[7]]
    if linked:
        at = lax.axis_index("dp")
        small = [lax.dynamic_slice_in_dim(v, at * n, n, 1) for v, n in zip(rows, sizes)]
    else:
        rows = [v[:, : n * owners].reshape(2, -1, n) for v, n in zip(rows, sizes)]
        g_small = to_owners(jnp.concatenate(rows, axis=2))[:, 0]
        small = [g_small[:, a:b] for a, b in zip(ends[:-1], ends[1:])]

    pairs = g_tab.reshape(2, 2, PLACES, GROUPS, 2, PLACES).transpose(0, 3, 4, 1, 2, 5)
    pairs = pairs.reshape(2, HEADS, PLACES * PLACES)
    g_table = lax.dot_general(
        jnp.broadcast_to(jnp.asarray(hot, pairs.dtype), (2,) + hot.shape),
        pairs,
        (((2,), (2,)), ((0,), (0,))),
        precision=None if linked else lax.Precision.HIGHEST,
        preferred_element_type=F32,
    )
    if linked:
        big = [out[name] for name in ("o_qkv", "o_proj", "o_fc1", "o_fc2")]
    else:
        g_table = lax.psum(g_table, ("pipe", "dp"))
        big = [to_owners(out[name]) for name in ("f_qkv", "f_proj", "f_fc1", "f_fc2")]

    return (
        out["act_hbm"][None],
        out["igrad_hbm"][None],
        small[0],
        small[1],
        big[0],
        small[6],
        g_table,
        big[1],
        small[2],
        small[3],
        small[4],
        big[2],
        small[7],
        big[3],
        small[5],
    )


def solution(mesh):
    cols = P(None, "dp")
    rows = P(None, "dp", None)
    return jax.shard_map(
        body,
        mesh=mesh,
        in_specs=(
            P(None, "dp", None, None),
            P(None, "dp", None, None),
            rows,
            rows,
            cols,
            cols,
            rows,
            cols,
            P(),
            rows,
            cols,
            cols,
            cols,
            rows,
            cols,
            rows,
            cols,
        ),
        out_specs=(
            P("pipe", None, "dp", None, None),
            P("pipe", None, "dp", None, None),
            cols,
            cols,
            rows,
            cols,
            P(),
            rows,
            cols,
            cols,
            cols,
            rows,
            cols,
            rows,
            cols,
        ),
        check_vma=False,
    )
```

```python
import functools
import types

import jax
import jax.numpy as jnp
import numpy as np
from jax import lax
from jax.experimental import pallas as pl
from jax.experimental.pallas import tpu as pltpu
from jax.sharding import PartitionSpec as P

HEADS = 12
WIN = 7
SHIFT = 3
GRID = 28
CELLS = 784
D = 384
FF = 1536
HEAD = 32
SIDE = 4
WINDOWS = 16
PLACES = 64
WROWS = WINDOWS * PLACES
GROUPS = 3
TILE = 112
SCALE = HEAD**-0.5
NORM_EPS = 1e-05
MASKED = -1e30
BF = jnp.bfloat16
F32 = jnp.float32

RSQRT_2 = 1.0 / np.sqrt(2.0)
PHI_0 = 1.0 / np.sqrt(2.0 * np.pi)


def nn(a, b):
    return lax.dot_general(a, b, (((1,), (0,)), ((), ())), preferred_element_type=F32)


def nt(a, b):
    return lax.dot_general(a, b, (((1,), (1,)), ((), ())), preferred_element_type=F32)


def tn(a, b):
    return lax.dot_general(a, b, (((0,), (0,)), ((), ())), preferred_element_type=F32)


def segments(shift):
    runs = []
    for wr in range(SIDE):
        for r in range(WIN):
            row = (wr * WIN + r + shift) % GRID
            for wc in range(SIDE):
                col = (wc * WIN + shift) % GRID
                place = (wr * SIDE + wc) * PLACES + r * 8
                first = min(WIN, GRID - col)
                runs.append((row * GRID + col, place, first))
                if first < WIN:
                    runs.append((row * GRID, place + first, WIN - first))
    return runs


def to_windows(src, dst, shift):
    for cell, place, count in segments(shift):
        dst[pl.ds(place, count), :] = src[pl.ds(cell, count), :]


def to_canvas(src, dst, shift):
    for cell, place, count in segments(shift):
        dst[pl.ds(cell, count), :] = src[pl.ds(place, count), :]


def row_block(t, size):
    return pl.ds(pl.multiple_of(t * size, 16), size)


def standardized(v):
    centered = v - jnp.mean(v, axis=-1, keepdims=True)
    spread = jnp.mean(centered * centered, axis=-1, keepdims=True)
    rs = lax.rsqrt(spread + NORM_EPS)
    return centered * rs, rs


def by_eights(v):
    return jnp.sum(v.reshape(v.shape[0] // 8, 8, v.shape[1]), axis=0)


def gelu_parts(x):
    cdf = 0.5 + 0.5 * lax.erf(x * RSQRT_2)
    return x * cdf, cdf + x * (jnp.exp(-0.5 * x * x) * PHI_0)


def real_places(rows):
    place = lax.broadcasted_iota(jnp.int32, (rows, 1), 0)
    return ((place & 7) < WIN) & (((place >> 3) & 7) < WIN)


def head_of_lane():
    return lax.broadcasted_iota(jnp.int32, (PLACES, 128), 1) >> 5


def by_low(x, lanes):
    zero = jnp.zeros_like(x)
    return jnp.concatenate([jnp.where((lanes & 1) == h, x, zero) for h in range(2)], axis=0)


def by_high(x, lanes):
    zero = jnp.zeros_like(x)
    return jnp.concatenate([jnp.where((lanes >> 1) == h, x, zero) for h in range(2)], axis=0)


def own_low(wide, lanes):
    return jnp.where((lanes & 1) == 0, wide[:PLACES], wide[PLACES:])


def own_high(wide, lanes):
    return jnp.where((lanes >> 1) == 0, wide[:PLACES], wide[PLACES:])


MESH = pl.DeviceIdType.MESH
ATT_ROWS = 256
MLP_ROWS = 384
SMALL = 192


def kernel(names, linked, canvases, *refs):
    r = types.SimpleNamespace(**dict(zip(names, refs)))
    me = lax.axis_index("pipe")
    code, codew, buf = r.code, r.codew, r.buf
    hqw, qkv, probs, att = r.hqw, r.qkv, r.probs, r.att
    hq2, hid, dgelu = r.hq2, r.hid, r.dgelu
    canvf, winf, gzw, gqkv, go = r.canvf, r.winf, r.gzw, r.gqkv, r.go
    g_qkv, g_proj, g_fc1, g_fc2, g_vec, g_tab = r.g_qkv, r.g_proj, r.g_fc1, r.g_fc2, r.g_vec, r.g_tab
    wat, fc1, fc2, vec, bias = r.wat, r.fc1, r.fc2, r.vec, r.bias
    if linked:
        d = lax.axis_index("dp")
        z, c = d // 2, d % 2
        sibling = {"dp": 2 * z + 1 - c}

    def z_peer(k):
        return {"dp": 2 * lax.rem(z + k, 4) + c}

    def pipe_peer(k):
        return {"pipe": lax.rem(me + k, 4)}

    def dp_peer(k):
        return {"dp": lax.rem(d + k, 8)}

    def remote(src, dst, send, recv, device):
        return pltpu.make_async_remote_copy(
            src_ref=src, dst_ref=dst, send_sem=send, recv_sem=recv, device_id=device, device_id_type=MESH
        )

    barrier = pltpu.get_barrier_semaphore()
    partners = [pipe_peer(k) for k in range(1, 4)]
    if linked:
        partners += [dp_peer(k) for k in range(1, 8)]
    for partner in partners:
        pl.semaphore_signal(barrier, inc=1, device_id=partner, device_id_type=MESH)

    full = ((wat,), (fc1, fc2), (wat,), (fc1, fc2))

    def owner_back(k):
        return 2 * lax.rem(z + 4 - k, 4) + c

    def shard(sec, a, owner):
        h = 192 if a else 48
        return full[sec][a].at[sec // 2, pl.ds(pl.multiple_of(owner * h, 16), h), :]

    def part(sec, a, owner, place):
        if a:
            return fc2.at[sec // 2, pl.ds(pl.multiple_of(owner * 192 + place * 48, 16), 48), :]
        rows = pl.ds(pl.multiple_of(owner * 48, 16), 48)
        return full[sec][0].at[sec // 2, rows, pl.ds(pl.multiple_of(place * D, 128), D)]

    def to_z(sec, a, k):
        own = part(sec, a, d, me)
        return remote(own, own, r.wz_send.at[sec, a, k - 1], r.wz_recv.at[sec, a, k - 1], z_peer(k))

    def to_places(sec, a, k, j):
        got = part(sec, a, owner_back(k), me)
        return remote(
            got, got, r.wx_send.at[sec, a, k - 1, j - 1], r.wx_recv.at[sec, a, k - 1, j - 1], pipe_peer(j)
        )

    def to_sibling(sec, a, k):
        block = shard(sec, a, owner_back(k))
        return remote(block, block, r.ws_send.at[sec, a, k], r.ws_recv.at[sec, a, k], sibling)

    def weights_1(sec):
        for a in range(len(full[sec])):
            for k in range(1, 4):
                to_z(sec, a, k).start()
            to_sibling(sec, a, 0).start()

    def weights_2(sec):
        for k in range(1, 4):
            for a in range(len(full[sec])):
                got = part(sec, a, owner_back(k), me)
                remote(got, got, r.wz_send.at[sec, a, k - 1], r.wz_recv.at[sec, a, k - 1], z_peer(k)).wait_recv()
                for j in range(1, 4):
                    to_places(sec, a, k, j).start()

    def weights_3(sec):
        for k in range(1, 4):
            for a in range(len(full[sec])):
                for j in range(1, 4):
                    got = part(sec, a, owner_back(k), lax.rem(me + 4 - j, 4))
                    remote(
                        got, got, r.wx_send.at[sec, a, k - 1, j - 1], r.wx_recv.at[sec, a, k - 1, j - 1], pipe_peer(j)
                    ).wait_recv()
                to_sibling(sec, a, k).start()

    def weights_4(sec):
        for k in range(4):
            for a in range(len(full[sec])):
                block = shard(sec, a, 2 * lax.rem(z + 4 - k, 4) + 1 - c)
                remote(block, block, r.ws_send.at[sec, a, k], r.ws_recv.at[sec, a, k], sibling).wait_recv()

    def weights_sent():
        for sec in range(4):
            for a in range(len(full[sec])):
                for k in range(4):
                    to_sibling(sec, a, k).wait_send()
                    if k:
                        to_z(sec, a, k).wait_send()
                        for j in range(1, 4):
                            to_places(sec, a, k, j).wait_send()

    def pack_copy(k):
        return remote(
            r.packs.at[d], r.packs.at[d], r.pk_send.at[k - 1], r.pk_recv.at[k - 1], dp_peer(k)
        )

    def pack_arrival(k):
        slot = r.packs.at[lax.rem(d + 8 - k, 8)]
        return remote(slot, slot, r.pk_send.at[k - 1], r.pk_recv.at[k - 1], dp_peer(k))

    def place_vectors():
        kind = lax.broadcasted_iota(jnp.int32, (16, 256), 0) & 7
        lane = lax.broadcasted_iota(jnp.int32, (16, 256), 1)
        vec[...] = jnp.zeros_like(vec)
        for width, kinds in ((48, kind < 6), (96, kind == 6), (192, kind == 7)):
            for owner in range(8):
                at = owner * width
                if width == 96 and owner >= 4:
                    at += D
                start = at // 128 * 128
                part = jnp.where(kinds & (lane < width), r.packs[owner].astype(F32), 0.0)
                if at > start:
                    part = pltpu.roll(part, at - start, 1)
                for b in range(2):
                    vec[b, :, start : start + 256] += part[8 * b : 8 * b + 8]

    def pieces(sec, owner):
        b = sec // 2
        out = []

        def matrix(ref, h):
            for t in range(h // 48):
                rows = pl.ds(pl.multiple_of(owner * h + t * 48, 16), 48)
                for j in range(ref.shape[1] // D):
                    load = functools.partial(lambda ref, rows, j: ref[rows, j * D : (j + 1) * D], ref, rows, j)
                    out.append((len(out) * 48, 48, load))

        def small():
            parts = [g_tab[b, pl.ds(pl.multiple_of(owner * 16, 16), 16), :]]
            parts += [g_vec[b, owner, :, j * D : (j + 1) * D] for j in range(4)]
            return jnp.concatenate(parts + [jnp.zeros((16, D), F32)], axis=0)

        if sec % 2:
            matrix(g_fc1, 48)
            matrix(g_fc2, 192)
        else:
            matrix(g_qkv, 48)
            matrix(g_proj, 48)
            out.append((SMALL, 64, small))
        return out

    def reduce_refs(sec):
        kind = "m" if sec % 2 else "a"
        return types.SimpleNamespace(
            **{n: getattr(r, kind + "_" + n) for n in ("st_a", "rc_a", "st_b", "rc_b", "st_c", "rc_c", "fin")}
        )

    def step_1(sec):
        q = reduce_refs(sec)
        if sec < 2:
            copy_a(sec + 2).wait_send()
            for k in range(1, 4):
                copy_b(sec + 2, k).wait_send()
                copy_c(sec + 2, k).wait_send()
        for k in range(4):
            i = lax.rem(z + k, 4)
            kept = q.st_b.at[k - 1] if k else q.st_c
            for row, rows, load in pieces(sec, 2 * i + 1 - c):
                q.st_a[i, row : row + rows, :] = load().astype(BF)
            for row, rows, load in pieces(sec, 2 * i + c):
                kept[row : row + rows, :] = load().astype(BF)
        copy_a(sec).start()

    def copy_a(sec):
        q = reduce_refs(sec)
        return remote(q.st_a, q.rc_a, r.ra_send.at[sec], r.ra_recv.at[sec], sibling)

    def copy_b(sec, k):
        q = reduce_refs(sec)
        return remote(
            q.st_b.at[k - 1], q.rc_b.at[k - 1], r.rb_send.at[sec, k - 1], r.rb_recv.at[sec, k - 1], z_peer(k)
        )

    def step_2(sec):
        q = reduce_refs(sec)
        copy_a(sec).wait_recv()
        for k in (1, 2, 3, 0):
            i = lax.rem(z + k, 4)
            kept = q.st_b.at[k - 1] if k else q.st_c
            for row in range(0, kept.shape[0], 64):
                at = slice(row, row + 64)
                kept[at, :] = (kept[at, :].astype(F32) + q.rc_a[i, at, :].astype(F32)).astype(BF)
            if k:
                copy_b(sec, k).start()

    def quarter(sec, ref, who):
        rows = (MLP_ROWS if sec % 2 else ATT_ROWS) // 4
        return ref.at[pl.ds(pl.multiple_of(who * rows, 16), rows), :]

    def copy_c(sec, k):
        q = reduce_refs(sec)
        return remote(
            quarter(sec, q.st_c, lax.rem(me + k, 4)),
            q.rc_c.at[k - 1],
            r.rc_send.at[sec, k - 1],
            r.rc_recv.at[sec, k - 1],
            pipe_peer(k),
        )

    def step_3(sec):
        q = reduce_refs(sec)
        for k in range(1, 4):
            copy_b(sec, k).wait_recv()
        for row in range(0, q.st_c.shape[0], 64):
            at = slice(row, row + 64)
            total = q.st_c[at, :].astype(F32)
            for k in range(3):
                total = total + q.rc_b[k, at, :].astype(F32)
            q.st_c[at, :] = total.astype(BF)
        for k in range(1, 4):
            copy_c(sec, k).start()

    def copy_f(sec, k):
        q = reduce_refs(sec)
        own = quarter(sec, q.fin, me)
        return remote(own, own, r.rf_send.at[sec, k - 1], r.rf_recv.at[sec, k - 1], pipe_peer(k))

    def step_4(sec):
        q = reduce_refs(sec)
        for k in range(1, 4):
            copy_c(sec, k).wait_recv()
            if sec < 2:
                copy_f(sec + 2, k).wait_send()
        total = quarter(sec, q.st_c, me)[...].astype(F32)
        for k in range(3):
            total = total + q.rc_c[k].astype(F32)
        quarter(sec, q.fin, me)[...] = total.astype(BF)
        for k in range(1, 4):
            copy_f(sec, k).start()

    def copy_s(b, k):
        rows = pl.ds(SMALL, 64)
        return remote(
            r.a_fin.at[rows, :], r.o_small.at[b, d], r.rs_send.at[b, k - 1], r.rs_recv.at[b, k - 1], dp_peer(k)
        )

    def own_small(b):
        return pltpu.make_async_copy(r.a_fin.at[pl.ds(SMALL, 64), :], r.o_small.at[b, d], r.os_sem.at[b])

    def outputs(sec):
        pairs = ((r.l_fc1, r.o_fc1), (r.l_fc2, r.o_fc2)) if sec % 2 else ((r.l_qkv, r.o_qkv), (r.l_proj, r.o_proj))
        return [
            pltpu.make_async_copy(ref, out.at[sec // 2], r.go_sem.at[sec, i]) for i, (ref, out) in enumerate(pairs)
        ]

    def step_5(sec):
        q = reduce_refs(sec)
        b = sec // 2
        for k in range(1, 4):
            got = quarter(sec, q.fin, lax.rem(me + 4 - k, 4))
            remote(got, got, r.rf_send.at[sec, k - 1], r.rf_recv.at[sec, k - 1], pipe_peer(k)).wait_recv()
        if sec % 2 == 0:
            for k in range(1, 8):
                copy_s(b, k).start()
            own_small(b).start()
        if sec < 2:
            for out in outputs(sec + 2):
                out.wait()
        row = 0
        for ref in (r.l_fc1, r.l_fc2) if sec % 2 else (r.l_qkv, r.l_proj):
            for t in range(ref.shape[0] // 48):
                for j in range(ref.shape[1] // D):
                    ref[t * 48 : (t + 1) * 48, j * D : (j + 1) * D] = q.fin[row : row + 48, :].astype(F32)
                    row += 48
        for out in outputs(sec):
            out.start()

    def smalls_sent(b):
        for k in range(1, 8):
            copy_s(b, k).wait_send()
        own_small(b).wait()

    def reductions_done():
        for sec in (1, 0):
            copy_a(sec).wait_send()
            for k in range(1, 4):
                copy_b(sec, k).wait_send()
                copy_c(sec, k).wait_send()
                copy_f(sec, k).wait_send()
        for sec in range(2):
            for out in outputs(sec):
                out.wait()
        smalls_sent(0)
        for b in range(2):
            for k in range(1, 8):
                rows = pl.ds(SMALL, 64)
                remote(
                    r.a_fin.at[rows, :],
                    r.o_small.at[b, lax.rem(d + 8 - k, 8)],
                    r.rs_send.at[b, k - 1],
                    r.rs_recv.at[b, k - 1],
                    dp_peer(k),
                ).wait_recv()

    if linked:
        lands = ((r.s_qkv, g_qkv, wat, 0), (r.s_proj, g_proj, wat, 3 * D), (r.s_fc1, g_fc1, fc1, 0), (r.s_fc2, g_fc2, fc2, 0))

        def landing(i, b):
            src, dst, _, _ = lands[i]
            h, n = src.shape[1:]
            return pltpu.make_async_copy(
                src.at[b], dst.at[pl.ds(192 * b, h), pl.ds(0, n)], r.sh_sem.at[i, b]
            )

        for i in range(4):
            for b in range(2):
                landing(i, b).start()
        r.packs[d] = r.pack[...]
        for i, (src, dst, ref, col) in enumerate(lands):
            h, n = src.shape[1:]
            for b in range(2):
                landing(i, b).wait()
                for t in range(0, h, 48):
                    rows = pl.ds(pl.multiple_of(d * h + t, 16), 48)
                    ref[b, rows, col : col + n] = dst[192 * b + t : 192 * b + t + 48, :n].astype(BF)
    pl.semaphore_wait(barrier, len(partners))
    if linked:
        for k in range(1, 8):
            pack_copy(k).start()
        weights_1(0)

    def cleared(*refs):
        for ref in refs:

            @pl.loop(0, ref.shape[0] // 16)
            def _(i):
                ref[row_block(i, 16), :] = jnp.zeros((16, ref.shape[1]), F32)

    g_vec[...] = jnp.zeros_like(g_vec)
    g_tab[...] = jnp.zeros_like(g_tab)
    codew[...] = jnp.zeros_like(codew)

    if linked:
        weights_2(0)
        for sec in range(1, 4):
            weights_1(sec)
        for k in range(1, 8):
            pack_arrival(k).wait_recv()
        place_vectors()

    def vector(b, kind, width=D):
        return vec[b, kind : kind + 1, :width]

    def add_vec(b, kind, part):
        g_vec[b, kind, :, : part.shape[1]] += part

    def windowed(rows, count):
        return jnp.where(real_places(count), winf[rows, :], 0.0).astype(BF)

    def by_block(b, move):
        for i in range(2):

            @pl.when(b == i)
            def _():
                move(SHIFT * i)

    def attention_forward(b, n, x, out, hook):
        lanes = head_of_lane()

        @pl.loop(0, CELLS // TILE)
        def _(t):
            rows = row_block(t, TILE)
            xhat, _ = standardized(x[rows, :].astype(F32))
            canvf[rows, :] = xhat * vector(b, 0) + vector(b, 1)

        def arrange(shift):
            to_windows(canvf, winf, shift)
            to_windows(code.at[n], codew, shift)

        by_block(b, arrange)
        hook(4)

        @pl.loop(0, 4)
        def _(t):
            rows = row_block(t, 256)
            hq = windowed(rows, 256)
            hqw[n, rows, :] = hq
            for part in range(3):
                cols = slice(part * D, (part + 1) * D)
                acc = nn(hq, wat[b, :, cols]) + vec[b, 6:7, cols]
                if part == 0:
                    acc = acc * SCALE
                qkv[n, rows, cols] = acc.astype(BF)

        hook(0)

        @pl.loop(0, WINDOWS)
        def _(w):
            rows = row_block(w, PLACES)
            cells = codew[rows, :]
            region = (cells >> 1) * b
            pad = (cells & 1).astype(F32)
            lane = lax.broadcasted_iota(jnp.int32, (PLACES, 128), 1)
            same = jnp.where(lane == region, 1.0, 0.0)
            left = jnp.where(lane == 127, 1.0 - pad, same).astype(BF)
            right = jnp.where(lane == 127, -pad, same).astype(BF)
            agree = nt(left, jnp.concatenate([right, right], axis=0))
            mask = jnp.where(agree > 0.5, 0.0, MASKED)
            for g in range(GROUPS):
                q = qkv[n, rows, g * 128 : (g + 1) * 128]
                k = qkv[n, rows, D + g * 128 : D + (g + 1) * 128]
                v = qkv[n, rows, 2 * D + g * 128 : 2 * D + (g + 1) * 128]
                scores = nt(by_low(k, lanes), by_high(q, lanes)) + bias[b, g]
                halves = []
                for h in range(2):
                    s = scores[h * PLACES : (h + 1) * PLACES] + mask
                    e = jnp.exp(s - jnp.max(s, axis=0, keepdims=True))
                    halves.append((e * (1.0 / jnp.sum(e, axis=0, keepdims=True))).astype(BF))
                p = jnp.concatenate(halves, axis=0)
                probs[n, w * GROUPS + g] = p
                att[n, rows, g * 128 : (g + 1) * 128] = own_high(tn(p, by_low(v, lanes)), lanes).astype(BF)

        hook(1)

        @pl.loop(0, 4)
        def _(t):
            rows = row_block(t, 256)
            winf[rows, :] = nn(att[n, rows, :], wat[b, :, 3 * D :])

        by_block(b, functools.partial(to_canvas, winf, canvf))

        @pl.loop(0, CELLS // TILE)
        def _(t):
            rows = row_block(t, TILE)
            out[rows, :] = (x[rows, :].astype(F32) + (canvf[rows, :] + vector(b, 2))).astype(BF)

    def mlp_forward(b, n, x, out, hook):
        @pl.loop(0, CELLS // TILE)
        def _(t):
            rows = row_block(t, TILE)
            xhat, _ = standardized(x[rows, :].astype(F32))
            hq2[n, rows, :] = (xhat * vector(b, 3) + vector(b, 4)).astype(BF)

        @pl.loop(0, FF // 256)
        def _(i):
            cols = pl.ds(pl.multiple_of(i * 256, 256), 256)
            pre = nn(hq2[n], fc1[b, :, cols]) + vec[b, 7:8, cols]
            for at in range(0, CELLS, 16):
                h, dg = gelu_parts(pre[at : at + 16])
                hid[n, at : at + 16, cols] = h.astype(BF)
                dgelu[n, at : at + 16, cols] = dg.astype(BF)

        hook(0)
        total = nn(hid[n], fc2[b])
        for at in range(0, CELLS, TILE):
            rows = slice(at, at + TILE)
            out[rows, :] = (x[rows, :].astype(F32) + (total[rows] + vector(b, 5))).astype(BF)

    def norm_backward(b, kind, x, gz, out):
        @pl.loop(0, CELLS // TILE)
        def _(t):
            rows = row_block(t, TILE)
            xhat, rs = standardized(x[rows, :].astype(F32))
            gn = canvf[rows, :]
            gzf = gz[rows, :].astype(F32)
            add_vec(b, kind, by_eights(gn * xhat))
            add_vec(b, kind + 1, by_eights(gn))
            add_vec(b, 5 if kind else 2, by_eights(gzf))
            g = gn * vector(b, kind)
            mg = jnp.mean(g, axis=-1, keepdims=True)
            mgx = jnp.mean(g * xhat, axis=-1, keepdims=True)
            out[rows, :] = (gzf + rs * (g - mg - xhat * mgx)).astype(BF)

    def mlp_backward(b, n, x, gz, out, free_out, hook):
        @pl.loop(0, FF // 256)
        def _(i):
            cols = pl.ds(pl.multiple_of(i * 256, 256), 256)
            gh = nt(gz[...], fc2[b, cols, :])
            sums = jnp.zeros((8, 256), F32)
            for at in range(0, CELLS, 16):
                gp = (gh[at : at + 16] * dgelu[n, at : at + 16, cols].astype(F32)).astype(BF)
                dgelu[n, at : at + 16, cols] = gp
                sums = sums + by_eights(gp.astype(F32))
            g_vec[b, 7, :, cols] += sums
            g_fc1[:, cols] += tn(hq2[n], dgelu[n, :, cols])
            g_fc2[cols, :] += tn(hid[n, :, cols], gz[...])

        hook(0)
        canvf[...] = nt(dgelu[n], fc1[b])
        free_out()
        norm_backward(b, 3, x, gz, out)

    def attention_backward(b, n, x, gz, out, free_out, hook):
        lanes = head_of_lane()

        @pl.loop(0, CELLS // TILE)
        def _(t):
            rows = row_block(t, TILE)
            canvf[rows, :] = gz[rows, :].astype(F32)

        by_block(b, functools.partial(to_windows, canvf, winf))

        @pl.loop(0, 4)
        def _(t):
            rows = row_block(t, 256)
            gzw[rows, :] = windowed(rows, 256)

        g_proj[...] += tn(att[n], gzw[...])

        @pl.loop(0, 4)
        def _(t):
            rows = row_block(t, 256)
            go[rows, :] = nt(gzw[rows, :], wat[b, :, 3 * D :]).astype(BF)

        hook(0)

        @pl.loop(0, WINDOWS)
        def _(w):
            rows = row_block(w, PLACES)
            for g in range(GROUPS):
                at = [slice(part * D + g * 128, part * D + (g + 1) * 128) for part in range(3)]
                q, k, v = (qkv[n, rows, cols] for cols in at)
                go_wide = by_high(go[rows, at[0]], lanes)
                p_low = probs[n, w * GROUPS + g]
                p = p_low.astype(F32)
                pd = p * nt(by_low(v, lanes), go_wide)
                halves = []
                for h in range(2):
                    half = slice(h * PLACES, (h + 1) * PLACES)
                    halves.append((pd[half] - p[half] * jnp.sum(pd[half], axis=0, keepdims=True)).astype(BF))
                ds = jnp.concatenate(halves, axis=0)
                g_tab[b, :, g * 128 : (g + 1) * 128] += ds.astype(F32)
                gqkv[rows, at[0]] = (own_high(tn(ds, by_low(k, lanes)), lanes) * SCALE).astype(BF)
                gqkv[rows, at[1]] = own_low(nn(ds, by_high(q, lanes)), lanes).astype(BF)
                gqkv[rows, at[2]] = own_low(nn(p_low, go_wide), lanes).astype(BF)

        hook(1)

        @pl.loop(0, 4)
        def _(t):
            rows = row_block(t, 256)
            gq = gqkv[rows, :]
            add_vec(b, 6, by_eights(gq.astype(F32)))
            winf[rows, :] = nt(gq, wat[b, :, : 3 * D])

        by_block(b, functools.partial(to_canvas, winf, canvf))
        free_out()
        norm_backward(b, 0, x, gz, out)

    def attention_weights(n):
        @pl.loop(0, 3)
        def _(part):
            cols = pl.ds(pl.multiple_of(part * D, 128), D)
            g_qkv[:, cols] += tn(hqw[n], gqkv[:, cols])

    def partner(k):
        x, y = me % 2, me // 2
        return 2 * (1 - y if k & 2 else y) + (1 - x if k & 1 else x)

    def away(kind, k, n):
        dst, send, recv = ((r.act_hbm, r.act_send, r.act_recv), (r.igrad_hbm, r.ig_send, r.ig_recv))[kind]
        return remote(
            buf.at[partner(k) + 1, n], dst.at[me, n], send.at[k - 1, n], recv.at[k - 1, n], {"pipe": partner(k)}
        )

    def at_home(kind, n):
        dst = (r.act_hbm, r.igrad_hbm)[kind]
        return pltpu.make_async_copy(buf.at[me + 1, n], dst.at[me, n], r.local_sem.at[kind, n])

    def send_acts(n):
        first = lax.axis_index("dp") % 2

        @pl.when(first == 0)
        def _():
            away(0, 1, n).start()
            away(0, 2, n).start()

        @pl.when(first == 1)
        def _():
            away(0, 2, n).start()
            away(0, 1, n).start()

        away(0, 3, n).start()
        at_home(0, n).start()

    def acts_sent(n):
        for k in (1, 2, 3):
            away(0, k, n).wait_send()
        at_home(0, n).wait()

    def push_row(row, n):
        @pl.when(me // 2 == row)
        def _():
            away(1, 1, n).start()
            at_home(1, n).start()

        @pl.when(me // 2 != row)
        def _():
            away(1, 2, n).start()
            away(1, 3, n).start()

    def pushed(n):
        for k in (1, 2, 3):
            away(1, k, n).wait_send()
        at_home(1, n).wait()

    def arrived(k, n):
        for dst, send, recv in ((r.act_hbm, r.act_send, r.act_recv), (r.igrad_hbm, r.ig_send, r.ig_recv)):
            got = dst.at[partner(k), n]
            remote(got, got, send.at[k - 1, n], recv.at[k - 1, n], {"pipe": partner(k)}).wait_recv()

    attention_stash = ((hqw, r.h_hqw), (qkv, r.h_qkv), (probs, r.h_probs), (att, r.h_att))
    mlp_stash = ((hq2, r.h_hq2), (hid, r.h_hid), (dgelu, r.h_dgelu))

    def stash(sec, n, back):
        pairs = mlp_stash if sec else attention_stash
        return [
            pltpu.make_async_copy(*((far.at[n], near.at[n]) if back else (near.at[n], far.at[n])), r.st_sem.at[sec, n, i])
            for i, (near, far) in enumerate(pairs)
        ]

    def load(i, n):
        src = r.cot_hbm if i else r.x_hbm
        return pltpu.make_async_copy(src.at[me, n], buf.at[5 if i else 0, n], r.in_sem.at[i, n])

    def start(copies):
        for copy in copies:
            copy.start()

    def wait(copies):
        for copy in copies:
            copy.wait()

    steps = (step_1, step_2, step_3, step_4, step_5)
    schedule = {
        (2, 0, 0): ((2, 3),),
        (2, 1, 1): ((3, 3),),
        (1, 0, 0): ((2, 2),),
        (1, 1, 0): ((4, 3),),
        (0, 0, 0): ((3, 2), (2, 1), (5, 3)),
        (0, 0, 1): ((4, 2),),
        (0, 1, 0): ((5, 2),),
        (0, 1, 1): ((3, 1),),
    }
    after = {3: ((1, 3),), 2: ((1, 2),), 1: ((1, 1),), 0: ()}
    weight_steps = (weights_1, weights_2, weights_3, weights_4) if linked else ()
    gathering = {
        (0, 4): ((3, 0), (4, 0)),
        (0, 0): ((2, 1),),
        (0, 1): ((2, 2), (2, 3), (3, 1)),
        (0, 3): ((4, 1), (3, 2)),
        (1, 3): ((4, 2),),
        (2, 0): ((3, 3),),
        (2, 3): ((4, 3),),
    }

    codes = [pltpu.make_async_copy(r.code_hbm, code, r.code_sem.at[0])]
    start(codes)
    start([load(i, n) for i in range(2) for n in range(canvases)])
    wait(codes)
    for i in range(2):
        wait([load(i, n) for n in range(canvases)])

    @pl.loop(0, canvases)
    def _(n):
        @pl.loop(0, 2)
        def _(b):
            def gather(half, i):
                for (sec, at), todo in gathering.items():
                    if linked and sec % 2 == half and at == i:

                        @pl.when((n == 0) & (b == sec // 2))
                        def _():
                            for step, of in todo:
                                weight_steps[step - 1](of)

            for half, forward in enumerate((attention_forward, mlp_forward)):

                @pl.when(b == 1)
                def _():
                    wait(stash(half, n, False))

                s = 2 * b + half
                forward(b, n, buf.at[s, n], buf.at[s + 1, n], functools.partial(gather, half))

                @pl.when(b == 0)
                def _():
                    start(stash(half, n, False))

                gather(half, 3)

        send_acts(n)

    @pl.loop(0, 2)
    def _(flipped):
        b = 1 - flipped
        for half, backward in ((1, mlp_backward), (0, attention_backward)):
            sums = ((g_fc1, g_fc2) if half else (g_qkv, g_proj))
            cleared(*sums)

            @pl.loop(0, canvases)
            def _(n):
                def hook(i):
                    for (sec, at, point), todo in schedule.items():
                        if linked and sec % 2 == half and point == i:

                            @pl.when((n == (canvases - 1 if at else 0)) & (b == sec // 2))
                            def _():
                                for step, of in todo:
                                    steps[step - 1](of)

                def free_out():
                    if half:

                        @pl.when(b == 1)
                        def _():
                            acts_sent(n)

                @pl.when(b == 0)
                def _():
                    wait(stash(half, n, True))

                s = 2 * b + half
                backward(b, n, buf.at[s, n], buf.at[s + 2, n], buf.at[s + 1, n], free_out, hook)
                if half == 0:
                    attention_weights(n)

                    @pl.when(b == 1)
                    def _():
                        push_row(1, n)

                    @pl.when((b == 0) & (n < canvases - 1))
                    def _():
                        push_row(0, n)

                @pl.when(b == 1)
                def _():
                    start(stash(half, n, True))

            if linked:
                for i in range(2):
                    todo = after[2 * i + half]
                    if todo:

                        @pl.when(b == i)
                        def _():
                            for step, of in todo:
                                steps[step - 1](of)
            else:
                whole = zip(sums, (r.f_fc1, r.f_fc2) if half else (r.f_qkv, r.f_proj))
                copies = [pltpu.make_async_copy(g, o.at[b], r.go_sem.at[half, i]) for i, (g, o) in enumerate(whole)]
                start(copies)
                wait(copies)

    if linked:
        step_1(0)
        step_4(1)
        step_2(0)
    push_row(0, canvases - 1)
    if linked:
        step_5(1)
        smalls_sent(1)
        step_3(0)
        step_4(0)
        step_5(0)
        reductions_done()
        weights_sent()
        for k in range(1, 8):
            pack_copy(k).wait_send()
    for k in range(1, 4):
        for n in range(canvases):
            arrived(k, n)
    for n in range(canvases):
        pushed(n)


def compute(linked, operands):
    canvases = operands["x_hbm"].shape[1]
    shape = jax.ShapeDtypeStruct
    hbm = pl.BlockSpec(memory_space=pl.ANY)
    vmem = pl.BlockSpec(memory_space=pltpu.VMEM)
    dma = pltpu.SemaphoreType.DMA
    full = {
        "wat": ((2, D, 4 * D), BF),
        "fc1": ((2, D, FF), BF),
        "fc2": ((2, FF, D), BF),
        "vec": ((2, 8, FF), F32),
    }
    grads = {
        "g_qkv": ((D, 3 * D), F32),
        "g_proj": ((D, D), F32),
        "g_fc1": ((D, FF), F32),
        "g_fc2": ((FF, D), F32),
        "g_vec": ((2, 8, 8, FF), F32),
        "g_tab": ((2, 2 * PLACES, GROUPS * 128), F32),
    }
    outs = {"act_hbm": ((4, canvases, CELLS, D), BF), "igrad_hbm": ((4, canvases, CELLS, D), BF)}
    kept = {
        "hqw": ((canvases, WROWS, D), BF),
        "qkv": ((canvases, WROWS, 3 * D), BF),
        "probs": ((canvases, WINDOWS * GROUPS, 128, 128), BF),
        "att": ((canvases, WROWS, D), BF),
        "hq2": ((canvases, CELLS, D), BF),
        "hid": ((canvases, CELLS, FF), BF),
        "dgelu": ((canvases, CELLS, FF), BF),
    }
    outs |= {"h_" + name: kind for name, kind in kept.items()}
    scratch = kept | {
        "code": ((canvases, CELLS, 128), jnp.int32),
        "codew": ((WROWS, 128), jnp.int32),
        "buf": ((6, canvases, CELLS, D), BF),
        "canvf": ((CELLS, D), F32),
        "winf": ((WROWS, D), F32),
        "gzw": ((WROWS, D), BF),
        "go": ((WROWS, D), BF),
        "gqkv": ((WROWS, 3 * D), BF),
    }
    sems = {
        "in_sem": (2, canvases),
        "code_sem": (1,),
        "st_sem": (2, canvases, 4),
        "local_sem": (2, canvases),
        "act_send": (3, canvases),
        "act_recv": (3, canvases),
        "ig_send": (3, canvases),
        "ig_recv": (3, canvases),
    }
    if linked:
        outs |= {
            "o_qkv": ((2, 48, 3 * D), F32),
            "o_proj": ((2, 48, D), F32),
            "o_fc1": ((2, 48, FF), F32),
            "o_fc2": ((2, 192, D), F32),
            "o_small": ((2, 8, 64, D), BF),
        }
        scratch |= full | grads
        scratch |= {
            "packs": ((8, 16, 256), BF),
            "l_qkv": ((48, 3 * D), F32),
            "l_proj": ((48, D), F32),
            "l_fc1": ((48, FF), F32),
            "l_fc2": ((192, D), F32),
        }
        for kind, rows in (("m_", MLP_ROWS), ("a_", ATT_ROWS)):
            scratch |= {
                kind + "st_a": ((4, rows, D), BF),
                kind + "rc_a": ((4, rows, D), BF),
                kind + "st_b": ((3, rows, D), BF),
                kind + "rc_b": ((3, rows, D), BF),
                kind + "st_c": ((rows, D), BF),
                kind + "rc_c": ((3, rows // 4, D), BF),
                kind + "fin": ((rows, D), BF),
            }
        sems |= {
            "sh_sem": (4, 2),
            "os_sem": (2,),
            "go_sem": (4, 2),
            "wz_send": (4, 2, 3),
            "wz_recv": (4, 2, 3),
            "wx_send": (4, 2, 3, 3),
            "wx_recv": (4, 2, 3, 3),
            "ws_send": (4, 2, 4),
            "ws_recv": (4, 2, 4),
            "pk_send": (7,),
            "pk_recv": (7,),
            "ra_send": (4,),
            "ra_recv": (4,),
            "rb_send": (4, 3),
            "rb_recv": (4, 3),
            "rc_send": (4, 3),
            "rc_recv": (4, 3),
            "rf_send": (4, 3),
            "rf_recv": (4, 3),
            "rs_send": (2, 7),
            "rs_recv": (2, 7),
        }
    else:
        for name in ("g_vec", "g_tab"):
            outs[name] = grads.pop(name)
        outs |= {name.replace("g_", "f_"): ((2,) + dims, F32) for name, (dims, _) in grads.items()}
        scratch |= grads
        sems["go_sem"] = (4, 2)
    in_vmem = set(full) | {"bias", "pack", "g_vec", "g_tab"}
    names = tuple(operands) + tuple(outs) + tuple(scratch) + tuple(sems)
    results = pl.pallas_call(
        functools.partial(kernel, names, linked, canvases),
        out_shape=tuple(shape(*o) for o in outs.values()),
        in_specs=[vmem if name in in_vmem else hbm for name in operands],
        out_specs=tuple(vmem if name in in_vmem else hbm for name in outs),
        scratch_shapes=[pltpu.VMEM(*v) for v in scratch.values()] + [dma(v) for v in sems.values()],
        compiler_params=pltpu.CompilerParams(
            vmem_limit_bytes=64 * 1024 * 1024 - 65536, collective_id=0, has_side_effects=True
        ),
    )(*operands.values())
    return dict(zip(outs, results))


def place_pairs():
    place = np.arange(PLACES)
    r, c = place // 8, place % 8
    index = (r[None, :] - r[:, None] + WIN - 1) * (2 * WIN - 1) + c[None, :] - c[:, None] + WIN - 1
    real = (r < WIN) & (c < WIN)
    return index, real[:, None] & real[None, :], real


def pair_onehot():
    index, both, _ = place_pairs()
    table = (2 * WIN - 1) ** 2
    hot = (np.where(both, index, -1).reshape(-1)[None, :] == np.arange(table)[:, None])
    return hot.astype(np.float32)


def body(
    inputs,
    cotangent,
    pad_mask,
    region_ids,
    norm1_gain,
    norm1_bias,
    qkv_weight,
    qv_bias,
    rel_table,
    proj_weight,
    proj_bias,
    norm2_gain,
    norm2_bias,
    fc1_weight,
    fc1_bias,
    fc2_weight,
    fc2_bias,
):
    owners = lax.axis_size("dp")
    linked = owners == 8
    mine = lax.axis_index("pipe")

    def own(a):
        return lax.dynamic_index_in_dim(a, mine, 0, keepdims=False)

    code = own(region_ids) * 2 + own(pad_mask)
    code = jnp.broadcast_to(code[:, :, None], code.shape + (128,))

    hot = pair_onehot()
    _, _, real = place_pairs()
    rel = lax.dot_general(
        rel_table.astype(BF), jnp.asarray(hot, BF), (((1,), (0,)), ((), ())), preferred_element_type=F32
    )
    rel = rel.reshape(2, GROUPS, 2, 2, PLACES, PLACES)
    rel = jnp.where(jnp.asarray(real)[None, None, None, None, :, None], rel, MASKED)
    rel = rel.transpose(0, 1, 3, 4, 2, 5).reshape(2, GROUPS, 128, 128)

    operands = {"x_hbm": inputs, "cot_hbm": cotangent, "code_hbm": code, "bias": rel}
    vectors = (norm1_gain, norm1_bias, proj_bias, norm2_gain, norm2_bias, fc2_bias, qv_bias, fc1_bias)
    sizes = [v.shape[1] for v in vectors]
    ends = np.cumsum([0] + sizes)
    if linked:
        pack = jnp.stack([jnp.pad(v, ((0, 0), (0, 256 - v.shape[1]))) for v in vectors], axis=1)
        operands |= {
            "pack": pack.reshape(16, 256).astype(BF),
            "s_qkv": qkv_weight,
            "s_proj": proj_weight,
            "s_fc1": fc1_weight,
            "s_fc2": fc2_weight,
        }
    else:

        def gathered(a):
            return lax.all_gather(a.astype(BF), "dp", axis=1, tiled=True)

        packed = lax.all_gather(jnp.concatenate(vectors, axis=1).astype(BF), "dp", axis=1)
        parts = [packed[:, :, a:b].reshape(2, -1).astype(F32) for a, b in zip(ends[:-1], ends[1:])]
        qv = parts[6]
        parts[6] = jnp.concatenate([qv[:, :D], jnp.zeros_like(qv[:, :D]), qv[:, D:]], axis=1)
        vec = jnp.stack([jnp.pad(p, ((0, 0), (0, FF - p.shape[1]))) for p in parts], axis=1)
        operands |= {
            "wat": jnp.concatenate([gathered(qkv_weight), gathered(proj_weight)], axis=2),
            "fc1": gathered(fc1_weight),
            "fc2": gathered(fc2_weight),
            "vec": vec,
        }

    out = compute(linked, operands)

    def to_owners(g):
        shared = lax.psum_scatter(g, "dp", scatter_dimension=1, tiled=True)
        return lax.psum(shared, "pipe")

    if linked:
        small = out["o_small"]
        g_tab = small[:, :, :16].reshape(2, 128, GROUPS * 128)
        g_vec = jnp.concatenate([small[:, :, 16 + 8 * j : 24 + 8 * j] for j in range(4)], axis=3)
    else:
        g_tab, g_vec = out["g_tab"], out["g_vec"]

    g_vec = jnp.sum(g_vec.astype(F32), axis=2)
    kinds = [g_vec[:, i] for i in range(8)]
    qv_sum = jnp.concatenate([kinds[6][:, :D], kinds[6][:, 2 * D : 3 * D]], axis=1)
    rows = [kinds[0], kinds[1], kinds[2], kinds[3], kinds[4], kinds[5], qv_sum, kinds[7]]
    if linked:
        at = lax.axis_index("dp")
        small = [lax.dynamic_slice_in_dim(v, at * n, n, 1) for v, n in zip(rows, sizes)]
    else:
        rows = [v[:, : n * owners].reshape(2, -1, n) for v, n in zip(rows, sizes)]
        g_small = to_owners(jnp.concatenate(rows, axis=2))[:, 0]
        small = [g_small[:, a:b] for a, b in zip(ends[:-1], ends[1:])]

    pairs = g_tab.reshape(2, 2, PLACES, GROUPS, 2, PLACES).transpose(0, 3, 4, 1, 2, 5)
    pairs = pairs.reshape(2, HEADS, PLACES * PLACES)
    g_table = lax.dot_general(
        jnp.broadcast_to(jnp.asarray(hot, pairs.dtype), (2,) + hot.shape),
        pairs,
        (((2,), (2,)), ((0,), (0,))),
        precision=None if linked else lax.Precision.HIGHEST,
        preferred_element_type=F32,
    )
    if linked:
        big = [out[name] for name in ("o_qkv", "o_proj", "o_fc1", "o_fc2")]
    else:
        g_table = lax.psum(g_table, ("pipe", "dp"))
        big = [to_owners(out[name]) for name in ("f_qkv", "f_proj", "f_fc1", "f_fc2")]

    return (
        out["act_hbm"][None],
        out["igrad_hbm"][None],
        small[0],
        small[1],
        big[0],
        small[6],
        g_table,
        big[1],
        small[2],
        small[3],
        small[4],
        big[2],
        small[7],
        big[3],
        small[5],
    )


def solution(mesh):
    cols = P(None, "dp")
    rows = P(None, "dp", None)
    return jax.shard_map(
        body,
        mesh=mesh,
        in_specs=(
            P(None, "dp", None, None),
            P(None, "dp", None, None),
            rows,
            rows,
            cols,
            cols,
            rows,
            cols,
            P(),
            rows,
            cols,
            cols,
            cols,
            rows,
            cols,
            rows,
            cols,
        ),
        out_specs=(
            P("pipe", None, "dp", None, None),
            P("pipe", None, "dp", None, None),
            cols,
            cols,
            rows,
            cols,
            P(),
            rows,
            cols,
            cols,
            cols,
            rows,
            cols,
            rows,
            cols,
        ),
        check_vma=False,
    )
```

```python
import functools
import types

import jax
import jax.numpy as jnp
import numpy as np
from jax import lax
from jax.experimental import pallas as pl
from jax.experimental.pallas import tpu as pltpu
from jax.sharding import PartitionSpec as P

HEADS = 12
WIN = 7
SHIFT = 3
GRID = 28
CELLS = 784
D = 384
FF = 1536
HEAD = 32
SIDE = 4
WINDOWS = 16
PLACES = 64
WROWS = WINDOWS * PLACES
GROUPS = 3
TILE = 112
SCALE = HEAD**-0.5
NORM_EPS = 1e-05
MASKED = -1e30
BF = jnp.bfloat16
F32 = jnp.float32

RSQRT_2 = 1.0 / np.sqrt(2.0)
PHI_0 = 1.0 / np.sqrt(2.0 * np.pi)


def nn(a, b):
    return lax.dot_general(a, b, (((1,), (0,)), ((), ())), preferred_element_type=F32)


def nt(a, b):
    return lax.dot_general(a, b, (((1,), (1,)), ((), ())), preferred_element_type=F32)


def tn(a, b):
    return lax.dot_general(a, b, (((0,), (0,)), ((), ())), preferred_element_type=F32)


def segments(shift):
    runs = []
    for wr in range(SIDE):
        for r in range(WIN):
            row = (wr * WIN + r + shift) % GRID
            for wc in range(SIDE):
                col = (wc * WIN + shift) % GRID
                place = (wr * SIDE + wc) * PLACES + r * 8
                first = min(WIN, GRID - col)
                runs.append((row * GRID + col, place, first))
                if first < WIN:
                    runs.append((row * GRID, place + first, WIN - first))
    return runs


def to_windows(src, dst, shift):
    for cell, place, count in segments(shift):
        dst[pl.ds(place, count), :] = src[pl.ds(cell, count), :]


def to_canvas(src, dst, shift):
    for cell, place, count in segments(shift):
        dst[pl.ds(cell, count), :] = src[pl.ds(place, count), :]


def row_block(t, size):
    return pl.ds(pl.multiple_of(t * size, 16), size)


def standardized(v):
    centered = v - jnp.mean(v, axis=-1, keepdims=True)
    spread = jnp.mean(centered * centered, axis=-1, keepdims=True)
    rs = lax.rsqrt(spread + NORM_EPS)
    return centered * rs, rs


def by_eights(v):
    return jnp.sum(v.reshape(v.shape[0] // 8, 8, v.shape[1]), axis=0)


def gelu_parts(x):
    cdf = 0.5 + 0.5 * lax.erf(x * RSQRT_2)
    return x * cdf, cdf + x * (jnp.exp(-0.5 * x * x) * PHI_0)


def real_places(rows):
    place = lax.broadcasted_iota(jnp.int32, (rows, 1), 0)
    return ((place & 7) < WIN) & (((place >> 3) & 7) < WIN)


def head_of_lane():
    return lax.broadcasted_iota(jnp.int32, (PLACES, 128), 1) >> 5


def by_low(x, lanes):
    zero = jnp.zeros_like(x)
    return jnp.concatenate([jnp.where((lanes & 1) == h, x, zero) for h in range(2)], axis=0)


def by_high(x, lanes):
    zero = jnp.zeros_like(x)
    return jnp.concatenate([jnp.where((lanes >> 1) == h, x, zero) for h in range(2)], axis=0)


def own_low(wide, lanes):
    return jnp.where((lanes & 1) == 0, wide[:PLACES], wide[PLACES:])


def own_high(wide, lanes):
    return jnp.where((lanes >> 1) == 0, wide[:PLACES], wide[PLACES:])


MESH = pl.DeviceIdType.MESH
ATT_ROWS = 256
MLP_ROWS = 384
SMALL = 192


def kernel(names, linked, canvases, *refs):
    r = types.SimpleNamespace(**dict(zip(names, refs)))
    me = lax.axis_index("pipe")
    code, codew, buf = r.code, r.codew, r.buf
    hqw, qkv, probs, att = r.hqw, r.qkv, r.probs, r.att
    hq2, hid, dgelu = r.hq2, r.hid, r.dgelu
    canvf, winf, gzw, gqkv, go = r.canvf, r.winf, r.gzw, r.gqkv, r.go
    g_qkv, g_proj, g_fc1, g_fc2, g_vec, g_tab = r.g_qkv, r.g_proj, r.g_fc1, r.g_fc2, r.g_vec, r.g_tab
    wat, fc1, fc2, vec, bias = r.wat, r.fc1, r.fc2, r.vec, r.bias
    if linked:
        d = lax.axis_index("dp")
        z, c = d // 2, d % 2
        sibling = {"dp": 2 * z + 1 - c}

    def z_peer(k):
        return {"dp": 2 * lax.rem(z + k, 4) + c}

    def pipe_peer(k):
        return {"pipe": lax.rem(me + k, 4)}

    def dp_peer(k):
        return {"dp": lax.rem(d + k, 8)}

    def remote(src, dst, send, recv, device):
        return pltpu.make_async_remote_copy(
            src_ref=src, dst_ref=dst, send_sem=send, recv_sem=recv, device_id=device, device_id_type=MESH
        )

    barrier = pltpu.get_barrier_semaphore()
    partners = [pipe_peer(k) for k in range(1, 4)]
    if linked:
        partners += [dp_peer(k) for k in range(1, 8)]
    for partner in partners:
        pl.semaphore_signal(barrier, inc=1, device_id=partner, device_id_type=MESH)

    full = ((wat,), (fc1, fc2), (wat,), (fc1, fc2))

    def owner_back(k):
        return 2 * lax.rem(z + 4 - k, 4) + c

    def shard(sec, a, owner):
        h = 192 if a else 48
        return full[sec][a].at[sec // 2, pl.ds(pl.multiple_of(owner * h, 16), h), :]

    def part(sec, a, owner, place):
        if a:
            return fc2.at[sec // 2, pl.ds(pl.multiple_of(owner * 192 + place * 48, 16), 48), :]
        rows = pl.ds(pl.multiple_of(owner * 48, 16), 48)
        return full[sec][0].at[sec // 2, rows, pl.ds(pl.multiple_of(place * D, 128), D)]

    def to_z(sec, a, k):
        own = part(sec, a, d, me)
        return remote(own, own, r.wz_send.at[sec, a, k - 1], r.wz_recv.at[sec, a, k - 1], z_peer(k))

    def to_places(sec, a, k, j):
        got = part(sec, a, owner_back(k), me)
        return remote(
            got, got, r.wx_send.at[sec, a, k - 1, j - 1], r.wx_recv.at[sec, a, k - 1, j - 1], pipe_peer(j)
        )

    def to_sibling(sec, a, k):
        block = shard(sec, a, owner_back(k))
        return remote(block, block, r.ws_send.at[sec, a, k], r.ws_recv.at[sec, a, k], sibling)

    def weights_1(sec):
        for a in range(len(full[sec])):
            for k in range(1, 4):
                to_z(sec, a, k).start()
            to_sibling(sec, a, 0).start()

    def weights_2(sec):
        for k in range(1, 4):
            for a in range(len(full[sec])):
                got = part(sec, a, owner_back(k), me)
                remote(got, got, r.wz_send.at[sec, a, k - 1], r.wz_recv.at[sec, a, k - 1], z_peer(k)).wait_recv()
                for j in range(1, 4):
                    to_places(sec, a, k, j).start()

    def weights_3(sec):
        for k in range(1, 4):
            for a in range(len(full[sec])):
                for j in range(1, 4):
                    got = part(sec, a, owner_back(k), lax.rem(me + 4 - j, 4))
                    remote(
                        got, got, r.wx_send.at[sec, a, k - 1, j - 1], r.wx_recv.at[sec, a, k - 1, j - 1], pipe_peer(j)
                    ).wait_recv()
                to_sibling(sec, a, k).start()

    def weights_4(sec):
        for k in range(4):
            for a in range(len(full[sec])):
                block = shard(sec, a, 2 * lax.rem(z + 4 - k, 4) + 1 - c)
                remote(block, block, r.ws_send.at[sec, a, k], r.ws_recv.at[sec, a, k], sibling).wait_recv()

    def weights_sent():
        for sec in range(4):
            for a in range(len(full[sec])):
                for k in range(4):
                    to_sibling(sec, a, k).wait_send()
                    if k:
                        to_z(sec, a, k).wait_send()
                        for j in range(1, 4):
                            to_places(sec, a, k, j).wait_send()

    def pack_copy(k):
        return remote(
            r.packs.at[d], r.packs.at[d], r.pk_send.at[k - 1], r.pk_recv.at[k - 1], dp_peer(k)
        )

    def pack_arrival(k):
        slot = r.packs.at[lax.rem(d + 8 - k, 8)]
        return remote(slot, slot, r.pk_send.at[k - 1], r.pk_recv.at[k - 1], dp_peer(k))

    def place_vectors():
        kind = lax.broadcasted_iota(jnp.int32, (16, 256), 0) & 7
        lane = lax.broadcasted_iota(jnp.int32, (16, 256), 1)
        vec[...] = jnp.zeros_like(vec)
        for width, kinds in ((48, kind < 6), (96, kind == 6), (192, kind == 7)):
            for owner in range(8):
                at = owner * width
                if width == 96 and owner >= 4:
                    at += D
                start = at // 128 * 128
                part = jnp.where(kinds & (lane < width), r.packs[owner].astype(F32), 0.0)
                if at > start:
                    part = pltpu.roll(part, at - start, 1)
                for b in range(2):
                    vec[b, :, start : start + 256] += part[8 * b : 8 * b + 8]

    def pieces(sec, owner):
        b = sec // 2
        out = []

        def matrix(ref, h):
            for t in range(h // 48):
                rows = pl.ds(pl.multiple_of(owner * h + t * 48, 16), 48)
                for j in range(ref.shape[1] // D):
                    load = functools.partial(lambda ref, rows, j: ref[rows, j * D : (j + 1) * D], ref, rows, j)
                    out.append((len(out) * 48, 48, load))

        def small():
            parts = [g_tab[b, pl.ds(pl.multiple_of(owner * 16, 16), 16), :]]
            parts += [g_vec[b, owner, :, j * D : (j + 1) * D] for j in range(4)]
            return jnp.concatenate(parts + [jnp.zeros((16, D), F32)], axis=0)

        if sec % 2:
            matrix(g_fc1, 48)
            matrix(g_fc2, 192)
        else:
            matrix(g_qkv, 48)
            matrix(g_proj, 48)
            out.append((SMALL, 64, small))
        return out

    def reduce_refs(sec):
        kind = "m" if sec % 2 else "a"
        return types.SimpleNamespace(
            **{n: getattr(r, kind + "_" + n) for n in ("st_a", "rc_a", "st_b", "rc_b", "st_c", "rc_c", "fin")}
        )

    def step_1(sec):
        q = reduce_refs(sec)
        if sec < 2:
            copy_a(sec + 2).wait_send()
            for k in range(1, 4):
                copy_b(sec + 2, k).wait_send()
                copy_c(sec + 2, k).wait_send()
        for k in range(4):
            i = lax.rem(z + k, 4)
            kept = q.st_b.at[k - 1] if k else q.st_c
            for row, rows, load in pieces(sec, 2 * i + 1 - c):
                q.st_a[i, row : row + rows, :] = load().astype(BF)
            for row, rows, load in pieces(sec, 2 * i + c):
                kept[row : row + rows, :] = load().astype(BF)
        copy_a(sec).start()

    def copy_a(sec):
        q = reduce_refs(sec)
        return remote(q.st_a, q.rc_a, r.ra_send.at[sec], r.ra_recv.at[sec], sibling)

    def copy_b(sec, k):
        q = reduce_refs(sec)
        return remote(
            q.st_b.at[k - 1], q.rc_b.at[k - 1], r.rb_send.at[sec, k - 1], r.rb_recv.at[sec, k - 1], z_peer(k)
        )

    def step_2(sec):
        q = reduce_refs(sec)
        copy_a(sec).wait_recv()
        for k in (1, 2, 3, 0):
            i = lax.rem(z + k, 4)
            kept = q.st_b.at[k - 1] if k else q.st_c
            for row in range(0, kept.shape[0], 64):
                at = slice(row, row + 64)
                kept[at, :] = (kept[at, :].astype(F32) + q.rc_a[i, at, :].astype(F32)).astype(BF)
            if k:
                copy_b(sec, k).start()

    def quarter(sec, ref, who):
        rows = (MLP_ROWS if sec % 2 else ATT_ROWS) // 4
        return ref.at[pl.ds(pl.multiple_of(who * rows, 16), rows), :]

    def copy_c(sec, k):
        q = reduce_refs(sec)
        return remote(
            quarter(sec, q.st_c, lax.rem(me + k, 4)),
            q.rc_c.at[k - 1],
            r.rc_send.at[sec, k - 1],
            r.rc_recv.at[sec, k - 1],
            pipe_peer(k),
        )

    def step_3(sec):
        q = reduce_refs(sec)
        for k in range(1, 4):
            copy_b(sec, k).wait_recv()
        for row in range(0, q.st_c.shape[0], 64):
            at = slice(row, row + 64)
            total = q.st_c[at, :].astype(F32)
            for k in range(3):
                total = total + q.rc_b[k, at, :].astype(F32)
            q.st_c[at, :] = total.astype(BF)
        for k in range(1, 4):
            copy_c(sec, k).start()

    def copy_f(sec, k):
        q = reduce_refs(sec)
        own = quarter(sec, q.fin, me)
        return remote(own, own, r.rf_send.at[sec, k - 1], r.rf_recv.at[sec, k - 1], pipe_peer(k))

    def step_4(sec):
        q = reduce_refs(sec)
        for k in range(1, 4):
            copy_c(sec, k).wait_recv()
            if sec < 2:
                copy_f(sec + 2, k).wait_send()
        total = quarter(sec, q.st_c, me)[...].astype(F32)
        for k in range(3):
            total = total + q.rc_c[k].astype(F32)
        quarter(sec, q.fin, me)[...] = total.astype(BF)
        for k in range(1, 4):
            copy_f(sec, k).start()

    def copy_s(b, k):
        rows = pl.ds(SMALL, 64)
        return remote(
            r.a_fin.at[rows, :], r.o_small.at[b, d], r.rs_send.at[b, k - 1], r.rs_recv.at[b, k - 1], dp_peer(k)
        )

    def own_small(b):
        return pltpu.make_async_copy(r.a_fin.at[pl.ds(SMALL, 64), :], r.o_small.at[b, d], r.os_sem.at[b])

    def outputs(sec):
        pairs = ((r.l_fc1, r.o_fc1), (r.l_fc2, r.o_fc2)) if sec % 2 else ((r.l_qkv, r.o_qkv), (r.l_proj, r.o_proj))
        return [
            pltpu.make_async_copy(ref, out.at[sec // 2], r.go_sem.at[sec, i]) for i, (ref, out) in enumerate(pairs)
        ]

    def step_5(sec):
        q = reduce_refs(sec)
        b = sec // 2
        for k in range(1, 4):
            got = quarter(sec, q.fin, lax.rem(me + 4 - k, 4))
            remote(got, got, r.rf_send.at[sec, k - 1], r.rf_recv.at[sec, k - 1], pipe_peer(k)).wait_recv()
        if sec % 2 == 0:
            for k in range(1, 8):
                copy_s(b, k).start()
            own_small(b).start()
        if sec < 2:
            for out in outputs(sec + 2):
                out.wait()
        row = 0
        for ref in (r.l_fc1, r.l_fc2) if sec % 2 else (r.l_qkv, r.l_proj):
            for t in range(ref.shape[0] // 48):
                for j in range(ref.shape[1] // D):
                    ref[t * 48 : (t + 1) * 48, j * D : (j + 1) * D] = q.fin[row : row + 48, :].astype(F32)
                    row += 48
        for out in outputs(sec):
            out.start()

    def smalls_sent(b):
        for k in range(1, 8):
            copy_s(b, k).wait_send()
        own_small(b).wait()

    def reductions_done():
        for sec in (1, 0):
            copy_a(sec).wait_send()
            for k in range(1, 4):
                copy_b(sec, k).wait_send()
                copy_c(sec, k).wait_send()
                copy_f(sec, k).wait_send()
        for sec in range(2):
            for out in outputs(sec):
                out.wait()
        smalls_sent(0)
        for b in range(2):
            for k in range(1, 8):
                rows = pl.ds(SMALL, 64)
                remote(
                    r.a_fin.at[rows, :],
                    r.o_small.at[b, lax.rem(d + 8 - k, 8)],
                    r.rs_send.at[b, k - 1],
                    r.rs_recv.at[b, k - 1],
                    dp_peer(k),
                ).wait_recv()

    if linked:
        lands = ((r.s_qkv, g_qkv, wat, 0), (r.s_proj, g_proj, wat, 3 * D), (r.s_fc1, g_fc1, fc1, 0), (r.s_fc2, g_fc2, fc2, 0))

        def landing(i, b):
            src, dst, _, _ = lands[i]
            h, n = src.shape[1:]
            return pltpu.make_async_copy(
                src.at[b], dst.at[pl.ds(192 * b, h), pl.ds(0, n)], r.sh_sem.at[i, b]
            )

        for i in range(4):
            for b in range(2):
                landing(i, b).start()
        r.packs[d] = r.pack[...]
        for i, (src, dst, ref, col) in enumerate(lands):
            h, n = src.shape[1:]
            for b in range(2):
                landing(i, b).wait()
                for t in range(0, h, 48):
                    rows = pl.ds(pl.multiple_of(d * h + t, 16), 48)
                    ref[b, rows, col : col + n] = dst[192 * b + t : 192 * b + t + 48, :n].astype(BF)
    pl.semaphore_wait(barrier, len(partners))
    if linked:
        for k in range(1, 8):
            pack_copy(k).start()
        weights_1(0)

    def cleared(*refs):
        for ref in refs:

            @pl.loop(0, ref.shape[0] // 16)
            def _(i):
                ref[row_block(i, 16), :] = jnp.zeros((16, ref.shape[1]), F32)

    g_vec[...] = jnp.zeros_like(g_vec)
    g_tab[...] = jnp.zeros_like(g_tab)
    codew[...] = jnp.zeros_like(codew)

    if linked:
        weights_2(0)
        for sec in range(1, 4):
            weights_1(sec)
        for k in range(1, 8):
            pack_arrival(k).wait_recv()
        place_vectors()

    def vector(b, kind, width=D):
        return vec[b, kind : kind + 1, :width]

    def add_vec(b, kind, part):
        g_vec[b, kind, :, : part.shape[1]] += part

    def windowed(rows, count):
        return jnp.where(real_places(count), winf[rows, :], 0.0).astype(BF)

    def by_block(b, move):
        for i in range(2):

            @pl.when(b == i)
            def _():
                move(SHIFT * i)

    def attention_forward(b, n, x, out, hook):
        lanes = head_of_lane()

        @pl.loop(0, CELLS // TILE)
        def _(t):
            rows = row_block(t, TILE)
            xhat, _ = standardized(x[rows, :].astype(F32))
            canvf[rows, :] = xhat * vector(b, 0) + vector(b, 1)

        def arrange(shift):
            to_windows(canvf, winf, shift)
            to_windows(code.at[n], codew, shift)

        by_block(b, arrange)
        hook(4)

        @pl.loop(0, 4)
        def _(t):
            rows = row_block(t, 256)
            hq = windowed(rows, 256)
            hqw[n, rows, :] = hq
            for part in range(3):
                cols = slice(part * D, (part + 1) * D)
                acc = nn(hq, wat[b, :, cols]) + vec[b, 6:7, cols]
                if part == 0:
                    acc = acc * SCALE
                qkv[n, rows, cols] = acc.astype(BF)

        hook(0)

        @pl.loop(0, WINDOWS)
        def _(w):
            rows = row_block(w, PLACES)
            cells = codew[rows, :]
            region = (cells >> 1) * b
            pad = (cells & 1).astype(F32)
            lane = lax.broadcasted_iota(jnp.int32, (PLACES, 128), 1)
            same = jnp.where(lane == region, 1.0, 0.0)
            left = jnp.where(lane == 127, 1.0 - pad, same).astype(BF)
            right = jnp.where(lane == 127, -pad, same).astype(BF)
            agree = nt(left, jnp.concatenate([right, right], axis=0))
            mask = jnp.where(agree > 0.5, 0.0, MASKED)
            for g in range(GROUPS):
                q = qkv[n, rows, g * 128 : (g + 1) * 128]
                k = qkv[n, rows, D + g * 128 : D + (g + 1) * 128]
                v = qkv[n, rows, 2 * D + g * 128 : 2 * D + (g + 1) * 128]
                scores = nt(by_low(k, lanes), by_high(q, lanes)) + bias[b, g]
                halves = []
                for h in range(2):
                    s = scores[h * PLACES : (h + 1) * PLACES] + mask
                    e = jnp.exp(s - jnp.max(s, axis=0, keepdims=True))
                    halves.append((e * (1.0 / jnp.sum(e, axis=0, keepdims=True))).astype(BF))
                p = jnp.concatenate(halves, axis=0)
                probs[n, w * GROUPS + g] = p
                att[n, rows, g * 128 : (g + 1) * 128] = own_high(tn(p, by_low(v, lanes)), lanes).astype(BF)

        hook(1)

        @pl.loop(0, 4)
        def _(t):
            rows = row_block(t, 256)
            winf[rows, :] = nn(att[n, rows, :], wat[b, :, 3 * D :])

        by_block(b, functools.partial(to_canvas, winf, canvf))

        @pl.loop(0, CELLS // TILE)
        def _(t):
            rows = row_block(t, TILE)
            out[rows, :] = (x[rows, :].astype(F32) + (canvf[rows, :] + vector(b, 2))).astype(BF)

    def mlp_forward(b, n, x, out, hook):
        @pl.loop(0, CELLS // TILE)
        def _(t):
            rows = row_block(t, TILE)
            xhat, _ = standardized(x[rows, :].astype(F32))
            hq2[n, rows, :] = (xhat * vector(b, 3) + vector(b, 4)).astype(BF)

        hook(4)

        @pl.loop(0, FF // 256)
        def _(i):
            cols = pl.ds(pl.multiple_of(i * 256, 256), 256)
            pre = nn(hq2[n], fc1[b, :, cols]) + vec[b, 7:8, cols]
            for at in range(0, CELLS, 16):
                h, dg = gelu_parts(pre[at : at + 16])
                hid[n, at : at + 16, cols] = h.astype(BF)
                dgelu[n, at : at + 16, cols] = dg.astype(BF)

        hook(0)
        total = nn(hid[n], fc2[b])
        for at in range(0, CELLS, TILE):
            rows = slice(at, at + TILE)
            out[rows, :] = (x[rows, :].astype(F32) + (total[rows] + vector(b, 5))).astype(BF)

    def norm_backward(b, kind, x, gz, out):
        @pl.loop(0, CELLS // TILE)
        def _(t):
            rows = row_block(t, TILE)
            xhat, rs = standardized(x[rows, :].astype(F32))
            gn = canvf[rows, :]
            gzf = gz[rows, :].astype(F32)
            add_vec(b, kind, by_eights(gn * xhat))
            add_vec(b, kind + 1, by_eights(gn))
            add_vec(b, 5 if kind else 2, by_eights(gzf))
            g = gn * vector(b, kind)
            mg = jnp.mean(g, axis=-1, keepdims=True)
            mgx = jnp.mean(g * xhat, axis=-1, keepdims=True)
            out[rows, :] = (gzf + rs * (g - mg - xhat * mgx)).astype(BF)

    def mlp_backward(b, n, x, gz, out, free_out, hook):
        @pl.loop(0, FF // 256)
        def _(i):
            cols = pl.ds(pl.multiple_of(i * 256, 256), 256)
            gh = nt(gz[...], fc2[b, cols, :])
            sums = jnp.zeros((8, 256), F32)
            for at in range(0, CELLS, 16):
                gp = (gh[at : at + 16] * dgelu[n, at : at + 16, cols].astype(F32)).astype(BF)
                dgelu[n, at : at + 16, cols] = gp
                sums = sums + by_eights(gp.astype(F32))
            g_vec[b, 7, :, cols] += sums
            g_fc1[:, cols] += tn(hq2[n], dgelu[n, :, cols])
            g_fc2[cols, :] += tn(hid[n, :, cols], gz[...])

        hook(0)
        canvf[...] = nt(dgelu[n], fc1[b])
        free_out()
        norm_backward(b, 3, x, gz, out)

    def attention_backward(b, n, x, gz, out, free_out, hook):
        lanes = head_of_lane()

        @pl.loop(0, CELLS // TILE)
        def _(t):
            rows = row_block(t, TILE)
            canvf[rows, :] = gz[rows, :].astype(F32)

        by_block(b, functools.partial(to_windows, canvf, winf))

        @pl.loop(0, 4)
        def _(t):
            rows = row_block(t, 256)
            gzw[rows, :] = windowed(rows, 256)

        g_proj[...] += tn(att[n], gzw[...])

        @pl.loop(0, 4)
        def _(t):
            rows = row_block(t, 256)
            go[rows, :] = nt(gzw[rows, :], wat[b, :, 3 * D :]).astype(BF)

        hook(0)

        @pl.loop(0, WINDOWS)
        def _(w):
            rows = row_block(w, PLACES)
            for g in range(GROUPS):
                at = [slice(part * D + g * 128, part * D + (g + 1) * 128) for part in range(3)]
                q, k, v = (qkv[n, rows, cols] for cols in at)
                go_wide = by_high(go[rows, at[0]], lanes)
                p_low = probs[n, w * GROUPS + g]
                p = p_low.astype(F32)
                pd = p * nt(by_low(v, lanes), go_wide)
                halves = []
                for h in range(2):
                    half = slice(h * PLACES, (h + 1) * PLACES)
                    halves.append((pd[half] - p[half] * jnp.sum(pd[half], axis=0, keepdims=True)).astype(BF))
                ds = jnp.concatenate(halves, axis=0)
                g_tab[b, :, g * 128 : (g + 1) * 128] += ds.astype(F32)
                gqkv[rows, at[0]] = (own_high(tn(ds, by_low(k, lanes)), lanes) * SCALE).astype(BF)
                gqkv[rows, at[1]] = own_low(nn(ds, by_high(q, lanes)), lanes).astype(BF)
                gqkv[rows, at[2]] = own_low(nn(p_low, go_wide), lanes).astype(BF)

        hook(1)

        @pl.loop(0, 4)
        def _(t):
            rows = row_block(t, 256)
            gq = gqkv[rows, :]
            add_vec(b, 6, by_eights(gq.astype(F32)))
            winf[rows, :] = nt(gq, wat[b, :, : 3 * D])

        by_block(b, functools.partial(to_canvas, winf, canvf))
        free_out()
        norm_backward(b, 0, x, gz, out)

    def attention_weights(n):
        @pl.loop(0, 3)
        def _(part):
            cols = pl.ds(pl.multiple_of(part * D, 128), D)
            g_qkv[:, cols] += tn(hqw[n], gqkv[:, cols])

    def partner(k):
        x, y = me % 2, me // 2
        return 2 * (1 - y if k & 2 else y) + (1 - x if k & 1 else x)

    def away(kind, k, n):
        dst, send, recv = ((r.act_hbm, r.act_send, r.act_recv), (r.igrad_hbm, r.ig_send, r.ig_recv))[kind]
        return remote(
            buf.at[partner(k) + 1, n], dst.at[me, n], send.at[k - 1, n], recv.at[k - 1, n], {"pipe": partner(k)}
        )

    def at_home(kind, n):
        dst = (r.act_hbm, r.igrad_hbm)[kind]
        return pltpu.make_async_copy(buf.at[me + 1, n], dst.at[me, n], r.local_sem.at[kind, n])

    def send_acts(n):
        first = lax.axis_index("dp") % 2

        @pl.when(first == 0)
        def _():
            away(0, 1, n).start()
            away(0, 2, n).start()

        @pl.when(first == 1)
        def _():
            away(0, 2, n).start()
            away(0, 1, n).start()

        away(0, 3, n).start()
        at_home(0, n).start()

    def acts_sent(n):
        for k in (1, 2, 3):
            away(0, k, n).wait_send()
        at_home(0, n).wait()

    def push_row(row, n):
        @pl.when(me // 2 == row)
        def _():
            away(1, 1, n).start()
            at_home(1, n).start()

        @pl.when(me // 2 != row)
        def _():
            away(1, 2, n).start()
            away(1, 3, n).start()

    def pushed(n):
        for k in (1, 2, 3):
            away(1, k, n).wait_send()
        at_home(1, n).wait()

    def arrived(k, n):
        for dst, send, recv in ((r.act_hbm, r.act_send, r.act_recv), (r.igrad_hbm, r.ig_send, r.ig_recv)):
            got = dst.at[partner(k), n]
            remote(got, got, send.at[k - 1, n], recv.at[k - 1, n], {"pipe": partner(k)}).wait_recv()

    attention_stash = ((hqw, r.h_hqw), (qkv, r.h_qkv), (probs, r.h_probs), (att, r.h_att))
    mlp_stash = ((hq2, r.h_hq2), (hid, r.h_hid), (dgelu, r.h_dgelu))

    def stash(sec, n, back):
        pairs = mlp_stash if sec else attention_stash
        return [
            pltpu.make_async_copy(*((far.at[n], near.at[n]) if back else (near.at[n], far.at[n])), r.st_sem.at[sec, n, i])
            for i, (near, far) in enumerate(pairs)
        ]

    def load(i, n):
        src = r.cot_hbm if i else r.x_hbm
        return pltpu.make_async_copy(src.at[me, n], buf.at[5 if i else 0, n], r.in_sem.at[i, n])

    def start(copies):
        for copy in copies:
            copy.start()

    def wait(copies):
        for copy in copies:
            copy.wait()

    steps = (step_1, step_2, step_3, step_4, step_5)
    schedule = {
        (2, 0, 1): ((2, 3),),
        (1, 0, 0): ((2, 2), (4, 3)),
        (1, 1, 0): ((5, 3),),
        (0, 0, 0): ((3, 2),),
        (0, 0, 1): ((2, 1), (4, 2)),
        (0, 1, 0): ((5, 2),),
    }
    after = {3: ((1, 3),), 2: ((3, 3), (1, 2)), 1: ((1, 1),), 0: ()}
    weight_steps = (weights_1, weights_2, weights_3, weights_4) if linked else ()
    gathering = {
        (0, 4): ((2, 1), (3, 0), (4, 0)),
        (0, 0): ((2, 2),),
        (0, 1): ((3, 1), (2, 3)),
        (1, 4): ((4, 1),),
        (1, 0): ((3, 2),),
        (2, 4): ((4, 2),),
        (2, 0): ((3, 3),),
        (3, 4): ((4, 3),),
    }

    codes = [pltpu.make_async_copy(r.code_hbm, code, r.code_sem.at[0])]
    start(codes)
    start([load(i, n) for i in range(2) for n in range(canvases)])
    wait(codes)
    for i in range(2):
        wait([load(i, n) for n in range(canvases)])

    @pl.loop(0, canvases)
    def _(n):
        @pl.loop(0, 2)
        def _(b):
            def gather(half, i):
                for (sec, at), todo in gathering.items():
                    if linked and sec % 2 == half and at == i:

                        @pl.when((n == 0) & (b == sec // 2))
                        def _():
                            for step, of in todo:
                                weight_steps[step - 1](of)

            for half, forward in enumerate((attention_forward, mlp_forward)):

                @pl.when(b == 1)
                def _():
                    wait(stash(half, n, False))

                s = 2 * b + half
                forward(b, n, buf.at[s, n], buf.at[s + 1, n], functools.partial(gather, half))

                @pl.when(b == 0)
                def _():
                    start(stash(half, n, False))

        send_acts(n)

    @pl.loop(0, 2)
    def _(flipped):
        b = 1 - flipped
        for half, backward in ((1, mlp_backward), (0, attention_backward)):
            sums = ((g_fc1, g_fc2) if half else (g_qkv, g_proj))
            cleared(*sums)

            @pl.loop(0, canvases)
            def _(n):
                def hook(i):
                    for (sec, at, point), todo in schedule.items():
                        if linked and sec % 2 == half and point == i:

                            @pl.when((n == (canvases - 1 if at else 0)) & (b == sec // 2))
                            def _():
                                for step, of in todo:
                                    steps[step - 1](of)

                def free_out():
                    if half:

                        @pl.when(b == 1)
                        def _():
                            acts_sent(n)

                @pl.when(b == 0)
                def _():
                    wait(stash(half, n, True))

                s = 2 * b + half
                backward(b, n, buf.at[s, n], buf.at[s + 2, n], buf.at[s + 1, n], free_out, hook)
                if half == 0:
                    for row in range(2):

                        @pl.when(b == row)
                        def _():
                            push_row(row, n)

                    attention_weights(n)

                @pl.when(b == 1)
                def _():
                    start(stash(half, n, True))

            if linked:
                for i in range(2):
                    todo = after[2 * i + half]
                    if todo:

                        @pl.when(b == i)
                        def _():
                            for step, of in todo:
                                steps[step - 1](of)
            else:
                whole = zip(sums, (r.f_fc1, r.f_fc2) if half else (r.f_qkv, r.f_proj))
                copies = [pltpu.make_async_copy(g, o.at[b], r.go_sem.at[half, i]) for i, (g, o) in enumerate(whole)]
                start(copies)
                wait(copies)

    if linked:
        step_1(0)
        step_3(1)
        step_2(0)
        step_4(1)
        smalls_sent(1)
        step_5(1)
        step_3(0)
        step_4(0)
        step_5(0)
        reductions_done()
        weights_sent()
        for k in range(1, 8):
            pack_copy(k).wait_send()
    for k in range(1, 4):
        for n in range(canvases):
            arrived(k, n)
    for n in range(canvases):
        pushed(n)


def compute(linked, operands):
    canvases = operands["x_hbm"].shape[1]
    shape = jax.ShapeDtypeStruct
    hbm = pl.BlockSpec(memory_space=pl.ANY)
    vmem = pl.BlockSpec(memory_space=pltpu.VMEM)
    dma = pltpu.SemaphoreType.DMA
    full = {
        "wat": ((2, D, 4 * D), BF),
        "fc1": ((2, D, FF), BF),
        "fc2": ((2, FF, D), BF),
        "vec": ((2, 8, FF), F32),
    }
    grads = {
        "g_qkv": ((D, 3 * D), F32),
        "g_proj": ((D, D), F32),
        "g_fc1": ((D, FF), F32),
        "g_fc2": ((FF, D), F32),
        "g_vec": ((2, 8, 8, FF), F32),
        "g_tab": ((2, 2 * PLACES, GROUPS * 128), F32),
    }
    outs = {"act_hbm": ((4, canvases, CELLS, D), BF), "igrad_hbm": ((4, canvases, CELLS, D), BF)}
    kept = {
        "hqw": ((canvases, WROWS, D), BF),
        "qkv": ((canvases, WROWS, 3 * D), BF),
        "probs": ((canvases, WINDOWS * GROUPS, 128, 128), BF),
        "att": ((canvases, WROWS, D), BF),
        "hq2": ((canvases, CELLS, D), BF),
        "hid": ((canvases, CELLS, FF), BF),
        "dgelu": ((canvases, CELLS, FF), BF),
    }
    outs |= {"h_" + name: kind for name, kind in kept.items()}
    scratch = kept | {
        "code": ((canvases, CELLS, 128), jnp.int32),
        "codew": ((WROWS, 128), jnp.int32),
        "buf": ((6, canvases, CELLS, D), BF),
        "canvf": ((CELLS, D), F32),
        "winf": ((WROWS, D), F32),
        "gzw": ((WROWS, D), BF),
        "go": ((WROWS, D), BF),
        "gqkv": ((WROWS, 3 * D), BF),
    }
    sems = {
        "in_sem": (2, canvases),
        "code_sem": (1,),
        "st_sem": (2, canvases, 4),
        "local_sem": (2, canvases),
        "act_send": (3, canvases),
        "act_recv": (3, canvases),
        "ig_send": (3, canvases),
        "ig_recv": (3, canvases),
    }
    if linked:
        outs |= {
            "o_qkv": ((2, 48, 3 * D), F32),
            "o_proj": ((2, 48, D), F32),
            "o_fc1": ((2, 48, FF), F32),
            "o_fc2": ((2, 192, D), F32),
            "o_small": ((2, 8, 64, D), BF),
        }
        scratch |= full | grads
        scratch |= {
            "packs": ((8, 16, 256), BF),
            "l_qkv": ((48, 3 * D), F32),
            "l_proj": ((48, D), F32),
            "l_fc1": ((48, FF), F32),
            "l_fc2": ((192, D), F32),
        }
        for kind, rows in (("m_", MLP_ROWS), ("a_", ATT_ROWS)):
            scratch |= {
                kind + "st_a": ((4, rows, D), BF),
                kind + "rc_a": ((4, rows, D), BF),
                kind + "st_b": ((3, rows, D), BF),
                kind + "rc_b": ((3, rows, D), BF),
                kind + "st_c": ((rows, D), BF),
                kind + "rc_c": ((3, rows // 4, D), BF),
                kind + "fin": ((rows, D), BF),
            }
        sems |= {
            "sh_sem": (4, 2),
            "os_sem": (2,),
            "go_sem": (4, 2),
            "wz_send": (4, 2, 3),
            "wz_recv": (4, 2, 3),
            "wx_send": (4, 2, 3, 3),
            "wx_recv": (4, 2, 3, 3),
            "ws_send": (4, 2, 4),
            "ws_recv": (4, 2, 4),
            "pk_send": (7,),
            "pk_recv": (7,),
            "ra_send": (4,),
            "ra_recv": (4,),
            "rb_send": (4, 3),
            "rb_recv": (4, 3),
            "rc_send": (4, 3),
            "rc_recv": (4, 3),
            "rf_send": (4, 3),
            "rf_recv": (4, 3),
            "rs_send": (2, 7),
            "rs_recv": (2, 7),
        }
    else:
        for name in ("g_vec", "g_tab"):
            outs[name] = grads.pop(name)
        outs |= {name.replace("g_", "f_"): ((2,) + dims, F32) for name, (dims, _) in grads.items()}
        scratch |= grads
        sems["go_sem"] = (4, 2)
    in_vmem = set(full) | {"bias", "pack", "g_vec", "g_tab"}
    names = tuple(operands) + tuple(outs) + tuple(scratch) + tuple(sems)
    results = pl.pallas_call(
        functools.partial(kernel, names, linked, canvases),
        out_shape=tuple(shape(*o) for o in outs.values()),
        in_specs=[vmem if name in in_vmem else hbm for name in operands],
        out_specs=tuple(vmem if name in in_vmem else hbm for name in outs),
        scratch_shapes=[pltpu.VMEM(*v) for v in scratch.values()] + [dma(v) for v in sems.values()],
        compiler_params=pltpu.CompilerParams(
            vmem_limit_bytes=64 * 1024 * 1024 - 65536, collective_id=0, has_side_effects=True
        ),
    )(*operands.values())
    return dict(zip(outs, results))


def place_pairs():
    place = np.arange(PLACES)
    r, c = place // 8, place % 8
    index = (r[None, :] - r[:, None] + WIN - 1) * (2 * WIN - 1) + c[None, :] - c[:, None] + WIN - 1
    real = (r < WIN) & (c < WIN)
    return index, real[:, None] & real[None, :], real


def pair_onehot():
    index, both, _ = place_pairs()
    table = (2 * WIN - 1) ** 2
    hot = (np.where(both, index, -1).reshape(-1)[None, :] == np.arange(table)[:, None])
    return hot.astype(np.float32)


def body(
    inputs,
    cotangent,
    pad_mask,
    region_ids,
    norm1_gain,
    norm1_bias,
    qkv_weight,
    qv_bias,
    rel_table,
    proj_weight,
    proj_bias,
    norm2_gain,
    norm2_bias,
    fc1_weight,
    fc1_bias,
    fc2_weight,
    fc2_bias,
):
    owners = lax.axis_size("dp")
    linked = owners == 8
    mine = lax.axis_index("pipe")

    def own(a):
        return lax.dynamic_index_in_dim(a, mine, 0, keepdims=False)

    code = own(region_ids) * 2 + own(pad_mask)
    code = jnp.broadcast_to(code[:, :, None], code.shape + (128,))

    hot = pair_onehot()
    _, _, real = place_pairs()
    rel = lax.dot_general(
        rel_table.astype(BF), jnp.asarray(hot, BF), (((1,), (0,)), ((), ())), preferred_element_type=F32
    )
    rel = rel.reshape(2, GROUPS, 2, 2, PLACES, PLACES)
    rel = jnp.where(jnp.asarray(real)[None, None, None, None, :, None], rel, MASKED)
    rel = rel.transpose(0, 1, 3, 4, 2, 5).reshape(2, GROUPS, 128, 128)

    operands = {"x_hbm": inputs, "cot_hbm": cotangent, "code_hbm": code, "bias": rel}
    vectors = (norm1_gain, norm1_bias, proj_bias, norm2_gain, norm2_bias, fc2_bias, qv_bias, fc1_bias)
    sizes = [v.shape[1] for v in vectors]
    ends = np.cumsum([0] + sizes)
    if linked:
        pack = jnp.stack([jnp.pad(v, ((0, 0), (0, 256 - v.shape[1]))) for v in vectors], axis=1)
        operands |= {
            "pack": pack.reshape(16, 256).astype(BF),
            "s_qkv": qkv_weight,
            "s_proj": proj_weight,
            "s_fc1": fc1_weight,
            "s_fc2": fc2_weight,
        }
    else:

        def gathered(a):
            return lax.all_gather(a.astype(BF), "dp", axis=1, tiled=True)

        packed = lax.all_gather(jnp.concatenate(vectors, axis=1).astype(BF), "dp", axis=1)
        parts = [packed[:, :, a:b].reshape(2, -1).astype(F32) for a, b in zip(ends[:-1], ends[1:])]
        qv = parts[6]
        parts[6] = jnp.concatenate([qv[:, :D], jnp.zeros_like(qv[:, :D]), qv[:, D:]], axis=1)
        vec = jnp.stack([jnp.pad(p, ((0, 0), (0, FF - p.shape[1]))) for p in parts], axis=1)
        operands |= {
            "wat": jnp.concatenate([gathered(qkv_weight), gathered(proj_weight)], axis=2),
            "fc1": gathered(fc1_weight),
            "fc2": gathered(fc2_weight),
            "vec": vec,
        }

    out = compute(linked, operands)

    def to_owners(g):
        shared = lax.psum_scatter(g, "dp", scatter_dimension=1, tiled=True)
        return lax.psum(shared, "pipe")

    if linked:
        small = out["o_small"]
        g_tab = small[:, :, :16].reshape(2, 128, GROUPS * 128)
        g_vec = jnp.concatenate([small[:, :, 16 + 8 * j : 24 + 8 * j] for j in range(4)], axis=3)
    else:
        g_tab, g_vec = out["g_tab"], out["g_vec"]

    g_vec = jnp.sum(g_vec.astype(F32), axis=2)
    kinds = [g_vec[:, i] for i in range(8)]
    qv_sum = jnp.concatenate([kinds[6][:, :D], kinds[6][:, 2 * D : 3 * D]], axis=1)
    rows = [kinds[0], kinds[1], kinds[2], kinds[3], kinds[4], kinds[5], qv_sum, kinds[7]]
    if linked:
        at = lax.axis_index("dp")
        small = [lax.dynamic_slice_in_dim(v, at * n, n, 1) for v, n in zip(rows, sizes)]
    else:
        rows = [v[:, : n * owners].reshape(2, -1, n) for v, n in zip(rows, sizes)]
        g_small = to_owners(jnp.concatenate(rows, axis=2))[:, 0]
        small = [g_small[:, a:b] for a, b in zip(ends[:-1], ends[1:])]

    pairs = g_tab.reshape(2, 2, PLACES, GROUPS, 2, PLACES).transpose(0, 3, 4, 1, 2, 5)
    pairs = pairs.reshape(2, HEADS, PLACES * PLACES)
    g_table = lax.dot_general(
        jnp.broadcast_to(jnp.asarray(hot, pairs.dtype), (2,) + hot.shape),
        pairs,
        (((2,), (2,)), ((0,), (0,))),
        precision=None if linked else lax.Precision.HIGHEST,
        preferred_element_type=F32,
    )
    if linked:
        big = [out[name] for name in ("o_qkv", "o_proj", "o_fc1", "o_fc2")]
    else:
        g_table = lax.psum(g_table, ("pipe", "dp"))
        big = [to_owners(out[name]) for name in ("f_qkv", "f_proj", "f_fc1", "f_fc2")]

    return (
        out["act_hbm"][None],
        out["igrad_hbm"][None],
        small[0],
        small[1],
        big[0],
        small[6],
        g_table,
        big[1],
        small[2],
        small[3],
        small[4],
        big[2],
        small[7],
        big[3],
        small[5],
    )


def solution(mesh):
    cols = P(None, "dp")
    rows = P(None, "dp", None)
    return jax.shard_map(
        body,
        mesh=mesh,
        in_specs=(
            P(None, "dp", None, None),
            P(None, "dp", None, None),
            rows,
            rows,
            cols,
            cols,
            rows,
            cols,
            P(),
            rows,
            cols,
            cols,
            cols,
            rows,
            cols,
            rows,
            cols,
        ),
        out_specs=(
            P("pipe", None, "dp", None, None),
            P("pipe", None, "dp", None, None),
            cols,
            cols,
            rows,
            cols,
            P(),
            rows,
            cols,
            cols,
            cols,
            rows,
            cols,
            rows,
            cols,
        ),
        check_vma=False,
    )
```

```python
import functools
import types

import jax
import jax.numpy as jnp
import numpy as np
from jax import lax
from jax.experimental import pallas as pl
from jax.experimental.pallas import tpu as pltpu
from jax.sharding import PartitionSpec as P

HEADS = 12
WIN = 7
SHIFT = 3
GRID = 28
CELLS = 784
D = 384
FF = 1536
HEAD = 32
SIDE = 4
WINDOWS = 16
PLACES = 64
WROWS = WINDOWS * PLACES
GROUPS = 3
TILE = 112
SCALE = HEAD**-0.5
NORM_EPS = 1e-05
MASKED = -1e30
BF = jnp.bfloat16
F32 = jnp.float32

RSQRT_2 = 1.0 / np.sqrt(2.0)
PHI_0 = 1.0 / np.sqrt(2.0 * np.pi)


def nn(a, b):
    return lax.dot_general(a, b, (((1,), (0,)), ((), ())), preferred_element_type=F32)


def nt(a, b):
    return lax.dot_general(a, b, (((1,), (1,)), ((), ())), preferred_element_type=F32)


def tn(a, b):
    return lax.dot_general(a, b, (((0,), (0,)), ((), ())), preferred_element_type=F32)


def segments(shift):
    runs = []
    for wr in range(SIDE):
        for r in range(WIN):
            row = (wr * WIN + r + shift) % GRID
            for wc in range(SIDE):
                col = (wc * WIN + shift) % GRID
                place = (wr * SIDE + wc) * PLACES + r * 8
                first = min(WIN, GRID - col)
                runs.append((row * GRID + col, place, first))
                if first < WIN:
                    runs.append((row * GRID, place + first, WIN - first))
    return runs


def to_windows(src, dst, shift):
    for cell, place, count in segments(shift):
        dst[pl.ds(place, count), :] = src[pl.ds(cell, count), :]


def to_canvas(src, dst, shift):
    for cell, place, count in segments(shift):
        dst[pl.ds(cell, count), :] = src[pl.ds(place, count), :]


def row_block(t, size):
    return pl.ds(pl.multiple_of(t * size, 16), size)


def standardized(v):
    centered = v - jnp.mean(v, axis=-1, keepdims=True)
    spread = jnp.mean(centered * centered, axis=-1, keepdims=True)
    rs = lax.rsqrt(spread + NORM_EPS)
    return centered * rs, rs


def by_eights(v):
    return jnp.sum(v.reshape(v.shape[0] // 8, 8, v.shape[1]), axis=0)


def gelu_parts(x):
    cdf = 0.5 + 0.5 * lax.erf(x * RSQRT_2)
    return x * cdf, cdf + x * (jnp.exp(-0.5 * x * x) * PHI_0)


def real_places(rows):
    place = lax.broadcasted_iota(jnp.int32, (rows, 1), 0)
    return ((place & 7) < WIN) & (((place >> 3) & 7) < WIN)


def head_of_lane():
    return lax.broadcasted_iota(jnp.int32, (PLACES, 128), 1) >> 5


def by_low(x, lanes):
    zero = jnp.zeros_like(x)
    return jnp.concatenate([jnp.where((lanes & 1) == h, x, zero) for h in range(2)], axis=0)


def by_high(x, lanes):
    zero = jnp.zeros_like(x)
    return jnp.concatenate([jnp.where((lanes >> 1) == h, x, zero) for h in range(2)], axis=0)


def own_low(wide, lanes):
    return jnp.where((lanes & 1) == 0, wide[:PLACES], wide[PLACES:])


def own_high(wide, lanes):
    return jnp.where((lanes >> 1) == 0, wide[:PLACES], wide[PLACES:])


MESH = pl.DeviceIdType.MESH
KINDS = ("a", "m", "a", "m", "t", "t")
ROWS = {"a": 192, "m": 384, "t": 64}
BLOCK = (0, 0, 1, 1, 0, 1)
BEFORE = {0: 2, 1: 3, 4: 5}


def kernel(names, linked, canvases, *refs):
    r = types.SimpleNamespace(**dict(zip(names, refs)))
    me = lax.axis_index("pipe")
    code, codew, buf = r.code, r.codew, r.buf
    hqw, qkv, probs, att = r.hqw, r.qkv, r.probs, r.att
    hq2, hid, dgelu = r.hq2, r.hid, r.dgelu
    canvf, winf, gzw, gqkv, go = r.canvf, r.winf, r.gzw, r.gqkv, r.go
    g_qkv, g_proj, g_fc1, g_fc2, g_vec, g_tab = r.g_qkv, r.g_proj, r.g_fc1, r.g_fc2, r.g_vec, r.g_tab
    wat, fc1, fc2, vec, bias = r.wat, r.fc1, r.fc2, r.vec, r.bias
    if linked:
        d = lax.axis_index("dp")
        z, c = d // 2, d % 2
        sibling = {"dp": 2 * z + 1 - c}

    def z_peer(k):
        return {"dp": 2 * lax.rem(z + k, 4) + c}

    def pipe_peer(k):
        return {"pipe": lax.rem(me + k, 4)}

    def dp_peer(k):
        return {"dp": lax.rem(d + k, 8)}

    def remote(src, dst, send, recv, device):
        return pltpu.make_async_remote_copy(
            src_ref=src, dst_ref=dst, send_sem=send, recv_sem=recv, device_id=device, device_id_type=MESH
        )

    barrier = pltpu.get_barrier_semaphore()
    partners = [pipe_peer(k) for k in range(1, 4)]
    if linked:
        partners += [dp_peer(k) for k in range(1, 8)]
    for partner in partners:
        pl.semaphore_signal(barrier, inc=1, device_id=partner, device_id_type=MESH)

    full = ((wat,), (fc1, fc2), (wat,), (fc1, fc2))

    def owner_back(k):
        return 2 * lax.rem(z + 4 - k, 4) + c

    def shard(sec, a, owner):
        h = 192 if a else 48
        return full[sec][a].at[sec // 2, pl.ds(pl.multiple_of(owner * h, 16), h), :]

    def part(sec, a, owner, place):
        if a:
            return fc2.at[sec // 2, pl.ds(pl.multiple_of(owner * 192 + place * 48, 16), 48), :]
        rows = pl.ds(pl.multiple_of(owner * 48, 16), 48)
        return full[sec][0].at[sec // 2, rows, pl.ds(pl.multiple_of(place * D, 128), D)]

    def to_z(sec, a, k):
        own = part(sec, a, d, me)
        return remote(own, own, r.wz_send.at[sec, a, k - 1], r.wz_recv.at[sec, a, k - 1], z_peer(k))

    def to_places(sec, a, k, j):
        got = part(sec, a, owner_back(k), me)
        return remote(
            got, got, r.wx_send.at[sec, a, k - 1, j - 1], r.wx_recv.at[sec, a, k - 1, j - 1], pipe_peer(j)
        )

    def to_sibling(sec, a, k):
        block = shard(sec, a, owner_back(k))
        return remote(block, block, r.ws_send.at[sec, a, k], r.ws_recv.at[sec, a, k], sibling)

    def weights_1(sec):
        for a in range(len(full[sec])):
            for k in range(1, 4):
                to_z(sec, a, k).start()
            to_sibling(sec, a, 0).start()

    def weights_2(sec):
        for k in range(1, 4):
            for a in range(len(full[sec])):
                got = part(sec, a, owner_back(k), me)
                remote(got, got, r.wz_send.at[sec, a, k - 1], r.wz_recv.at[sec, a, k - 1], z_peer(k)).wait_recv()
                for j in range(1, 4):
                    to_places(sec, a, k, j).start()

    def weights_3(sec):
        for k in range(1, 4):
            for a in range(len(full[sec])):
                for j in range(1, 4):
                    got = part(sec, a, owner_back(k), lax.rem(me + 4 - j, 4))
                    remote(
                        got, got, r.wx_send.at[sec, a, k - 1, j - 1], r.wx_recv.at[sec, a, k - 1, j - 1], pipe_peer(j)
                    ).wait_recv()
                to_sibling(sec, a, k).start()

    def weights_4(sec):
        for k in range(4):
            for a in range(len(full[sec])):
                block = shard(sec, a, 2 * lax.rem(z + 4 - k, 4) + 1 - c)
                remote(block, block, r.ws_send.at[sec, a, k], r.ws_recv.at[sec, a, k], sibling).wait_recv()

    def weights_sent():
        for sec in range(4):
            for a in range(len(full[sec])):
                for k in range(4):
                    to_sibling(sec, a, k).wait_send()
                    if k:
                        to_z(sec, a, k).wait_send()
                        for j in range(1, 4):
                            to_places(sec, a, k, j).wait_send()

    def pack_copy(k):
        return remote(
            r.packs.at[d], r.packs.at[d], r.pk_send.at[k - 1], r.pk_recv.at[k - 1], dp_peer(k)
        )

    def pack_arrival(k):
        slot = r.packs.at[lax.rem(d + 8 - k, 8)]
        return remote(slot, slot, r.pk_send.at[k - 1], r.pk_recv.at[k - 1], dp_peer(k))

    def place_vectors():
        kind = lax.broadcasted_iota(jnp.int32, (16, 256), 0) & 7
        lane = lax.broadcasted_iota(jnp.int32, (16, 256), 1)
        vec[...] = jnp.zeros_like(vec)
        for width, kinds in ((48, kind < 6), (96, kind == 6), (192, kind == 7)):
            for owner in range(8):
                at = owner * width
                if width == 96 and owner >= 4:
                    at += D
                start = at // 128 * 128
                part = jnp.where(kinds & (lane < width), r.packs[owner].astype(F32), 0.0)
                if at > start:
                    part = pltpu.roll(part, at - start, 1)
                for b in range(2):
                    vec[b, :, start : start + 256] += part[8 * b : 8 * b + 8]

    def pieces(sec, owner):
        b = BLOCK[sec]
        out = []

        def matrix(ref, h):
            for t in range(h // 48):
                rows = pl.ds(pl.multiple_of(owner * h + t * 48, 16), 48)
                for j in range(ref.shape[1] // D):
                    load = functools.partial(lambda ref, rows, j: ref[rows, j * D : (j + 1) * D], ref, rows, j)
                    out.append((len(out) * 48, 48, load))

        def small():
            parts = [g_tab[b, pl.ds(pl.multiple_of(owner * 16, 16), 16), :]]
            parts += [g_vec[b, owner, :, j * D : (j + 1) * D] for j in range(4)]
            return jnp.concatenate(parts + [jnp.zeros((16, D), F32)], axis=0)

        if KINDS[sec] == "m":
            matrix(g_fc1, 48)
            matrix(g_fc2, 192)
        elif KINDS[sec] == "a":
            matrix(g_qkv, 48)
            matrix(g_proj, 48)
        else:
            out.append((0, 64, small))
        return out

    def reduce_refs(sec):
        kind = KINDS[sec]
        return types.SimpleNamespace(
            **{n: getattr(r, kind + "_" + n) for n in ("st_a", "rc_a", "st_b", "rc_b", "st_c", "rc_c", "fin")}
        )

    def step_1(sec):
        q = reduce_refs(sec)
        if sec in BEFORE:
            copy_a(BEFORE[sec]).wait_send()
            for k in range(1, 4):
                copy_b(BEFORE[sec], k).wait_send()
                copy_c(BEFORE[sec], k).wait_send()
        for k in range(4):
            i = lax.rem(z + k, 4)
            kept = q.st_b.at[k - 1] if k else q.st_c
            for row, rows, load in pieces(sec, 2 * i + 1 - c):
                q.st_a[i, row : row + rows, :] = load().astype(BF)
            for row, rows, load in pieces(sec, 2 * i + c):
                kept[row : row + rows, :] = load().astype(BF)
        copy_a(sec).start()

    def copy_a(sec):
        q = reduce_refs(sec)
        return remote(q.st_a, q.rc_a, r.ra_send.at[sec], r.ra_recv.at[sec], sibling)

    def copy_b(sec, k):
        q = reduce_refs(sec)
        return remote(
            q.st_b.at[k - 1], q.rc_b.at[k - 1], r.rb_send.at[sec, k - 1], r.rb_recv.at[sec, k - 1], z_peer(k)
        )

    def step_2(sec):
        q = reduce_refs(sec)
        copy_a(sec).wait_recv()
        for k in (1, 2, 3, 0):
            i = lax.rem(z + k, 4)
            kept = q.st_b.at[k - 1] if k else q.st_c
            for row in range(0, kept.shape[0], 64):
                at = slice(row, row + 64)
                kept[at, :] = (kept[at, :].astype(F32) + q.rc_a[i, at, :].astype(F32)).astype(BF)
            if k:
                copy_b(sec, k).start()

    def quarter(sec, ref, who):
        rows = ROWS[KINDS[sec]] // 4
        return ref.at[pl.ds(pl.multiple_of(who * rows, 16), rows), :]

    def copy_c(sec, k):
        q = reduce_refs(sec)
        return remote(
            quarter(sec, q.st_c, lax.rem(me + k, 4)),
            q.rc_c.at[k - 1],
            r.rc_send.at[sec, k - 1],
            r.rc_recv.at[sec, k - 1],
            pipe_peer(k),
        )

    def step_3(sec):
        q = reduce_refs(sec)
        for k in range(1, 4):
            copy_b(sec, k).wait_recv()
        for row in range(0, q.st_c.shape[0], 64):
            at = slice(row, row + 64)
            total = q.st_c[at, :].astype(F32)
            for k in range(3):
                total = total + q.rc_b[k, at, :].astype(F32)
            q.st_c[at, :] = total.astype(BF)
        for k in range(1, 4):
            copy_c(sec, k).start()

    def copy_f(sec, k):
        q = reduce_refs(sec)
        own = quarter(sec, q.fin, me)
        return remote(own, own, r.rf_send.at[sec, k - 1], r.rf_recv.at[sec, k - 1], pipe_peer(k))

    def step_4(sec):
        q = reduce_refs(sec)
        for k in range(1, 4):
            copy_c(sec, k).wait_recv()
            if sec in BEFORE:
                copy_f(BEFORE[sec], k).wait_send()
        total = quarter(sec, q.st_c, me)[...].astype(F32)
        for k in range(3):
            total = total + q.rc_c[k].astype(F32)
        quarter(sec, q.fin, me)[...] = total.astype(BF)
        for k in range(1, 4):
            copy_f(sec, k).start()

    def copy_s(b, k):
        return remote(r.t_fin, r.o_small.at[b, d], r.rs_send.at[b, k - 1], r.rs_recv.at[b, k - 1], dp_peer(k))

    def own_small(b):
        return pltpu.make_async_copy(r.t_fin, r.o_small.at[b, d], r.os_sem.at[b])

    def outputs(sec):
        pairs = ((r.l_fc1, r.o_fc1), (r.l_fc2, r.o_fc2)) if sec % 2 else ((r.l_qkv, r.o_qkv), (r.l_proj, r.o_proj))
        return [
            pltpu.make_async_copy(ref, out.at[sec // 2], r.go_sem.at[sec, i]) for i, (ref, out) in enumerate(pairs)
        ]

    def step_5(sec):
        q = reduce_refs(sec)
        for k in range(1, 4):
            got = quarter(sec, q.fin, lax.rem(me + 4 - k, 4))
            remote(got, got, r.rf_send.at[sec, k - 1], r.rf_recv.at[sec, k - 1], pipe_peer(k)).wait_recv()
        if sec >= 4:
            for k in range(1, 8):
                copy_s(BLOCK[sec], k).start()
            own_small(BLOCK[sec]).start()
            return
        if sec < 2:
            for out in outputs(sec + 2):
                out.wait()
        row = 0
        for ref in (r.l_fc1, r.l_fc2) if sec % 2 else (r.l_qkv, r.l_proj):
            for t in range(ref.shape[0] // 48):
                for j in range(ref.shape[1] // D):
                    ref[t * 48 : (t + 1) * 48, j * D : (j + 1) * D] = q.fin[row : row + 48, :].astype(F32)
                    row += 48
        for out in outputs(sec):
            out.start()

    def smalls_sent(b):
        for k in range(1, 8):
            copy_s(b, k).wait_send()
        own_small(b).wait()

    def reductions_done():
        for sec in BEFORE:
            copy_a(sec).wait_send()
            for k in range(1, 4):
                copy_b(sec, k).wait_send()
                copy_c(sec, k).wait_send()
                copy_f(sec, k).wait_send()
        for sec in range(2):
            for out in outputs(sec):
                out.wait()
        smalls_sent(0)
        for b in range(2):
            for k in range(1, 8):
                remote(
                    r.t_fin,
                    r.o_small.at[b, lax.rem(d + 8 - k, 8)],
                    r.rs_send.at[b, k - 1],
                    r.rs_recv.at[b, k - 1],
                    dp_peer(k),
                ).wait_recv()

    if linked:
        lands = ((r.s_qkv, g_qkv, wat, 0), (r.s_proj, g_proj, wat, 3 * D), (r.s_fc1, g_fc1, fc1, 0), (r.s_fc2, g_fc2, fc2, 0))

        def landing(i, b):
            src, dst, _, _ = lands[i]
            h, n = src.shape[1:]
            return pltpu.make_async_copy(
                src.at[b], dst.at[pl.ds(192 * b, h), pl.ds(0, n)], r.sh_sem.at[i, b]
            )

        for i in range(4):
            for b in range(2):
                landing(i, b).start()
        r.packs[d] = r.pack[...]
        for i, (src, dst, ref, col) in enumerate(lands):
            h, n = src.shape[1:]
            for b in range(2):
                landing(i, b).wait()
                for t in range(0, h, 48):
                    rows = pl.ds(pl.multiple_of(d * h + t, 16), 48)
                    ref[b, rows, col : col + n] = dst[192 * b + t : 192 * b + t + 48, :n].astype(BF)
    pl.semaphore_wait(barrier, len(partners))
    if linked:
        for k in range(1, 8):
            pack_copy(k).start()
        weights_1(0)

    def cleared(*refs):
        for ref in refs:

            @pl.loop(0, ref.shape[0] // 16)
            def _(i):
                ref[row_block(i, 16), :] = jnp.zeros((16, ref.shape[1]), F32)

    g_vec[...] = jnp.zeros_like(g_vec)
    g_tab[...] = jnp.zeros_like(g_tab)
    codew[...] = jnp.zeros_like(codew)

    if linked:
        weights_2(0)
        for sec in range(1, 4):
            weights_1(sec)
        for k in range(1, 8):
            pack_arrival(k).wait_recv()
        place_vectors()

    def vector(b, kind, width=D):
        return vec[b, kind : kind + 1, :width]

    def add_vec(b, kind, part):
        g_vec[b, kind, :, : part.shape[1]] += part

    def windowed(rows, count):
        return jnp.where(real_places(count), winf[rows, :], 0.0).astype(BF)

    def by_block(b, move):
        for i in range(2):

            @pl.when(b == i)
            def _():
                move(SHIFT * i)

    def attention_forward(b, n, x, out, hook):
        lanes = head_of_lane()

        @pl.loop(0, CELLS // TILE)
        def _(t):
            rows = row_block(t, TILE)
            xhat, _ = standardized(x[rows, :].astype(F32))
            canvf[rows, :] = xhat * vector(b, 0) + vector(b, 1)

        def arrange(shift):
            to_windows(canvf, winf, shift)
            to_windows(code.at[n], codew, shift)

        by_block(b, arrange)
        hook(4)

        @pl.loop(0, 4)
        def _(t):
            rows = row_block(t, 256)
            hq = windowed(rows, 256)
            hqw[n, rows, :] = hq
            for part in range(3):
                cols = slice(part * D, (part + 1) * D)
                acc = nn(hq, wat[b, :, cols]) + vec[b, 6:7, cols]
                if part == 0:
                    acc = acc * SCALE
                qkv[n, rows, cols] = acc.astype(BF)

        hook(0)

        @pl.loop(0, WINDOWS)
        def _(w):
            rows = row_block(w, PLACES)
            cells = codew[rows, :]
            region = (cells >> 1) * b
            pad = (cells & 1).astype(F32)
            lane = lax.broadcasted_iota(jnp.int32, (PLACES, 128), 1)
            same = jnp.where(lane == region, 1.0, 0.0)
            left = jnp.where(lane == 127, 1.0 - pad, same).astype(BF)
            right = jnp.where(lane == 127, -pad, same).astype(BF)
            agree = nt(left, jnp.concatenate([right, right], axis=0))
            mask = jnp.where(agree > 0.5, 0.0, MASKED)
            for g in range(GROUPS):
                q = qkv[n, rows, g * 128 : (g + 1) * 128]
                k = qkv[n, rows, D + g * 128 : D + (g + 1) * 128]
                v = qkv[n, rows, 2 * D + g * 128 : 2 * D + (g + 1) * 128]
                scores = nt(by_low(k, lanes), by_high(q, lanes)) + bias[b, g]
                halves = []
                for h in range(2):
                    s = scores[h * PLACES : (h + 1) * PLACES] + mask
                    e = jnp.exp(s - jnp.max(s, axis=0, keepdims=True))
                    halves.append((e * (1.0 / jnp.sum(e, axis=0, keepdims=True))).astype(BF))
                p = jnp.concatenate(halves, axis=0)
                probs[n, w * GROUPS + g] = p
                att[n, rows, g * 128 : (g + 1) * 128] = own_high(tn(p, by_low(v, lanes)), lanes).astype(BF)

        hook(1)

        @pl.loop(0, 4)
        def _(t):
            rows = row_block(t, 256)
            winf[rows, :] = nn(att[n, rows, :], wat[b, :, 3 * D :])

        by_block(b, functools.partial(to_canvas, winf, canvf))

        @pl.loop(0, CELLS // TILE)
        def _(t):
            rows = row_block(t, TILE)
            out[rows, :] = (x[rows, :].astype(F32) + (canvf[rows, :] + vector(b, 2))).astype(BF)

    def mlp_forward(b, n, x, out, hook):
        @pl.loop(0, CELLS // TILE)
        def _(t):
            rows = row_block(t, TILE)
            xhat, _ = standardized(x[rows, :].astype(F32))
            hq2[n, rows, :] = (xhat * vector(b, 3) + vector(b, 4)).astype(BF)

        @pl.loop(0, FF // 256)
        def _(i):
            cols = pl.ds(pl.multiple_of(i * 256, 256), 256)
            pre = nn(hq2[n], fc1[b, :, cols]) + vec[b, 7:8, cols]
            for at in range(0, CELLS, 16):
                h, dg = gelu_parts(pre[at : at + 16])
                hid[n, at : at + 16, cols] = h.astype(BF)
                dgelu[n, at : at + 16, cols] = dg.astype(BF)

        hook(0)
        total = nn(hid[n], fc2[b])
        for at in range(0, CELLS, TILE):
            rows = slice(at, at + TILE)
            out[rows, :] = (x[rows, :].astype(F32) + (total[rows] + vector(b, 5))).astype(BF)

    def norm_backward(b, kind, x, gz, out):
        @pl.loop(0, CELLS // TILE)
        def _(t):
            rows = row_block(t, TILE)
            xhat, rs = standardized(x[rows, :].astype(F32))
            gn = canvf[rows, :]
            gzf = gz[rows, :].astype(F32)
            add_vec(b, kind, by_eights(gn * xhat))
            add_vec(b, kind + 1, by_eights(gn))
            add_vec(b, 5 if kind else 2, by_eights(gzf))
            g = gn * vector(b, kind)
            mg = jnp.mean(g, axis=-1, keepdims=True)
            mgx = jnp.mean(g * xhat, axis=-1, keepdims=True)
            out[rows, :] = (gzf + rs * (g - mg - xhat * mgx)).astype(BF)

    def mlp_backward(b, n, x, gz, out, free_out, hook):
        @pl.loop(0, FF // 256)
        def _(i):
            cols = pl.ds(pl.multiple_of(i * 256, 256), 256)
            gh = nt(gz[...], fc2[b, cols, :])
            sums = jnp.zeros((8, 256), F32)
            for at in range(0, CELLS, 16):
                gp = (gh[at : at + 16] * dgelu[n, at : at + 16, cols].astype(F32)).astype(BF)
                dgelu[n, at : at + 16, cols] = gp
                sums = sums + by_eights(gp.astype(F32))
            g_vec[b, 7, :, cols] += sums
            g_fc1[:, cols] += tn(hq2[n], dgelu[n, :, cols])
            g_fc2[cols, :] += tn(hid[n, :, cols], gz[...])

        hook(0)
        canvf[...] = nt(dgelu[n], fc1[b])
        free_out()
        norm_backward(b, 3, x, gz, out)

    def attention_backward(b, n, x, gz, out, free_out, hook):
        lanes = head_of_lane()

        @pl.loop(0, CELLS // TILE)
        def _(t):
            rows = row_block(t, TILE)
            canvf[rows, :] = gz[rows, :].astype(F32)

        by_block(b, functools.partial(to_windows, canvf, winf))

        @pl.loop(0, 4)
        def _(t):
            rows = row_block(t, 256)
            gzw[rows, :] = windowed(rows, 256)

        g_proj[...] += tn(att[n], gzw[...])

        @pl.loop(0, 4)
        def _(t):
            rows = row_block(t, 256)
            go[rows, :] = nt(gzw[rows, :], wat[b, :, 3 * D :]).astype(BF)

        hook(0)

        @pl.loop(0, WINDOWS)
        def _(w):
            rows = row_block(w, PLACES)
            for g in range(GROUPS):
                at = [slice(part * D + g * 128, part * D + (g + 1) * 128) for part in range(3)]
                q, k, v = (qkv[n, rows, cols] for cols in at)
                go_wide = by_high(go[rows, at[0]], lanes)
                p_low = probs[n, w * GROUPS + g]
                p = p_low.astype(F32)
                pd = p * nt(by_low(v, lanes), go_wide)
                halves = []
                for h in range(2):
                    half = slice(h * PLACES, (h + 1) * PLACES)
                    halves.append((pd[half] - p[half] * jnp.sum(pd[half], axis=0, keepdims=True)).astype(BF))
                ds = jnp.concatenate(halves, axis=0)
                g_tab[b, :, g * 128 : (g + 1) * 128] += ds.astype(F32)
                gqkv[rows, at[0]] = (own_high(tn(ds, by_low(k, lanes)), lanes) * SCALE).astype(BF)
                gqkv[rows, at[1]] = own_low(nn(ds, by_high(q, lanes)), lanes).astype(BF)
                gqkv[rows, at[2]] = own_low(nn(p_low, go_wide), lanes).astype(BF)

        hook(1)
        attention_weights(n)
        hook(2)

        @pl.loop(0, 4)
        def _(t):
            rows = row_block(t, 256)
            gq = gqkv[rows, :]
            add_vec(b, 6, by_eights(gq.astype(F32)))
            winf[rows, :] = nt(gq, wat[b, :, : 3 * D])

        by_block(b, functools.partial(to_canvas, winf, canvf))
        free_out()
        norm_backward(b, 0, x, gz, out)

    def attention_weights(n):
        @pl.loop(0, 3)
        def _(part):
            cols = pl.ds(pl.multiple_of(part * D, 128), D)
            g_qkv[:, cols] += tn(hqw[n], gqkv[:, cols])

    def partner(k):
        x, y = me % 2, me // 2
        return 2 * (1 - y if k & 2 else y) + (1 - x if k & 1 else x)

    def away(kind, k, n):
        dst, send, recv = ((r.act_hbm, r.act_send, r.act_recv), (r.igrad_hbm, r.ig_send, r.ig_recv))[kind]
        return remote(
            buf.at[partner(k) + 1, n], dst.at[me, n], send.at[k - 1, n], recv.at[k - 1, n], {"pipe": partner(k)}
        )

    def at_home(kind, n):
        dst = (r.act_hbm, r.igrad_hbm)[kind]
        return pltpu.make_async_copy(buf.at[me + 1, n], dst.at[me, n], r.local_sem.at[kind, n])

    def send_acts(n):
        first = lax.axis_index("dp") % 2

        @pl.when(first == 0)
        def _():
            away(0, 1, n).start()
            away(0, 2, n).start()

        @pl.when(first == 1)
        def _():
            away(0, 2, n).start()
            away(0, 1, n).start()

        away(0, 3, n).start()
        at_home(0, n).start()

    def acts_sent(n):
        for k in (1, 2, 3):
            away(0, k, n).wait_send()
        at_home(0, n).wait()

    def push_row(row, n):
        @pl.when(me // 2 == row)
        def _():
            away(1, 1, n).start()
            at_home(1, n).start()

        @pl.when(me // 2 != row)
        def _():
            away(1, 2, n).start()
            away(1, 3, n).start()

    def pushed(n):
        for k in (1, 2, 3):
            away(1, k, n).wait_send()
        at_home(1, n).wait()

    def arrived(k, n):
        for dst, send, recv in ((r.act_hbm, r.act_send, r.act_recv), (r.igrad_hbm, r.ig_send, r.ig_recv)):
            got = dst.at[partner(k), n]
            remote(got, got, send.at[k - 1, n], recv.at[k - 1, n], {"pipe": partner(k)}).wait_recv()

    attention_stash = ((hqw, r.h_hqw), (qkv, r.h_qkv), (probs, r.h_probs), (att, r.h_att))
    mlp_stash = ((hq2, r.h_hq2), (hid, r.h_hid), (dgelu, r.h_dgelu))

    def stash(sec, n, back):
        pairs = mlp_stash if sec else attention_stash
        return [
            pltpu.make_async_copy(*((far.at[n], near.at[n]) if back else (near.at[n], far.at[n])), r.st_sem.at[sec, n, i])
            for i, (near, far) in enumerate(pairs)
        ]

    def load(i, n):
        src = r.cot_hbm if i else r.x_hbm
        return pltpu.make_async_copy(src.at[me, n], buf.at[5 if i else 0, n], r.in_sem.at[i, n])

    def start(copies):
        for copy in copies:
            copy.start()

    def wait(copies):
        for copy in copies:
            copy.wait()

    steps = (step_1, step_2, step_3, step_4, step_5)
    schedule = {
        (2, 0, 0): ((2, 3),),
        (2, 1, 1): ((3, 3),),
        (2, 1, 2): ((1, 2),),
        (1, 0, 0): ((2, 2), (2, 5)),
        (1, 1, 0): ((4, 3),),
        (0, 0, 0): ((3, 2), (3, 5), (2, 1), (5, 3)),
        (0, 0, 1): ((4, 2), (4, 5)),
        (0, 1, 0): ((5, 2), (5, 5)),
        (0, 1, 1): ((3, 1),),
        (0, 1, 2): ((1, 0),),
    }
    after = {3: ((1, 3),), 2: ((1, 5),), 1: ((1, 1),), 0: ()}
    weight_steps = (weights_1, weights_2, weights_3, weights_4) if linked else ()
    gathering = {
        (0, 4): ((3, 0), (4, 0)),
        (0, 0): ((2, 1),),
        (0, 1): ((2, 2), (2, 3), (3, 1)),
        (0, 3): ((4, 1), (3, 2)),
        (1, 3): ((4, 2),),
        (2, 0): ((3, 3),),
        (2, 3): ((4, 3),),
    }

    codes = [pltpu.make_async_copy(r.code_hbm, code, r.code_sem.at[0])]
    start(codes)
    start([load(i, n) for i in range(2) for n in range(canvases)])
    wait(codes)
    for i in range(2):
        wait([load(i, n) for n in range(canvases)])

    @pl.loop(0, canvases)
    def _(n):
        @pl.loop(0, 2)
        def _(b):
            def gather(half, i):
                for (sec, at), todo in gathering.items():
                    if linked and sec % 2 == half and at == i:

                        @pl.when((n == 0) & (b == sec // 2))
                        def _():
                            for step, of in todo:
                                weight_steps[step - 1](of)

            for half, forward in enumerate((attention_forward, mlp_forward)):

                @pl.when(b == 1)
                def _():
                    wait(stash(half, n, False))

                s = 2 * b + half
                forward(b, n, buf.at[s, n], buf.at[s + 1, n], functools.partial(gather, half))

                @pl.when(b == 0)
                def _():
                    start(stash(half, n, False))

                gather(half, 3)

        send_acts(n)

    @pl.loop(0, 2)
    def _(flipped):
        b = 1 - flipped
        for half, backward in ((1, mlp_backward), (0, attention_backward)):
            sums = ((g_fc1, g_fc2) if half else (g_qkv, g_proj))
            cleared(*sums)

            @pl.loop(0, canvases)
            def _(n):
                def hook(i):
                    for (sec, at, point), todo in schedule.items():
                        if linked and sec % 2 == half and point == i:

                            @pl.when((n == (canvases - 1 if at else 0)) & (b == sec // 2))
                            def _():
                                for step, of in todo:
                                    steps[step - 1](of)

                def free_out():
                    if half:

                        @pl.when(b == 1)
                        def _():
                            acts_sent(n)

                @pl.when(b == 0)
                def _():
                    wait(stash(half, n, True))

                s = 2 * b + half
                backward(b, n, buf.at[s, n], buf.at[s + 2, n], buf.at[s + 1, n], free_out, hook)
                if half == 0:

                    @pl.when(b == 1)
                    def _():
                        push_row(1, n)

                    @pl.when((b == 0) & (n < canvases - 1))
                    def _():
                        push_row(0, n)

                @pl.when(b == 1)
                def _():
                    start(stash(half, n, True))

            if linked:
                for i in range(2):
                    todo = after[2 * i + half]
                    if todo:

                        @pl.when(b == i)
                        def _():
                            for step, of in todo:
                                steps[step - 1](of)
            else:
                whole = zip(sums, (r.f_fc1, r.f_fc2) if half else (r.f_qkv, r.f_proj))
                copies = [pltpu.make_async_copy(g, o.at[b], r.go_sem.at[half, i]) for i, (g, o) in enumerate(whole)]
                start(copies)
                wait(copies)

    if linked:
        step_1(4)
        step_2(0)
    push_row(0, canvases - 1)
    if linked:
        step_2(4)
        step_4(1)
        smalls_sent(1)
        step_5(1)
        for step in (step_3, step_4, step_5):
            step(0)
            step(4)
        reductions_done()
        weights_sent()
        for k in range(1, 8):
            pack_copy(k).wait_send()
    for k in range(1, 4):
        for n in range(canvases):
            arrived(k, n)
    for n in range(canvases):
        pushed(n)


def compute(linked, operands):
    canvases = operands["x_hbm"].shape[1]
    shape = jax.ShapeDtypeStruct
    hbm = pl.BlockSpec(memory_space=pl.ANY)
    vmem = pl.BlockSpec(memory_space=pltpu.VMEM)
    dma = pltpu.SemaphoreType.DMA
    full = {
        "wat": ((2, D, 4 * D), BF),
        "fc1": ((2, D, FF), BF),
        "fc2": ((2, FF, D), BF),
        "vec": ((2, 8, FF), F32),
    }
    grads = {
        "g_qkv": ((D, 3 * D), F32),
        "g_proj": ((D, D), F32),
        "g_fc1": ((D, FF), F32),
        "g_fc2": ((FF, D), F32),
        "g_vec": ((2, 8, 8, FF), F32),
        "g_tab": ((2, 2 * PLACES, GROUPS * 128), F32),
    }
    outs = {"act_hbm": ((4, canvases, CELLS, D), BF), "igrad_hbm": ((4, canvases, CELLS, D), BF)}
    kept = {
        "hqw": ((canvases, WROWS, D), BF),
        "qkv": ((canvases, WROWS, 3 * D), BF),
        "probs": ((canvases, WINDOWS * GROUPS, 128, 128), BF),
        "att": ((canvases, WROWS, D), BF),
        "hq2": ((canvases, CELLS, D), BF),
        "hid": ((canvases, CELLS, FF), BF),
        "dgelu": ((canvases, CELLS, FF), BF),
    }
    outs |= {"h_" + name: kind for name, kind in kept.items()}
    scratch = kept | {
        "code": ((canvases, CELLS, 128), jnp.int32),
        "codew": ((WROWS, 128), jnp.int32),
        "buf": ((6, canvases, CELLS, D), BF),
        "canvf": ((CELLS, D), F32),
        "winf": ((WROWS, D), F32),
        "gzw": ((WROWS, D), BF),
        "go": ((WROWS, D), BF),
        "gqkv": ((WROWS, 3 * D), BF),
    }
    sems = {
        "in_sem": (2, canvases),
        "code_sem": (1,),
        "st_sem": (2, canvases, 4),
        "local_sem": (2, canvases),
        "act_send": (3, canvases),
        "act_recv": (3, canvases),
        "ig_send": (3, canvases),
        "ig_recv": (3, canvases),
    }
    if linked:
        outs |= {
            "o_qkv": ((2, 48, 3 * D), F32),
            "o_proj": ((2, 48, D), F32),
            "o_fc1": ((2, 48, FF), F32),
            "o_fc2": ((2, 192, D), F32),
            "o_small": ((2, 8, 64, D), BF),
        }
        scratch |= full | grads
        scratch |= {
            "packs": ((8, 16, 256), BF),
            "l_qkv": ((48, 3 * D), F32),
            "l_proj": ((48, D), F32),
            "l_fc1": ((48, FF), F32),
            "l_fc2": ((192, D), F32),
        }
        for kind, rows in ((kind + "_", rows) for kind, rows in ROWS.items()):
            scratch |= {
                kind + "st_a": ((4, rows, D), BF),
                kind + "rc_a": ((4, rows, D), BF),
                kind + "st_b": ((3, rows, D), BF),
                kind + "rc_b": ((3, rows, D), BF),
                kind + "st_c": ((rows, D), BF),
                kind + "rc_c": ((3, rows // 4, D), BF),
                kind + "fin": ((rows, D), BF),
            }
        sems |= {
            "sh_sem": (4, 2),
            "os_sem": (2,),
            "go_sem": (4, 2),
            "wz_send": (4, 2, 3),
            "wz_recv": (4, 2, 3),
            "wx_send": (4, 2, 3, 3),
            "wx_recv": (4, 2, 3, 3),
            "ws_send": (4, 2, 4),
            "ws_recv": (4, 2, 4),
            "pk_send": (7,),
            "pk_recv": (7,),
            "ra_send": (6,),
            "ra_recv": (6,),
            "rb_send": (6, 3),
            "rb_recv": (6, 3),
            "rc_send": (6, 3),
            "rc_recv": (6, 3),
            "rf_send": (6, 3),
            "rf_recv": (6, 3),
            "rs_send": (2, 7),
            "rs_recv": (2, 7),
        }
    else:
        for name in ("g_vec", "g_tab"):
            outs[name] = grads.pop(name)
        outs |= {name.replace("g_", "f_"): ((2,) + dims, F32) for name, (dims, _) in grads.items()}
        scratch |= grads
        sems["go_sem"] = (4, 2)
    in_vmem = set(full) | {"bias", "pack", "g_vec", "g_tab"}
    names = tuple(operands) + tuple(outs) + tuple(scratch) + tuple(sems)
    results = pl.pallas_call(
        functools.partial(kernel, names, linked, canvases),
        out_shape=tuple(shape(*o) for o in outs.values()),
        in_specs=[vmem if name in in_vmem else hbm for name in operands],
        out_specs=tuple(vmem if name in in_vmem else hbm for name in outs),
        scratch_shapes=[pltpu.VMEM(*v) for v in scratch.values()] + [dma(v) for v in sems.values()],
        compiler_params=pltpu.CompilerParams(
            vmem_limit_bytes=64 * 1024 * 1024 - 65536, collective_id=0, has_side_effects=True
        ),
    )(*operands.values())
    return dict(zip(outs, results))


def place_pairs():
    place = np.arange(PLACES)
    r, c = place // 8, place % 8
    index = (r[None, :] - r[:, None] + WIN - 1) * (2 * WIN - 1) + c[None, :] - c[:, None] + WIN - 1
    real = (r < WIN) & (c < WIN)
    return index, real[:, None] & real[None, :], real


def pair_onehot():
    index, both, _ = place_pairs()
    table = (2 * WIN - 1) ** 2
    hot = (np.where(both, index, -1).reshape(-1)[None, :] == np.arange(table)[:, None])
    return hot.astype(np.float32)


def body(
    inputs,
    cotangent,
    pad_mask,
    region_ids,
    norm1_gain,
    norm1_bias,
    qkv_weight,
    qv_bias,
    rel_table,
    proj_weight,
    proj_bias,
    norm2_gain,
    norm2_bias,
    fc1_weight,
    fc1_bias,
    fc2_weight,
    fc2_bias,
):
    owners = lax.axis_size("dp")
    linked = owners == 8
    mine = lax.axis_index("pipe")

    def own(a):
        return lax.dynamic_index_in_dim(a, mine, 0, keepdims=False)

    code = own(region_ids) * 2 + own(pad_mask)
    code = jnp.broadcast_to(code[:, :, None], code.shape + (128,))

    hot = pair_onehot()
    _, _, real = place_pairs()
    rel = lax.dot_general(
        rel_table.astype(BF), jnp.asarray(hot, BF), (((1,), (0,)), ((), ())), preferred_element_type=F32
    )
    rel = rel.reshape(2, GROUPS, 2, 2, PLACES, PLACES)
    rel = jnp.where(jnp.asarray(real)[None, None, None, None, :, None], rel, MASKED)
    rel = rel.transpose(0, 1, 3, 4, 2, 5).reshape(2, GROUPS, 128, 128)

    operands = {"x_hbm": inputs, "cot_hbm": cotangent, "code_hbm": code, "bias": rel}
    vectors = (norm1_gain, norm1_bias, proj_bias, norm2_gain, norm2_bias, fc2_bias, qv_bias, fc1_bias)
    sizes = [v.shape[1] for v in vectors]
    ends = np.cumsum([0] + sizes)
    if linked:
        pack = jnp.stack([jnp.pad(v, ((0, 0), (0, 256 - v.shape[1]))) for v in vectors], axis=1)
        operands |= {
            "pack": pack.reshape(16, 256).astype(BF),
            "s_qkv": qkv_weight,
            "s_proj": proj_weight,
            "s_fc1": fc1_weight,
            "s_fc2": fc2_weight,
        }
    else:

        def gathered(a):
            return lax.all_gather(a.astype(BF), "dp", axis=1, tiled=True)

        packed = lax.all_gather(jnp.concatenate(vectors, axis=1).astype(BF), "dp", axis=1)
        parts = [packed[:, :, a:b].reshape(2, -1).astype(F32) for a, b in zip(ends[:-1], ends[1:])]
        qv = parts[6]
        parts[6] = jnp.concatenate([qv[:, :D], jnp.zeros_like(qv[:, :D]), qv[:, D:]], axis=1)
        vec = jnp.stack([jnp.pad(p, ((0, 0), (0, FF - p.shape[1]))) for p in parts], axis=1)
        operands |= {
            "wat": jnp.concatenate([gathered(qkv_weight), gathered(proj_weight)], axis=2),
            "fc1": gathered(fc1_weight),
            "fc2": gathered(fc2_weight),
            "vec": vec,
        }

    out = compute(linked, operands)

    def to_owners(g):
        shared = lax.psum_scatter(g, "dp", scatter_dimension=1, tiled=True)
        return lax.psum(shared, "pipe")

    if linked:
        small = out["o_small"]
        g_tab = small[:, :, :16].reshape(2, 128, GROUPS * 128)
        g_vec = jnp.concatenate([small[:, :, 16 + 8 * j : 24 + 8 * j] for j in range(4)], axis=3)
    else:
        g_tab, g_vec = out["g_tab"], out["g_vec"]

    g_vec = jnp.sum(g_vec.astype(F32), axis=2)
    kinds = [g_vec[:, i] for i in range(8)]
    qv_sum = jnp.concatenate([kinds[6][:, :D], kinds[6][:, 2 * D : 3 * D]], axis=1)
    rows = [kinds[0], kinds[1], kinds[2], kinds[3], kinds[4], kinds[5], qv_sum, kinds[7]]
    if linked:
        at = lax.axis_index("dp")
        small = [lax.dynamic_slice_in_dim(v, at * n, n, 1) for v, n in zip(rows, sizes)]
    else:
        rows = [v[:, : n * owners].reshape(2, -1, n) for v, n in zip(rows, sizes)]
        g_small = to_owners(jnp.concatenate(rows, axis=2))[:, 0]
        small = [g_small[:, a:b] for a, b in zip(ends[:-1], ends[1:])]

    pairs = g_tab.reshape(2, 2, PLACES, GROUPS, 2, PLACES).transpose(0, 3, 4, 1, 2, 5)
    pairs = pairs.reshape(2, HEADS, PLACES * PLACES)
    g_table = lax.dot_general(
        jnp.broadcast_to(jnp.asarray(hot, pairs.dtype), (2,) + hot.shape),
        pairs,
        (((2,), (2,)), ((0,), (0,))),
        precision=None if linked else lax.Precision.HIGHEST,
        preferred_element_type=F32,
    )
    if linked:
        big = [out[name] for name in ("o_qkv", "o_proj", "o_fc1", "o_fc2")]
    else:
        g_table = lax.psum(g_table, ("pipe", "dp"))
        big = [to_owners(out[name]) for name in ("f_qkv", "f_proj", "f_fc1", "f_fc2")]

    return (
        out["act_hbm"][None],
        out["igrad_hbm"][None],
        small[0],
        small[1],
        big[0],
        small[6],
        g_table,
        big[1],
        small[2],
        small[3],
        small[4],
        big[2],
        small[7],
        big[3],
        small[5],
    )


def solution(mesh):
    cols = P(None, "dp")
    rows = P(None, "dp", None)
    return jax.shard_map(
        body,
        mesh=mesh,
        in_specs=(
            P(None, "dp", None, None),
            P(None, "dp", None, None),
            rows,
            rows,
            cols,
            cols,
            rows,
            cols,
            P(),
            rows,
            cols,
            cols,
            cols,
            rows,
            cols,
            rows,
            cols,
        ),
        out_specs=(
            P("pipe", None, "dp", None, None),
            P("pipe", None, "dp", None, None),
            cols,
            cols,
            rows,
            cols,
            P(),
            rows,
            cols,
            cols,
            cols,
            rows,
            cols,
            rows,
            cols,
        ),
        check_vma=False,
    )
```

```python
import functools
import types

import jax
import jax.numpy as jnp
import numpy as np
from jax import lax
from jax.experimental import pallas as pl
from jax.experimental.pallas import tpu as pltpu
from jax.sharding import PartitionSpec as P

HEADS = 12
WIN = 7
SHIFT = 3
GRID = 28
CELLS = 784
D = 384
FF = 1536
HEAD = 32
SIDE = 4
WINDOWS = 16
PLACES = 64
WROWS = WINDOWS * PLACES
GROUPS = 3
TILE = 112
SCALE = HEAD**-0.5
NORM_EPS = 1e-05
MASKED = -1e30
BF = jnp.bfloat16
F32 = jnp.float32

RSQRT_2 = 1.0 / np.sqrt(2.0)
PHI_0 = 1.0 / np.sqrt(2.0 * np.pi)


def nn(a, b):
    return lax.dot_general(a, b, (((1,), (0,)), ((), ())), preferred_element_type=F32)


def nt(a, b):
    return lax.dot_general(a, b, (((1,), (1,)), ((), ())), preferred_element_type=F32)


def tn(a, b):
    return lax.dot_general(a, b, (((0,), (0,)), ((), ())), preferred_element_type=F32)


def segments(shift):
    runs = []
    for wr in range(SIDE):
        for r in range(WIN):
            row = (wr * WIN + r + shift) % GRID
            for wc in range(SIDE):
                col = (wc * WIN + shift) % GRID
                place = (wr * SIDE + wc) * PLACES + r * 8
                first = min(WIN, GRID - col)
                runs.append((row * GRID + col, place, first))
                if first < WIN:
                    runs.append((row * GRID, place + first, WIN - first))
    return runs


def to_windows(src, dst, shift):
    for cell, place, count in segments(shift):
        dst[pl.ds(place, count), :] = src[pl.ds(cell, count), :]


def to_canvas(src, dst, shift):
    for cell, place, count in segments(shift):
        dst[pl.ds(cell, count), :] = src[pl.ds(place, count), :]


def row_block(t, size):
    return pl.ds(pl.multiple_of(t * size, 16), size)


def standardized(v):
    centered = v - jnp.mean(v, axis=-1, keepdims=True)
    spread = jnp.mean(centered * centered, axis=-1, keepdims=True)
    rs = lax.rsqrt(spread + NORM_EPS)
    return centered * rs, rs


def by_eights(v):
    return jnp.sum(v.reshape(v.shape[0] // 8, 8, v.shape[1]), axis=0)


def gelu_parts(x):
    cdf = 0.5 + 0.5 * lax.erf(x * RSQRT_2)
    return x * cdf, cdf + x * (jnp.exp(-0.5 * x * x) * PHI_0)


def real_places(rows):
    place = lax.broadcasted_iota(jnp.int32, (rows, 1), 0)
    return ((place & 7) < WIN) & (((place >> 3) & 7) < WIN)


def head_of_lane():
    return lax.broadcasted_iota(jnp.int32, (PLACES, 128), 1) >> 5


def by_low(x, lanes):
    zero = jnp.zeros_like(x)
    return jnp.concatenate([jnp.where((lanes & 1) == h, x, zero) for h in range(2)], axis=0)


def by_high(x, lanes):
    zero = jnp.zeros_like(x)
    return jnp.concatenate([jnp.where((lanes >> 1) == h, x, zero) for h in range(2)], axis=0)


def own_low(wide, lanes):
    return jnp.where((lanes & 1) == 0, wide[:PLACES], wide[PLACES:])


def own_high(wide, lanes):
    return jnp.where((lanes >> 1) == 0, wide[:PLACES], wide[PLACES:])


MESH = pl.DeviceIdType.MESH
KINDS = ("a", "m", "a", "m", "t", "t")
ROWS = {"a": 192, "m": 384, "t": 64}
BLOCK = (0, 0, 1, 1, 0, 1)
BEFORE = {0: 2, 1: 3, 4: 5}


def kernel(names, linked, canvases, *refs):
    r = types.SimpleNamespace(**dict(zip(names, refs)))
    me = lax.axis_index("pipe")
    code, codew, buf = r.code, r.codew, r.buf
    hqw, qkv, probs, att = r.hqw, r.qkv, r.probs, r.att
    hq2, hid, dgelu = r.hq2, r.hid, r.dgelu
    canvf, winf, gzw, gqkv, go = r.canvf, r.winf, r.gzw, r.gqkv, r.go
    g_qkv, g_proj, g_fc1, g_fc2, g_vec, g_tab = r.g_qkv, r.g_proj, r.g_fc1, r.g_fc2, r.g_vec, r.g_tab
    wat, fc1, fc2, vec, bias = r.wat, r.fc1, r.fc2, r.vec, r.bias
    if linked:
        d = lax.axis_index("dp")
        z, c = d // 2, d % 2
        sibling = {"dp": 2 * z + 1 - c}

    def z_peer(k):
        return {"dp": 2 * lax.rem(z + k, 4) + c}

    def pipe_peer(k):
        return {"pipe": lax.rem(me + k, 4)}

    def dp_peer(k):
        return {"dp": lax.rem(d + k, 8)}

    def remote(src, dst, send, recv, device):
        return pltpu.make_async_remote_copy(
            src_ref=src, dst_ref=dst, send_sem=send, recv_sem=recv, device_id=device, device_id_type=MESH
        )

    barrier = pltpu.get_barrier_semaphore()
    partners = [pipe_peer(k) for k in range(1, 4)]
    if linked:
        partners += [dp_peer(k) for k in range(1, 8)]
    for partner in partners:
        pl.semaphore_signal(barrier, inc=1, device_id=partner, device_id_type=MESH)

    full = ((wat,), (fc1, fc2), (wat,), (fc1, fc2))

    def owner_back(k):
        return 2 * lax.rem(z + 4 - k, 4) + c

    def shard(sec, a, owner):
        h = 192 if a else 48
        return full[sec][a].at[sec // 2, pl.ds(pl.multiple_of(owner * h, 16), h), :]

    def part(sec, a, owner, place):
        if a:
            return fc2.at[sec // 2, pl.ds(pl.multiple_of(owner * 192 + place * 48, 16), 48), :]
        rows = pl.ds(pl.multiple_of(owner * 48, 16), 48)
        return full[sec][0].at[sec // 2, rows, pl.ds(pl.multiple_of(place * D, 128), D)]

    def to_z(sec, a, k):
        own = part(sec, a, d, me)
        return remote(own, own, r.wz_send.at[sec, a, k - 1], r.wz_recv.at[sec, a, k - 1], z_peer(k))

    def to_places(sec, a, k, j):
        got = part(sec, a, owner_back(k), me)
        return remote(
            got, got, r.wx_send.at[sec, a, k - 1, j - 1], r.wx_recv.at[sec, a, k - 1, j - 1], pipe_peer(j)
        )

    def to_sibling(sec, a, k):
        block = shard(sec, a, owner_back(k))
        return remote(block, block, r.ws_send.at[sec, a, k], r.ws_recv.at[sec, a, k], sibling)

    def weights_1(sec):
        for a in range(len(full[sec])):
            for k in range(1, 4):
                to_z(sec, a, k).start()
            to_sibling(sec, a, 0).start()

    def weights_2(sec):
        for k in range(1, 4):
            for a in range(len(full[sec])):
                got = part(sec, a, owner_back(k), me)
                remote(got, got, r.wz_send.at[sec, a, k - 1], r.wz_recv.at[sec, a, k - 1], z_peer(k)).wait_recv()
                for j in range(1, 4):
                    to_places(sec, a, k, j).start()

    def weights_3(sec):
        for k in range(1, 4):
            for a in range(len(full[sec])):
                for j in range(1, 4):
                    got = part(sec, a, owner_back(k), lax.rem(me + 4 - j, 4))
                    remote(
                        got, got, r.wx_send.at[sec, a, k - 1, j - 1], r.wx_recv.at[sec, a, k - 1, j - 1], pipe_peer(j)
                    ).wait_recv()
                to_sibling(sec, a, k).start()

    def weights_4(sec):
        for k in range(4):
            for a in range(len(full[sec])):
                block = shard(sec, a, 2 * lax.rem(z + 4 - k, 4) + 1 - c)
                remote(block, block, r.ws_send.at[sec, a, k], r.ws_recv.at[sec, a, k], sibling).wait_recv()

    def weights_sent():
        for sec in range(4):
            for a in range(len(full[sec])):
                for k in range(4):
                    to_sibling(sec, a, k).wait_send()
                    if k:
                        to_z(sec, a, k).wait_send()
                        for j in range(1, 4):
                            to_places(sec, a, k, j).wait_send()

    def pack_copy(k):
        return remote(
            r.packs.at[d], r.packs.at[d], r.pk_send.at[k - 1], r.pk_recv.at[k - 1], dp_peer(k)
        )

    def pack_arrival(k):
        slot = r.packs.at[lax.rem(d + 8 - k, 8)]
        return remote(slot, slot, r.pk_send.at[k - 1], r.pk_recv.at[k - 1], dp_peer(k))

    def place_vectors():
        kind = lax.broadcasted_iota(jnp.int32, (16, 256), 0) & 7
        lane = lax.broadcasted_iota(jnp.int32, (16, 256), 1)
        vec[...] = jnp.zeros_like(vec)
        for width, kinds in ((48, kind < 6), (96, kind == 6), (192, kind == 7)):
            for owner in range(8):
                at = owner * width
                if width == 96 and owner >= 4:
                    at += D
                start = at // 128 * 128
                part = jnp.where(kinds & (lane < width), r.packs[owner].astype(F32), 0.0)
                if at > start:
                    part = pltpu.roll(part, at - start, 1)
                for b in range(2):
                    vec[b, :, start : start + 256] += part[8 * b : 8 * b + 8]

    def pieces(sec, owner):
        b = BLOCK[sec]
        out = []

        def matrix(ref, h):
            for t in range(h // 48):
                rows = pl.ds(pl.multiple_of(owner * h + t * 48, 16), 48)
                for j in range(ref.shape[1] // D):
                    load = functools.partial(lambda ref, rows, j: ref[rows, j * D : (j + 1) * D], ref, rows, j)
                    out.append((len(out) * 48, 48, load))

        def small():
            parts = [g_tab[b, pl.ds(pl.multiple_of(owner * 16, 16), 16), :]]
            parts += [g_vec[b, owner, :, j * D : (j + 1) * D] for j in range(4)]
            return jnp.concatenate(parts + [jnp.zeros((16, D), F32)], axis=0)

        if KINDS[sec] == "m":
            matrix(g_fc1, 48)
            matrix(g_fc2, 192)
        elif KINDS[sec] == "a":
            matrix(g_qkv, 48)
            matrix(g_proj, 48)
        else:
            out.append((0, 64, small))
        return out

    def reduce_refs(sec):
        kind = KINDS[sec]
        return types.SimpleNamespace(
            **{n: getattr(r, kind + "_" + n) for n in ("st_a", "rc_a", "st_b", "rc_b", "st_c", "rc_c", "fin")}
        )

    def step_1(sec):
        q = reduce_refs(sec)
        if sec in BEFORE:
            copy_a(BEFORE[sec]).wait_send()
            for k in range(1, 4):
                copy_b(BEFORE[sec], k).wait_send()
                copy_c(BEFORE[sec], k).wait_send()
        for k in range(4):
            i = lax.rem(z + k, 4)
            kept = q.st_b.at[k - 1] if k else q.st_c
            for row, rows, load in pieces(sec, 2 * i + 1 - c):
                q.st_a[i, row : row + rows, :] = load().astype(BF)
            for row, rows, load in pieces(sec, 2 * i + c):
                kept[row : row + rows, :] = load().astype(BF)
        copy_a(sec).start()

    def copy_a(sec):
        q = reduce_refs(sec)
        return remote(q.st_a, q.rc_a, r.ra_send.at[sec], r.ra_recv.at[sec], sibling)

    def copy_b(sec, k):
        q = reduce_refs(sec)
        return remote(
            q.st_b.at[k - 1], q.rc_b.at[k - 1], r.rb_send.at[sec, k - 1], r.rb_recv.at[sec, k - 1], z_peer(k)
        )

    def step_2(sec):
        q = reduce_refs(sec)
        copy_a(sec).wait_recv()
        for k in (1, 2, 3, 0):
            i = lax.rem(z + k, 4)
            kept = q.st_b.at[k - 1] if k else q.st_c
            for row in range(0, kept.shape[0], 64):
                at = slice(row, row + 64)
                kept[at, :] = (kept[at, :].astype(F32) + q.rc_a[i, at, :].astype(F32)).astype(BF)
            if k:
                copy_b(sec, k).start()

    def quarter(sec, ref, who):
        rows = ROWS[KINDS[sec]] // 4
        return ref.at[pl.ds(pl.multiple_of(who * rows, 16), rows), :]

    def copy_c(sec, k):
        q = reduce_refs(sec)
        return remote(
            quarter(sec, q.st_c, lax.rem(me + k, 4)),
            q.rc_c.at[k - 1],
            r.rc_send.at[sec, k - 1],
            r.rc_recv.at[sec, k - 1],
            pipe_peer(k),
        )

    def step_3(sec):
        q = reduce_refs(sec)
        for k in range(1, 4):
            copy_b(sec, k).wait_recv()
        for row in range(0, q.st_c.shape[0], 64):
            at = slice(row, row + 64)
            total = q.st_c[at, :].astype(F32)
            for k in range(3):
                total = total + q.rc_b[k, at, :].astype(F32)
            q.st_c[at, :] = total.astype(BF)
        for k in range(1, 4):
            copy_c(sec, k).start()

    def copy_f(sec, k):
        q = reduce_refs(sec)
        own = quarter(sec, q.fin, me)
        return remote(own, own, r.rf_send.at[sec, k - 1], r.rf_recv.at[sec, k - 1], pipe_peer(k))

    def step_4(sec):
        q = reduce_refs(sec)
        for k in range(1, 4):
            copy_c(sec, k).wait_recv()
            if sec in BEFORE:
                copy_f(BEFORE[sec], k).wait_send()
        total = quarter(sec, q.st_c, me)[...].astype(F32)
        for k in range(3):
            total = total + q.rc_c[k].astype(F32)
        quarter(sec, q.fin, me)[...] = total.astype(BF)
        for k in range(1, 4):
            copy_f(sec, k).start()

    def copy_s(b, k):
        return remote(r.t_fin, r.o_small.at[b, d], r.rs_send.at[b, k - 1], r.rs_recv.at[b, k - 1], dp_peer(k))

    def own_small(b):
        return pltpu.make_async_copy(r.t_fin, r.o_small.at[b, d], r.os_sem.at[b])

    def outputs(sec):
        pairs = ((r.l_fc1, r.o_fc1), (r.l_fc2, r.o_fc2)) if sec % 2 else ((r.l_qkv, r.o_qkv), (r.l_proj, r.o_proj))
        return [
            pltpu.make_async_copy(ref, out.at[sec // 2], r.go_sem.at[sec, i]) for i, (ref, out) in enumerate(pairs)
        ]

    def step_5(sec):
        q = reduce_refs(sec)
        for k in range(1, 4):
            got = quarter(sec, q.fin, lax.rem(me + 4 - k, 4))
            remote(got, got, r.rf_send.at[sec, k - 1], r.rf_recv.at[sec, k - 1], pipe_peer(k)).wait_recv()
        if sec >= 4:
            for k in range(1, 8):
                copy_s(BLOCK[sec], k).start()
            own_small(BLOCK[sec]).start()
            return
        if sec < 2:
            for out in outputs(sec + 2):
                out.wait()
        row = 0
        for ref in (r.l_fc1, r.l_fc2) if sec % 2 else (r.l_qkv, r.l_proj):
            for t in range(ref.shape[0] // 48):
                for j in range(ref.shape[1] // D):
                    ref[t * 48 : (t + 1) * 48, j * D : (j + 1) * D] = q.fin[row : row + 48, :].astype(F32)
                    row += 48
        for out in outputs(sec):
            out.start()

    def smalls_sent(b):
        for k in range(1, 8):
            copy_s(b, k).wait_send()
        own_small(b).wait()

    def reductions_done():
        for sec in BEFORE:
            copy_a(sec).wait_send()
            for k in range(1, 4):
                copy_b(sec, k).wait_send()
                copy_c(sec, k).wait_send()
                copy_f(sec, k).wait_send()
        for sec in range(2):
            for out in outputs(sec):
                out.wait()
        smalls_sent(0)
        for b in range(2):
            for k in range(1, 8):
                remote(
                    r.t_fin,
                    r.o_small.at[b, lax.rem(d + 8 - k, 8)],
                    r.rs_send.at[b, k - 1],
                    r.rs_recv.at[b, k - 1],
                    dp_peer(k),
                ).wait_recv()

    if linked:
        lands = ((r.s_qkv, g_qkv, wat, 0), (r.s_proj, g_proj, wat, 3 * D), (r.s_fc1, g_fc1, fc1, 0), (r.s_fc2, g_fc2, fc2, 0))

        def landing(i, b):
            src, dst, _, _ = lands[i]
            h, n = src.shape[1:]
            return pltpu.make_async_copy(
                src.at[b], dst.at[pl.ds(192 * b, h), pl.ds(0, n)], r.sh_sem.at[i, b]
            )

        for i in range(4):
            for b in range(2):
                landing(i, b).start()
        r.packs[d] = r.pack[...]
        for i, (src, dst, ref, col) in enumerate(lands):
            h, n = src.shape[1:]
            for b in range(2):
                landing(i, b).wait()
                for t in range(0, h, 48):
                    rows = pl.ds(pl.multiple_of(d * h + t, 16), 48)
                    ref[b, rows, col : col + n] = dst[192 * b + t : 192 * b + t + 48, :n].astype(BF)
    pl.semaphore_wait(barrier, len(partners))
    if linked:
        for k in range(1, 8):
            pack_copy(k).start()
        weights_1(0)

    def cleared(*refs):
        for ref in refs:

            @pl.loop(0, ref.shape[0] // 16)
            def _(i):
                ref[row_block(i, 16), :] = jnp.zeros((16, ref.shape[1]), F32)

    g_vec[...] = jnp.zeros_like(g_vec)
    g_tab[...] = jnp.zeros_like(g_tab)
    codew[...] = jnp.zeros_like(codew)

    if linked:
        weights_2(0)
        for sec in range(1, 4):
            weights_1(sec)
        for k in range(1, 8):
            pack_arrival(k).wait_recv()
        place_vectors()

    def vector(b, kind, width=D):
        return vec[b, kind : kind + 1, :width]

    def add_vec(b, kind, part):
        g_vec[b, kind, :, : part.shape[1]] += part

    def windowed(rows, count):
        return jnp.where(real_places(count), winf[rows, :], 0.0).astype(BF)

    def by_block(b, move):
        for i in range(2):

            @pl.when(b == i)
            def _():
                move(SHIFT * i)

    def attention_forward(b, n, x, out, hook):
        lanes = head_of_lane()

        @pl.loop(0, CELLS // TILE)
        def _(t):
            rows = row_block(t, TILE)
            xhat, _ = standardized(x[rows, :].astype(F32))
            canvf[rows, :] = xhat * vector(b, 0) + vector(b, 1)

        def arrange(shift):
            to_windows(canvf, winf, shift)
            to_windows(code.at[n], codew, shift)

        by_block(b, arrange)
        hook(4)

        @pl.loop(0, 4)
        def _(t):
            rows = row_block(t, 256)
            hq = windowed(rows, 256)
            hqw[n, rows, :] = hq
            for part in range(3):
                cols = slice(part * D, (part + 1) * D)
                acc = nn(hq, wat[b, :, cols]) + vec[b, 6:7, cols]
                if part == 0:
                    acc = acc * SCALE
                qkv[n, rows, cols] = acc.astype(BF)

        hook(0)

        @pl.loop(0, WINDOWS)
        def _(w):
            rows = row_block(w, PLACES)
            cells = codew[rows, :]
            region = (cells >> 1) * b
            pad = (cells & 1).astype(F32)
            lane = lax.broadcasted_iota(jnp.int32, (PLACES, 128), 1)
            same = jnp.where(lane == region, 1.0, 0.0)
            left = jnp.where(lane == 127, 1.0 - pad, same).astype(BF)
            right = jnp.where(lane == 127, -pad, same).astype(BF)
            agree = nt(left, jnp.concatenate([right, right], axis=0))
            mask = jnp.where(agree > 0.5, 0.0, MASKED)
            for g in range(GROUPS):
                q = qkv[n, rows, g * 128 : (g + 1) * 128]
                k = qkv[n, rows, D + g * 128 : D + (g + 1) * 128]
                v = qkv[n, rows, 2 * D + g * 128 : 2 * D + (g + 1) * 128]
                scores = nt(by_low(k, lanes), by_high(q, lanes)) + bias[b, g]
                halves = []
                for h in range(2):
                    s = scores[h * PLACES : (h + 1) * PLACES] + mask
                    e = jnp.exp(s - jnp.max(s, axis=0, keepdims=True))
                    halves.append((e * (1.0 / jnp.sum(e, axis=0, keepdims=True))).astype(BF))
                p = jnp.concatenate(halves, axis=0)
                probs[n, w * GROUPS + g] = p
                att[n, rows, g * 128 : (g + 1) * 128] = own_high(tn(p, by_low(v, lanes)), lanes).astype(BF)

        hook(1)

        @pl.loop(0, 4)
        def _(t):
            rows = row_block(t, 256)
            winf[rows, :] = nn(att[n, rows, :], wat[b, :, 3 * D :])

        by_block(b, functools.partial(to_canvas, winf, canvf))

        @pl.loop(0, CELLS // TILE)
        def _(t):
            rows = row_block(t, TILE)
            out[rows, :] = (x[rows, :].astype(F32) + (canvf[rows, :] + vector(b, 2))).astype(BF)

    def mlp_forward(b, n, x, out, hook):
        @pl.loop(0, CELLS // TILE)
        def _(t):
            rows = row_block(t, TILE)
            xhat, _ = standardized(x[rows, :].astype(F32))
            hq2[n, rows, :] = (xhat * vector(b, 3) + vector(b, 4)).astype(BF)

        @pl.loop(0, FF // 256)
        def _(i):
            cols = pl.ds(pl.multiple_of(i * 256, 256), 256)
            pre = nn(hq2[n], fc1[b, :, cols]) + vec[b, 7:8, cols]
            for at in range(0, CELLS, 16):
                h, dg = gelu_parts(pre[at : at + 16])
                hid[n, at : at + 16, cols] = h.astype(BF)
                dgelu[n, at : at + 16, cols] = dg.astype(BF)

        hook(0)
        total = nn(hid[n], fc2[b])
        for at in range(0, CELLS, TILE):
            rows = slice(at, at + TILE)
            out[rows, :] = (x[rows, :].astype(F32) + (total[rows] + vector(b, 5))).astype(BF)

    def norm_backward(b, kind, x, gz, out):
        @pl.loop(0, CELLS // TILE)
        def _(t):
            rows = row_block(t, TILE)
            xhat, rs = standardized(x[rows, :].astype(F32))
            gn = canvf[rows, :]
            gzf = gz[rows, :].astype(F32)
            add_vec(b, kind, by_eights(gn * xhat))
            add_vec(b, kind + 1, by_eights(gn))
            add_vec(b, 5 if kind else 2, by_eights(gzf))
            g = gn * vector(b, kind)
            mg = jnp.mean(g, axis=-1, keepdims=True)
            mgx = jnp.mean(g * xhat, axis=-1, keepdims=True)
            out[rows, :] = (gzf + rs * (g - mg - xhat * mgx)).astype(BF)

    def mlp_backward(b, n, x, gz, out, free_out, hook):
        @pl.loop(0, FF // 256)
        def _(i):
            cols = pl.ds(pl.multiple_of(i * 256, 256), 256)
            gh = nt(gz[...], fc2[b, cols, :])
            sums = jnp.zeros((8, 256), F32)
            for at in range(0, CELLS, 16):
                gp = (gh[at : at + 16] * dgelu[n, at : at + 16, cols].astype(F32)).astype(BF)
                dgelu[n, at : at + 16, cols] = gp
                sums = sums + by_eights(gp.astype(F32))
            g_vec[b, 7, :, cols] += sums
            g_fc1[:, cols] += tn(hq2[n], dgelu[n, :, cols])
            g_fc2[cols, :] += tn(hid[n, :, cols], gz[...])

        hook(0)
        canvf[...] = nt(dgelu[n], fc1[b])
        free_out()
        norm_backward(b, 3, x, gz, out)

    def attention_backward(b, n, x, gz, out, free_out, hook):
        lanes = head_of_lane()

        @pl.loop(0, CELLS // TILE)
        def _(t):
            rows = row_block(t, TILE)
            canvf[rows, :] = gz[rows, :].astype(F32)

        by_block(b, functools.partial(to_windows, canvf, winf))

        @pl.loop(0, 4)
        def _(t):
            rows = row_block(t, 256)
            gzw[rows, :] = windowed(rows, 256)

        g_proj[...] += tn(att[n], gzw[...])

        @pl.loop(0, 4)
        def _(t):
            rows = row_block(t, 256)
            go[rows, :] = nt(gzw[rows, :], wat[b, :, 3 * D :]).astype(BF)

        hook(0)

        @pl.loop(0, WINDOWS)
        def _(w):
            rows = row_block(w, PLACES)
            for g in range(GROUPS):
                at = [slice(part * D + g * 128, part * D + (g + 1) * 128) for part in range(3)]
                q, k, v = (qkv[n, rows, cols] for cols in at)
                go_wide = by_high(go[rows, at[0]], lanes)
                p_low = probs[n, w * GROUPS + g]
                p = p_low.astype(F32)
                pd = p * nt(by_low(v, lanes), go_wide)
                halves = []
                for h in range(2):
                    half = slice(h * PLACES, (h + 1) * PLACES)
                    halves.append((pd[half] - p[half] * jnp.sum(pd[half], axis=0, keepdims=True)).astype(BF))
                ds = jnp.concatenate(halves, axis=0)
                g_tab[b, :, g * 128 : (g + 1) * 128] += ds.astype(F32)
                gqkv[rows, at[0]] = (own_high(tn(ds, by_low(k, lanes)), lanes) * SCALE).astype(BF)
                gqkv[rows, at[1]] = own_low(nn(ds, by_high(q, lanes)), lanes).astype(BF)
                gqkv[rows, at[2]] = own_low(nn(p_low, go_wide), lanes).astype(BF)

        hook(1)
        attention_weights(n)
        hook(2)

        @pl.loop(0, 4)
        def _(t):
            rows = row_block(t, 256)
            gq = gqkv[rows, :]
            add_vec(b, 6, by_eights(gq.astype(F32)))
            winf[rows, :] = nt(gq, wat[b, :, : 3 * D])

        by_block(b, functools.partial(to_canvas, winf, canvf))
        free_out()
        norm_backward(b, 0, x, gz, out)

    def attention_weights(n):
        @pl.loop(0, 3)
        def _(part):
            cols = pl.ds(pl.multiple_of(part * D, 128), D)
            g_qkv[:, cols] += tn(hqw[n], gqkv[:, cols])

    def partner(k):
        x, y = me % 2, me // 2
        return 2 * (1 - y if k & 2 else y) + (1 - x if k & 1 else x)

    def away(kind, k, n):
        dst, send, recv = ((r.act_hbm, r.act_send, r.act_recv), (r.igrad_hbm, r.ig_send, r.ig_recv))[kind]
        return remote(
            buf.at[partner(k) + 1, n], dst.at[me, n], send.at[k - 1, n], recv.at[k - 1, n], {"pipe": partner(k)}
        )

    def at_home(kind, n):
        dst = (r.act_hbm, r.igrad_hbm)[kind]
        return pltpu.make_async_copy(buf.at[me + 1, n], dst.at[me, n], r.local_sem.at[kind, n])

    def send_acts(n):
        first = lax.axis_index("dp") % 2

        @pl.when(first == 0)
        def _():
            away(0, 1, n).start()
            away(0, 2, n).start()

        @pl.when(first == 1)
        def _():
            away(0, 2, n).start()
            away(0, 1, n).start()

        away(0, 3, n).start()
        at_home(0, n).start()

    def acts_sent(n):
        for k in (1, 2, 3):
            away(0, k, n).wait_send()
        at_home(0, n).wait()

    def push_row(row, n):
        @pl.when(me // 2 == row)
        def _():
            away(1, 1, n).start()
            at_home(1, n).start()

        @pl.when(me // 2 != row)
        def _():
            away(1, 2, n).start()
            away(1, 3, n).start()

    def push_section(s, n):
        for k in (1, 2, 3):

            @pl.when(partner(k) == s)
            def _():
                away(1, k, n).start()

        @pl.when(me == s)
        def _():
            at_home(1, n).start()

    def pushed(n):
        for k in (1, 2, 3):
            away(1, k, n).wait_send()
        at_home(1, n).wait()

    def arrived(k, n):
        for dst, send, recv in ((r.act_hbm, r.act_send, r.act_recv), (r.igrad_hbm, r.ig_send, r.ig_recv)):
            got = dst.at[partner(k), n]
            remote(got, got, send.at[k - 1, n], recv.at[k - 1, n], {"pipe": partner(k)}).wait_recv()

    attention_stash = ((hqw, r.h_hqw), (qkv, r.h_qkv), (probs, r.h_probs), (att, r.h_att))
    mlp_stash = ((hq2, r.h_hq2), (hid, r.h_hid), (dgelu, r.h_dgelu))

    def stash(sec, n, back):
        pairs = mlp_stash if sec else attention_stash
        return [
            pltpu.make_async_copy(*((far.at[n], near.at[n]) if back else (near.at[n], far.at[n])), r.st_sem.at[sec, n, i])
            for i, (near, far) in enumerate(pairs)
        ]

    def load(i, n):
        src = r.cot_hbm if i else r.x_hbm
        return pltpu.make_async_copy(src.at[me, n], buf.at[5 if i else 0, n], r.in_sem.at[i, n])

    def start(copies):
        for copy in copies:
            copy.start()

    def wait(copies):
        for copy in copies:
            copy.wait()

    steps = (step_1, step_2, step_3, step_4, step_5)
    schedule = {
        (2, 0, 0): ((2, 3),),
        (2, 1, 1): ((3, 3),),
        (2, 1, 2): ((1, 2),),
        (1, 0, 0): ((2, 2), (2, 5)),
        (1, 1, 0): ((4, 3),),
        (0, 0, 0): ((3, 2), (3, 5), (2, 1), (5, 3)),
        (0, 0, 1): ((4, 2), (4, 5)),
        (0, 1, 0): ((5, 2), (5, 5)),
        (0, 1, 1): ((3, 1),),
        (0, 1, 2): ((1, 0),),
    }
    after = {3: ((1, 3),), 2: ((1, 5),), 1: ((1, 1),), 0: ()}
    weight_steps = (weights_1, weights_2, weights_3, weights_4) if linked else ()
    gathering = {
        (0, 4): ((3, 0), (4, 0)),
        (0, 0): ((2, 1),),
        (0, 1): ((2, 2), (2, 3), (3, 1)),
        (0, 3): ((4, 1), (3, 2)),
        (1, 3): ((4, 2),),
        (2, 0): ((3, 3),),
        (2, 3): ((4, 3),),
    }

    codes = [pltpu.make_async_copy(r.code_hbm, code, r.code_sem.at[0])]
    start(codes)
    start([load(i, n) for i in range(2) for n in range(canvases)])
    wait(codes)
    for i in range(2):
        wait([load(i, n) for n in range(canvases)])

    @pl.loop(0, canvases)
    def _(n):
        @pl.loop(0, 2)
        def _(b):
            def gather(half, i):
                for (sec, at), todo in gathering.items():
                    if linked and sec % 2 == half and at == i:

                        @pl.when((n == 0) & (b == sec // 2))
                        def _():
                            for step, of in todo:
                                weight_steps[step - 1](of)

            for half, forward in enumerate((attention_forward, mlp_forward)):

                @pl.when(b == 1)
                def _():
                    wait(stash(half, n, False))

                s = 2 * b + half
                forward(b, n, buf.at[s, n], buf.at[s + 1, n], functools.partial(gather, half))

                @pl.when(b == 0)
                def _():
                    start(stash(half, n, False))

                gather(half, 3)

        send_acts(n)

    @pl.loop(0, 2)
    def _(flipped):
        b = 1 - flipped
        for half, backward in ((1, mlp_backward), (0, attention_backward)):
            sums = ((g_fc1, g_fc2) if half else (g_qkv, g_proj))
            cleared(*sums)

            @pl.loop(0, canvases)
            def _(n):
                def hook(i):
                    for (sec, at, point), todo in schedule.items():
                        if linked and sec % 2 == half and point == i:

                            @pl.when((n == (canvases - 1 if at else 0)) & (b == sec // 2))
                            def _():
                                for step, of in todo:
                                    steps[step - 1](of)

                def free_out():
                    if half:

                        @pl.when(b == 1)
                        def _():
                            acts_sent(n)

                @pl.when(b == 0)
                def _():
                    wait(stash(half, n, True))

                s = 2 * b + half
                backward(b, n, buf.at[s, n], buf.at[s + 2, n], buf.at[s + 1, n], free_out, hook)
                if half:

                    @pl.when(b == 0)
                    def _():
                        push_section(1, n)

                else:

                    @pl.when(b == 1)
                    def _():
                        push_row(1, n)

                    @pl.when((b == 0) & (n < canvases - 1))
                    def _():
                        push_section(0, n)

                @pl.when(b == 1)
                def _():
                    start(stash(half, n, True))

            if linked:
                for i in range(2):
                    todo = after[2 * i + half]
                    if todo:

                        @pl.when(b == i)
                        def _():
                            for step, of in todo:
                                steps[step - 1](of)
            else:
                whole = zip(sums, (r.f_fc1, r.f_fc2) if half else (r.f_qkv, r.f_proj))
                copies = [pltpu.make_async_copy(g, o.at[b], r.go_sem.at[half, i]) for i, (g, o) in enumerate(whole)]
                start(copies)
                wait(copies)

    if linked:
        step_1(4)
        step_2(0)
    push_section(0, canvases - 1)
    if linked:
        step_2(4)
        step_4(1)
        smalls_sent(1)
        step_5(1)
        for step in (step_3, step_4, step_5):
            step(0)
            step(4)
        reductions_done()
        weights_sent()
        for k in range(1, 8):
            pack_copy(k).wait_send()
    for k in range(1, 4):
        for n in range(canvases):
            arrived(k, n)
    for n in range(canvases):
        pushed(n)


def compute(linked, operands):
    canvases = operands["x_hbm"].shape[1]
    shape = jax.ShapeDtypeStruct
    hbm = pl.BlockSpec(memory_space=pl.ANY)
    vmem = pl.BlockSpec(memory_space=pltpu.VMEM)
    dma = pltpu.SemaphoreType.DMA
    full = {
        "wat": ((2, D, 4 * D), BF),
        "fc1": ((2, D, FF), BF),
        "fc2": ((2, FF, D), BF),
        "vec": ((2, 8, FF), F32),
    }
    grads = {
        "g_qkv": ((D, 3 * D), F32),
        "g_proj": ((D, D), F32),
        "g_fc1": ((D, FF), F32),
        "g_fc2": ((FF, D), F32),
        "g_vec": ((2, 8, 8, FF), F32),
        "g_tab": ((2, 2 * PLACES, GROUPS * 128), F32),
    }
    outs = {"act_hbm": ((4, canvases, CELLS, D), BF), "igrad_hbm": ((4, canvases, CELLS, D), BF)}
    kept = {
        "hqw": ((canvases, WROWS, D), BF),
        "qkv": ((canvases, WROWS, 3 * D), BF),
        "probs": ((canvases, WINDOWS * GROUPS, 128, 128), BF),
        "att": ((canvases, WROWS, D), BF),
        "hq2": ((canvases, CELLS, D), BF),
        "hid": ((canvases, CELLS, FF), BF),
        "dgelu": ((canvases, CELLS, FF), BF),
    }
    outs |= {"h_" + name: kind for name, kind in kept.items()}
    scratch = kept | {
        "code": ((canvases, CELLS, 128), jnp.int32),
        "codew": ((WROWS, 128), jnp.int32),
        "buf": ((6, canvases, CELLS, D), BF),
        "canvf": ((CELLS, D), F32),
        "winf": ((WROWS, D), F32),
        "gzw": ((WROWS, D), BF),
        "go": ((WROWS, D), BF),
        "gqkv": ((WROWS, 3 * D), BF),
    }
    sems = {
        "in_sem": (2, canvases),
        "code_sem": (1,),
        "st_sem": (2, canvases, 4),
        "local_sem": (2, canvases),
        "act_send": (3, canvases),
        "act_recv": (3, canvases),
        "ig_send": (3, canvases),
        "ig_recv": (3, canvases),
    }
    if linked:
        outs |= {
            "o_qkv": ((2, 48, 3 * D), F32),
            "o_proj": ((2, 48, D), F32),
            "o_fc1": ((2, 48, FF), F32),
            "o_fc2": ((2, 192, D), F32),
            "o_small": ((2, 8, 64, D), BF),
        }
        scratch |= full | grads
        scratch |= {
            "packs": ((8, 16, 256), BF),
            "l_qkv": ((48, 3 * D), F32),
            "l_proj": ((48, D), F32),
            "l_fc1": ((48, FF), F32),
            "l_fc2": ((192, D), F32),
        }
        for kind, rows in ((kind + "_", rows) for kind, rows in ROWS.items()):
            scratch |= {
                kind + "st_a": ((4, rows, D), BF),
                kind + "rc_a": ((4, rows, D), BF),
                kind + "st_b": ((3, rows, D), BF),
                kind + "rc_b": ((3, rows, D), BF),
                kind + "st_c": ((rows, D), BF),
                kind + "rc_c": ((3, rows // 4, D), BF),
                kind + "fin": ((rows, D), BF),
            }
        sems |= {
            "sh_sem": (4, 2),
            "os_sem": (2,),
            "go_sem": (4, 2),
            "wz_send": (4, 2, 3),
            "wz_recv": (4, 2, 3),
            "wx_send": (4, 2, 3, 3),
            "wx_recv": (4, 2, 3, 3),
            "ws_send": (4, 2, 4),
            "ws_recv": (4, 2, 4),
            "pk_send": (7,),
            "pk_recv": (7,),
            "ra_send": (6,),
            "ra_recv": (6,),
            "rb_send": (6, 3),
            "rb_recv": (6, 3),
            "rc_send": (6, 3),
            "rc_recv": (6, 3),
            "rf_send": (6, 3),
            "rf_recv": (6, 3),
            "rs_send": (2, 7),
            "rs_recv": (2, 7),
        }
    else:
        for name in ("g_vec", "g_tab"):
            outs[name] = grads.pop(name)
        outs |= {name.replace("g_", "f_"): ((2,) + dims, F32) for name, (dims, _) in grads.items()}
        scratch |= grads
        sems["go_sem"] = (4, 2)
    in_vmem = set(full) | {"bias", "pack", "g_vec", "g_tab"}
    names = tuple(operands) + tuple(outs) + tuple(scratch) + tuple(sems)
    results = pl.pallas_call(
        functools.partial(kernel, names, linked, canvases),
        out_shape=tuple(shape(*o) for o in outs.values()),
        in_specs=[vmem if name in in_vmem else hbm for name in operands],
        out_specs=tuple(vmem if name in in_vmem else hbm for name in outs),
        scratch_shapes=[pltpu.VMEM(*v) for v in scratch.values()] + [dma(v) for v in sems.values()],
        compiler_params=pltpu.CompilerParams(
            vmem_limit_bytes=64 * 1024 * 1024 - 65536, collective_id=0, has_side_effects=True
        ),
    )(*operands.values())
    return dict(zip(outs, results))


def place_pairs():
    place = np.arange(PLACES)
    r, c = place // 8, place % 8
    index = (r[None, :] - r[:, None] + WIN - 1) * (2 * WIN - 1) + c[None, :] - c[:, None] + WIN - 1
    real = (r < WIN) & (c < WIN)
    return index, real[:, None] & real[None, :], real


def pair_onehot():
    index, both, _ = place_pairs()
    table = (2 * WIN - 1) ** 2
    hot = (np.where(both, index, -1).reshape(-1)[None, :] == np.arange(table)[:, None])
    return hot.astype(np.float32)


def body(
    inputs,
    cotangent,
    pad_mask,
    region_ids,
    norm1_gain,
    norm1_bias,
    qkv_weight,
    qv_bias,
    rel_table,
    proj_weight,
    proj_bias,
    norm2_gain,
    norm2_bias,
    fc1_weight,
    fc1_bias,
    fc2_weight,
    fc2_bias,
):
    owners = lax.axis_size("dp")
    linked = owners == 8
    mine = lax.axis_index("pipe")

    def own(a):
        return lax.dynamic_index_in_dim(a, mine, 0, keepdims=False)

    code = own(region_ids) * 2 + own(pad_mask)
    code = jnp.broadcast_to(code[:, :, None], code.shape + (128,))

    hot = pair_onehot()
    _, _, real = place_pairs()
    rel = lax.dot_general(
        rel_table.astype(BF), jnp.asarray(hot, BF), (((1,), (0,)), ((), ())), preferred_element_type=F32
    )
    rel = rel.reshape(2, GROUPS, 2, 2, PLACES, PLACES)
    rel = jnp.where(jnp.asarray(real)[None, None, None, None, :, None], rel, MASKED)
    rel = rel.transpose(0, 1, 3, 4, 2, 5).reshape(2, GROUPS, 128, 128)

    operands = {"x_hbm": inputs, "cot_hbm": cotangent, "code_hbm": code, "bias": rel}
    vectors = (norm1_gain, norm1_bias, proj_bias, norm2_gain, norm2_bias, fc2_bias, qv_bias, fc1_bias)
    sizes = [v.shape[1] for v in vectors]
    ends = np.cumsum([0] + sizes)
    if linked:
        pack = jnp.stack([jnp.pad(v, ((0, 0), (0, 256 - v.shape[1]))) for v in vectors], axis=1)
        operands |= {
            "pack": pack.reshape(16, 256).astype(BF),
            "s_qkv": qkv_weight,
            "s_proj": proj_weight,
            "s_fc1": fc1_weight,
            "s_fc2": fc2_weight,
        }
    else:

        def gathered(a):
            return lax.all_gather(a.astype(BF), "dp", axis=1, tiled=True)

        packed = lax.all_gather(jnp.concatenate(vectors, axis=1).astype(BF), "dp", axis=1)
        parts = [packed[:, :, a:b].reshape(2, -1).astype(F32) for a, b in zip(ends[:-1], ends[1:])]
        qv = parts[6]
        parts[6] = jnp.concatenate([qv[:, :D], jnp.zeros_like(qv[:, :D]), qv[:, D:]], axis=1)
        vec = jnp.stack([jnp.pad(p, ((0, 0), (0, FF - p.shape[1]))) for p in parts], axis=1)
        operands |= {
            "wat": jnp.concatenate([gathered(qkv_weight), gathered(proj_weight)], axis=2),
            "fc1": gathered(fc1_weight),
            "fc2": gathered(fc2_weight),
            "vec": vec,
        }

    out = compute(linked, operands)

    def to_owners(g):
        shared = lax.psum_scatter(g, "dp", scatter_dimension=1, tiled=True)
        return lax.psum(shared, "pipe")

    if linked:
        small = out["o_small"]
        g_tab = small[:, :, :16].reshape(2, 128, GROUPS * 128)
        g_vec = jnp.concatenate([small[:, :, 16 + 8 * j : 24 + 8 * j] for j in range(4)], axis=3)
    else:
        g_tab, g_vec = out["g_tab"], out["g_vec"]

    g_vec = jnp.sum(g_vec.astype(F32), axis=2)
    kinds = [g_vec[:, i] for i in range(8)]
    qv_sum = jnp.concatenate([kinds[6][:, :D], kinds[6][:, 2 * D : 3 * D]], axis=1)
    rows = [kinds[0], kinds[1], kinds[2], kinds[3], kinds[4], kinds[5], qv_sum, kinds[7]]
    if linked:
        at = lax.axis_index("dp")
        small = [lax.dynamic_slice_in_dim(v, at * n, n, 1) for v, n in zip(rows, sizes)]
    else:
        rows = [v[:, : n * owners].reshape(2, -1, n) for v, n in zip(rows, sizes)]
        g_small = to_owners(jnp.concatenate(rows, axis=2))[:, 0]
        small = [g_small[:, a:b] for a, b in zip(ends[:-1], ends[1:])]

    pairs = g_tab.reshape(2, 2, PLACES, GROUPS, 2, PLACES).transpose(0, 3, 4, 1, 2, 5)
    pairs = pairs.reshape(2, HEADS, PLACES * PLACES)
    g_table = lax.dot_general(
        jnp.broadcast_to(jnp.asarray(hot, pairs.dtype), (2,) + hot.shape),
        pairs,
        (((2,), (2,)), ((0,), (0,))),
        precision=None if linked else lax.Precision.HIGHEST,
        preferred_element_type=F32,
    )
    if linked:
        big = [out[name] for name in ("o_qkv", "o_proj", "o_fc1", "o_fc2")]
    else:
        g_table = lax.psum(g_table, ("pipe", "dp"))
        big = [to_owners(out[name]) for name in ("f_qkv", "f_proj", "f_fc1", "f_fc2")]

    return (
        out["act_hbm"][None],
        out["igrad_hbm"][None],
        small[0],
        small[1],
        big[0],
        small[6],
        g_table,
        big[1],
        small[2],
        small[3],
        small[4],
        big[2],
        small[7],
        big[3],
        small[5],
    )


def solution(mesh):
    cols = P(None, "dp")
    rows = P(None, "dp", None)
    return jax.shard_map(
        body,
        mesh=mesh,
        in_specs=(
            P(None, "dp", None, None),
            P(None, "dp", None, None),
            rows,
            rows,
            cols,
            cols,
            rows,
            cols,
            P(),
            rows,
            cols,
            cols,
            cols,
            rows,
            cols,
            rows,
            cols,
        ),
        out_specs=(
            P("pipe", None, "dp", None, None),
            P("pipe", None, "dp", None, None),
            cols,
            cols,
            rows,
            cols,
            P(),
            rows,
            cols,
            cols,
            cols,
            rows,
            cols,
            rows,
            cols,
        ),
        check_vma=False,
    )
```

```python
import functools
import types

import jax
import jax.numpy as jnp
import numpy as np
from jax import lax
from jax.experimental import pallas as pl
from jax.experimental.pallas import tpu as pltpu
from jax.sharding import PartitionSpec as P

HEADS = 12
WIN = 7
SHIFT = 3
GRID = 28
CELLS = 784
D = 384
FF = 1536
HEAD = 32
SIDE = 4
WINDOWS = 16
PLACES = 64
WROWS = WINDOWS * PLACES
GROUPS = 3
TILE = 112
SCALE = HEAD**-0.5
NORM_EPS = 1e-05
MASKED = -1e30
BF = jnp.bfloat16
F32 = jnp.float32

RSQRT_2 = 1.0 / np.sqrt(2.0)
PHI_0 = 1.0 / np.sqrt(2.0 * np.pi)


def nn(a, b):
    return lax.dot_general(a, b, (((1,), (0,)), ((), ())), preferred_element_type=F32)


def nt(a, b):
    return lax.dot_general(a, b, (((1,), (1,)), ((), ())), preferred_element_type=F32)


def tn(a, b):
    return lax.dot_general(a, b, (((0,), (0,)), ((), ())), preferred_element_type=F32)


def segments(shift):
    runs = []
    for wr in range(SIDE):
        for r in range(WIN):
            row = (wr * WIN + r + shift) % GRID
            for wc in range(SIDE):
                col = (wc * WIN + shift) % GRID
                place = (wr * SIDE + wc) * PLACES + r * 8
                first = min(WIN, GRID - col)
                runs.append((row * GRID + col, place, first))
                if first < WIN:
                    runs.append((row * GRID, place + first, WIN - first))
    return runs


def to_windows(src, dst, shift):
    for cell, place, count in segments(shift):
        dst[pl.ds(place, count), :] = src[pl.ds(cell, count), :]


def to_canvas(src, dst, shift):
    for cell, place, count in segments(shift):
        dst[pl.ds(cell, count), :] = src[pl.ds(place, count), :]


def row_block(t, size):
    return pl.ds(pl.multiple_of(t * size, 16), size)


def standardized(v):
    centered = v - jnp.mean(v, axis=-1, keepdims=True)
    spread = jnp.mean(centered * centered, axis=-1, keepdims=True)
    rs = lax.rsqrt(spread + NORM_EPS)
    return centered * rs, rs


def by_eights(v):
    return jnp.sum(v.reshape(v.shape[0] // 8, 8, v.shape[1]), axis=0)


def gelu_parts(x):
    cdf = 0.5 + 0.5 * lax.erf(x * RSQRT_2)
    return x * cdf, cdf + x * (jnp.exp(-0.5 * x * x) * PHI_0)


def real_places(rows):
    place = lax.broadcasted_iota(jnp.int32, (rows, 1), 0)
    return ((place & 7) < WIN) & (((place >> 3) & 7) < WIN)


def head_of_lane():
    return lax.broadcasted_iota(jnp.int32, (PLACES, 128), 1) >> 5


def by_low(x, lanes):
    zero = jnp.zeros_like(x)
    return jnp.concatenate([jnp.where((lanes & 1) == h, x, zero) for h in range(2)], axis=0)


def by_high(x, lanes):
    zero = jnp.zeros_like(x)
    return jnp.concatenate([jnp.where((lanes >> 1) == h, x, zero) for h in range(2)], axis=0)


def own_low(wide, lanes):
    return jnp.where((lanes & 1) == 0, wide[:PLACES], wide[PLACES:])


def own_high(wide, lanes):
    return jnp.where((lanes >> 1) == 0, wide[:PLACES], wide[PLACES:])


MESH = pl.DeviceIdType.MESH
KINDS = ("a", "m", "a", "m", "t", "t")
ROWS = {"a": 192, "m": 384, "t": 64}
BLOCK = (0, 0, 1, 1, 0, 1)
BEFORE = {0: 2, 1: 3, 4: 5}


def kernel(names, linked, canvases, *refs):
    r = types.SimpleNamespace(**dict(zip(names, refs)))
    me = lax.axis_index("pipe")
    code, codew, buf = r.code, r.codew, r.buf
    hqw, qkv, probs, att = r.hqw, r.qkv, r.probs, r.att
    hq2, hid, dgelu = r.hq2, r.hid, r.dgelu
    canvf, winf, gzw, gqkv, go = r.canvf, r.winf, r.gzw, r.gqkv, r.go
    g_qkv, g_proj, g_fc1, g_fc2, g_vec, g_tab = r.g_qkv, r.g_proj, r.g_fc1, r.g_fc2, r.g_vec, r.g_tab
    wat, fc1, fc2, vec, bias = r.wat, r.fc1, r.fc2, r.vec, r.bias
    if linked:
        d = lax.axis_index("dp")
        z, c = d // 2, d % 2
        sibling = {"dp": 2 * z + 1 - c}

    def z_peer(k):
        return {"dp": 2 * lax.rem(z + k, 4) + c}

    def pipe_peer(k):
        return {"pipe": lax.rem(me + k, 4)}

    def dp_peer(k):
        return {"dp": lax.rem(d + k, 8)}

    def remote(src, dst, send, recv, device):
        return pltpu.make_async_remote_copy(
            src_ref=src, dst_ref=dst, send_sem=send, recv_sem=recv, device_id=device, device_id_type=MESH
        )

    barrier = pltpu.get_barrier_semaphore()
    partners = [pipe_peer(k) for k in range(1, 4)]
    if linked:
        partners += [dp_peer(k) for k in range(1, 8)]
    for partner in partners:
        pl.semaphore_signal(barrier, inc=1, device_id=partner, device_id_type=MESH)

    full = ((wat,), (fc1, fc2), (wat,), (fc1, fc2))

    def owner_back(k):
        return 2 * lax.rem(z + 4 - k, 4) + c

    def shard(sec, a, owner):
        h = 192 if a else 48
        return full[sec][a].at[sec // 2, pl.ds(pl.multiple_of(owner * h, 16), h), :]

    def part(sec, a, owner, place):
        if a:
            return fc2.at[sec // 2, pl.ds(pl.multiple_of(owner * 192 + place * 48, 16), 48), :]
        rows = pl.ds(pl.multiple_of(owner * 48, 16), 48)
        return full[sec][0].at[sec // 2, rows, pl.ds(pl.multiple_of(place * D, 128), D)]

    def to_z(sec, a, k):
        own = part(sec, a, d, me)
        return remote(own, own, r.wz_send.at[sec, a, k - 1], r.wz_recv.at[sec, a, k - 1], z_peer(k))

    def to_places(sec, a, k, j):
        got = part(sec, a, owner_back(k), me)
        return remote(
            got, got, r.wx_send.at[sec, a, k - 1, j - 1], r.wx_recv.at[sec, a, k - 1, j - 1], pipe_peer(j)
        )

    def to_sibling(sec, a, k):
        block = shard(sec, a, owner_back(k))
        return remote(block, block, r.ws_send.at[sec, a, k], r.ws_recv.at[sec, a, k], sibling)

    def weights_1(sec):
        for a in range(len(full[sec])):
            for k in range(1, 4):
                to_z(sec, a, k).start()
            to_sibling(sec, a, 0).start()

    def weights_2(sec):
        for k in range(1, 4):
            for a in range(len(full[sec])):
                got = part(sec, a, owner_back(k), me)
                remote(got, got, r.wz_send.at[sec, a, k - 1], r.wz_recv.at[sec, a, k - 1], z_peer(k)).wait_recv()
                for j in range(1, 4):
                    to_places(sec, a, k, j).start()

    def weights_3(sec):
        for k in range(1, 4):
            for a in range(len(full[sec])):
                for j in range(1, 4):
                    got = part(sec, a, owner_back(k), lax.rem(me + 4 - j, 4))
                    remote(
                        got, got, r.wx_send.at[sec, a, k - 1, j - 1], r.wx_recv.at[sec, a, k - 1, j - 1], pipe_peer(j)
                    ).wait_recv()
                to_sibling(sec, a, k).start()

    def weights_4(sec):
        for k in range(4):
            for a in range(len(full[sec])):
                block = shard(sec, a, 2 * lax.rem(z + 4 - k, 4) + 1 - c)
                remote(block, block, r.ws_send.at[sec, a, k], r.ws_recv.at[sec, a, k], sibling).wait_recv()

    def weights_sent():
        for sec in range(4):
            for a in range(len(full[sec])):
                for k in range(4):
                    to_sibling(sec, a, k).wait_send()
                    if k:
                        to_z(sec, a, k).wait_send()
                        for j in range(1, 4):
                            to_places(sec, a, k, j).wait_send()

    def pack_copy(k):
        return remote(
            r.packs.at[d], r.packs.at[d], r.pk_send.at[k - 1], r.pk_recv.at[k - 1], dp_peer(k)
        )

    def pack_arrival(k):
        slot = r.packs.at[lax.rem(d + 8 - k, 8)]
        return remote(slot, slot, r.pk_send.at[k - 1], r.pk_recv.at[k - 1], dp_peer(k))

    def place_vectors():
        kind = lax.broadcasted_iota(jnp.int32, (16, 256), 0) & 7
        lane = lax.broadcasted_iota(jnp.int32, (16, 256), 1)
        vec[...] = jnp.zeros_like(vec)
        for width, kinds in ((48, kind < 6), (96, kind == 6), (192, kind == 7)):
            for owner in range(8):
                at = owner * width
                if width == 96 and owner >= 4:
                    at += D
                start = at // 128 * 128
                part = jnp.where(kinds & (lane < width), r.packs[owner].astype(F32), 0.0)
                if at > start:
                    part = pltpu.roll(part, at - start, 1)
                for b in range(2):
                    vec[b, :, start : start + 256] += part[8 * b : 8 * b + 8]

    def pieces(sec, owner):
        b = BLOCK[sec]
        out = []

        def matrix(ref, h):
            for t in range(h // 48):
                rows = pl.ds(pl.multiple_of(owner * h + t * 48, 16), 48)
                for j in range(ref.shape[1] // D):
                    load = functools.partial(lambda ref, rows, j: ref[rows, j * D : (j + 1) * D], ref, rows, j)
                    out.append((len(out) * 48, 48, load))

        def small():
            parts = [g_tab[b, pl.ds(pl.multiple_of(owner * 16, 16), 16), :]]
            parts += [g_vec[b, owner, :, j * D : (j + 1) * D] for j in range(4)]
            return jnp.concatenate(parts + [jnp.zeros((16, D), F32)], axis=0)

        if KINDS[sec] == "m":
            matrix(g_fc1, 48)
            matrix(g_fc2, 192)
        elif KINDS[sec] == "a":
            matrix(g_qkv, 48)
            matrix(g_proj, 48)
        else:
            out.append((0, 64, small))
        return out

    def reduce_refs(sec):
        kind = KINDS[sec]
        return types.SimpleNamespace(
            **{n: getattr(r, kind + "_" + n) for n in ("st_a", "rc_a", "st_b", "rc_b", "st_c", "rc_c", "fin")}
        )

    def step_1(sec):
        q = reduce_refs(sec)
        if sec in BEFORE:
            copy_a(BEFORE[sec]).wait_send()
            for k in range(1, 4):
                copy_b(BEFORE[sec], k).wait_send()
                copy_c(BEFORE[sec], k).wait_send()
        for k in range(4):
            i = lax.rem(z + k, 4)
            kept = q.st_b.at[k - 1] if k else q.st_c
            for row, rows, load in pieces(sec, 2 * i + 1 - c):
                q.st_a[i, row : row + rows, :] = load().astype(BF)
            for row, rows, load in pieces(sec, 2 * i + c):
                kept[row : row + rows, :] = load().astype(BF)
        copy_a(sec).start()

    def copy_a(sec):
        q = reduce_refs(sec)
        return remote(q.st_a, q.rc_a, r.ra_send.at[sec], r.ra_recv.at[sec], sibling)

    def copy_b(sec, k):
        q = reduce_refs(sec)
        return remote(
            q.st_b.at[k - 1], q.rc_b.at[k - 1], r.rb_send.at[sec, k - 1], r.rb_recv.at[sec, k - 1], z_peer(k)
        )

    def step_2(sec):
        q = reduce_refs(sec)
        copy_a(sec).wait_recv()
        for k in (1, 2, 3, 0):
            i = lax.rem(z + k, 4)
            kept = q.st_b.at[k - 1] if k else q.st_c
            for row in range(0, kept.shape[0], 64):
                at = slice(row, row + 64)
                kept[at, :] = (kept[at, :].astype(F32) + q.rc_a[i, at, :].astype(F32)).astype(BF)
            if k:
                copy_b(sec, k).start()

    def quarter(sec, ref, who):
        rows = ROWS[KINDS[sec]] // 4
        return ref.at[pl.ds(pl.multiple_of(who * rows, 16), rows), :]

    def copy_c(sec, k):
        q = reduce_refs(sec)
        return remote(
            quarter(sec, q.st_c, lax.rem(me + k, 4)),
            q.rc_c.at[k - 1],
            r.rc_send.at[sec, k - 1],
            r.rc_recv.at[sec, k - 1],
            pipe_peer(k),
        )

    def step_3(sec):
        q = reduce_refs(sec)
        for k in range(1, 4):
            copy_b(sec, k).wait_recv()
        for row in range(0, q.st_c.shape[0], 64):
            at = slice(row, row + 64)
            total = q.st_c[at, :].astype(F32)
            for k in range(3):
                total = total + q.rc_b[k, at, :].astype(F32)
            q.st_c[at, :] = total.astype(BF)
        for k in range(1, 4):
            copy_c(sec, k).start()

    def copy_f(sec, k):
        q = reduce_refs(sec)
        own = quarter(sec, q.fin, me)
        return remote(own, own, r.rf_send.at[sec, k - 1], r.rf_recv.at[sec, k - 1], pipe_peer(k))

    def step_4(sec):
        q = reduce_refs(sec)
        for k in range(1, 4):
            copy_c(sec, k).wait_recv()
            if sec in BEFORE:
                copy_f(BEFORE[sec], k).wait_send()
        total = quarter(sec, q.st_c, me)[...].astype(F32)
        for k in range(3):
            total = total + q.rc_c[k].astype(F32)
        quarter(sec, q.fin, me)[...] = total.astype(BF)
        for k in range(1, 4):
            copy_f(sec, k).start()

    def copy_s(b, k):
        return remote(r.t_fin, r.o_small.at[b, d], r.rs_send.at[b, k - 1], r.rs_recv.at[b, k - 1], dp_peer(k))

    def own_small(b):
        return pltpu.make_async_copy(r.t_fin, r.o_small.at[b, d], r.os_sem.at[b])

    def outputs(sec):
        pairs = ((r.l_fc1, r.o_fc1), (r.l_fc2, r.o_fc2)) if sec % 2 else ((r.l_qkv, r.o_qkv), (r.l_proj, r.o_proj))
        return [
            pltpu.make_async_copy(ref, out.at[sec // 2], r.go_sem.at[sec, i]) for i, (ref, out) in enumerate(pairs)
        ]

    def step_5(sec):
        q = reduce_refs(sec)
        for k in range(1, 4):
            got = quarter(sec, q.fin, lax.rem(me + 4 - k, 4))
            remote(got, got, r.rf_send.at[sec, k - 1], r.rf_recv.at[sec, k - 1], pipe_peer(k)).wait_recv()
        if sec >= 4:
            for k in range(1, 8):
                copy_s(BLOCK[sec], k).start()
            own_small(BLOCK[sec]).start()
            return
        if sec < 2:
            for out in outputs(sec + 2):
                out.wait()
        row = 0
        for ref in (r.l_fc1, r.l_fc2) if sec % 2 else (r.l_qkv, r.l_proj):
            for t in range(ref.shape[0] // 48):
                for j in range(ref.shape[1] // D):
                    ref[t * 48 : (t + 1) * 48, j * D : (j + 1) * D] = q.fin[row : row + 48, :].astype(F32)
                    row += 48
        for out in outputs(sec):
            out.start()

    def smalls_sent(b):
        for k in range(1, 8):
            copy_s(b, k).wait_send()
        own_small(b).wait()

    def reductions_done():
        for sec in BEFORE:
            copy_a(sec).wait_send()
            for k in range(1, 4):
                copy_b(sec, k).wait_send()
                copy_c(sec, k).wait_send()
                copy_f(sec, k).wait_send()
        for sec in range(2):
            for out in outputs(sec):
                out.wait()
        smalls_sent(0)
        for b in range(2):
            for k in range(1, 8):
                remote(
                    r.t_fin,
                    r.o_small.at[b, lax.rem(d + 8 - k, 8)],
                    r.rs_send.at[b, k - 1],
                    r.rs_recv.at[b, k - 1],
                    dp_peer(k),
                ).wait_recv()

    if linked:
        lands = ((r.s_qkv, g_qkv, wat, 0), (r.s_proj, g_proj, wat, 3 * D), (r.s_fc1, g_fc1, fc1, 0), (r.s_fc2, g_fc2, fc2, 0))

        def landing(i, b):
            src, dst, _, _ = lands[i]
            h, n = src.shape[1:]
            return pltpu.make_async_copy(
                src.at[b], dst.at[pl.ds(192 * b, h), pl.ds(0, n)], r.sh_sem.at[i, b]
            )

        for i in range(4):
            for b in range(2):
                landing(i, b).start()
        r.packs[d] = r.pack[...]
        for i, (src, dst, ref, col) in enumerate(lands):
            h, n = src.shape[1:]
            for b in range(2):
                landing(i, b).wait()
                for t in range(0, h, 48):
                    rows = pl.ds(pl.multiple_of(d * h + t, 16), 48)
                    ref[b, rows, col : col + n] = dst[192 * b + t : 192 * b + t + 48, :n].astype(BF)
    pl.semaphore_wait(barrier, len(partners))
    if linked:
        for k in range(1, 8):
            pack_copy(k).start()
        weights_1(0)

    def cleared(*refs):
        for ref in refs:

            @pl.loop(0, ref.shape[0] // 16)
            def _(i):
                ref[row_block(i, 16), :] = jnp.zeros((16, ref.shape[1]), F32)

    g_vec[...] = jnp.zeros_like(g_vec)
    g_tab[...] = jnp.zeros_like(g_tab)
    codew[...] = jnp.zeros_like(codew)

    if linked:
        weights_2(0)
        for sec in range(1, 4):
            weights_1(sec)
        for k in range(1, 8):
            pack_arrival(k).wait_recv()
        place_vectors()

    def vector(b, kind, width=D):
        return vec[b, kind : kind + 1, :width]

    def add_vec(b, kind, part):
        g_vec[b, kind, :, : part.shape[1]] += part

    def windowed(rows, count):
        return jnp.where(real_places(count), winf[rows, :], 0.0).astype(BF)

    def by_block(b, move):
        for i in range(2):

            @pl.when(b == i)
            def _():
                move(SHIFT * i)

    def attention_forward(b, n, x, out, hook):
        lanes = head_of_lane()

        @pl.loop(0, CELLS // TILE)
        def _(t):
            rows = row_block(t, TILE)
            xhat, _ = standardized(x[rows, :].astype(F32))
            canvf[rows, :] = xhat * vector(b, 0) + vector(b, 1)

        def arrange(shift):
            to_windows(canvf, winf, shift)
            to_windows(code.at[n], codew, shift)

        by_block(b, arrange)
        hook(4)

        @pl.loop(0, 4)
        def _(t):
            rows = row_block(t, 256)
            hq = windowed(rows, 256)
            hqw[n, rows, :] = hq
            for part in range(3):
                cols = slice(part * D, (part + 1) * D)
                acc = nn(hq, wat[b, :, cols]) + vec[b, 6:7, cols]
                if part == 0:
                    acc = acc * SCALE
                qkv[n, rows, cols] = acc.astype(BF)

        hook(0)

        @pl.loop(0, WINDOWS)
        def _(w):
            rows = row_block(w, PLACES)
            cells = codew[rows, :]
            region = (cells >> 1) * b
            pad = (cells & 1).astype(F32)
            lane = lax.broadcasted_iota(jnp.int32, (PLACES, 128), 1)
            same = jnp.where(lane == region, 1.0, 0.0)
            left = jnp.where(lane == 127, 1.0 - pad, same).astype(BF)
            right = jnp.where(lane == 127, -pad, same).astype(BF)
            agree = nt(left, jnp.concatenate([right, right], axis=0))
            mask = jnp.where(agree > 0.5, 0.0, MASKED)
            for g in range(GROUPS):
                q = qkv[n, rows, g * 128 : (g + 1) * 128]
                k = qkv[n, rows, D + g * 128 : D + (g + 1) * 128]
                v = qkv[n, rows, 2 * D + g * 128 : 2 * D + (g + 1) * 128]
                scores = nt(by_low(k, lanes), by_high(q, lanes)) + bias[b, g]
                halves = []
                for h in range(2):
                    s = scores[h * PLACES : (h + 1) * PLACES] + mask
                    e = jnp.exp(s - jnp.max(s, axis=0, keepdims=True))
                    halves.append((e * (1.0 / jnp.sum(e, axis=0, keepdims=True))).astype(BF))
                p = jnp.concatenate(halves, axis=0)
                probs[n, w * GROUPS + g] = p
                att[n, rows, g * 128 : (g + 1) * 128] = own_high(tn(p, by_low(v, lanes)), lanes).astype(BF)

        hook(1)

        @pl.loop(0, 4)
        def _(t):
            rows = row_block(t, 256)
            winf[rows, :] = nn(att[n, rows, :], wat[b, :, 3 * D :])

        by_block(b, functools.partial(to_canvas, winf, canvf))

        @pl.loop(0, CELLS // TILE)
        def _(t):
            rows = row_block(t, TILE)
            out[rows, :] = (x[rows, :].astype(F32) + (canvf[rows, :] + vector(b, 2))).astype(BF)

    def mlp_forward(b, n, x, out, hook):
        @pl.loop(0, CELLS // TILE)
        def _(t):
            rows = row_block(t, TILE)
            xhat, _ = standardized(x[rows, :].astype(F32))
            hq2[n, rows, :] = (xhat * vector(b, 3) + vector(b, 4)).astype(BF)

        @pl.loop(0, FF // 256)
        def _(i):
            cols = pl.ds(pl.multiple_of(i * 256, 256), 256)
            pre = nn(hq2[n], fc1[b, :, cols]) + vec[b, 7:8, cols]
            for at in range(0, CELLS, 16):
                h, dg = gelu_parts(pre[at : at + 16])
                hid[n, at : at + 16, cols] = h.astype(BF)
                dgelu[n, at : at + 16, cols] = dg.astype(BF)

        hook(0)
        total = nn(hid[n], fc2[b])
        for at in range(0, CELLS, TILE):
            rows = slice(at, at + TILE)
            out[rows, :] = (x[rows, :].astype(F32) + (total[rows] + vector(b, 5))).astype(BF)

    def norm_backward(b, kind, x, gz, out):
        @pl.loop(0, CELLS // TILE)
        def _(t):
            rows = row_block(t, TILE)
            xhat, rs = standardized(x[rows, :].astype(F32))
            gn = canvf[rows, :]
            gzf = gz[rows, :].astype(F32)
            add_vec(b, kind, by_eights(gn * xhat))
            add_vec(b, kind + 1, by_eights(gn))
            add_vec(b, 5 if kind else 2, by_eights(gzf))
            g = gn * vector(b, kind)
            mg = jnp.mean(g, axis=-1, keepdims=True)
            mgx = jnp.mean(g * xhat, axis=-1, keepdims=True)
            out[rows, :] = (gzf + rs * (g - mg - xhat * mgx)).astype(BF)

    def mlp_backward(b, n, x, gz, out, free_out, hook):
        @pl.loop(0, FF // 256)
        def _(i):
            cols = pl.ds(pl.multiple_of(i * 256, 256), 256)
            gh = nt(gz[...], fc2[b, cols, :])
            sums = jnp.zeros((8, 256), F32)
            for at in range(0, CELLS, 16):
                gp = (gh[at : at + 16] * dgelu[n, at : at + 16, cols].astype(F32)).astype(BF)
                dgelu[n, at : at + 16, cols] = gp
                sums = sums + by_eights(gp.astype(F32))
            g_vec[b, 7, :, cols] += sums
            g_fc1[:, cols] += tn(hq2[n], dgelu[n, :, cols])
            g_fc2[cols, :] += tn(hid[n, :, cols], gz[...])

        hook(0)
        canvf[...] = nt(dgelu[n], fc1[b])
        free_out()
        norm_backward(b, 3, x, gz, out)

    def attention_backward(b, n, x, gz, out, free_out, hook):
        lanes = head_of_lane()

        @pl.loop(0, CELLS // TILE)
        def _(t):
            rows = row_block(t, TILE)
            canvf[rows, :] = gz[rows, :].astype(F32)

        by_block(b, functools.partial(to_windows, canvf, winf))

        @pl.loop(0, 4)
        def _(t):
            rows = row_block(t, 256)
            gzw[rows, :] = windowed(rows, 256)

        g_proj[...] += tn(att[n], gzw[...])

        @pl.loop(0, 4)
        def _(t):
            rows = row_block(t, 256)
            go[rows, :] = nt(gzw[rows, :], wat[b, :, 3 * D :]).astype(BF)

        hook(0)

        @pl.loop(0, WINDOWS)
        def _(w):
            rows = row_block(w, PLACES)
            for g in range(GROUPS):
                at = [slice(part * D + g * 128, part * D + (g + 1) * 128) for part in range(3)]
                q, k, v = (qkv[n, rows, cols] for cols in at)
                go_wide = by_high(go[rows, at[0]], lanes)
                p_low = probs[n, w * GROUPS + g]
                p = p_low.astype(F32)
                pd = p * nt(by_low(v, lanes), go_wide)
                halves = []
                for h in range(2):
                    half = slice(h * PLACES, (h + 1) * PLACES)
                    halves.append((pd[half] - p[half] * jnp.sum(pd[half], axis=0, keepdims=True)).astype(BF))
                ds = jnp.concatenate(halves, axis=0)
                g_tab[b, :, g * 128 : (g + 1) * 128] += ds.astype(F32)
                gqkv[rows, at[0]] = (own_high(tn(ds, by_low(k, lanes)), lanes) * SCALE).astype(BF)
                gqkv[rows, at[1]] = own_low(nn(ds, by_high(q, lanes)), lanes).astype(BF)
                gqkv[rows, at[2]] = own_low(nn(p_low, go_wide), lanes).astype(BF)

        hook(1)
        attention_weights(n)
        hook(2)

        @pl.loop(0, 4)
        def _(t):
            rows = row_block(t, 256)
            gq = gqkv[rows, :]
            add_vec(b, 6, by_eights(gq.astype(F32)))
            winf[rows, :] = nt(gq, wat[b, :, : 3 * D])

        by_block(b, functools.partial(to_canvas, winf, canvf))
        free_out()
        norm_backward(b, 0, x, gz, out)

    def attention_weights(n):
        @pl.loop(0, 3)
        def _(part):
            cols = pl.ds(pl.multiple_of(part * D, 128), D)
            g_qkv[:, cols] += tn(hqw[n], gqkv[:, cols])

    def partner(k):
        x, y = me % 2, me // 2
        return 2 * (1 - y if k & 2 else y) + (1 - x if k & 1 else x)

    def away(kind, k, n):
        dst, send, recv = ((r.act_hbm, r.act_send, r.act_recv), (r.igrad_hbm, r.ig_send, r.ig_recv))[kind]
        return remote(
            buf.at[partner(k) + 1, n], dst.at[me, n], send.at[k - 1, n], recv.at[k - 1, n], {"pipe": partner(k)}
        )

    def at_home(kind, n):
        dst = (r.act_hbm, r.igrad_hbm)[kind]
        return pltpu.make_async_copy(buf.at[me + 1, n], dst.at[me, n], r.local_sem.at[kind, n])

    def send_all(kind, n):
        first = lax.axis_index("dp") % 2

        @pl.when(first == 0)
        def _():
            away(kind, 1, n).start()
            away(kind, 2, n).start()

        @pl.when(first == 1)
        def _():
            away(kind, 2, n).start()
            away(kind, 1, n).start()

        away(kind, 3, n).start()
        at_home(kind, n).start()

    def acts_sent(n):
        for k in (1, 2, 3):
            away(0, k, n).wait_send()
        at_home(0, n).wait()

    def pushed(n):
        for k in (1, 2, 3):
            away(1, k, n).wait_send()
        at_home(1, n).wait()

    def arrived(k, n):
        for dst, send, recv in ((r.act_hbm, r.act_send, r.act_recv), (r.igrad_hbm, r.ig_send, r.ig_recv)):
            got = dst.at[partner(k), n]
            remote(got, got, send.at[k - 1, n], recv.at[k - 1, n], {"pipe": partner(k)}).wait_recv()

    attention_stash = ((hqw, r.h_hqw), (qkv, r.h_qkv), (probs, r.h_probs), (att, r.h_att))
    mlp_stash = ((hq2, r.h_hq2), (hid, r.h_hid), (dgelu, r.h_dgelu))

    def stash(sec, n, back):
        pairs = mlp_stash if sec else attention_stash
        return [
            pltpu.make_async_copy(*((far.at[n], near.at[n]) if back else (near.at[n], far.at[n])), r.st_sem.at[sec, n, i])
            for i, (near, far) in enumerate(pairs)
        ]

    def load(i, n):
        src = r.cot_hbm if i else r.x_hbm
        return pltpu.make_async_copy(src.at[me, n], buf.at[5 if i else 0, n], r.in_sem.at[i, n])

    def start(copies):
        for copy in copies:
            copy.start()

    def wait(copies):
        for copy in copies:
            copy.wait()

    steps = (step_1, step_2, step_3, step_4, step_5)
    schedule = {
        (2, 0, 0): ((2, 3),),
        (2, 1, 1): ((3, 3),),
        (2, 1, 2): ((1, 2),),
        (1, 0, 0): ((2, 2), (2, 5)),
        (1, 1, 0): ((4, 3),),
        (0, 0, 0): ((3, 2), (3, 5), (2, 1), (5, 3)),
        (0, 0, 1): ((4, 2), (4, 5)),
        (0, 1, 0): ((5, 2), (5, 5)),
        (0, 1, 1): ((3, 1),),
        (0, 1, 2): ((1, 0),),
    }
    after = {3: ((1, 3),), 2: ((1, 5),), 1: ((1, 1),), 0: ()}
    weight_steps = (weights_1, weights_2, weights_3, weights_4) if linked else ()
    gathering = {
        (0, 4): ((3, 0), (4, 0)),
        (0, 0): ((2, 1),),
        (0, 1): ((2, 2), (2, 3), (3, 1)),
        (0, 3): ((4, 1), (3, 2)),
        (1, 3): ((4, 2),),
        (2, 0): ((3, 3),),
        (2, 3): ((4, 3),),
    }

    codes = [pltpu.make_async_copy(r.code_hbm, code, r.code_sem.at[0])]
    start(codes)
    start([load(i, n) for i in range(2) for n in range(canvases)])
    wait(codes)
    for i in range(2):
        wait([load(i, n) for n in range(canvases)])

    @pl.loop(0, canvases)
    def _(n):
        @pl.loop(0, 2)
        def _(b):
            def gather(half, i):
                for (sec, at), todo in gathering.items():
                    if linked and sec % 2 == half and at == i:

                        @pl.when((n == 0) & (b == sec // 2))
                        def _():
                            for step, of in todo:
                                weight_steps[step - 1](of)

            for half, forward in enumerate((attention_forward, mlp_forward)):

                @pl.when(b == 1)
                def _():
                    wait(stash(half, n, False))

                s = 2 * b + half
                forward(b, n, buf.at[s, n], buf.at[s + 1, n], functools.partial(gather, half))

                @pl.when(b == 0)
                def _():
                    start(stash(half, n, False))

                gather(half, 3)

        send_all(0, n)

    @pl.loop(0, 2)
    def _(flipped):
        b = 1 - flipped
        for half, backward in ((1, mlp_backward), (0, attention_backward)):
            sums = ((g_fc1, g_fc2) if half else (g_qkv, g_proj))
            cleared(*sums)

            @pl.loop(0, canvases)
            def _(n):
                def hook(i):
                    for (sec, at, point), todo in schedule.items():
                        if linked and sec % 2 == half and point == i:

                            @pl.when((n == (canvases - 1 if at else 0)) & (b == sec // 2))
                            def _():
                                for step, of in todo:
                                    steps[step - 1](of)

                def free_out():
                    if half:

                        @pl.when(b == 1)
                        def _():
                            acts_sent(n)

                @pl.when(b == 0)
                def _():
                    wait(stash(half, n, True))

                s = 2 * b + half
                backward(b, n, buf.at[s, n], buf.at[s + 2, n], buf.at[s + 1, n], free_out, hook)
                if half == 0:

                    @pl.when((b == 0) & (n < canvases - 1))
                    def _():
                        send_all(1, n)

                @pl.when(b == 1)
                def _():
                    start(stash(half, n, True))

            if linked:
                for i in range(2):
                    todo = after[2 * i + half]
                    if todo:

                        @pl.when(b == i)
                        def _():
                            for step, of in todo:
                                steps[step - 1](of)
            else:
                whole = zip(sums, (r.f_fc1, r.f_fc2) if half else (r.f_qkv, r.f_proj))
                copies = [pltpu.make_async_copy(g, o.at[b], r.go_sem.at[half, i]) for i, (g, o) in enumerate(whole)]
                start(copies)
                wait(copies)

    if linked:
        step_1(4)
        step_2(0)
    send_all(1, canvases - 1)
    if linked:
        step_2(4)
        step_4(1)
        smalls_sent(1)
        step_5(1)
        for step in (step_3, step_4, step_5):
            step(0)
            step(4)
        reductions_done()
        weights_sent()
        for k in range(1, 8):
            pack_copy(k).wait_send()
    for k in range(1, 4):
        for n in range(canvases):
            arrived(k, n)
    for n in range(canvases):
        pushed(n)


def compute(linked, operands):
    canvases = operands["x_hbm"].shape[1]
    shape = jax.ShapeDtypeStruct
    hbm = pl.BlockSpec(memory_space=pl.ANY)
    vmem = pl.BlockSpec(memory_space=pltpu.VMEM)
    dma = pltpu.SemaphoreType.DMA
    full = {
        "wat": ((2, D, 4 * D), BF),
        "fc1": ((2, D, FF), BF),
        "fc2": ((2, FF, D), BF),
        "vec": ((2, 8, FF), F32),
    }
    grads = {
        "g_qkv": ((D, 3 * D), F32),
        "g_proj": ((D, D), F32),
        "g_fc1": ((D, FF), F32),
        "g_fc2": ((FF, D), F32),
        "g_vec": ((2, 8, 8, FF), F32),
        "g_tab": ((2, 2 * PLACES, GROUPS * 128), F32),
    }
    outs = {"act_hbm": ((4, canvases, CELLS, D), BF), "igrad_hbm": ((4, canvases, CELLS, D), BF)}
    kept = {
        "hqw": ((canvases, WROWS, D), BF),
        "qkv": ((canvases, WROWS, 3 * D), BF),
        "probs": ((canvases, WINDOWS * GROUPS, 128, 128), BF),
        "att": ((canvases, WROWS, D), BF),
        "hq2": ((canvases, CELLS, D), BF),
        "hid": ((canvases, CELLS, FF), BF),
        "dgelu": ((canvases, CELLS, FF), BF),
    }
    outs |= {"h_" + name: kind for name, kind in kept.items()}
    scratch = kept | {
        "code": ((canvases, CELLS, 128), jnp.int32),
        "codew": ((WROWS, 128), jnp.int32),
        "buf": ((6, canvases, CELLS, D), BF),
        "canvf": ((CELLS, D), F32),
        "winf": ((WROWS, D), F32),
        "gzw": ((WROWS, D), BF),
        "go": ((WROWS, D), BF),
        "gqkv": ((WROWS, 3 * D), BF),
    }
    sems = {
        "in_sem": (2, canvases),
        "code_sem": (1,),
        "st_sem": (2, canvases, 4),
        "local_sem": (2, canvases),
        "act_send": (3, canvases),
        "act_recv": (3, canvases),
        "ig_send": (3, canvases),
        "ig_recv": (3, canvases),
    }
    if linked:
        outs |= {
            "o_qkv": ((2, 48, 3 * D), F32),
            "o_proj": ((2, 48, D), F32),
            "o_fc1": ((2, 48, FF), F32),
            "o_fc2": ((2, 192, D), F32),
            "o_small": ((2, 8, 64, D), BF),
        }
        scratch |= full | grads
        scratch |= {
            "packs": ((8, 16, 256), BF),
            "l_qkv": ((48, 3 * D), F32),
            "l_proj": ((48, D), F32),
            "l_fc1": ((48, FF), F32),
            "l_fc2": ((192, D), F32),
        }
        for kind, rows in ((kind + "_", rows) for kind, rows in ROWS.items()):
            scratch |= {
                kind + "st_a": ((4, rows, D), BF),
                kind + "rc_a": ((4, rows, D), BF),
                kind + "st_b": ((3, rows, D), BF),
                kind + "rc_b": ((3, rows, D), BF),
                kind + "st_c": ((rows, D), BF),
                kind + "rc_c": ((3, rows // 4, D), BF),
                kind + "fin": ((rows, D), BF),
            }
        sems |= {
            "sh_sem": (4, 2),
            "os_sem": (2,),
            "go_sem": (4, 2),
            "wz_send": (4, 2, 3),
            "wz_recv": (4, 2, 3),
            "wx_send": (4, 2, 3, 3),
            "wx_recv": (4, 2, 3, 3),
            "ws_send": (4, 2, 4),
            "ws_recv": (4, 2, 4),
            "pk_send": (7,),
            "pk_recv": (7,),
            "ra_send": (6,),
            "ra_recv": (6,),
            "rb_send": (6, 3),
            "rb_recv": (6, 3),
            "rc_send": (6, 3),
            "rc_recv": (6, 3),
            "rf_send": (6, 3),
            "rf_recv": (6, 3),
            "rs_send": (2, 7),
            "rs_recv": (2, 7),
        }
    else:
        for name in ("g_vec", "g_tab"):
            outs[name] = grads.pop(name)
        outs |= {name.replace("g_", "f_"): ((2,) + dims, F32) for name, (dims, _) in grads.items()}
        scratch |= grads
        sems["go_sem"] = (4, 2)
    in_vmem = set(full) | {"bias", "pack", "g_vec", "g_tab"}
    names = tuple(operands) + tuple(outs) + tuple(scratch) + tuple(sems)
    results = pl.pallas_call(
        functools.partial(kernel, names, linked, canvases),
        out_shape=tuple(shape(*o) for o in outs.values()),
        in_specs=[vmem if name in in_vmem else hbm for name in operands],
        out_specs=tuple(vmem if name in in_vmem else hbm for name in outs),
        scratch_shapes=[pltpu.VMEM(*v) for v in scratch.values()] + [dma(v) for v in sems.values()],
        compiler_params=pltpu.CompilerParams(
            vmem_limit_bytes=64 * 1024 * 1024 - 65536, collective_id=0, has_side_effects=True
        ),
    )(*operands.values())
    return dict(zip(outs, results))


def place_pairs():
    place = np.arange(PLACES)
    r, c = place // 8, place % 8
    index = (r[None, :] - r[:, None] + WIN - 1) * (2 * WIN - 1) + c[None, :] - c[:, None] + WIN - 1
    real = (r < WIN) & (c < WIN)
    return index, real[:, None] & real[None, :], real


def pair_onehot():
    index, both, _ = place_pairs()
    table = (2 * WIN - 1) ** 2
    hot = (np.where(both, index, -1).reshape(-1)[None, :] == np.arange(table)[:, None])
    return hot.astype(np.float32)


def body(
    inputs,
    cotangent,
    pad_mask,
    region_ids,
    norm1_gain,
    norm1_bias,
    qkv_weight,
    qv_bias,
    rel_table,
    proj_weight,
    proj_bias,
    norm2_gain,
    norm2_bias,
    fc1_weight,
    fc1_bias,
    fc2_weight,
    fc2_bias,
):
    owners = lax.axis_size("dp")
    linked = owners == 8
    mine = lax.axis_index("pipe")

    def own(a):
        return lax.dynamic_index_in_dim(a, mine, 0, keepdims=False)

    code = own(region_ids) * 2 + own(pad_mask)
    code = jnp.broadcast_to(code[:, :, None], code.shape + (128,))

    hot = pair_onehot()
    _, _, real = place_pairs()
    rel = lax.dot_general(
        rel_table.astype(BF), jnp.asarray(hot, BF), (((1,), (0,)), ((), ())), preferred_element_type=F32
    )
    rel = rel.reshape(2, GROUPS, 2, 2, PLACES, PLACES)
    rel = jnp.where(jnp.asarray(real)[None, None, None, None, :, None], rel, MASKED)
    rel = rel.transpose(0, 1, 3, 4, 2, 5).reshape(2, GROUPS, 128, 128)

    operands = {"x_hbm": inputs, "cot_hbm": cotangent, "code_hbm": code, "bias": rel}
    vectors = (norm1_gain, norm1_bias, proj_bias, norm2_gain, norm2_bias, fc2_bias, qv_bias, fc1_bias)
    sizes = [v.shape[1] for v in vectors]
    ends = np.cumsum([0] + sizes)
    if linked:
        pack = jnp.stack([jnp.pad(v, ((0, 0), (0, 256 - v.shape[1]))) for v in vectors], axis=1)
        operands |= {
            "pack": pack.reshape(16, 256).astype(BF),
            "s_qkv": qkv_weight,
            "s_proj": proj_weight,
            "s_fc1": fc1_weight,
            "s_fc2": fc2_weight,
        }
    else:

        def gathered(a):
            return lax.all_gather(a.astype(BF), "dp", axis=1, tiled=True)

        packed = lax.all_gather(jnp.concatenate(vectors, axis=1).astype(BF), "dp", axis=1)
        parts = [packed[:, :, a:b].reshape(2, -1).astype(F32) for a, b in zip(ends[:-1], ends[1:])]
        qv = parts[6]
        parts[6] = jnp.concatenate([qv[:, :D], jnp.zeros_like(qv[:, :D]), qv[:, D:]], axis=1)
        vec = jnp.stack([jnp.pad(p, ((0, 0), (0, FF - p.shape[1]))) for p in parts], axis=1)
        operands |= {
            "wat": jnp.concatenate([gathered(qkv_weight), gathered(proj_weight)], axis=2),
            "fc1": gathered(fc1_weight),
            "fc2": gathered(fc2_weight),
            "vec": vec,
        }

    out = compute(linked, operands)

    def to_owners(g):
        shared = lax.psum_scatter(g, "dp", scatter_dimension=1, tiled=True)
        return lax.psum(shared, "pipe")

    if linked:
        small = out["o_small"]
        g_tab = small[:, :, :16].reshape(2, 128, GROUPS * 128)
        g_vec = jnp.concatenate([small[:, :, 16 + 8 * j : 24 + 8 * j] for j in range(4)], axis=3)
    else:
        g_tab, g_vec = out["g_tab"], out["g_vec"]

    g_vec = jnp.sum(g_vec.astype(F32), axis=2)
    kinds = [g_vec[:, i] for i in range(8)]
    qv_sum = jnp.concatenate([kinds[6][:, :D], kinds[6][:, 2 * D : 3 * D]], axis=1)
    rows = [kinds[0], kinds[1], kinds[2], kinds[3], kinds[4], kinds[5], qv_sum, kinds[7]]
    if linked:
        at = lax.axis_index("dp")
        small = [lax.dynamic_slice_in_dim(v, at * n, n, 1) for v, n in zip(rows, sizes)]
    else:
        rows = [v[:, : n * owners].reshape(2, -1, n) for v, n in zip(rows, sizes)]
        g_small = to_owners(jnp.concatenate(rows, axis=2))[:, 0]
        small = [g_small[:, a:b] for a, b in zip(ends[:-1], ends[1:])]

    pairs = g_tab.reshape(2, 2, PLACES, GROUPS, 2, PLACES).transpose(0, 3, 4, 1, 2, 5)
    pairs = pairs.reshape(2, HEADS, PLACES * PLACES)
    g_table = lax.dot_general(
        jnp.broadcast_to(jnp.asarray(hot, pairs.dtype), (2,) + hot.shape),
        pairs,
        (((2,), (2,)), ((0,), (0,))),
        precision=None if linked else lax.Precision.HIGHEST,
        preferred_element_type=F32,
    )
    if linked:
        big = [out[name] for name in ("o_qkv", "o_proj", "o_fc1", "o_fc2")]
    else:
        g_table = lax.psum(g_table, ("pipe", "dp"))
        big = [to_owners(out[name]) for name in ("f_qkv", "f_proj", "f_fc1", "f_fc2")]

    return (
        out["act_hbm"][None],
        out["igrad_hbm"][None],
        small[0],
        small[1],
        big[0],
        small[6],
        g_table,
        big[1],
        small[2],
        small[3],
        small[4],
        big[2],
        small[7],
        big[3],
        small[5],
    )


def solution(mesh):
    cols = P(None, "dp")
    rows = P(None, "dp", None)
    return jax.shard_map(
        body,
        mesh=mesh,
        in_specs=(
            P(None, "dp", None, None),
            P(None, "dp", None, None),
            rows,
            rows,
            cols,
            cols,
            rows,
            cols,
            P(),
            rows,
            cols,
            cols,
            cols,
            rows,
            cols,
            rows,
            cols,
        ),
        out_specs=(
            P("pipe", None, "dp", None, None),
            P("pipe", None, "dp", None, None),
            cols,
            cols,
            rows,
            cols,
            P(),
            rows,
            cols,
            cols,
            cols,
            rows,
            cols,
            rows,
            cols,
        ),
        check_vma=False,
    )
```
